32 devices in a mesh: exp: 8 (over y, x, core), tp: 4 (over z).
Axes of the slice: x: 2, y: 2, z: 4, core: 2. Of those that a mesh axis runs over, the one named last changes fastest.
Arguments:
- tokens: bfloat16 [4096, 1536], P('exp'), may hold values from -6 to 6
- attn_gain: float32 [1536], replicated, may hold values from 0.1 to 1.9
- moe_gain: float32 [1536], replicated, may hold values from 0.1 to 1.9
- w_qkv: bfloat16 [1536, 2560], P(None, 'tp'), may hold values from -0.15625 to 0.15625
- w_out: bfloat16 [1536, 1536], P('tp'), may hold values from -0.625 to 0.625
- w_router: bfloat16 [1536, 16], replicated, may hold values from -0.078125 to 0.078125
- w_gate: bfloat16 [16, 1536, 512], P('exp', None, 'tp'), may hold values from -0.15625 to 0.15625
- w_up: bfloat16 [16, 1536, 512], P('exp', None, 'tp'), may hold values from -0.15625 to 0.15625
- w_down: bfloat16 [16, 512, 1536], P('exp', 'tp'), may hold values from -1.5 to 1.5
- qkv_down: bfloat16 [1536, 128], replicated, may hold values from -0.15625 to 0.15625
- qkv_up: bfloat16 [128, 2560], P(None, 'tp'), may hold values from -1.5 to 1.5
- out_down: bfloat16 [1536, 128], P('tp'), may hold values from -0.625 to 0.625
- out_up: bfloat16 [128, 1536], replicated, may hold values from -1.5 to 1.5
- lengths: int32 [8, 4], P('exp'), may hold values from 1 to 341, 448 in all within a row
- adapter_index: int32 [8, 4], P('exp'), may hold values from 0 to 7
- loss_mask: int32 [4096], P('exp'), may hold values 0 or 1
- routes: int32 [4096, 8], P('exp'), may hold values from 0 to 15, all different within a row; in each aligned block of 512 rows (0 to 511, 512 to 1023, ...) at most 512 rows name the same one
- upstream: bfloat16 [4096, 1536], P('exp'), may hold values from -6 to 6
Outputs:
- output: bfloat16 [4096, 1536], P('exp')
- input_grad: bfloat16 [4096, 1536], P('exp')
- grad_qkv_down: float32 [1536, 128], replicated
- grad_qkv_up: float32 [128, 2560], P(None, 'tp')
- grad_out_down: float32 [1536, 128], P('tp')
- grad_out_up: float32 [128, 1536], replicated
The draws below stay inside these ranges and needn't reach their ends.
Inputs may be any that keep to these rules, and one draw needn't show every extreme that they name: `routes`: each row names 8 different experts; in each aligned block of 512 rows (the rows of one device) no expert is named more than 512 times, a bound that some block reaches. Each device's 4 lengths sum to 448, and the largest is exactly 341.
All inputs are finite; a program needn't handle non-finite values. No bound on the sum of `loss_mask` on one device may be relied on, other than what follows from the above.
Results may differ from the reference program's by a relative error of at most 0.025.
Values may be sent and summed in bfloat16 or wider, within the bound.
No kernel may reach another device: no remote copies, remote signals or barrier semaphores. Data moves between devices by JAX's collectives and lax.ppermute only.
A program may use at most 256 MiB of HBM per device.

```python
import math
import jax
import jax.numpy as jnp
import numpy as np
from jax import lax

D = 1536
HEADS = 24
KV_HEADS = 8
HD = 64
FF = 512
TOP = 8
RANK = 16
ADAPTERS = 8
DOCS = 4
TOK_DEV = 512
EXPERTS = 16
TOKENS = 4096
LIVE = 448
DOC_MOST = 341
CAP = 512
QKV_W = 2560
BLOCK_ROWS = 512
N_EXP = 8
N_TP = 4


def touch_ends(entries, rng, low, high):
    longest = entries.shape.index(max(entries.shape))
    spots = []
    for shift in (0, 1):
        where = [jax.random.randint(jax.random.fold_in(rng, axis), (), 0, length) for axis, length in enumerate(entries.shape)]
        where[longest] = (where[longest] + shift) % entries.shape[longest]
        spots.append(tuple(where))
    return entries.at[spots[0]].set(low).at[spots[1]].set(high)


def level_of(rng, dims, cuts, least, high):
    loudness = 1.0
    for axis_at, blocks in cuts:
        steps = jax.random.uniform(jax.random.fold_in(jax.random.fold_in(rng, 6), axis_at), (blocks,), jnp.float32, least / len(cuts), high / len(cuts))
        loudness = loudness * jnp.repeat(jnp.exp(steps), dims[axis_at] // blocks).reshape((-1,) + (1,) * (len(dims) - 1 - axis_at))
    return loudness


def split_up(number_of, total, reach, slope):
    weights = [(1 << 20) // math.isqrt(grade ** slope) + 1 for grade in range(2, number_of + 1)]
    rest, holding = total - reach - (number_of - 1), [1] * (number_of - 1)
    while rest > 0:
        candidates = [i for i in range(number_of - 1) if holding[i] < reach]
        pool, remaining = sum([weights[i] for i in candidates]), rest
        for i in candidates:
            extra = min(reach - holding[i], max(1, remaining * weights[i] // pool), rest)
            holding[i] = holding[i] + extra
            rest = rest - extra
    return np.array([reach] + holding)


def ragged_sizes(rng, amount, total, most, skew):
    if amount == 2:
        one = jax.random.randint(rng, (), max(1, total - most), min(most, total - 1) + 1)
        return jnp.stack([one, total - one])
    sizes = jnp.asarray(split_up(amount, total, most, skew), jnp.int32)
    pairs = (amount - 1) // 2
    source_of, receiver = sizes[1:1 + 2 * pairs:2], sizes[2:2 + 2 * pairs:2]
    margin = jnp.minimum(source_of - 1, most - receiver)
    shifted = jax.random.randint(jax.random.fold_in(rng, 1), (pairs,), 0, 1 << 20) % (margin + 1)
    sizes = sizes.at[1:1 + 2 * pairs:2].set(source_of - shifted).at[2:2 + 2 * pairs:2].set(receiver + shifted)
    return sizes[jax.random.permutation(jax.random.fold_in(rng, 2), amount)]


def assign_block(rng, own, number, rows, count, top, limit, lean):
    sequence = jax.random.permutation(rng, count)
    crowded, common = shares(count, rows * top, limit, lean, True), shares(count, rows * top, limit, lean, False)
    places = jnp.arange(count)

    def named(sizes, rotation):
        used = int((sizes > 0).sum())
        fixed = max(1, used // 4)
        passed = fixed + (places - fixed + rotation * (used - fixed)) % max(1, count - fixed)
        return jnp.zeros((count,), jnp.int32).at[sequence[jnp.where(places < fixed, places, passed)]].set(jnp.asarray(sizes, jnp.int32))

    sizes = jnp.where(number % 4 == 0, named(crowded, number // 4), named(common, number - number // 4 - 1))
    mixed = jax.random.permutation(jax.random.fold_in(own, 3), count)
    source_of, sink = mixed[0:count // 2 * 2:2], mixed[1:count // 2 * 2:2]
    room = jnp.minimum(sizes[source_of] - 1, limit - sizes[sink]) // 2
    room = jnp.where((source_of == sequence[0]) | (sink == sequence[0]) | (sizes[sink] == 0), 0, jnp.maximum(room, 0))
    passed = jax.random.randint(jax.random.fold_in(own, 4), (count // 2,), 0, 1 << 20) % (room + 1)
    sizes = sizes.at[source_of].add(-passed).at[sink].add(passed)
    items = jnp.searchsorted(jnp.cumsum(sizes), jnp.arange(rows * top), side="right").astype(jnp.int32)
    table = items.reshape(top, rows).T
    table = table[jax.random.permutation(jax.random.fold_in(own, 1), rows)]
    rotation = jax.random.randint(jax.random.fold_in(own, 2), (rows, 1), 0, top)
    return jnp.take_along_axis(table, (jnp.arange(top)[None, :] + rotation) % top, axis=1)


def shares(count, total, bound, slope, full):
    loads = [(1 << 20) // math.isqrt(grade ** slope) + 1 for grade in range(1, count + 1)]
    largest = bound if full else min(bound, max(-(-total // count), total * loads[0] // sum(loads)))
    least = 1 if total - largest >= count - 1 else 0
    counts, surplus = [largest] + [least] * (count - 1), total - largest - least * (count - 1)
    while surplus > 0:
        free = [i for i in range(1, count) if counts[i] < largest] or [i for i in range(1, count) if counts[i] < bound]
        pool, left = sum([loads[i] for i in free]), surplus
        for i in free:
            more = min(bound - counts[i], max(1, left * loads[i] // pool), surplus)
            counts[i] = counts[i] + more
            surplus = surplus - more
    return np.array(counts)


def centred(rng, extent, deviation, bound, cuts=(), kind=jnp.bfloat16):
    values = jax.random.normal(rng, extent, jnp.float32) * deviation
    if len(cuts) > 0:
        values = level_of(rng, extent, cuts, -0.22, 0.18) * values
    return jnp.clip(values, min=-bound, max=bound).astype(kind)


def setup_inputs(seed: int = 0) -> dict:
    key_of = jax.random.split(jax.random.key(seed), 19)
    tokens = centred(key_of[0], (TOKENS, D), 1.0, 6.0, ((0, 8),))
    attn_gain = jnp.clip(1.0 + 0.18 * jax.random.normal(key_of[1], (D,), jnp.float32), 0.1, 1.9)
    moe_gain = jnp.clip(1.0 + 0.18 * jax.random.normal(key_of[2], (D,), jnp.float32), 0.1, 1.9)
    w_qkv = centred(key_of[3], (D, QKV_W), D ** -0.5, 0.15625, ((1, 4),))
    w_out = centred(key_of[4], (HEADS * HD, D), (HEADS * HD // 16) ** -0.5, 0.625, ((0, 4),))
    w_router = centred(key_of[5], (D, EXPERTS), (4 * D) ** -0.5, 0.078125)
    w_gate = centred(key_of[6], (EXPERTS, D, FF), D ** -0.5, 0.15625, ((0, 8), (2, 4)))
    w_up = centred(key_of[7], (EXPERTS, D, FF), D ** -0.5, 0.15625, ((0, 8), (2, 4)))
    w_down = centred(key_of[8], (EXPERTS, FF, D), (FF // 32) ** -0.5, 1.5, ((0, 8), (1, 4)))
    qkv_down = centred(key_of[9], (D, ADAPTERS * RANK), D ** -0.5, 0.15625)
    qkv_up = centred(key_of[10], (ADAPTERS * RANK, QKV_W), RANK ** -0.5, 1.5, ((1, 4),))
    out_down = centred(key_of[11], (HEADS * HD, ADAPTERS * RANK), (HEADS * HD // 16) ** -0.5, 0.625, ((0, 4),))
    out_up = centred(key_of[12], (ADAPTERS * RANK, D), RANK ** -0.5, 1.5)
    lengths = jax.vmap(lambda own: ragged_sizes(own, DOCS, LIVE, DOC_MOST, 2))(jax.random.split(key_of[13], N_EXP)).reshape((N_EXP, DOCS)).astype(jnp.int32)
    adapter_index = touch_ends(jax.random.randint(key_of[14], (N_EXP, DOCS), 0, ADAPTERS), jax.random.fold_in(key_of[14], 1), 0, ADAPTERS - 1).astype(jnp.int32)
    loss_mask = touch_ends((jax.random.randint(key_of[15], (TOKENS,), 0, 4) < 3).astype(jnp.int32), jax.random.fold_in(key_of[15], 1), 0, 1)
    routes_keys = jax.random.split(jax.random.fold_in(key_of[16], 1), TOKENS // TOK_DEV)
    routes_turns = jax.random.permutation(jax.random.fold_in(key_of[16], 3), TOKENS // TOK_DEV)
    routes = jax.vmap(lambda own, number: assign_block(jax.random.fold_in(key_of[16], 2), own, number, TOK_DEV, EXPERTS, TOP, CAP, 2))(routes_keys, routes_turns).reshape((TOKENS, TOP))
    upstream = centred(key_of[17], (TOKENS, D), 1.0, 6.0, ((0, 8),))
    return {"tokens": tokens, "attn_gain": attn_gain, "moe_gain": moe_gain, "w_qkv": w_qkv, "w_out": w_out, "w_router": w_router, "w_gate": w_gate, "w_up": w_up, "w_down": w_down, "qkv_down": qkv_down, "qkv_up": qkv_up, "out_down": out_down, "out_up": out_up, "lengths": lengths, "adapter_index": adapter_index, "loss_mask": loss_mask, "routes": routes, "upstream": upstream}


EPS = 1e-06
ROPE_BASE = 10000.0
EXACT_PREC = lax.Precision.HIGHEST

@jax.custom_vjp
def low(v):
    return lax.optimization_barrier(v.astype(jnp.bfloat16)).astype(jnp.float32)

@jax.custom_vjp
def low_back(v):
    return v

def low_keep(v):
    return (low(v), None)

def low_pass(kept, grad):
    return (grad,)

def back_keep(v):
    return (v, None)

def back_low(kept, grad):
    return (low(grad),)
low.defvjp(low_keep, low_pass)
low_back.defvjp(back_keep, back_low)

def rms_norm(vectors, gain_vec):
    inv_root = lax.rsqrt(lax.optimization_barrier(jnp.mean(vectors * vectors, axis=-1, keepdims=True)) + EPS)
    return vectors * inv_root * gain_vec

def layout(length_row, index_row):
    places = jnp.arange(TOK_DEV, dtype=jnp.int32)
    doc_ends = jnp.cumsum(length_row).astype(jnp.int32)
    doc_starts = (doc_ends - length_row).astype(jnp.int32)
    member = (places[:, None] >= doc_starts[None, :]) & (places[:, None] < doc_ends[None, :])
    occupied = jnp.any(member, axis=1)
    position = lax.optimization_barrier(jnp.sum(jnp.where(member, places[:, None] - doc_starts[None, :], 0), axis=1)).astype(jnp.int32)
    owner_doc = lax.optimization_barrier(jnp.sum(jnp.where(member, jnp.arange(DOCS, dtype=jnp.int32)[None, :], 0), axis=1)).astype(jnp.int32)
    doc_ident = jnp.where(occupied, owner_doc, DOCS + places).astype(jnp.int32)
    chosen = lax.optimization_barrier(jnp.sum(jnp.where(member, index_row[None, :], 0), axis=1)).astype(jnp.int32)
    adapter_pick = occupied[:, None] & (chosen[:, None] == jnp.arange(ADAPTERS, dtype=jnp.int32)[None, :])
    rank_mask = jnp.repeat(jnp.where(adapter_pick, 1.0, 0.0).astype(jnp.float32), RANK, axis=1)
    return (occupied, position, doc_ident, rank_mask)

def angles(position):
    half_width = HD // 2
    frequency = jnp.exp(-math.log(ROPE_BASE) * jnp.arange(half_width, dtype=jnp.float32) * 2.0 / HD)
    turned = position.astype(jnp.float32)[:, None] * frequency[None, :]
    return (jnp.cos(turned), jnp.sin(turned))

def rotate(vectors, cosine, sine_table):
    half_width = vectors.shape[-1] // 2
    front_half = vectors[..., :half_width]
    back_half = vectors[..., half_width:]
    return jnp.concatenate([front_half * cosine - back_half * sine_table, back_half * cosine + front_half * sine_table], axis=-1)

def tables(route_rows, experts, capacity):
    flat_route = route_rows.reshape(-1)
    pair_count = flat_route.shape[0]
    one_hot = (flat_route[:, None] == jnp.arange(experts, dtype=jnp.int32)[None, :]).astype(jnp.int32)
    slot_rank = lax.optimization_barrier(jnp.sum(one_hot * (jnp.cumsum(one_hot, axis=0) - 1), axis=1))
    slot_of = (flat_route * capacity + slot_rank).astype(jnp.int32)
    source = jnp.full((experts * capacity,), pair_count, jnp.int32).at[slot_of].set(jnp.arange(pair_count, dtype=jnp.int32))
    return (slot_of.reshape(route_rows.shape), source)

def expert_apply(pieces):
    row_block, gate_w, up_w, down_w = pieces
    part_width = FF // N_TP
    copies = low_back(jnp.broadcast_to(row_block[None], (N_TP,) + row_block.shape))
    gate_split = gate_w.reshape(D, N_TP, part_width).transpose(1, 0, 2)
    up_split = up_w.reshape(D, N_TP, part_width).transpose(1, 0, 2)
    down_split = down_w.reshape(N_TP, part_width, D)
    pre_gate = low_back(jnp.einsum('jcd,jdf->jcf', copies, gate_split, precision=EXACT_PREC))
    pre_up = low_back(jnp.einsum('jcd,jdf->jcf', copies, up_split, precision=EXACT_PREC))
    hidden = low(jax.nn.silu(pre_gate) * pre_up)
    partial_value = low(jnp.einsum('jcf,jfd->jcd', hidden, down_split, precision=EXACT_PREC))
    return lax.optimization_barrier(jnp.sum(partial_value, axis=0))

def layer_forward(inputs, qkv_down, qkv_up, out_down, out_up, constants):
    attn_gain, moe_gain, w_qkv, w_out, w_router, w_gate, w_up, w_down, cosine, sine_table, doc_ident, rank_mask, route_rows, slot_of, row_of = constants
    per_group = HEADS // KV_HEADS
    attn_in = low(rms_norm(inputs, attn_gain))
    low_q = low(low_back(jnp.dot(attn_in, qkv_down, precision=EXACT_PREC) * rank_mask))
    projected = low_back(jnp.dot(attn_in, w_qkv, precision=EXACT_PREC) + jnp.dot(low_q, qkv_up, precision=EXACT_PREC))
    projected = projected.reshape(TOK_DEV, KV_HEADS, per_group + 2, HD)
    query_rows = low(rotate(projected[:, :, :per_group], cosine[:, None, None], sine_table[:, None, None]))
    key_rows = low(rotate(projected[:, :, per_group], cosine[:, None], sine_table[:, None]))
    val_rows = low(projected[:, :, per_group + 1])
    score_scale = 1.0 / math.sqrt(HD)
    places = jnp.arange(TOK_DEV, dtype=jnp.int32)
    blocks = TOK_DEV // BLOCK_ROWS

    def attend(pieces):
        q_blk, q_place, q_ident = pieces
        scores = low_back(jnp.einsum('qgrd,kgd->grqk', q_blk, key_rows, precision=EXACT_PREC) * score_scale)
        allowed = (q_ident[:, None] == doc_ident[None, :]) & (places[None, :] <= q_place[:, None])
        scores = jnp.where(allowed, scores, -1e+30)
        row_max = lax.optimization_barrier(jnp.max(scores, axis=-1, keepdims=True))
        lifted = jnp.exp(scores - row_max)
        weights = low(lifted / lax.optimization_barrier(jnp.sum(lifted, axis=-1, keepdims=True)))
        return jnp.einsum('grqk,kgd->qgrd', weights, val_rows, precision=EXACT_PREC)
    attended = lax.map(jax.checkpoint(attend), (query_rows.reshape(blocks, BLOCK_ROWS, KV_HEADS, per_group, HD), places.reshape(blocks, BLOCK_ROWS), doc_ident.reshape(blocks, BLOCK_ROWS)))
    head_out = low(low_back(attended.reshape(TOK_DEV, HEADS * HD)))
    low_o = low(low_back(jnp.dot(head_out, out_down, precision=EXACT_PREC) * rank_mask))
    branch = low_back(jnp.dot(head_out, w_out, precision=EXACT_PREC) + jnp.dot(low_o, out_up, precision=EXACT_PREC))
    residual = inputs + branch
    normed = low(rms_norm(residual, moe_gain))
    logits = low_back(jnp.dot(normed, w_router, precision=EXACT_PREC))
    one_hot = route_rows[:, :, None] == jnp.arange(EXPERTS, dtype=jnp.int32)[None, None, :]
    chosen = lax.optimization_barrier(jnp.sum(jnp.where(one_hot, logits[:, None, :], 0.0), axis=-1))
    gate_probs = jax.nn.softmax(chosen, axis=-1)
    padded = jnp.concatenate([normed, jnp.zeros((1, D), normed.dtype)], axis=0)
    grouped = padded[row_of].reshape(EXPERTS, CAP, D)
    expert_out = lax.map(jax.checkpoint(expert_apply), (grouped, w_gate, w_up, w_down))
    routed = low_back(expert_out.reshape(EXPERTS * CAP, D)[slot_of])
    return residual + lax.optimization_barrier(jnp.sum(gate_probs[:, :, None] * routed, axis=1))

def reference(tokens, attn_gain, moe_gain, w_qkv, w_out, w_router, w_gate, w_up, w_down, qkv_down, qkv_up, out_down, out_up, lengths, adapter_index, loss_mask, routes, upstream):
    frozen = tuple((member.astype(jnp.float32) for member in (w_qkv, w_out, w_router, w_gate, w_up, w_down)))
    adapters = tuple((member.astype(jnp.float32) for member in (qkv_down, qkv_up, out_down, out_up)))

    def block_step(totals, pieces):
        token_rows, length_row, index_row, mask_row, route_rows, upstream_rows = pieces
        occupied, position, doc_ident, rank_mask = layout(length_row, index_row)
        cosine, sine_table = angles(position)
        slot_of, source = tables(route_rows, EXPERTS, CAP)
        constants = (attn_gain, moe_gain) + frozen + (cosine, sine_table, doc_ident, rank_mask, route_rows, slot_of, source // TOP)

        def forward(inputs, first_a, second_a, third_a, fourth_a):
            return layer_forward(inputs, first_a, second_a, third_a, fourth_a, constants)
        outputs, pullback = jax.vjp(forward, token_rows.astype(jnp.float32), *adapters)
        live_mask = jnp.where(occupied & (mask_row > 0), 1.0, 0.0).astype(jnp.float32)
        gradients = pullback(upstream_rows.astype(jnp.float32) * live_mask[:, None])
        totals = tuple((running + update for running, update in zip(totals, gradients[1:])))
        return (totals, (outputs.astype(jnp.bfloat16), gradients[0].astype(jnp.bfloat16)))
    initial = tuple((jnp.zeros(member.shape, jnp.float32) for member in adapters))
    totals, (out_rows, grad_rows) = lax.scan(block_step, initial, (tokens.reshape(N_EXP, TOK_DEV, D), lengths, adapter_index, loss_mask.reshape(N_EXP, TOK_DEV), routes.reshape(N_EXP, TOK_DEV, TOP), upstream.reshape(N_EXP, TOK_DEV, D)))
    return (out_rows.reshape(TOKENS, D), grad_rows.reshape(TOKENS, D), totals[0], totals[1], totals[2], totals[3])
```

```python
import math

import jax
import jax.numpy as jnp
from jax import lax
from jax.sharding import PartitionSpec as P

D = 1536
HEADS = 24
KV_HEADS = 8
HD = 64
TOP = 8
RANK = 16
ADAPTERS = 8
EXP_DEV = 2
DOCS = 4
TOK_DEV = 512


EPS = 1e-06
ROPE_BASE = 10000.0


def product(left_m, right_m):
    return jnp.dot(left_m, right_m, preferred_element_type=jnp.float32)


def contract(einsum_form, left_m, right_m):
    return jnp.einsum(einsum_form, left_m, right_m, preferred_element_type=jnp.float32)


def rms_norm(vectors, gain_vec):
    inv_root = lax.rsqrt(jnp.mean(vectors * vectors, axis=-1, keepdims=True) + EPS)
    return vectors * inv_root * gain_vec


def rms_norm_back(vectors, gain_vec, upstream_grad):
    inv_root = lax.rsqrt(jnp.mean(vectors * vectors, axis=-1, keepdims=True) + EPS)
    weighted = upstream_grad * gain_vec
    return inv_root * weighted - vectors * (inv_root * inv_root * inv_root) * jnp.mean(
        vectors * weighted, axis=-1, keepdims=True
    )


def layout(length_row, index_row):
    places = jnp.arange(TOK_DEV, dtype=jnp.int32)
    doc_ends = jnp.cumsum(length_row)
    doc_starts = doc_ends - length_row
    member = (places[:, None] >= doc_starts[None, :]) & (places[:, None] < doc_ends[None, :])
    occupied = jnp.any(member, axis=1)
    position = jnp.sum(jnp.where(member, places[:, None] - doc_starts[None, :], 0), axis=1)
    owner_doc = jnp.sum(jnp.where(member, jnp.arange(DOCS, dtype=jnp.int32)[None, :], 0), axis=1)
    doc_ident = jnp.where(occupied, owner_doc, DOCS + places)
    chosen = jnp.sum(jnp.where(member, index_row[None, :], 0), axis=1)
    adapter_pick = occupied[:, None] & (
        chosen[:, None] == jnp.arange(ADAPTERS, dtype=jnp.int32)[None, :]
    )
    rank_mask = jnp.repeat(jnp.where(adapter_pick, 1.0, 0.0).astype(jnp.float32), RANK, axis=1)
    return (occupied, position, doc_ident, rank_mask)


def angles(position):
    half_width = HD // 2
    frequency = jnp.exp(-math.log(ROPE_BASE) * jnp.arange(half_width, dtype=jnp.float32) * 2.0 / HD)
    turned = position.astype(jnp.float32)[:, None] * frequency[None, :]
    return (jnp.cos(turned), jnp.sin(turned))


def rotate(vectors, cosine, sine_table):
    half_width = vectors.shape[-1] // 2
    front_half = vectors[..., :half_width]
    back_half = vectors[..., half_width:]
    return jnp.concatenate(
        [
            front_half * cosine - back_half * sine_table,
            back_half * cosine + front_half * sine_table,
        ],
        axis=-1,
    )


def moe(normed, cot_low, gates, gate_up, down):
    width = down.shape[1]
    both = contract("td,edf->tef", normed, gate_up)
    pre_gate = both[:, :, :width]
    pre_up = both[:, :, width:]
    sigmoid_g = jax.nn.sigmoid(pre_gate)
    activated = pre_gate * sigmoid_g
    hidden = (activated * pre_up).astype(jnp.bfloat16).astype(jnp.float32)
    inner_raw = contract("td,efd->tef", cot_low, down)
    gate_part = jnp.sum(hidden * inner_raw, axis=-1)
    moe_part = contract("tef,efd->td", (gates[:, :, None] * hidden).astype(jnp.bfloat16), down)
    inner_grad = inner_raw * gates[:, :, None]
    grad_gate = inner_grad * pre_up * sigmoid_g * (1.0 + pre_gate * (1.0 - sigmoid_g))
    grad_up = inner_grad * activated
    grad_both = jnp.concatenate([grad_gate, grad_up], axis=2).astype(jnp.bfloat16)
    normed_part = contract("tef,edf->td", grad_both, gate_up)
    return (moe_part, gate_part, normed_part)


def body(
    tokens,
    attn_gain,
    moe_gain,
    w_qkv,
    w_out,
    w_router,
    w_gate,
    w_up,
    w_down,
    qkv_down,
    qkv_up,
    out_down,
    out_up,
    lengths,
    adapter_index,
    loss_mask,
    routes,
    upstream,
):
    n_exp = lax.axis_size("exp")
    groups = KV_HEADS // lax.axis_size("tp")
    per_group = HEADS // KV_HEADS
    experts = EXP_DEV * n_exp
    gate_up = lax.all_gather(jnp.concatenate([w_gate, w_up], axis=2), "exp", axis=0, tiled=True)
    down = lax.all_gather(w_down, "exp", axis=0, tiled=True)
    block_rows = min(512, TOK_DEV)
    blocks = TOK_DEV // block_rows
    score_scale = 1.0 / math.sqrt(HD)
    places = jnp.arange(TOK_DEV, dtype=jnp.int32)
    occupied, position, doc_ident, rank_mask = layout(lengths[0], adapter_index[0])
    mask_low = rank_mask.astype(jnp.bfloat16)
    cosine, sine_table = angles(position)
    inputs = tokens.astype(jnp.float32)
    attn_in = rms_norm(inputs, attn_gain).astype(jnp.bfloat16)
    low_q = (product(attn_in, qkv_down) * rank_mask).astype(jnp.bfloat16)
    projected = (product(attn_in, w_qkv) + product(low_q, qkv_up)).reshape(
        TOK_DEV, groups, per_group + 2, HD
    )
    query_rows = rotate(
        projected[:, :, :per_group], cosine[:, None, None], sine_table[:, None, None]
    ).astype(jnp.bfloat16)
    key_rows = rotate(projected[:, :, per_group], cosine[:, None], sine_table[:, None]).astype(
        jnp.bfloat16
    )
    val_rows = projected[:, :, per_group + 1].astype(jnp.bfloat16)

    def masked_scores(q_blk, q_place, q_ident):
        scores = contract("qgrd,kgd->grqk", q_blk, key_rows) * score_scale
        allowed = (q_ident[:, None] == doc_ident[None, :]) & (places[None, :] <= q_place[:, None])
        return jnp.where(allowed, scores, -1e30)

    def attend(pieces):
        q_blk, q_place, q_ident = pieces
        scores = masked_scores(q_blk, q_place, q_ident)
        row_max = jnp.max(scores, axis=-1, keepdims=True)
        lifted = jnp.exp(scores - row_max)
        row_total = jnp.sum(lifted, axis=-1, keepdims=True)
        weights = (lifted / row_total).astype(jnp.bfloat16)
        return (
            contract("grqk,kgd->qgrd", weights, val_rows),
            row_max[..., 0] + jnp.log(row_total[..., 0]),
        )

    query_blocks = query_rows.reshape(blocks, block_rows, groups, per_group, HD)
    place_blocks = places.reshape(blocks, block_rows)
    ident_blocks = doc_ident.reshape(blocks, block_rows)
    attended, log_totals = lax.map(attend, (query_blocks, place_blocks, ident_blocks))
    head_rows = attended.reshape(TOK_DEV, groups * per_group * HD).astype(jnp.bfloat16)
    attn_base, low_rank = (
        lax.psum(product(head_rows, w_out).astype(jnp.bfloat16), "tp").astype(jnp.float32),
        lax.psum((product(head_rows, out_down) * rank_mask).astype(jnp.bfloat16), "tp").astype(
            jnp.float32
        ),
    )
    low_o = low_rank.astype(jnp.bfloat16)
    residual = inputs + attn_base + product(low_o, out_up)
    normed = rms_norm(residual, moe_gain).astype(jnp.bfloat16)
    logits = product(normed, w_router)
    one_hot = routes[:, :, None] == jnp.arange(experts, dtype=jnp.int32)[None, None, :]
    routed = jnp.any(one_hot, axis=1)
    gates = jax.nn.softmax(jnp.where(routed, logits, -1e30), axis=-1)
    live_mask = jnp.where(occupied & (loss_mask > 0), 1.0, 0.0).astype(jnp.float32)
    cotangent = upstream.astype(jnp.float32) * live_mask[:, None]
    cot_low = cotangent.astype(jnp.bfloat16)
    moe_part, gate_part, normed_part = moe(normed, cot_low, gates, gate_up, down)
    logit_grad = (
        gates * (gate_part - jnp.sum(gates * gate_part, axis=-1, keepdims=True))
    ).astype(jnp.bfloat16)
    normed_part = (normed_part + product(logit_grad, w_router.T)).astype(jnp.bfloat16)
    normed_sum = lax.psum(normed_part, "tp")
    normed_sum, moe_part = lax.optimization_barrier((normed_sum, moe_part.astype(jnp.bfloat16)))
    normed_grad = normed_sum.astype(jnp.float32)
    moe_out = lax.psum(moe_part, "tp").astype(jnp.float32)
    output = (residual + moe_out).astype(jnp.bfloat16)
    residual_grad = cotangent + rms_norm_back(residual, moe_gain, normed_grad)
    branch_grad = residual_grad.astype(jnp.bfloat16)
    low_o_grad = product(branch_grad, out_up.T).astype(jnp.bfloat16) * mask_low
    out_up_part = contract("tr,td->rd", low_o, branch_grad)
    head_grad = (product(branch_grad, w_out.T) + product(low_o_grad, out_down.T)).astype(
        jnp.bfloat16
    )
    out_down_part = contract("tc,tr->cr", head_rows, low_o_grad)
    grad_blocks = head_grad.reshape(blocks, block_rows, groups, per_group, HD)

    def attend_back(carried, pieces):
        key_acc, val_acc = carried
        q_blk, q_place, q_ident, lse_blk, g_blk = pieces
        weights = jnp.exp(masked_scores(q_blk, q_place, q_ident) - lse_blk[..., None])
        weight_grad = contract("qgrd,kgd->grqk", g_blk, val_rows)
        score_grad = (
            weights * (weight_grad - jnp.sum(weights * weight_grad, axis=-1, keepdims=True))
        ).astype(jnp.bfloat16)
        query_grad = contract("grqk,kgd->qgrd", score_grad, key_rows) * score_scale
        key_acc = key_acc + contract("grqk,qgrd->kgd", score_grad, q_blk) * score_scale
        val_acc = val_acc + contract("grqk,qgrd->kgd", weights.astype(jnp.bfloat16), g_blk)
        return ((key_acc, val_acc), query_grad)

    zero_acc = jnp.zeros((TOK_DEV, groups, HD), jnp.float32)
    (key_grad, val_grad), query_grad = lax.scan(
        attend_back,
        (zero_acc, zero_acc),
        (query_blocks, place_blocks, ident_blocks, log_totals, grad_blocks),
    )
    query_grad = rotate(
        query_grad.reshape(TOK_DEV, groups, per_group, HD),
        cosine[:, None, None],
        -sine_table[:, None, None],
    )
    key_grad = rotate(key_grad, cosine[:, None], -sine_table[:, None])
    projected_grad = (
        jnp.concatenate([query_grad, key_grad[:, :, None], val_grad[:, :, None]], axis=2)
        .reshape(TOK_DEV, -1)
        .astype(jnp.bfloat16)
    )
    qkv_up_part = contract("tr,tc->rc", low_q, projected_grad)
    attn_grad, low_q_grad = (
        lax.psum(contract("tc,dc->td", projected_grad, w_qkv).astype(jnp.bfloat16), "tp").astype(
            jnp.float32
        ),
        lax.psum(contract("tc,rc->tr", projected_grad, qkv_up).astype(jnp.bfloat16), "tp").astype(
            jnp.float32
        ),
    )
    low_q_grad = low_q_grad.astype(jnp.bfloat16) * mask_low
    attn_grad = attn_grad + contract("tr,dr->td", low_q_grad, qkv_down)
    qkv_down_part = contract("td,tr->dr", attn_in, low_q_grad)
    input_grad = (residual_grad + rms_norm_back(inputs, attn_gain, attn_grad)).astype(jnp.bfloat16)
    summed = (
        lax.psum(qkv_down_part.astype(jnp.bfloat16), "exp").astype(jnp.float32),
        lax.psum(qkv_up_part.astype(jnp.bfloat16), "exp").astype(jnp.float32),
        lax.psum(out_down_part.astype(jnp.bfloat16), "exp").astype(jnp.float32),
        lax.psum(out_up_part.astype(jnp.bfloat16), "exp").astype(jnp.float32),
    )
    return (output, input_grad, summed[0], summed[1], summed[2], summed[3])


def solution(mesh):
    placed = (
        P("exp", None),
        P(),
        P(),
        P(None, "tp"),
        P("tp", None),
        P(),
        P("exp", None, "tp"),
        P("exp", None, "tp"),
        P("exp", "tp", None),
        P(),
        P(None, "tp"),
        P("tp", None),
        P(),
        P("exp", None),
        P("exp", None),
        P("exp"),
        P("exp", None),
        P("exp", None),
    )
    return jax.shard_map(
        body,
        mesh=mesh,
        in_specs=placed,
        out_specs=(P("exp", None), P("exp", None), P(), P(None, "tp"), P("tp", None), P()),
        check_vma=False,
    )
```

```python
import functools
import math

import jax
import jax.numpy as jnp
import numpy as np
from jax import lax
from jax.experimental import pallas as pl
from jax.experimental.pallas import tpu as pltpu
from jax.sharding import PartitionSpec as P

D = 1536
HEADS = 24
KV_HEADS = 8
HD = 64
TOP = 8
RANK = 16
ADAPTERS = 8
EXP_DEV = 2
DOCS = 4
TOK_DEV = 512
FF = 512
EPS = 1e-06
ROPE_BASE = 10000.0

PER = HEADS // KV_HEADS
LANES = 128
ROWS = 128
F32 = jnp.float32
BF16 = jnp.bfloat16
MIB = 2**20
NT = (((1,), (1,)), ((), ()))
TN = (((0,), (0,)), ((), ()))
IN_VMEM = pl.BlockSpec(memory_space=pltpu.VMEM)
IN_SMEM = pl.BlockSpec(memory_space=pltpu.SMEM)
IN_HBM = pl.BlockSpec(memory_space=pl.ANY)


def dot(left, right):
    return jnp.dot(left, right, preferred_element_type=F32)


def dot_nt(left, right):
    return lax.dot_general(left, right, NT, preferred_element_type=F32)


def dot_tn(left, right):
    return lax.dot_general(left, right, TN, preferred_element_type=F32)


def shape(dims, dtype):
    return jax.ShapeDtypeStruct(dims, dtype)


def turn_tables(rows):
    half = HD // 2
    frequency = np.exp(-math.log(ROPE_BASE) * np.arange(half, dtype=np.float64) * 2.0 / HD)
    turned = np.arange(rows, dtype=np.float64)[:, None] * frequency[None, :]
    cosine, sine = np.cos(turned), np.sin(turned)
    return (
        jnp.asarray(np.concatenate([cosine] * 4, axis=1), F32),
        jnp.asarray(np.concatenate([-sine, sine, -sine, sine], axis=1), F32),
    )


def turned_pieces(groups):
    return [piece < PER + 1 for _ in range(groups) for piece in range(PER + 2)]


def turn(joined, cosine, sine, flags):
    lane = lax.broadcasted_iota(jnp.int32, cosine.shape, 1)
    front = (lane & 32) == 0
    left = lane < HD
    columns = []
    for at in range(joined.shape[1] // LANES):
        column = joined[:, at * LANES : (at + 1) * LANES]
        swapped = jnp.where(front, pltpu.roll(column, 96, 1), pltpu.roll(column, 32, 1))
        rotated = column * cosine + swapped * sine
        if not (flags[2 * at] and flags[2 * at + 1]):
            rotated = jnp.where(left if flags[2 * at] else jnp.logical_not(left), rotated, column)
        columns.append(rotated)
    return columns


def first_keys(length_ref, rows):
    row = lax.broadcasted_iota(jnp.int32, (rows, 1), 0)
    begin = jnp.zeros((rows, 1), jnp.int32)
    end = 0
    for doc in range(DOCS):
        if doc:
            begin = jnp.where(row >= end, end, begin)
        end = end + length_ref[0, doc]
    return jnp.where(row >= end, row, begin)


def adapter_mask(length_ref, index_ref, rows, width):
    row = lax.broadcasted_iota(jnp.int32, (rows, width), 0)
    adapter = lax.shift_right_logical(lax.broadcasted_iota(jnp.int32, (rows, width), 1), 4)
    mask = jnp.zeros((rows, width), F32)
    begin = 0
    for doc in range(DOCS):
        end = begin + length_ref[0, doc]
        inside = (row >= begin) & (row < end) & (adapter == index_ref[0, doc])
        mask = jnp.where(inside, 1.0, mask)
        begin = end
    return mask


def seen_block(first, block):
    keys = (block + 1) * ROWS
    row = lax.broadcasted_iota(jnp.int32, (ROWS, keys), 0) + block * ROWS
    key = lax.broadcasted_iota(jnp.int32, (ROWS, keys), 1)
    seen = (key <= row) & (key >= first[block * ROWS : (block + 1) * ROWS])
    return jnp.concatenate([seen] * PER, axis=0)


def store_heads(columns, slot, q_s, k_s, v_s):
    scale = 1.0 / math.sqrt(HD)
    blocks = q_s.shape[1]
    for at, column in enumerate(columns):
        halves = (column[:, :HD], pltpu.roll(column, HD, 1)[:, :HD])
        for piece, part in zip((2 * at, 2 * at + 1), halves):
            group, kind = divmod(piece, PER + 2)
            if kind == PER:
                k_s[slot + group] = part.astype(BF16)
            elif kind == PER + 1:
                v_s[slot + group] = part.astype(BF16)
            else:
                part = (part * scale).astype(BF16)
                for block in range(blocks):
                    q_s[slot + group, block, kind * ROWS : (kind + 1) * ROWS, :] = part[
                        block * ROWS : (block + 1) * ROWS
                    ]


def pack_kernel(
    n_exp, place_ref, gate, up, down, w_qkv, qkv_up, w_out, out_down, experts, shares, sem
):
    width = gate.shape[2]
    copies = []
    for expert in range(gate.shape[0]):
        copies.append((gate.at[expert], experts.at[expert, :, :width]))
        copies.append((up.at[expert], experts.at[expert, :, width : 2 * width]))
        for at in range(D // LANES):
            lanes = slice(at * LANES, (at + 1) * LANES)
            copies.append((down.at[expert, :, lanes], experts.at[expert, lanes, 2 * width :]))
    qkv_rows, up_rows, out_rows = share_rows(n_exp, w_out.shape[0])
    place = place_ref[0]
    own_qkv = pl.ds(pl.multiple_of(place * qkv_rows, 16), qkv_rows)
    own_up = pl.ds(pl.multiple_of(place * up_rows, 16), up_rows)
    own_out = pl.ds(pl.multiple_of(place * out_rows, 16), out_rows)
    wide = w_qkv.shape[1]
    copies.append((w_qkv.at[own_qkv, :], shares.at[:qkv_rows, :]))
    at = qkv_rows + up_rows
    copies.append((qkv_up.at[own_up, :], shares.at[qkv_rows:at, :]))
    for left in range(0, D, wide):
        taken = min(wide, D - left)
        target = shares.at[at : at + out_rows, :taken]
        copies.append((w_out.at[own_out, left : left + taken], target))
        at += out_rows
    at -= out_rows
    copies.append((out_down.at[own_out, :], shares.at[at : at + out_rows, taken : taken + LANES]))
    started = [
        pltpu.make_async_copy(source, target, sem.at[number])
        for number, (source, target) in enumerate(copies)
    ]
    for copy in started:
        copy.start()
    for copy in started:
        copy.wait()


def share_rows(n_exp, heads_wide):
    return (D // n_exp, LANES // n_exp, heads_wide // n_exp)


def pack(place, w_gate, w_up, w_down, w_qkv, qkv_up, w_out, out_down, n_exp):
    count, _, width = w_gate.shape
    qkv_rows, up_rows, out_rows = share_rows(n_exp, w_out.shape[0])
    wide = w_qkv.shape[1]
    pieces = -(-D // wide)
    copies = count * (2 + D // LANES) + 3 + pieces
    return pl.pallas_call(
        functools.partial(pack_kernel, n_exp),
        in_specs=[IN_SMEM] + [IN_HBM] * 7,
        out_specs=[IN_HBM] * 2,
        out_shape=[
            shape((count, D, 3 * width), BF16),
            shape((qkv_rows + up_rows + pieces * out_rows, wide), BF16),
        ],
        scratch_shapes=[pltpu.SemaphoreType.DMA((copies,))],
        name="pack_weights",
    )(place, w_gate, w_up, w_down, w_qkv, qkv_up, w_out, out_down)


def forward_kernel(
    length_ref, index_ref, tokens_hbm, gain_hbm, w_qkv_hbm, qkv_down_hbm, qkv_up_hbm, w_out_hbm,
    out_down_hbm, cosine_hbm, sine_hbm,
    attn_in_ref, low_q_ref, head_ref, base_ref, low_ref,
    tokens_s, gain_s, w_qkv_s, qkv_down_s, qkv_up_s, w_out_s, out_down_s, cosine_s, sine_s,
    q_s, k_s, v_s, sem,
):
    sources = (
        tokens_hbm, gain_hbm, qkv_down_hbm, w_qkv_hbm, qkv_up_hbm, cosine_hbm, sine_hbm,
        w_out_hbm, out_down_hbm,
    )
    targets = (
        tokens_s, gain_s, qkv_down_s, w_qkv_s, qkv_up_s, cosine_s, sine_s, w_out_s, out_down_s,
    )
    copies = [
        pltpu.make_async_copy(source, target, sem.at[number])
        for number, (source, target) in enumerate(zip(sources, targets))
    ]
    for copy in copies:
        copy.start()
    rows = tokens_s.shape[0]
    groups = k_s.shape[0]
    mask = adapter_mask(length_ref, index_ref, rows, LANES)
    first = first_keys(length_ref, rows)
    copies[0].wait()
    copies[1].wait()
    inputs = tokens_s[...].astype(F32)
    inv_root = lax.rsqrt(jnp.mean(inputs * inputs, axis=1, keepdims=True) + EPS)
    attn_in_ref[...] = (inputs * inv_root * gain_s[...]).astype(BF16)
    attn_in = attn_in_ref[...]
    copies[2].wait()
    low_q = (dot(attn_in, qkv_down_s[...]) * mask).astype(BF16)
    low_q_ref[...] = low_q
    for copy in copies[3:7]:
        copy.wait()
    projected = dot(attn_in, w_qkv_s[...]) + dot(low_q, qkv_up_s[...])
    columns = turn(projected, cosine_s[...], sine_s[...], turned_pieces(groups))
    store_heads(columns, 0, q_s, k_s, v_s)
    for block in range(rows // ROWS):
        here = slice(block * ROWS, (block + 1) * ROWS)
        keys = (block + 1) * ROWS
        seen = seen_block(first, block)
        heads = []
        for group in range(groups):
            scores = jnp.where(seen, dot_nt(q_s[group, block], k_s[group, :keys, :]), -1e30)
            lifted = jnp.exp(scores - jnp.max(scores, axis=1, keepdims=True))
            probs = (lifted * (1.0 / jnp.sum(lifted, axis=1, keepdims=True))).astype(BF16)
            out = dot(probs, v_s[group, :keys, :])
            heads += [out[head * ROWS : (head + 1) * ROWS] for head in range(PER)]
        head_ref[here, :] = jnp.concatenate(heads, axis=1).astype(BF16)
    copies[7].wait()
    copies[8].wait()
    head_out = head_ref[...]
    base_ref[...] = dot(head_out, w_out_s[...]).astype(BF16)
    low_ref[...] = (dot(head_out, out_down_s[...]) * mask).astype(BF16)


def forward(lengths, index, tokens, gain, w_qkv, qkv_down, qkv_up, w_out, out_down, tables):
    rows = tokens.shape[0]
    heads_wide = w_out.shape[0]
    groups = w_qkv.shape[1] // (HD * (PER + 2))
    blocks = rows // ROWS
    arrays = (tokens, gain.reshape(1, D), w_qkv, qkv_down, qkv_up, w_out, out_down) + tables
    return pl.pallas_call(
        forward_kernel,
        in_specs=[IN_SMEM] * 2 + [IN_HBM] * len(arrays),
        out_specs=[IN_VMEM] * 5,
        out_shape=[
            shape((rows, D), BF16),
            shape((rows, LANES), BF16),
            shape((rows, heads_wide), BF16),
            shape((rows, D), BF16),
            shape((rows, LANES), BF16),
        ],
        scratch_shapes=[pltpu.VMEM(array.shape, array.dtype) for array in arrays]
        + [
            pltpu.VMEM((groups, blocks, PER * ROWS, HD), BF16),
            pltpu.VMEM((groups, rows, HD), BF16),
            pltpu.VMEM((groups, rows, HD), BF16),
            pltpu.SemaphoreType.DMA((len(arrays),)),
        ],
        compiler_params=pltpu.CompilerParams(vmem_limit_bytes=48 * MIB),
        name="attention_forward",
    )(lengths, index, *arrays)


def experts_kernel(
    count, tokens_ref, base_ref, low_o_ref, out_up_ref, gain_ref, router_ref, routes_ref, cot_ref,
    weight_ref, residual_ref, moe_ref, grad_ref,
    normed_s, gates_s, part_s, moe_s, grad_s,
):
    step = pl.program_id(0)
    lane = lax.broadcasted_iota(jnp.int32, gates_s.shape, 1)
    width = weight_ref.shape[2] // 3

    @pl.when(step == 0)
    def _():
        residual = (
            tokens_ref[...].astype(F32)
            + base_ref[...].astype(F32)
            + dot(low_o_ref[...], out_up_ref[...])
        )
        residual_ref[...] = residual
        inv_root = lax.rsqrt(jnp.mean(residual * residual, axis=1, keepdims=True) + EPS)
        normed = (residual * inv_root * gain_ref[...]).astype(BF16)
        normed_s[...] = normed
        logits = dot(normed, router_ref[...])
        routed = lane == routes_ref[:, 0:1]
        for slot in range(1, TOP):
            routed = routed | (lane == routes_ref[:, slot : slot + 1])
        logits = jnp.where(routed, logits, -1e30)
        lifted = jnp.exp(logits - jnp.max(logits, axis=1, keepdims=True))
        gates_s[...] = lifted / jnp.sum(lifted, axis=1, keepdims=True)
        part_s[...] = jnp.zeros_like(part_s)
        moe_s[...] = jnp.zeros_like(moe_s)
        grad_s[...] = jnp.zeros_like(grad_s)

    normed = normed_s[...]
    cot = cot_ref[...]
    gates = gates_s[...]
    part = jnp.zeros(gates.shape, F32)
    downs = [
        jnp.concatenate(
            [
                weight_ref[expert, at * LANES : (at + 1) * LANES, 2 * width :]
                for at in range(D // LANES)
            ],
            axis=1,
        )
        for expert in range(count)
    ]
    hidden, grads = [], []
    for pair in range(count // 2):
        both_down = jnp.concatenate(downs[2 * pair : 2 * pair + 2], axis=0)
        both_raw = dot_nt(cot, both_down)
        for half in range(2):
            expert = 2 * pair + half
            joined = dot(normed, weight_ref[expert, :, : 2 * width])
            pre_gate = joined[:, :width]
            pre_up = joined[:, width:]
            raw = both_raw[:, half * width : (half + 1) * width]
            sigmoid = 0.5 * jnp.tanh(0.5 * pre_gate) + 0.5
            activated = pre_gate * sigmoid
            value = activated * pre_up
            here = lane == step * count + expert
            gate = jnp.sum(jnp.where(here, gates, 0.0), axis=1, keepdims=True)
            part += jnp.where(here, jnp.sum(value * raw, axis=1, keepdims=True), 0.0)
            hidden.append((gate * value).astype(BF16))
            inner = raw * gate
            grads.append((inner * pre_up * (sigmoid + activated * (1.0 - sigmoid))).astype(BF16))
            grads.append((inner * activated).astype(BF16))
    part_s[...] += part
    moe_s[...] += dot(jnp.concatenate(hidden, axis=1), jnp.concatenate(downs, axis=0))
    ups = jnp.concatenate([weight_ref[expert, :, : 2 * width] for expert in range(count)], axis=1)
    grad_s[...] += dot_nt(jnp.concatenate(grads, axis=1), ups)

    @pl.when(step == pl.num_programs(0) - 1)
    def _():
        gate_part = part_s[...]
        spread = jnp.sum(gates * gate_part, axis=1, keepdims=True)
        logit_grad = (gates * (gate_part - spread)).astype(BF16)
        moe_ref[...] = moe_s[...].astype(BF16)
        grad_ref[...] = (grad_s[...] + dot_nt(logit_grad, router_ref[...])).astype(BF16)


def experts_both(tokens, base, low_o, out_up, gain, router, routes, cot, weights, count=4):
    rows = tokens.shape[0]
    experts = weights.shape[0]
    arrays = (tokens, base, low_o, out_up, gain.reshape(1, D), router, routes, cot)
    whole = pl.BlockSpec((rows, D), lambda step: (0, 0))
    return pl.pallas_call(
        functools.partial(experts_kernel, count),
        grid=(experts // count,),
        in_specs=[pl.BlockSpec(array.shape, lambda step: (0, 0)) for array in arrays]
        + [pl.BlockSpec((count,) + weights.shape[1:], lambda step: (step, 0, 0))],
        out_specs=[whole] * 3,
        out_shape=[shape((rows, D), F32), shape((rows, D), BF16), shape((rows, D), BF16)],
        scratch_shapes=[
            pltpu.VMEM((rows, D), BF16),
            pltpu.VMEM((rows, experts), F32),
            pltpu.VMEM((rows, experts), F32),
            pltpu.VMEM((rows, D), F32),
            pltpu.VMEM((rows, D), F32),
        ],
        compiler_params=pltpu.CompilerParams(vmem_limit_bytes=60 * MIB),
        name="experts",
    )(*arrays, weights)


def norm_back(vectors, gain, upstream):
    inv_root = lax.rsqrt(jnp.mean(vectors * vectors, axis=1, keepdims=True) + EPS)
    weighted = upstream * gain
    slope = jnp.mean(vectors * weighted, axis=1, keepdims=True)
    return inv_root * weighted - vectors * (inv_root * inv_root * inv_root) * slope


def branch_kernel(
    length_ref, index_ref, residual_ref, low_o_ref, normed_grad_ref, cot_ref, gain_ref, out_up_ref,
    head_ref, shares, residual_grad_ref, head_grad_ref, part_ref, w_out_s, sem,
):
    n_exp, n_tp, _, wide = shares.shape
    rows = residual_ref.shape[0]
    qkv_rows, up_rows, out_rows = share_rows(n_exp, w_out_s.shape[1])
    copies = []
    for z in range(n_tp):
        for e in range(n_exp):
            at = qkv_rows + up_rows
            for left in range(0, D, wide):
                taken = min(wide, D + LANES - left)
                copies.append(
                    pltpu.make_async_copy(
                        shares.at[e, z, at : at + out_rows, :taken],
                        w_out_s.at[z, e * out_rows : (e + 1) * out_rows, left : left + taken],
                        sem.at[len(copies)],
                    )
                )
                at += out_rows
    for copy in copies:
        copy.start()
    mask = adapter_mask(length_ref, index_ref, rows, LANES)
    low_o = low_o_ref[...]
    residual_grad_ref[...] = cot_ref[...].astype(F32) + norm_back(
        residual_ref[...], gain_ref[...], normed_grad_ref[...].astype(F32)
    )
    branch_grad = residual_grad_ref[...].astype(BF16)
    low_o_grad = (dot_nt(branch_grad, out_up_ref[...]) * mask).astype(BF16)
    for at in range(D // LANES):
        lanes = slice(at * LANES, (at + 1) * LANES)
        part_ref[lanes, :] = dot_tn(low_o, branch_grad[:, lanes]).astype(BF16)
    part_ref[D:, :] = dot_tn(head_ref[...], low_o_grad).astype(BF16)
    for copy in copies:
        copy.wait()
    for z in range(n_tp):
        head_grad_ref[z] = (
            dot_nt(branch_grad, w_out_s[z, :, :D]) + dot_nt(low_o_grad, w_out_s[z, :, D:])
        ).astype(BF16)


def branch_back(lengths, index, residual, low_o, normed_grad, cot, gain, out_up, head, shares):
    rows, heads_wide = head.shape
    n_exp, n_tp, _, wide = shares.shape
    return pl.pallas_call(
        branch_kernel,
        in_specs=[IN_SMEM] * 2 + [IN_VMEM] * 7 + [IN_HBM],
        out_specs=[IN_VMEM] * 3,
        out_shape=[
            shape((rows, D), F32),
            shape((n_tp, rows, heads_wide), BF16),
            shape((D + heads_wide, LANES), BF16),
        ],
        scratch_shapes=[
            pltpu.VMEM((n_tp, heads_wide, D + LANES), BF16),
            pltpu.SemaphoreType.DMA((n_tp * n_exp * -(-D // wide),)),
        ],
        compiler_params=pltpu.CompilerParams(vmem_limit_bytes=48 * MIB),
        name="branch_backward",
    )(
        lengths, index, residual, low_o, normed_grad, cot, gain.reshape(1, D), out_up, head, shares
    )


def backward_kernel(
    place_ref, length_ref, index_ref, attn_in_ref, low_q_ref, head_grad_ref, residual_grad_ref,
    tokens_ref, gain_ref, qkv_down_ref, cosine_ref, sine_ref, shares,
    input_grad_ref, part_ref,
    w_qkv_s, q_s, k_s, v_s, g_s, grad_s, sum_s, sem,
):
    n_exp, n_tp, _, wide = shares.shape
    rows = tokens_ref.shape[0]
    blocks = rows // ROWS
    groups = k_s.shape[0] // n_tp
    flags = turned_pieces(groups)
    scale = 1.0 / math.sqrt(HD)
    qkv_rows, up_rows, _ = share_rows(n_exp, 0)
    copies = []
    for z in range(n_tp):
        for e in range(n_exp):
            for source, target in (
                (shares.at[e, z, :qkv_rows, :], pl.ds(e * qkv_rows, qkv_rows)),
                (
                    shares.at[e, z, qkv_rows : qkv_rows + up_rows, :],
                    pl.ds(D + e * up_rows, up_rows),
                ),
            ):
                copies.append(
                    pltpu.make_async_copy(source, w_qkv_s.at[z, target, :], sem.at[len(copies)])
                )
    for copy in copies:
        copy.start()
    first = first_keys(length_ref, rows)
    attn_in = attn_in_ref[...]
    low_q = low_q_ref[...]
    seen = [seen_block(first, block) for block in range(blocks)]
    for z in range(n_tp):
        for copy in copies[z * 2 * n_exp : (z + 1) * 2 * n_exp]:
            copy.wait()
        projected = dot(attn_in, w_qkv_s[z, :D, :]) + dot(low_q, w_qkv_s[z, D:, :])
        columns = turn(projected, cosine_ref[...], sine_ref[...], flags)
        store_heads(columns, z * groups, q_s, k_s, v_s)
        for head in range(groups * PER):
            group, kind = divmod(head, PER)
            part = head_grad_ref[z, :, head * HD : (head + 1) * HD]
            for block in range(blocks):
                g_s[z * groups + group, block, kind * ROWS : (kind + 1) * ROWS, :] = part[
                    block * ROWS : (block + 1) * ROWS
                ]

    def one_place(z, carried):
        pieces = []
        for group in range(groups):
            at = z * groups + group
            key_grad = jnp.zeros((HD, rows), F32)
            value_grad = jnp.zeros((HD, rows), F32)
            query_grads = []
            for block in range(blocks):
                count = (block + 1) * ROWS
                query, grad = q_s[at, block], g_s[at, block]
                key, value = k_s[at, :count, :], v_s[at, :count, :]
                scores = jnp.where(seen[block], dot_nt(query, key), -1e30)
                lifted = jnp.exp(scores - jnp.max(scores, axis=1, keepdims=True))
                probs = lifted * (1.0 / jnp.sum(lifted, axis=1, keepdims=True))
                weight_grad = dot_nt(grad, value)
                spread = jnp.sum(probs * weight_grad, axis=1, keepdims=True)
                score_grad = (probs * (weight_grad - spread)).astype(BF16)
                query_grads.append(dot(score_grad, key) * scale)

                def widen(part):
                    if count == rows:
                        return part
                    return jnp.concatenate([part, jnp.zeros((HD, rows - count), F32)], axis=1)

                key_grad += widen(dot_tn(query, score_grad))
                value_grad += widen(dot_tn(grad, probs.astype(BF16)))
            for head in range(PER):
                here = slice(head * ROWS, (head + 1) * ROWS)
                pieces.append(jnp.concatenate([part[here] for part in query_grads], axis=0))
            pieces += [key_grad.T, value_grad.T]
        joined = jnp.concatenate(pieces, axis=1)
        columns = turn(joined, cosine_ref[...], -sine_ref[...], flags)
        for at, column in enumerate(columns):
            grad_s[z, :, at * LANES : (at + 1) * LANES] = column.astype(BF16)
        return carried

    lax.fori_loop(0, n_tp, one_place, 0)
    sum_s[...] = dot_nt(grad_s[0], w_qkv_s[0])
    for z in range(1, n_tp):
        sum_s[...] += dot_nt(grad_s[z], w_qkv_s[z])
    mask = adapter_mask(length_ref, index_ref, rows, LANES)
    low_q_grad = (sum_s[:, D:] * mask).astype(BF16)
    part_ref[:D, :] = dot_tn(attn_in, low_q_grad).astype(BF16)
    own = grad_s[place_ref[0]]
    for at in range(wide // LANES):
        lanes = slice(at * LANES, (at + 1) * LANES)
        part_ref[D + at * LANES : D + (at + 1) * LANES, :] = dot_tn(low_q, own[:, lanes]).astype(
            BF16
        )
    attn_grad = sum_s[:, :D] + dot_nt(low_q_grad, qkv_down_ref[...])
    input_grad_ref[...] = (
        residual_grad_ref[...]
        + norm_back(tokens_ref[...].astype(F32), gain_ref[...], attn_grad)
    ).astype(BF16)


def attention_back(
    place, lengths, index, attn_in, low_q, head_grad, residual_grad, tokens, gain, qkv_down, tables,
    shares,
):
    rows = tokens.shape[0]
    n_exp, n_tp, _, wide = shares.shape
    count = KV_HEADS
    blocks = rows // ROWS
    arrays = (attn_in, low_q, head_grad, residual_grad, tokens, gain.reshape(1, D), qkv_down)
    return pl.pallas_call(
        backward_kernel,
        in_specs=[IN_SMEM] * 3 + [IN_VMEM] * 9 + [IN_HBM],
        out_specs=[IN_VMEM] * 2,
        out_shape=[shape((rows, D), BF16), shape((D + wide, LANES), BF16)],
        scratch_shapes=[
            pltpu.VMEM((n_tp, D + LANES, wide), BF16),
            pltpu.VMEM((count, blocks, PER * ROWS, HD), BF16),
            pltpu.VMEM((count, rows, HD), BF16),
            pltpu.VMEM((count, rows, HD), BF16),
            pltpu.VMEM((count, blocks, PER * ROWS, HD), BF16),
            pltpu.VMEM((n_tp, rows, wide), BF16),
            pltpu.VMEM((rows, D + LANES), F32),
            pltpu.SemaphoreType.DMA((n_tp * n_exp * 2,)),
        ],
        compiler_params=pltpu.CompilerParams(vmem_limit_bytes=60 * MIB),
        name="attention_backward",
    )(place, lengths, index, *arrays, *tables, shares)


def kernel_body(
    tokens, attn_gain, moe_gain, w_qkv, w_out, w_router, w_gate, w_up, w_down, qkv_down, qkv_up,
    out_down, out_up, lengths, adapter_index, loss_mask, routes, upstream,
):
    n_exp = lax.axis_size("exp")
    rows = tokens.shape[0]
    heads_wide = w_out.shape[0]
    wide = w_qkv.shape[1]
    exp_place = lax.axis_index("exp").astype(jnp.int32).reshape(1)
    tp_place = lax.axis_index("tp").astype(jnp.int32).reshape(1)
    tables = turn_tables(rows)
    own_experts, own_shares = pack(
        exp_place, w_gate, w_up, w_down, w_qkv, qkv_up, w_out, out_down, n_exp
    )
    weights = lax.all_gather(own_experts, "exp", axis=0, tiled=True)
    attn_in, low_q, head, base, low_o = forward(
        lengths, adapter_index, tokens, attn_gain, w_qkv, qkv_down, qkv_up, w_out, out_down, tables
    )
    base, low_o = lax.psum((base, low_o), "tp")
    own_shares, _ = lax.optimization_barrier((own_shares, base))
    shares = lax.all_gather(own_shares, "tp", axis=0)
    shares, _ = lax.optimization_barrier((shares, weights))
    shares = lax.all_gather(shares, "exp", axis=0)
    occupied = jnp.arange(rows, dtype=jnp.int32) < jnp.sum(lengths)
    kept = occupied & (loss_mask > 0)
    cot = jnp.where(kept[:, None], upstream, jnp.zeros((), BF16))
    residual, moe_part, normed_part = experts_both(
        tokens, base, low_o, out_up, moe_gain, w_router, routes, cot, weights
    )
    normed_grad = lax.psum(normed_part, "tp")
    moe_part, _ = lax.optimization_barrier((moe_part, normed_grad))
    moe_out = lax.psum(moe_part, "tp").astype(F32)
    output = (residual + moe_out).astype(BF16)
    residual_grad, head_grad, out_part = branch_back(
        lengths, adapter_index, residual, low_o, normed_grad, cot, moe_gain, out_up, head, shares
    )
    input_grad, qkv_part = attention_back(
        tp_place, lengths, adapter_index, attn_in, low_q, head_grad, residual_grad, tokens,
        attn_gain, qkv_down, tables, shares,
    )
    parts = jnp.concatenate([out_part, qkv_part], axis=0)
    share = parts.shape[0] // n_exp
    parts = lax.all_to_all(parts.reshape(n_exp, share, LANES), "exp", 0, 0, tiled=True)
    summed = jnp.sum(parts.astype(F32), axis=0).astype(BF16)
    summed = lax.all_gather(summed, "exp", axis=0, tiled=True).astype(F32)

    def side_by_side(stacked):
        pieces = stacked.reshape(-1, LANES, LANES)
        return pieces.transpose(1, 0, 2).reshape(LANES, -1)

    at = D + heads_wide
    return (
        output,
        input_grad,
        summed[at : at + D],
        side_by_side(summed[at + D :]),
        summed[D:at],
        side_by_side(summed[:D]),
    )


def product(left_m, right_m):
    return jnp.dot(left_m, right_m, preferred_element_type=jnp.float32)


def contract(einsum_form, left_m, right_m):
    return jnp.einsum(einsum_form, left_m, right_m, preferred_element_type=jnp.float32)


def rms_norm(vectors, gain_vec):
    inv_root = lax.rsqrt(jnp.mean(vectors * vectors, axis=-1, keepdims=True) + EPS)
    return vectors * inv_root * gain_vec


def rms_norm_back(vectors, gain_vec, upstream_grad):
    inv_root = lax.rsqrt(jnp.mean(vectors * vectors, axis=-1, keepdims=True) + EPS)
    weighted = upstream_grad * gain_vec
    return inv_root * weighted - vectors * (inv_root * inv_root * inv_root) * jnp.mean(
        vectors * weighted, axis=-1, keepdims=True
    )


def layout(length_row, index_row):
    places = jnp.arange(TOK_DEV, dtype=jnp.int32)
    doc_ends = jnp.cumsum(length_row)
    doc_starts = doc_ends - length_row
    member = (places[:, None] >= doc_starts[None, :]) & (places[:, None] < doc_ends[None, :])
    occupied = jnp.any(member, axis=1)
    position = jnp.sum(jnp.where(member, places[:, None] - doc_starts[None, :], 0), axis=1)
    owner_doc = jnp.sum(jnp.where(member, jnp.arange(DOCS, dtype=jnp.int32)[None, :], 0), axis=1)
    doc_ident = jnp.where(occupied, owner_doc, DOCS + places)
    chosen = jnp.sum(jnp.where(member, index_row[None, :], 0), axis=1)
    adapter_pick = occupied[:, None] & (
        chosen[:, None] == jnp.arange(ADAPTERS, dtype=jnp.int32)[None, :]
    )
    rank_mask = jnp.repeat(jnp.where(adapter_pick, 1.0, 0.0).astype(jnp.float32), RANK, axis=1)
    return (occupied, position, doc_ident, rank_mask)


def angles(position):
    half_width = HD // 2
    frequency = jnp.exp(-math.log(ROPE_BASE) * jnp.arange(half_width, dtype=jnp.float32) * 2.0 / HD)
    turned = position.astype(jnp.float32)[:, None] * frequency[None, :]
    return (jnp.cos(turned), jnp.sin(turned))


def rotate(vectors, cosine, sine_table):
    half_width = vectors.shape[-1] // 2
    front_half = vectors[..., :half_width]
    back_half = vectors[..., half_width:]
    return jnp.concatenate(
        [
            front_half * cosine - back_half * sine_table,
            back_half * cosine + front_half * sine_table,
        ],
        axis=-1,
    )


def moe(normed, cot_low, gates, gate_up, down):
    width = down.shape[1]
    both = contract("td,edf->tef", normed, gate_up)
    pre_gate = both[:, :, :width]
    pre_up = both[:, :, width:]
    sigmoid_g = jax.nn.sigmoid(pre_gate)
    activated = pre_gate * sigmoid_g
    hidden = (activated * pre_up).astype(jnp.bfloat16).astype(jnp.float32)
    inner_raw = contract("td,efd->tef", cot_low, down)
    gate_part = jnp.sum(hidden * inner_raw, axis=-1)
    moe_part = contract("tef,efd->td", (gates[:, :, None] * hidden).astype(jnp.bfloat16), down)
    inner_grad = inner_raw * gates[:, :, None]
    grad_gate = inner_grad * pre_up * sigmoid_g * (1.0 + pre_gate * (1.0 - sigmoid_g))
    grad_up = inner_grad * activated
    grad_both = jnp.concatenate([grad_gate, grad_up], axis=2).astype(jnp.bfloat16)
    normed_part = contract("tef,edf->td", grad_both, gate_up)
    return (moe_part, gate_part, normed_part)


def body(
    tokens,
    attn_gain,
    moe_gain,
    w_qkv,
    w_out,
    w_router,
    w_gate,
    w_up,
    w_down,
    qkv_down,
    qkv_up,
    out_down,
    out_up,
    lengths,
    adapter_index,
    loss_mask,
    routes,
    upstream,
):
    n_exp = lax.axis_size("exp")
    groups = KV_HEADS // lax.axis_size("tp")
    per_group = HEADS // KV_HEADS
    experts = EXP_DEV * n_exp
    gate_up = lax.all_gather(jnp.concatenate([w_gate, w_up], axis=2), "exp", axis=0, tiled=True)
    down = lax.all_gather(w_down, "exp", axis=0, tiled=True)
    block_rows = min(512, TOK_DEV)
    blocks = TOK_DEV // block_rows
    score_scale = 1.0 / math.sqrt(HD)
    places = jnp.arange(TOK_DEV, dtype=jnp.int32)
    occupied, position, doc_ident, rank_mask = layout(lengths[0], adapter_index[0])
    mask_low = rank_mask.astype(jnp.bfloat16)
    cosine, sine_table = angles(position)
    inputs = tokens.astype(jnp.float32)
    attn_in = rms_norm(inputs, attn_gain).astype(jnp.bfloat16)
    low_q = (product(attn_in, qkv_down) * rank_mask).astype(jnp.bfloat16)
    projected = (product(attn_in, w_qkv) + product(low_q, qkv_up)).reshape(
        TOK_DEV, groups, per_group + 2, HD
    )
    query_rows = rotate(
        projected[:, :, :per_group], cosine[:, None, None], sine_table[:, None, None]
    ).astype(jnp.bfloat16)
    key_rows = rotate(projected[:, :, per_group], cosine[:, None], sine_table[:, None]).astype(
        jnp.bfloat16
    )
    val_rows = projected[:, :, per_group + 1].astype(jnp.bfloat16)

    def masked_scores(q_blk, q_place, q_ident):
        scores = contract("qgrd,kgd->grqk", q_blk, key_rows) * score_scale
        allowed = (q_ident[:, None] == doc_ident[None, :]) & (places[None, :] <= q_place[:, None])
        return jnp.where(allowed, scores, -1e30)

    def attend(pieces):
        q_blk, q_place, q_ident = pieces
        scores = masked_scores(q_blk, q_place, q_ident)
        row_max = jnp.max(scores, axis=-1, keepdims=True)
        lifted = jnp.exp(scores - row_max)
        row_total = jnp.sum(lifted, axis=-1, keepdims=True)
        weights = (lifted / row_total).astype(jnp.bfloat16)
        return (
            contract("grqk,kgd->qgrd", weights, val_rows),
            row_max[..., 0] + jnp.log(row_total[..., 0]),
        )

    query_blocks = query_rows.reshape(blocks, block_rows, groups, per_group, HD)
    place_blocks = places.reshape(blocks, block_rows)
    ident_blocks = doc_ident.reshape(blocks, block_rows)
    attended, log_totals = lax.map(attend, (query_blocks, place_blocks, ident_blocks))
    head_rows = attended.reshape(TOK_DEV, groups * per_group * HD).astype(jnp.bfloat16)
    attn_base, low_rank = (
        lax.psum(product(head_rows, w_out).astype(jnp.bfloat16), "tp").astype(jnp.float32),
        lax.psum((product(head_rows, out_down) * rank_mask).astype(jnp.bfloat16), "tp").astype(
            jnp.float32
        ),
    )
    low_o = low_rank.astype(jnp.bfloat16)
    residual = inputs + attn_base + product(low_o, out_up)
    normed = rms_norm(residual, moe_gain).astype(jnp.bfloat16)
    logits = product(normed, w_router)
    one_hot = routes[:, :, None] == jnp.arange(experts, dtype=jnp.int32)[None, None, :]
    routed = jnp.any(one_hot, axis=1)
    gates = jax.nn.softmax(jnp.where(routed, logits, -1e30), axis=-1)
    live_mask = jnp.where(occupied & (loss_mask > 0), 1.0, 0.0).astype(jnp.float32)
    cotangent = upstream.astype(jnp.float32) * live_mask[:, None]
    cot_low = cotangent.astype(jnp.bfloat16)
    moe_part, gate_part, normed_part = moe(normed, cot_low, gates, gate_up, down)
    logit_grad = (
        gates * (gate_part - jnp.sum(gates * gate_part, axis=-1, keepdims=True))
    ).astype(jnp.bfloat16)
    normed_part = (normed_part + product(logit_grad, w_router.T)).astype(jnp.bfloat16)
    normed_sum = lax.psum(normed_part, "tp")
    normed_sum, moe_part = lax.optimization_barrier((normed_sum, moe_part.astype(jnp.bfloat16)))
    normed_grad = normed_sum.astype(jnp.float32)
    moe_out = lax.psum(moe_part, "tp").astype(jnp.float32)
    output = (residual + moe_out).astype(jnp.bfloat16)
    residual_grad = cotangent + rms_norm_back(residual, moe_gain, normed_grad)
    branch_grad = residual_grad.astype(jnp.bfloat16)
    low_o_grad = product(branch_grad, out_up.T).astype(jnp.bfloat16) * mask_low
    out_up_part = contract("tr,td->rd", low_o, branch_grad)
    head_grad = (product(branch_grad, w_out.T) + product(low_o_grad, out_down.T)).astype(
        jnp.bfloat16
    )
    out_down_part = contract("tc,tr->cr", head_rows, low_o_grad)
    grad_blocks = head_grad.reshape(blocks, block_rows, groups, per_group, HD)

    def attend_back(carried, pieces):
        key_acc, val_acc = carried
        q_blk, q_place, q_ident, lse_blk, g_blk = pieces
        weights = jnp.exp(masked_scores(q_blk, q_place, q_ident) - lse_blk[..., None])
        weight_grad = contract("qgrd,kgd->grqk", g_blk, val_rows)
        score_grad = (
            weights * (weight_grad - jnp.sum(weights * weight_grad, axis=-1, keepdims=True))
        ).astype(jnp.bfloat16)
        query_grad = contract("grqk,kgd->qgrd", score_grad, key_rows) * score_scale
        key_acc = key_acc + contract("grqk,qgrd->kgd", score_grad, q_blk) * score_scale
        val_acc = val_acc + contract("grqk,qgrd->kgd", weights.astype(jnp.bfloat16), g_blk)
        return ((key_acc, val_acc), query_grad)

    zero_acc = jnp.zeros((TOK_DEV, groups, HD), jnp.float32)
    (key_grad, val_grad), query_grad = lax.scan(
        attend_back,
        (zero_acc, zero_acc),
        (query_blocks, place_blocks, ident_blocks, log_totals, grad_blocks),
    )
    query_grad = rotate(
        query_grad.reshape(TOK_DEV, groups, per_group, HD),
        cosine[:, None, None],
        -sine_table[:, None, None],
    )
    key_grad = rotate(key_grad, cosine[:, None], -sine_table[:, None])
    projected_grad = (
        jnp.concatenate([query_grad, key_grad[:, :, None], val_grad[:, :, None]], axis=2)
        .reshape(TOK_DEV, -1)
        .astype(jnp.bfloat16)
    )
    qkv_up_part = contract("tr,tc->rc", low_q, projected_grad)
    attn_grad, low_q_grad = (
        lax.psum(contract("tc,dc->td", projected_grad, w_qkv).astype(jnp.bfloat16), "tp").astype(
            jnp.float32
        ),
        lax.psum(contract("tc,rc->tr", projected_grad, qkv_up).astype(jnp.bfloat16), "tp").astype(
            jnp.float32
        ),
    )
    low_q_grad = low_q_grad.astype(jnp.bfloat16) * mask_low
    attn_grad = attn_grad + contract("tr,dr->td", low_q_grad, qkv_down)
    qkv_down_part = contract("td,tr->dr", attn_in, low_q_grad)
    input_grad = (residual_grad + rms_norm_back(inputs, attn_gain, attn_grad)).astype(jnp.bfloat16)
    summed = (
        lax.psum(qkv_down_part.astype(jnp.bfloat16), "exp").astype(jnp.float32),
        lax.psum(qkv_up_part.astype(jnp.bfloat16), "exp").astype(jnp.float32),
        lax.psum(out_down_part.astype(jnp.bfloat16), "exp").astype(jnp.float32),
        lax.psum(out_up_part.astype(jnp.bfloat16), "exp").astype(jnp.float32),
    )
    return (output, input_grad, summed[0], summed[1], summed[2], summed[3])


def kernels_fit(mesh):
    n_exp, n_tp = mesh.shape["exp"], mesh.shape["tp"]
    groups = KV_HEADS // n_tp
    return groups % 2 == 0 and FF // n_tp == LANES and LANES // n_exp % 16 == 0


def solution(mesh):
    placed = (
        P("exp", None),
        P(),
        P(),
        P(None, "tp"),
        P("tp", None),
        P(),
        P("exp", None, "tp"),
        P("exp", None, "tp"),
        P("exp", "tp", None),
        P(),
        P(None, "tp"),
        P("tp", None),
        P(),
        P("exp", None),
        P("exp", None),
        P("exp"),
        P("exp", None),
        P("exp", None),
    )
    return jax.shard_map(
        kernel_body if kernels_fit(mesh) else body,
        mesh=mesh,
        in_specs=placed,
        out_specs=(P("exp", None), P("exp", None), P(), P(None, "tp"), P("tp", None), P()),
        check_vma=False,
    )
```

```python
import functools
import math

import jax
import jax.numpy as jnp
import numpy as np
from jax import lax
from jax.experimental import pallas as pl
from jax.experimental.pallas import tpu as pltpu
from jax.sharding import PartitionSpec as P

D = 1536
HEADS = 24
KV_HEADS = 8
HD = 64
TOP = 8
RANK = 16
ADAPTERS = 8
EXP_DEV = 2
DOCS = 4
TOK_DEV = 512
FF = 512
EPS = 1e-06
ROPE_BASE = 10000.0

PER = HEADS // KV_HEADS
LANES = 128
ROWS = 128
F32 = jnp.float32
BF16 = jnp.bfloat16
MIB = 2**20
NT = (((1,), (1,)), ((), ()))
TN = (((0,), (0,)), ((), ()))
WHOLE_VMEM = pltpu.CompilerParams(vmem_limit_bytes=63 * MIB)
IN_VMEM = pl.BlockSpec(memory_space=pltpu.VMEM)
IN_SMEM = pl.BlockSpec(memory_space=pltpu.SMEM)
IN_HBM = pl.BlockSpec(memory_space=pltpu.HBM)


def dot(left, right):
    return jnp.dot(left, right, preferred_element_type=F32)


def dot_nt(left, right):
    return lax.dot_general(left, right, NT, preferred_element_type=F32)


def dot_tn(left, right):
    return lax.dot_general(left, right, TN, preferred_element_type=F32)


def cost(flops, moved):
    return pl.CostEstimate(flops=int(flops), bytes_accessed=int(moved), transcendentals=0)


def shape(dims, dtype):
    return jax.ShapeDtypeStruct(dims, dtype)


def turn_tables(rows):
    half = HD // 2
    frequency = np.exp(-math.log(ROPE_BASE) * np.arange(half, dtype=np.float64) * 2.0 / HD)
    turned = np.arange(rows, dtype=np.float64)[:, None] * frequency[None, :]
    cosine, sine = np.cos(turned), np.sin(turned)
    return (
        jnp.asarray(np.concatenate([cosine] * 4, axis=1), F32),
        jnp.asarray(np.concatenate([-sine, sine, -sine, sine], axis=1), F32),
    )


def turned_pieces(groups):
    return [piece < PER + 1 for _ in range(groups) for piece in range(PER + 2)]


def turn(joined, cosine, sine, flags):
    lane = lax.broadcasted_iota(jnp.int32, cosine.shape, 1)
    front = (lane & 32) == 0
    left = lane < HD
    columns = []
    for at in range(joined.shape[1] // LANES):
        column = joined[:, at * LANES : (at + 1) * LANES]
        swapped = jnp.where(front, pltpu.roll(column, 96, 1), pltpu.roll(column, 32, 1))
        rotated = column * cosine + swapped * sine
        if not (flags[2 * at] and flags[2 * at + 1]):
            rotated = jnp.where(left if flags[2 * at] else jnp.logical_not(left), rotated, column)
        columns.append(rotated)
    return columns


def first_keys(length_ref, rows):
    row = lax.broadcasted_iota(jnp.int32, (rows, 1), 0)
    begin = jnp.zeros((rows, 1), jnp.int32)
    end = 0
    for doc in range(DOCS):
        if doc:
            begin = jnp.where(row >= end, end, begin)
        end = end + length_ref[0, doc]
    return jnp.where(row >= end, row, begin)


def adapter_mask(length_ref, index_ref, rows, width):
    row = lax.broadcasted_iota(jnp.int32, (rows, width), 0)
    adapter = lax.shift_right_logical(lax.broadcasted_iota(jnp.int32, (rows, width), 1), 4)
    mask = jnp.zeros((rows, width), F32)
    begin = 0
    for doc in range(DOCS):
        end = begin + length_ref[0, doc]
        inside = (row >= begin) & (row < end) & (adapter == index_ref[0, doc])
        mask = jnp.where(inside, 1.0, mask)
        begin = end
    return mask


def seen_block(first, block):
    keys = (block + 1) * ROWS
    row = lax.broadcasted_iota(jnp.int32, (ROWS, keys), 0) + block * ROWS
    key = lax.broadcasted_iota(jnp.int32, (ROWS, keys), 1)
    seen = (key <= row) & (key >= first[block * ROWS : (block + 1) * ROWS])
    return jnp.concatenate([seen] * PER, axis=0)


def store_heads(columns, slot, q_s, k_s, v_s):
    scale = 1.0 / math.sqrt(HD)
    blocks = q_s.shape[1]
    for at, column in enumerate(columns):
        halves = (column[:, :HD], pltpu.roll(column, HD, 1)[:, :HD])
        for piece, part in zip((2 * at, 2 * at + 1), halves):
            group, kind = divmod(piece, PER + 2)
            if kind == PER:
                k_s[slot + group] = part.astype(BF16)
            elif kind == PER + 1:
                v_s[slot + group] = part.astype(BF16)
            else:
                part = (part * scale).astype(BF16)
                for block in range(blocks):
                    q_s[slot + group, block, kind * ROWS : (kind + 1) * ROWS, :] = part[
                        block * ROWS : (block + 1) * ROWS
                    ]


def run_copies(pairs, sem):
    copies = [
        pltpu.make_async_copy(source, target, sem.at[number])
        for number, (source, target) in enumerate(pairs)
    ]
    for copy in copies:
        copy.start()
    for copy in copies:
        copy.wait()


def pack_experts_kernel(gate, up, down, packed, held, sem, out_sem):
    width = gate.shape[2]
    pairs = []
    for expert in range(gate.shape[0]):
        pairs.append((gate.at[expert], held.at[expert, :, :width]))
        pairs.append((up.at[expert], held.at[expert, :, width : 2 * width]))
        for at in range(D // LANES):
            lanes = slice(at * LANES, (at + 1) * LANES)
            pairs.append((down.at[expert, :, lanes], held.at[expert, lanes, 2 * width :]))
    run_copies(pairs, sem)
    run_copies([(held, packed)], out_sem)


def pack_experts(w_gate, w_up, w_down):
    count, _, width = w_gate.shape
    packed = shape((count, D, 3 * width), BF16)
    return pl.pallas_call(
        pack_experts_kernel,
        in_specs=[IN_HBM] * 3,
        out_specs=IN_HBM,
        out_shape=packed,
        scratch_shapes=[
            pltpu.VMEM(packed.shape, BF16),
            pltpu.SemaphoreType.DMA((count * (2 + D // LANES),)),
            pltpu.SemaphoreType.DMA((1,)),
        ],
        compiler_params=WHOLE_VMEM,
        cost_estimate=cost(0, 2 * 2 * count * D * 3 * width),
        name="pack_experts",
    )(w_gate, w_up, w_down)


def share_rows(n_exp, heads_wide):
    return (D // n_exp, LANES // n_exp, heads_wide // n_exp)


def pack_share_kernel(n_exp, place_ref, w_qkv, qkv_up, w_out, out_down, packed, held, sem, out_sem):
    qkv_rows, up_rows, out_rows = share_rows(n_exp, w_out.shape[0])
    place = place_ref[0]
    own_qkv = pl.ds(pl.multiple_of(place * qkv_rows, 16), qkv_rows)
    own_up = pl.ds(pl.multiple_of(place * up_rows, 16), up_rows)
    own_out = pl.ds(pl.multiple_of(place * out_rows, 16), out_rows)
    wide = w_qkv.shape[1]
    at = qkv_rows + up_rows
    pairs = [
        (w_qkv.at[own_qkv, :], held.at[:qkv_rows, :]),
        (qkv_up.at[own_up, :], held.at[qkv_rows:at, :]),
    ]
    for left in range(0, D, wide):
        taken = min(wide, D - left)
        target = held.at[at : at + out_rows, :taken]
        pairs.append((w_out.at[own_out, left : left + taken], target))
        at += out_rows
    at -= out_rows
    pairs.append((out_down.at[own_out, :], held.at[at : at + out_rows, taken : taken + LANES]))
    held[at : at + out_rows, taken + LANES :] = jnp.zeros(
        (out_rows, wide - taken - LANES), BF16
    )
    run_copies(pairs, sem)
    run_copies([(held, packed)], out_sem)


def pack_share(place, w_qkv, qkv_up, w_out, out_down, n_exp):
    qkv_rows, up_rows, out_rows = share_rows(n_exp, w_out.shape[0])
    wide = w_qkv.shape[1]
    pieces = -(-D // wide)
    packed = shape((qkv_rows + up_rows + pieces * out_rows, wide), BF16)
    return pl.pallas_call(
        functools.partial(pack_share_kernel, n_exp),
        in_specs=[IN_SMEM] + [IN_HBM] * 4,
        out_specs=IN_HBM,
        out_shape=packed,
        scratch_shapes=[
            pltpu.VMEM(packed.shape, BF16),
            pltpu.SemaphoreType.DMA((3 + pieces,)),
            pltpu.SemaphoreType.DMA((1,)),
        ],
        compiler_params=WHOLE_VMEM,
        cost_estimate=cost(0, 4 * packed.shape[0] * wide),
        name="pack_share",
    )(place, w_qkv, qkv_up, w_out, out_down)


class Loads:
    def __init__(self, names, sources, targets, sem):
        self.copies = {
            name: pltpu.make_async_copy(source, target, sem.at[number])
            for number, (name, source, target) in enumerate(zip(names, sources, targets))
        }
        self.targets = dict(zip(names, targets))
        for copy in self.copies.values():
            copy.start()

    def __getitem__(self, name):
        copy = self.copies.pop(name, None)
        if copy is not None:
            copy.wait()
        return self.targets[name]


def load_scratch(arrays):
    return [pltpu.VMEM(array.shape, array.dtype) for array in arrays] + [
        pltpu.SemaphoreType.DMA((len(arrays),))
    ]


FORWARD_LOADS = (
    "tokens", "gain", "qkv_down", "w_qkv", "qkv_up", "cosine", "sine", "w_out", "out_down",
)


def forward_kernel(length_ref, index_ref, *refs):
    count = len(FORWARD_LOADS)
    attn_in_ref, low_q_ref, head_ref, base_ref, low_ref = refs[count : count + 5]
    load_sem, q_s, k_s, v_s = refs[2 * count + 5 :]
    loads = Loads(FORWARD_LOADS, refs[:count], refs[count + 5 : 2 * count + 5], load_sem)
    rows = attn_in_ref.shape[0]
    groups = k_s.shape[0]
    mask = adapter_mask(length_ref, index_ref, rows, LANES)
    first = first_keys(length_ref, rows)
    inputs = loads["tokens"][...].astype(F32)
    inv_root = lax.rsqrt(jnp.mean(inputs * inputs, axis=1, keepdims=True) + EPS)
    attn_in_ref[...] = (inputs * inv_root * loads["gain"][...]).astype(BF16)
    attn_in = attn_in_ref[...]
    low_q = (dot(attn_in, loads["qkv_down"][...]) * mask).astype(BF16)
    low_q_ref[...] = low_q
    projected = dot(attn_in, loads["w_qkv"][...]) + dot(low_q, loads["qkv_up"][...])
    cosine, sine = loads["cosine"][...], loads["sine"][...]
    store_heads(turn(projected, cosine, sine, turned_pieces(groups)), 0, q_s, k_s, v_s)
    for block in range(rows // ROWS):
        here = slice(block * ROWS, (block + 1) * ROWS)
        keys = (block + 1) * ROWS
        seen = seen_block(first, block)
        heads = []
        for group in range(groups):
            scores = jnp.where(seen, dot_nt(q_s[group, block], k_s[group, :keys, :]), -1e30)
            lifted = jnp.exp(scores - jnp.max(scores, axis=1, keepdims=True))
            probs = (lifted * (1.0 / jnp.sum(lifted, axis=1, keepdims=True))).astype(BF16)
            out = dot(probs, v_s[group, :keys, :])
            heads += [out[head * ROWS : (head + 1) * ROWS] for head in range(PER)]
        head_ref[here, :] = jnp.concatenate(heads, axis=1).astype(BF16)
    head_out = head_ref[...]
    base_ref[...] = dot(head_out, loads["w_out"][...]).astype(BF16)
    low_ref[...] = (dot(head_out, loads["out_down"][...]) * mask).astype(BF16)


def forward(lengths, index, tokens, gain, w_qkv, qkv_down, qkv_up, w_out, out_down, tables):
    rows = tokens.shape[0]
    heads_wide = w_out.shape[0]
    groups = w_qkv.shape[1] // (HD * (PER + 2))
    arrays = (tokens, gain.reshape(1, D), qkv_down, w_qkv, qkv_up) + tables + (w_out, out_down)
    return pl.pallas_call(
        forward_kernel,
        in_specs=[IN_SMEM] * 2 + [IN_HBM] * len(arrays),
        out_specs=[IN_VMEM] * 5,
        out_shape=[
            shape((rows, D), BF16),
            shape((rows, LANES), BF16),
            shape((rows, heads_wide), BF16),
            shape((rows, D), BF16),
            shape((rows, LANES), BF16),
        ],
        scratch_shapes=load_scratch(arrays)
        + [
            pltpu.VMEM((groups, rows // ROWS, PER * ROWS, HD), BF16),
            pltpu.VMEM((groups, rows, HD), BF16),
            pltpu.VMEM((groups, rows, HD), BF16),
        ],
        compiler_params=WHOLE_VMEM,
        cost_estimate=cost(6e9, 10e6),
        name="attention_forward",
    )(lengths, index, *arrays)


def experts_kernel(
    count, tokens_ref, base_ref, low_o_ref, out_up_ref, gain_ref, router_ref, routes_ref, cot_ref,
    weight_ref, residual_ref, moe_ref, grad_ref,
    normed_s, gates_s, part_s, moe_s, grad_s,
):
    step = pl.program_id(0)
    lane = lax.broadcasted_iota(jnp.int32, gates_s.shape, 1)
    width = weight_ref.shape[2] // 3

    @pl.when(step == 0)
    def _():
        residual = (
            tokens_ref[...].astype(F32)
            + base_ref[...].astype(F32)
            + dot(low_o_ref[...], out_up_ref[...])
        )
        residual_ref[...] = residual
        inv_root = lax.rsqrt(jnp.mean(residual * residual, axis=1, keepdims=True) + EPS)
        normed = (residual * inv_root * gain_ref[...]).astype(BF16)
        normed_s[...] = normed
        logits = dot(normed, router_ref[...])
        routed = lane == routes_ref[:, 0:1]
        for slot in range(1, TOP):
            routed = routed | (lane == routes_ref[:, slot : slot + 1])
        logits = jnp.where(routed, logits, -1e30)
        lifted = jnp.exp(logits - jnp.max(logits, axis=1, keepdims=True))
        gates_s[...] = lifted / jnp.sum(lifted, axis=1, keepdims=True)
        part_s[...] = jnp.zeros_like(part_s)
        moe_s[...] = jnp.zeros_like(moe_s)
        grad_s[...] = jnp.zeros_like(grad_s)

    normed = normed_s[...]
    cot = cot_ref[...]
    gates = gates_s[...]
    part = jnp.zeros(gates.shape, F32)
    downs = [
        jnp.concatenate(
            [
                weight_ref[expert, at * LANES : (at + 1) * LANES, 2 * width :]
                for at in range(D // LANES)
            ],
            axis=1,
        )
        for expert in range(count)
    ]
    hidden, grads = [], []
    for pair in range(count // 2):
        both_down = jnp.concatenate(downs[2 * pair : 2 * pair + 2], axis=0)
        both_raw = dot_nt(cot, both_down)
        for half in range(2):
            expert = 2 * pair + half
            joined = dot(normed, weight_ref[expert, :, : 2 * width])
            pre_gate = joined[:, :width]
            pre_up = joined[:, width:]
            raw = both_raw[:, half * width : (half + 1) * width]
            sigmoid = 0.5 * jnp.tanh(0.5 * pre_gate) + 0.5
            activated = pre_gate * sigmoid
            value = activated * pre_up
            here = lane == step * count + expert
            gate = jnp.sum(jnp.where(here, gates, 0.0), axis=1, keepdims=True)
            part += jnp.where(here, jnp.sum(value * raw, axis=1, keepdims=True), 0.0)
            hidden.append((gate * value).astype(BF16))
            inner = raw * gate
            grads.append((inner * pre_up * (sigmoid + activated * (1.0 - sigmoid))).astype(BF16))
            grads.append((inner * activated).astype(BF16))
    part_s[...] += part
    moe_s[...] += dot(jnp.concatenate(hidden, axis=1), jnp.concatenate(downs, axis=0))
    ups = jnp.concatenate([weight_ref[expert, :, : 2 * width] for expert in range(count)], axis=1)
    grad_s[...] += dot_nt(jnp.concatenate(grads, axis=1), ups)

    @pl.when(step == pl.num_programs(0) - 1)
    def _():
        gate_part = part_s[...]
        spread = jnp.sum(gates * gate_part, axis=1, keepdims=True)
        logit_grad = (gates * (gate_part - spread)).astype(BF16)
        moe_ref[...] = moe_s[...].astype(BF16)
        grad_ref[...] = (grad_s[...] + dot_nt(logit_grad, router_ref[...])).astype(BF16)


def experts_both(tokens, base, low_o, out_up, gain, router, routes, cot, weights, count=4):
    rows = tokens.shape[0]
    experts = weights.shape[0]
    arrays = (tokens, base, low_o, out_up, gain.reshape(1, D), router, routes, cot)
    whole = pl.BlockSpec((rows, D), lambda step: (0, 0))
    return pl.pallas_call(
        functools.partial(experts_kernel, count),
        grid=(experts // count,),
        in_specs=[pl.BlockSpec(array.shape, lambda step: (0, 0)) for array in arrays]
        + [pl.BlockSpec((count,) + weights.shape[1:], lambda step: (step, 0, 0))],
        out_specs=[whole] * 3,
        out_shape=[shape((rows, D), F32), shape((rows, D), BF16), shape((rows, D), BF16)],
        scratch_shapes=[
            pltpu.VMEM((rows, D), BF16),
            pltpu.VMEM((rows, experts), F32),
            pltpu.VMEM((rows, experts), F32),
            pltpu.VMEM((rows, D), F32),
            pltpu.VMEM((rows, D), F32),
        ],
        compiler_params=WHOLE_VMEM,
        cost_estimate=cost(25e9, 30e6),
        name="experts",
    )(*arrays, weights)


def norm_back(vectors, gain, upstream):
    inv_root = lax.rsqrt(jnp.mean(vectors * vectors, axis=1, keepdims=True) + EPS)
    weighted = upstream * gain
    slope = jnp.mean(vectors * weighted, axis=1, keepdims=True)
    return inv_root * weighted - vectors * (inv_root * inv_root * inv_root) * slope


BRANCH_LOADS = ("residual", "normed_grad", "gain", "cot", "out_up", "low_o", "head")


def branch_kernel(length_ref, index_ref, shares, *refs):
    count = len(BRANCH_LOADS)
    residual_grad_ref, head_grad_ref, part_ref = refs[count : count + 3]
    load_sem, w_out_s, sem = refs[2 * count + 3 :]
    loads = Loads(BRANCH_LOADS, refs[:count], refs[count + 3 : 2 * count + 3], load_sem)
    n_exp, n_tp, _, wide = shares.shape
    rows = residual_grad_ref.shape[0]
    out_rows = w_out_s.shape[1] // n_exp
    copies = []
    for z in range(n_tp):
        for e in range(n_exp):
            at = 0
            for left in range(0, D, wide):
                taken = min(wide, D + LANES - left)
                copies.append(
                    pltpu.make_async_copy(
                        shares.at[e, z, at : at + out_rows, :taken],
                        w_out_s.at[z, e * out_rows : (e + 1) * out_rows, left : left + taken],
                        sem.at[len(copies)],
                    )
                )
                at += out_rows
    for copy in copies:
        copy.start()
    mask = adapter_mask(length_ref, index_ref, rows, LANES)
    residual, normed_grad = loads["residual"][...], loads["normed_grad"][...].astype(F32)
    residual_grad_ref[...] = loads["cot"][...].astype(F32) + norm_back(
        residual, loads["gain"][...], normed_grad
    )
    branch_grad = residual_grad_ref[...].astype(BF16)
    low_o_grad = (dot_nt(branch_grad, loads["out_up"][...]) * mask).astype(BF16)
    low_o = loads["low_o"][...]
    for at in range(D // LANES):
        lanes = slice(at * LANES, (at + 1) * LANES)
        part_ref[lanes, :] = dot_tn(low_o, branch_grad[:, lanes]).astype(BF16)
    part_ref[D:, :] = dot_tn(loads["head"][...], low_o_grad).astype(BF16)
    for copy in copies:
        copy.wait()
    for z in range(n_tp):
        head_grad_ref[z] = (
            dot_nt(branch_grad, w_out_s[z, :, :D]) + dot_nt(low_o_grad, w_out_s[z, :, D:])
        ).astype(BF16)


def branch_back(lengths, index, residual, low_o, normed_grad, cot, gain, out_up, head, shares):
    rows, heads_wide = head.shape
    n_exp, n_tp, _, wide = shares.shape
    arrays = (residual, normed_grad, gain.reshape(1, D), cot, out_up, low_o, head)
    return pl.pallas_call(
        branch_kernel,
        in_specs=[IN_SMEM] * 2 + [IN_HBM] * (1 + len(arrays)),
        out_specs=[IN_VMEM] * 3,
        out_shape=[
            shape((rows, D), F32),
            shape((n_tp, rows, heads_wide), BF16),
            shape((D + heads_wide, LANES), BF16),
        ],
        scratch_shapes=load_scratch(arrays)
        + [
            pltpu.VMEM((n_tp, heads_wide, D + LANES), BF16),
            pltpu.SemaphoreType.DMA((n_tp * n_exp * -(-D // wide),)),
        ],
        compiler_params=WHOLE_VMEM,
        cost_estimate=cost(5e9, 20e6),
        name="branch_backward",
    )(lengths, index, shares, *arrays)


BACKWARD_LOADS = (
    "attn_in", "low_q", "cosine", "sine", "head_grad", "residual_grad", "tokens", "gain",
    "qkv_down",
)


def backward_kernel(place_ref, length_ref, index_ref, shares, *refs):
    count = len(BACKWARD_LOADS)
    input_grad_ref, part_ref = refs[count : count + 2]
    load_sem, w_qkv_s, q_s, k_s, v_s, g_s, grad_s, sum_s, sem = refs[2 * count + 2 :]
    loads = Loads(BACKWARD_LOADS, refs[:count], refs[count + 2 : 2 * count + 2], load_sem)
    n_exp, n_tp, _, wide = shares.shape
    rows = input_grad_ref.shape[0]
    blocks = rows // ROWS
    groups = k_s.shape[0] // n_tp
    flags = turned_pieces(groups)
    scale = 1.0 / math.sqrt(HD)
    qkv_rows, up_rows, _ = share_rows(n_exp, 0)
    copies = []
    for z in range(n_tp):
        for e in range(n_exp):
            for source, target in (
                (shares.at[e, z, :qkv_rows, :], pl.ds(e * qkv_rows, qkv_rows)),
                (
                    shares.at[e, z, qkv_rows : qkv_rows + up_rows, :],
                    pl.ds(D + e * up_rows, up_rows),
                ),
            ):
                copies.append(
                    pltpu.make_async_copy(source, w_qkv_s.at[z, target, :], sem.at[len(copies)])
                )
    for copy in copies:
        copy.start()
    first = first_keys(length_ref, rows)
    attn_in = loads["attn_in"][...]
    low_q = loads["low_q"][...]
    cosine, sine = loads["cosine"], loads["sine"]
    head_grad = loads["head_grad"]
    seen = [seen_block(first, block) for block in range(blocks)]
    for z in range(n_tp):
        for copy in copies[z * 2 * n_exp : (z + 1) * 2 * n_exp]:
            copy.wait()
        projected = dot(attn_in, w_qkv_s[z, :D, :]) + dot(low_q, w_qkv_s[z, D:, :])
        columns = turn(projected, cosine[...], sine[...], flags)
        store_heads(columns, z * groups, q_s, k_s, v_s)
        for head in range(groups * PER):
            group, kind = divmod(head, PER)
            part = head_grad[z, :, head * HD : (head + 1) * HD]
            for block in range(blocks):
                g_s[z * groups + group, block, kind * ROWS : (kind + 1) * ROWS, :] = part[
                    block * ROWS : (block + 1) * ROWS
                ]

    def one_place(z, carried):
        pieces = []
        for group in range(groups):
            at = z * groups + group
            key_grad = jnp.zeros((HD, rows), F32)
            value_grad = jnp.zeros((HD, rows), F32)
            query_grads = []
            for block in range(blocks):
                count = (block + 1) * ROWS
                query, grad = q_s[at, block], g_s[at, block]
                key, value = k_s[at, :count, :], v_s[at, :count, :]
                scores = jnp.where(seen[block], dot_nt(query, key), -1e30)
                lifted = jnp.exp(scores - jnp.max(scores, axis=1, keepdims=True))
                probs = lifted * (1.0 / jnp.sum(lifted, axis=1, keepdims=True))
                weight_grad = dot_nt(grad, value)
                spread = jnp.sum(probs * weight_grad, axis=1, keepdims=True)
                score_grad = (probs * (weight_grad - spread)).astype(BF16)
                query_grads.append(dot(score_grad, key) * scale)

                def widen(part):
                    if count == rows:
                        return part
                    return jnp.concatenate([part, jnp.zeros((HD, rows - count), F32)], axis=1)

                key_grad += widen(dot_tn(query, score_grad))
                value_grad += widen(dot_tn(grad, probs.astype(BF16)))
            for head in range(PER):
                here = slice(head * ROWS, (head + 1) * ROWS)
                pieces.append(jnp.concatenate([part[here] for part in query_grads], axis=0))
            pieces += [key_grad.T, value_grad.T]
        joined = jnp.concatenate(pieces, axis=1)
        columns = turn(joined, cosine[...], -sine[...], flags)
        for at, column in enumerate(columns):
            grad_s[z, :, at * LANES : (at + 1) * LANES] = column.astype(BF16)
        return carried

    lax.fori_loop(0, n_tp, one_place, 0)
    sum_s[...] = dot_nt(grad_s[0], w_qkv_s[0])
    for z in range(1, n_tp):
        sum_s[...] += dot_nt(grad_s[z], w_qkv_s[z])
    mask = adapter_mask(length_ref, index_ref, rows, LANES)
    low_q_grad = (sum_s[:, D:] * mask).astype(BF16)
    part_ref[:D, :] = dot_tn(attn_in, low_q_grad).astype(BF16)
    own = grad_s[place_ref[0]]
    for at in range(wide // LANES):
        lanes = slice(at * LANES, (at + 1) * LANES)
        part_ref[D + at * LANES : D + (at + 1) * LANES, :] = dot_tn(low_q, own[:, lanes]).astype(
            BF16
        )
    attn_grad = sum_s[:, :D] + dot_nt(low_q_grad, loads["qkv_down"][...])
    tokens, gain = loads["tokens"][...].astype(F32), loads["gain"][...]
    residual_grad = loads["residual_grad"][...]
    input_grad_ref[...] = (residual_grad + norm_back(tokens, gain, attn_grad)).astype(BF16)


def attention_back(
    place, lengths, index, attn_in, low_q, head_grad, residual_grad, tokens, gain, qkv_down, tables,
    shares,
):
    rows = tokens.shape[0]
    n_exp, n_tp, _, wide = shares.shape
    count = KV_HEADS
    blocks = rows // ROWS
    arrays = (attn_in, low_q) + tables
    arrays += (head_grad, residual_grad, tokens, gain.reshape(1, D), qkv_down)
    return pl.pallas_call(
        backward_kernel,
        in_specs=[IN_SMEM] * 3 + [IN_HBM] * (1 + len(arrays)),
        out_specs=[IN_VMEM] * 2,
        out_shape=[shape((rows, D), BF16), shape((D + wide, LANES), BF16)],
        scratch_shapes=load_scratch(arrays)
        + [
            pltpu.VMEM((n_tp, D + LANES, wide), BF16),
            pltpu.VMEM((count, blocks, PER * ROWS, HD), BF16),
            pltpu.VMEM((count, rows, HD), BF16),
            pltpu.VMEM((count, rows, HD), BF16),
            pltpu.VMEM((count, blocks, PER * ROWS, HD), BF16),
            pltpu.VMEM((n_tp, rows, wide), BF16),
            pltpu.VMEM((rows, D + LANES), F32),
            pltpu.SemaphoreType.DMA((n_tp * n_exp * 2,)),
        ],
        compiler_params=WHOLE_VMEM,
        cost_estimate=cost(35e9, 20e6),
        name="attention_backward",
    )(place, lengths, index, shares, *arrays)


def kernel_body(
    tokens, attn_gain, moe_gain, w_qkv, w_out, w_router, w_gate, w_up, w_down, qkv_down, qkv_up,
    out_down, out_up, lengths, adapter_index, loss_mask, routes, upstream,
):
    n_exp = lax.axis_size("exp")
    rows = tokens.shape[0]
    exp_place = lax.axis_index("exp").astype(jnp.int32).reshape(1)
    tp_place = lax.axis_index("tp").astype(jnp.int32).reshape(1)
    tables = turn_tables(rows)
    own_experts = pack_experts(w_gate, w_up, w_down)
    weights = lax.all_gather(own_experts, "exp", axis=0, tiled=True)
    inputs, _ = lax.optimization_barrier((tokens, own_experts))
    attn_in, low_q, head, base, low_o = forward(
        lengths, adapter_index, inputs, attn_gain, w_qkv, qkv_down, qkv_up, w_out, out_down, tables
    )
    own_share = pack_share(exp_place, w_qkv, qkv_up, w_out, out_down, n_exp)
    z_shares = lax.all_gather(own_share, "tp", axis=0)
    base, low_o, _ = lax.optimization_barrier((base, low_o, z_shares))
    base, low_o = lax.psum((base, low_o), "tp")
    split = sum(share_rows(n_exp, 0))
    out_share, _ = lax.optimization_barrier((z_shares[:, split:], weights))
    out_shares = lax.all_gather(out_share, "exp", axis=0)
    occupied = jnp.arange(rows, dtype=jnp.int32) < jnp.sum(lengths)
    kept = occupied & (loss_mask > 0)
    cot = jnp.where(kept[:, None], upstream, jnp.zeros((), BF16))
    residual, moe_part, normed_part = experts_both(
        tokens, base, low_o, out_up, moe_gain, w_router, routes, cot, weights
    )
    normed_part, _ = lax.optimization_barrier((normed_part, out_shares))
    normed_grad = lax.psum(normed_part, "tp")
    qkv_share, _ = lax.optimization_barrier((z_shares[:, :split], normed_part))
    qkv_shares = lax.all_gather(qkv_share, "exp", axis=0)
    moe_part, _ = lax.optimization_barrier((moe_part, normed_grad))
    moe_out = lax.psum(moe_part, "tp")
    normed_grad, _ = lax.optimization_barrier((normed_grad, qkv_shares))
    residual_grad, head_grad, out_part = branch_back(
        lengths, adapter_index, residual, low_o, normed_grad, cot, moe_gain, out_up, head,
        out_shares,
    )
    out_parts = lax.all_gather(out_part, "exp", axis=0)
    input_grad, qkv_part = attention_back(
        tp_place, lengths, adapter_index, attn_in, low_q, head_grad, residual_grad, tokens,
        attn_gain, qkv_down, tables, qkv_shares,
    )
    moe_out, out_parts, _ = lax.optimization_barrier((moe_out, out_parts, qkv_part))
    output = (residual + moe_out.astype(F32)).astype(BF16)
    out_sum = jnp.sum(out_parts.astype(F32), axis=0)
    share = qkv_part.shape[0] // n_exp
    parts = lax.all_to_all(qkv_part.reshape(n_exp, share, LANES), "exp", 0, 0, tiled=True)
    qkv_sum = jnp.sum(parts.astype(F32), axis=0).astype(BF16)
    spread = jnp.broadcast_to(qkv_sum[None], (n_exp, share, LANES))
    qkv_sum = lax.all_to_all(spread, "exp", 0, 0, tiled=True).astype(F32).reshape(-1, LANES)

    def side_by_side(stacked):
        pieces = stacked.reshape(-1, LANES, LANES)
        return pieces.transpose(1, 0, 2).reshape(LANES, -1)

    return (
        output,
        input_grad,
        qkv_sum[:D],
        side_by_side(qkv_sum[D:]),
        out_sum[D:],
        side_by_side(out_sum[:D]),
    )


def product(left_m, right_m):
    return jnp.dot(left_m, right_m, preferred_element_type=jnp.float32)


def contract(einsum_form, left_m, right_m):
    return jnp.einsum(einsum_form, left_m, right_m, preferred_element_type=jnp.float32)


def rms_norm(vectors, gain_vec):
    inv_root = lax.rsqrt(jnp.mean(vectors * vectors, axis=-1, keepdims=True) + EPS)
    return vectors * inv_root * gain_vec


def rms_norm_back(vectors, gain_vec, upstream_grad):
    inv_root = lax.rsqrt(jnp.mean(vectors * vectors, axis=-1, keepdims=True) + EPS)
    weighted = upstream_grad * gain_vec
    return inv_root * weighted - vectors * (inv_root * inv_root * inv_root) * jnp.mean(
        vectors * weighted, axis=-1, keepdims=True
    )


def layout(length_row, index_row):
    places = jnp.arange(TOK_DEV, dtype=jnp.int32)
    doc_ends = jnp.cumsum(length_row)
    doc_starts = doc_ends - length_row
    member = (places[:, None] >= doc_starts[None, :]) & (places[:, None] < doc_ends[None, :])
    occupied = jnp.any(member, axis=1)
    position = jnp.sum(jnp.where(member, places[:, None] - doc_starts[None, :], 0), axis=1)
    owner_doc = jnp.sum(jnp.where(member, jnp.arange(DOCS, dtype=jnp.int32)[None, :], 0), axis=1)
    doc_ident = jnp.where(occupied, owner_doc, DOCS + places)
    chosen = jnp.sum(jnp.where(member, index_row[None, :], 0), axis=1)
    adapter_pick = occupied[:, None] & (
        chosen[:, None] == jnp.arange(ADAPTERS, dtype=jnp.int32)[None, :]
    )
    rank_mask = jnp.repeat(jnp.where(adapter_pick, 1.0, 0.0).astype(jnp.float32), RANK, axis=1)
    return (occupied, position, doc_ident, rank_mask)


def angles(position):
    half_width = HD // 2
    frequency = jnp.exp(-math.log(ROPE_BASE) * jnp.arange(half_width, dtype=jnp.float32) * 2.0 / HD)
    turned = position.astype(jnp.float32)[:, None] * frequency[None, :]
    return (jnp.cos(turned), jnp.sin(turned))


def rotate(vectors, cosine, sine_table):
    half_width = vectors.shape[-1] // 2
    front_half = vectors[..., :half_width]
    back_half = vectors[..., half_width:]
    return jnp.concatenate(
        [
            front_half * cosine - back_half * sine_table,
            back_half * cosine + front_half * sine_table,
        ],
        axis=-1,
    )


def moe(normed, cot_low, gates, gate_up, down):
    width = down.shape[1]
    both = contract("td,edf->tef", normed, gate_up)
    pre_gate = both[:, :, :width]
    pre_up = both[:, :, width:]
    sigmoid_g = jax.nn.sigmoid(pre_gate)
    activated = pre_gate * sigmoid_g
    hidden = (activated * pre_up).astype(jnp.bfloat16).astype(jnp.float32)
    inner_raw = contract("td,efd->tef", cot_low, down)
    gate_part = jnp.sum(hidden * inner_raw, axis=-1)
    moe_part = contract("tef,efd->td", (gates[:, :, None] * hidden).astype(jnp.bfloat16), down)
    inner_grad = inner_raw * gates[:, :, None]
    grad_gate = inner_grad * pre_up * sigmoid_g * (1.0 + pre_gate * (1.0 - sigmoid_g))
    grad_up = inner_grad * activated
    grad_both = jnp.concatenate([grad_gate, grad_up], axis=2).astype(jnp.bfloat16)
    normed_part = contract("tef,edf->td", grad_both, gate_up)
    return (moe_part, gate_part, normed_part)


def body(
    tokens,
    attn_gain,
    moe_gain,
    w_qkv,
    w_out,
    w_router,
    w_gate,
    w_up,
    w_down,
    qkv_down,
    qkv_up,
    out_down,
    out_up,
    lengths,
    adapter_index,
    loss_mask,
    routes,
    upstream,
):
    n_exp = lax.axis_size("exp")
    groups = KV_HEADS // lax.axis_size("tp")
    per_group = HEADS // KV_HEADS
    experts = EXP_DEV * n_exp
    gate_up = lax.all_gather(jnp.concatenate([w_gate, w_up], axis=2), "exp", axis=0, tiled=True)
    down = lax.all_gather(w_down, "exp", axis=0, tiled=True)
    block_rows = min(512, TOK_DEV)
    blocks = TOK_DEV // block_rows
    score_scale = 1.0 / math.sqrt(HD)
    places = jnp.arange(TOK_DEV, dtype=jnp.int32)
    occupied, position, doc_ident, rank_mask = layout(lengths[0], adapter_index[0])
    mask_low = rank_mask.astype(jnp.bfloat16)
    cosine, sine_table = angles(position)
    inputs = tokens.astype(jnp.float32)
    attn_in = rms_norm(inputs, attn_gain).astype(jnp.bfloat16)
    low_q = (product(attn_in, qkv_down) * rank_mask).astype(jnp.bfloat16)
    projected = (product(attn_in, w_qkv) + product(low_q, qkv_up)).reshape(
        TOK_DEV, groups, per_group + 2, HD
    )
    query_rows = rotate(
        projected[:, :, :per_group], cosine[:, None, None], sine_table[:, None, None]
    ).astype(jnp.bfloat16)
    key_rows = rotate(projected[:, :, per_group], cosine[:, None], sine_table[:, None]).astype(
        jnp.bfloat16
    )
    val_rows = projected[:, :, per_group + 1].astype(jnp.bfloat16)

    def masked_scores(q_blk, q_place, q_ident):
        scores = contract("qgrd,kgd->grqk", q_blk, key_rows) * score_scale
        allowed = (q_ident[:, None] == doc_ident[None, :]) & (places[None, :] <= q_place[:, None])
        return jnp.where(allowed, scores, -1e30)

    def attend(pieces):
        q_blk, q_place, q_ident = pieces
        scores = masked_scores(q_blk, q_place, q_ident)
        row_max = jnp.max(scores, axis=-1, keepdims=True)
        lifted = jnp.exp(scores - row_max)
        row_total = jnp.sum(lifted, axis=-1, keepdims=True)
        weights = (lifted / row_total).astype(jnp.bfloat16)
        return (
            contract("grqk,kgd->qgrd", weights, val_rows),
            row_max[..., 0] + jnp.log(row_total[..., 0]),
        )

    query_blocks = query_rows.reshape(blocks, block_rows, groups, per_group, HD)
    place_blocks = places.reshape(blocks, block_rows)
    ident_blocks = doc_ident.reshape(blocks, block_rows)
    attended, log_totals = lax.map(attend, (query_blocks, place_blocks, ident_blocks))
    head_rows = attended.reshape(TOK_DEV, groups * per_group * HD).astype(jnp.bfloat16)
    attn_base, low_rank = (
        lax.psum(product(head_rows, w_out).astype(jnp.bfloat16), "tp").astype(jnp.float32),
        lax.psum((product(head_rows, out_down) * rank_mask).astype(jnp.bfloat16), "tp").astype(
            jnp.float32
        ),
    )
    low_o = low_rank.astype(jnp.bfloat16)
    residual = inputs + attn_base + product(low_o, out_up)
    normed = rms_norm(residual, moe_gain).astype(jnp.bfloat16)
    logits = product(normed, w_router)
    one_hot = routes[:, :, None] == jnp.arange(experts, dtype=jnp.int32)[None, None, :]
    routed = jnp.any(one_hot, axis=1)
    gates = jax.nn.softmax(jnp.where(routed, logits, -1e30), axis=-1)
    live_mask = jnp.where(occupied & (loss_mask > 0), 1.0, 0.0).astype(jnp.float32)
    cotangent = upstream.astype(jnp.float32) * live_mask[:, None]
    cot_low = cotangent.astype(jnp.bfloat16)
    moe_part, gate_part, normed_part = moe(normed, cot_low, gates, gate_up, down)
    logit_grad = (
        gates * (gate_part - jnp.sum(gates * gate_part, axis=-1, keepdims=True))
    ).astype(jnp.bfloat16)
    normed_part = (normed_part + product(logit_grad, w_router.T)).astype(jnp.bfloat16)
    normed_sum = lax.psum(normed_part, "tp")
    normed_sum, moe_part = lax.optimization_barrier((normed_sum, moe_part.astype(jnp.bfloat16)))
    normed_grad = normed_sum.astype(jnp.float32)
    moe_out = lax.psum(moe_part, "tp").astype(jnp.float32)
    output = (residual + moe_out).astype(jnp.bfloat16)
    residual_grad = cotangent + rms_norm_back(residual, moe_gain, normed_grad)
    branch_grad = residual_grad.astype(jnp.bfloat16)
    low_o_grad = product(branch_grad, out_up.T).astype(jnp.bfloat16) * mask_low
    out_up_part = contract("tr,td->rd", low_o, branch_grad)
    head_grad = (product(branch_grad, w_out.T) + product(low_o_grad, out_down.T)).astype(
        jnp.bfloat16
    )
    out_down_part = contract("tc,tr->cr", head_rows, low_o_grad)
    grad_blocks = head_grad.reshape(blocks, block_rows, groups, per_group, HD)

    def attend_back(carried, pieces):
        key_acc, val_acc = carried
        q_blk, q_place, q_ident, lse_blk, g_blk = pieces
        weights = jnp.exp(masked_scores(q_blk, q_place, q_ident) - lse_blk[..., None])
        weight_grad = contract("qgrd,kgd->grqk", g_blk, val_rows)
        score_grad = (
            weights * (weight_grad - jnp.sum(weights * weight_grad, axis=-1, keepdims=True))
        ).astype(jnp.bfloat16)
        query_grad = contract("grqk,kgd->qgrd", score_grad, key_rows) * score_scale
        key_acc = key_acc + contract("grqk,qgrd->kgd", score_grad, q_blk) * score_scale
        val_acc = val_acc + contract("grqk,qgrd->kgd", weights.astype(jnp.bfloat16), g_blk)
        return ((key_acc, val_acc), query_grad)

    zero_acc = jnp.zeros((TOK_DEV, groups, HD), jnp.float32)
    (key_grad, val_grad), query_grad = lax.scan(
        attend_back,
        (zero_acc, zero_acc),
        (query_blocks, place_blocks, ident_blocks, log_totals, grad_blocks),
    )
    query_grad = rotate(
        query_grad.reshape(TOK_DEV, groups, per_group, HD),
        cosine[:, None, None],
        -sine_table[:, None, None],
    )
    key_grad = rotate(key_grad, cosine[:, None], -sine_table[:, None])
    projected_grad = (
        jnp.concatenate([query_grad, key_grad[:, :, None], val_grad[:, :, None]], axis=2)
        .reshape(TOK_DEV, -1)
        .astype(jnp.bfloat16)
    )
    qkv_up_part = contract("tr,tc->rc", low_q, projected_grad)
    attn_grad, low_q_grad = (
        lax.psum(contract("tc,dc->td", projected_grad, w_qkv).astype(jnp.bfloat16), "tp").astype(
            jnp.float32
        ),
        lax.psum(contract("tc,rc->tr", projected_grad, qkv_up).astype(jnp.bfloat16), "tp").astype(
            jnp.float32
        ),
    )
    low_q_grad = low_q_grad.astype(jnp.bfloat16) * mask_low
    attn_grad = attn_grad + contract("tr,dr->td", low_q_grad, qkv_down)
    qkv_down_part = contract("td,tr->dr", attn_in, low_q_grad)
    input_grad = (residual_grad + rms_norm_back(inputs, attn_gain, attn_grad)).astype(jnp.bfloat16)
    summed = (
        lax.psum(qkv_down_part.astype(jnp.bfloat16), "exp").astype(jnp.float32),
        lax.psum(qkv_up_part.astype(jnp.bfloat16), "exp").astype(jnp.float32),
        lax.psum(out_down_part.astype(jnp.bfloat16), "exp").astype(jnp.float32),
        lax.psum(out_up_part.astype(jnp.bfloat16), "exp").astype(jnp.float32),
    )
    return (output, input_grad, summed[0], summed[1], summed[2], summed[3])


def kernels_fit(mesh):
    n_exp, n_tp = mesh.shape["exp"], mesh.shape["tp"]
    groups = KV_HEADS // n_tp
    return groups % 2 == 0 and FF // n_tp == LANES and LANES // n_exp % 16 == 0


def solution(mesh):
    placed = (
        P("exp", None),
        P(),
        P(),
        P(None, "tp"),
        P("tp", None),
        P(),
        P("exp", None, "tp"),
        P("exp", None, "tp"),
        P("exp", "tp", None),
        P(),
        P(None, "tp"),
        P("tp", None),
        P(),
        P("exp", None),
        P("exp", None),
        P("exp"),
        P("exp", None),
        P("exp", None),
    )
    return jax.shard_map(
        kernel_body if kernels_fit(mesh) else body,
        mesh=mesh,
        in_specs=placed,
        out_specs=(P("exp", None), P("exp", None), P(), P(None, "tp"), P("tp", None), P()),
        check_vma=False,
    )
```

```python
import functools
import math

import jax
import jax.numpy as jnp
import numpy as np
from jax import lax
from jax.experimental import pallas as pl
from jax.experimental.pallas import tpu as pltpu
from jax.sharding import PartitionSpec as P

D = 1536
HEADS = 24
KV_HEADS = 8
HD = 64
TOP = 8
RANK = 16
ADAPTERS = 8
EXP_DEV = 2
DOCS = 4
TOK_DEV = 512
FF = 512
EPS = 1e-06
ROPE_BASE = 10000.0

PER = HEADS // KV_HEADS
LANES = 128
ROWS = 128
F32 = jnp.float32
BF16 = jnp.bfloat16
MIB = 2**20
NT = (((1,), (1,)), ((), ()))
TN = (((0,), (0,)), ((), ()))
WHOLE_VMEM = pltpu.CompilerParams(vmem_limit_bytes=63 * MIB)
IN_VMEM = pl.BlockSpec(memory_space=pltpu.VMEM)
IN_SMEM = pl.BlockSpec(memory_space=pltpu.SMEM)
IN_HBM = pl.BlockSpec(memory_space=pltpu.HBM)


def dot(left, right):
    return jnp.dot(left, right, preferred_element_type=F32)


def dot_nt(left, right):
    return lax.dot_general(left, right, NT, preferred_element_type=F32)


def dot_tn(left, right):
    return lax.dot_general(left, right, TN, preferred_element_type=F32)


def cost(flops, moved):
    return pl.CostEstimate(flops=int(flops), bytes_accessed=int(moved), transcendentals=0)


def shape(dims, dtype):
    return jax.ShapeDtypeStruct(dims, dtype)


def turn_tables(rows):
    half = HD // 2
    frequency = np.exp(-math.log(ROPE_BASE) * np.arange(half, dtype=np.float64) * 2.0 / HD)
    turned = np.arange(rows, dtype=np.float64)[:, None] * frequency[None, :]
    cosine, sine = np.cos(turned), np.sin(turned)
    return (
        jnp.asarray(np.concatenate([cosine] * 4, axis=1), F32),
        jnp.asarray(np.concatenate([-sine, sine, -sine, sine], axis=1), F32),
    )


def turned_pieces(groups):
    return [piece < PER + 1 for _ in range(groups) for piece in range(PER + 2)]


def turn(joined, cosine, sine, flags):
    lane = lax.broadcasted_iota(jnp.int32, cosine.shape, 1)
    front = (lane & 32) == 0
    left = lane < HD
    columns = []
    for at in range(joined.shape[1] // LANES):
        column = joined[:, at * LANES : (at + 1) * LANES]
        swapped = jnp.where(front, pltpu.roll(column, 96, 1), pltpu.roll(column, 32, 1))
        rotated = column * cosine + swapped * sine
        if not (flags[2 * at] and flags[2 * at + 1]):
            rotated = jnp.where(left if flags[2 * at] else jnp.logical_not(left), rotated, column)
        columns.append(rotated)
    return columns


def first_keys(length_ref, rows):
    row = lax.broadcasted_iota(jnp.int32, (rows, 1), 0)
    begin = jnp.zeros((rows, 1), jnp.int32)
    end = 0
    for doc in range(DOCS):
        if doc:
            begin = jnp.where(row >= end, end, begin)
        end = end + length_ref[0, doc]
    return jnp.where(row >= end, row, begin)


def adapter_mask(length_ref, index_ref, rows, width):
    row = lax.broadcasted_iota(jnp.int32, (rows, width), 0)
    adapter = lax.shift_right_logical(lax.broadcasted_iota(jnp.int32, (rows, width), 1), 4)
    mask = jnp.zeros((rows, width), F32)
    begin = 0
    for doc in range(DOCS):
        end = begin + length_ref[0, doc]
        inside = (row >= begin) & (row < end) & (adapter == index_ref[0, doc])
        mask = jnp.where(inside, 1.0, mask)
        begin = end
    return mask


def seen_block(first, block):
    keys = (block + 1) * ROWS
    row = lax.broadcasted_iota(jnp.int32, (ROWS, keys), 0) + block * ROWS
    key = lax.broadcasted_iota(jnp.int32, (ROWS, keys), 1)
    seen = (key <= row) & (key >= first[block * ROWS : (block + 1) * ROWS])
    return jnp.concatenate([seen] * PER, axis=0)


def store_heads(columns, slot, q_s, k_s, v_s):
    scale = 1.0 / math.sqrt(HD)
    blocks = q_s.shape[1]
    for at, column in enumerate(columns):
        halves = (column[:, :HD], pltpu.roll(column, HD, 1)[:, :HD])
        for piece, part in zip((2 * at, 2 * at + 1), halves):
            group, kind = divmod(piece, PER + 2)
            if kind == PER:
                k_s[slot + group] = part.astype(BF16)
            elif kind == PER + 1:
                v_s[slot + group] = part.astype(BF16)
            else:
                part = (part * scale).astype(BF16)
                for block in range(blocks):
                    q_s[slot + group, block, kind * ROWS : (kind + 1) * ROWS, :] = part[
                        block * ROWS : (block + 1) * ROWS
                    ]


def run_copies(pairs, sem):
    copies = [
        pltpu.make_async_copy(source, target, sem.at[number])
        for number, (source, target) in enumerate(pairs)
    ]
    for copy in copies:
        copy.start()
    for copy in copies:
        copy.wait()


def pack_experts_kernel(gate, up, down, packed, held, sem, out_sem):
    width = gate.shape[2]
    pairs = []
    for expert in range(gate.shape[0]):
        pairs.append((gate.at[expert], held.at[expert, :, :width]))
        pairs.append((up.at[expert], held.at[expert, :, width : 2 * width]))
        for at in range(D // LANES):
            lanes = slice(at * LANES, (at + 1) * LANES)
            pairs.append((down.at[expert, :, lanes], held.at[expert, lanes, 2 * width :]))
    run_copies(pairs, sem)
    run_copies([(held, packed)], out_sem)


def pack_experts(w_gate, w_up, w_down):
    count, _, width = w_gate.shape
    packed = shape((count, D, 3 * width), BF16)
    return pl.pallas_call(
        pack_experts_kernel,
        in_specs=[IN_HBM] * 3,
        out_specs=IN_HBM,
        out_shape=packed,
        scratch_shapes=[
            pltpu.VMEM(packed.shape, BF16),
            pltpu.SemaphoreType.DMA((count * (2 + D // LANES),)),
            pltpu.SemaphoreType.DMA((1,)),
        ],
        compiler_params=WHOLE_VMEM,
        cost_estimate=cost(0, 2 * 2 * count * D * 3 * width),
        name="pack_experts",
    )(w_gate, w_up, w_down)


def share_rows(n_exp, heads_wide):
    return (D // n_exp, LANES // n_exp, heads_wide // n_exp)


def pack_share_kernel(n_exp, place_ref, w_qkv, qkv_up, w_out, out_down, packed, held, sem, out_sem):
    qkv_rows, up_rows, out_rows = share_rows(n_exp, w_out.shape[0])
    place = place_ref[0]
    own_qkv = pl.ds(pl.multiple_of(place * qkv_rows, 16), qkv_rows)
    own_up = pl.ds(pl.multiple_of(place * up_rows, 16), up_rows)
    own_out = pl.ds(pl.multiple_of(place * out_rows, 16), out_rows)
    wide = w_qkv.shape[1]
    at = qkv_rows + up_rows
    pairs = [
        (w_qkv.at[own_qkv, :], held.at[:qkv_rows, :]),
        (qkv_up.at[own_up, :], held.at[qkv_rows:at, :]),
    ]
    for left in range(0, D, wide):
        taken = min(wide, D - left)
        target = held.at[at : at + out_rows, :taken]
        pairs.append((w_out.at[own_out, left : left + taken], target))
        at += out_rows
    at -= out_rows
    pairs.append((out_down.at[own_out, :], held.at[at : at + out_rows, taken : taken + LANES]))
    held[at : at + out_rows, taken + LANES :] = jnp.zeros(
        (out_rows, wide - taken - LANES), BF16
    )
    run_copies(pairs, sem)
    run_copies([(held, packed)], out_sem)


def pack_share(place, w_qkv, qkv_up, w_out, out_down, n_exp):
    qkv_rows, up_rows, out_rows = share_rows(n_exp, w_out.shape[0])
    wide = w_qkv.shape[1]
    pieces = -(-D // wide)
    packed = shape((qkv_rows + up_rows + pieces * out_rows, wide), BF16)
    return pl.pallas_call(
        functools.partial(pack_share_kernel, n_exp),
        in_specs=[IN_SMEM] + [IN_HBM] * 4,
        out_specs=IN_HBM,
        out_shape=packed,
        scratch_shapes=[
            pltpu.VMEM(packed.shape, BF16),
            pltpu.SemaphoreType.DMA((3 + pieces,)),
            pltpu.SemaphoreType.DMA((1,)),
        ],
        compiler_params=WHOLE_VMEM,
        cost_estimate=cost(0, 4 * packed.shape[0] * wide),
        name="pack_share",
    )(place, w_qkv, qkv_up, w_out, out_down)


class Loads:
    def __init__(self, names, sources, targets, sem):
        self.copies = {
            name: pltpu.make_async_copy(source, target, sem.at[number])
            for number, (name, source, target) in enumerate(zip(names, sources, targets))
        }
        self.targets = dict(zip(names, targets))
        for copy in self.copies.values():
            copy.start()

    def __getitem__(self, name):
        copy = self.copies.pop(name, None)
        if copy is not None:
            copy.wait()
        return self.targets[name]


def load_scratch(arrays):
    return [pltpu.VMEM(array.shape, array.dtype) for array in arrays] + [
        pltpu.SemaphoreType.DMA((len(arrays),))
    ]


FORWARD_LOADS = (
    "tokens", "gain", "qkv_down", "w_qkv", "qkv_up", "cosine", "sine", "w_out", "out_down",
)


def forward_kernel(length_ref, index_ref, *refs):
    count = len(FORWARD_LOADS)
    attn_in_ref, low_q_ref, head_ref, base_ref, low_ref = refs[count : count + 5]
    load_sem, q_s, k_s, v_s = refs[2 * count + 5 :]
    loads = Loads(FORWARD_LOADS, refs[:count], refs[count + 5 : 2 * count + 5], load_sem)
    rows = attn_in_ref.shape[0]
    groups = k_s.shape[0]
    mask = adapter_mask(length_ref, index_ref, rows, LANES)
    first = first_keys(length_ref, rows)
    inputs = loads["tokens"][...].astype(F32)
    inv_root = lax.rsqrt(jnp.mean(inputs * inputs, axis=1, keepdims=True) + EPS)
    attn_in_ref[...] = (inputs * inv_root * loads["gain"][...]).astype(BF16)
    attn_in = attn_in_ref[...]
    low_q = (dot(attn_in, loads["qkv_down"][...]) * mask).astype(BF16)
    low_q_ref[...] = low_q
    projected = dot(attn_in, loads["w_qkv"][...]) + dot(low_q, loads["qkv_up"][...])
    cosine, sine = loads["cosine"][...], loads["sine"][...]
    store_heads(turn(projected, cosine, sine, turned_pieces(groups)), 0, q_s, k_s, v_s)
    for block in range(rows // ROWS):
        here = slice(block * ROWS, (block + 1) * ROWS)
        keys = (block + 1) * ROWS
        seen = seen_block(first, block)
        heads = []
        for group in range(groups):
            scores = jnp.where(seen, dot_nt(q_s[group, block], k_s[group, :keys, :]), -1e30)
            lifted = jnp.exp(scores - jnp.max(scores, axis=1, keepdims=True))
            probs = (lifted * (1.0 / jnp.sum(lifted, axis=1, keepdims=True))).astype(BF16)
            out = dot(probs, v_s[group, :keys, :])
            heads += [out[head * ROWS : (head + 1) * ROWS] for head in range(PER)]
        head_ref[here, :] = jnp.concatenate(heads, axis=1).astype(BF16)
    head_out = head_ref[...]
    base_ref[...] = dot(head_out, loads["w_out"][...]).astype(BF16)
    low_ref[...] = (dot(head_out, loads["out_down"][...]) * mask).astype(BF16)


def forward(lengths, index, tokens, gain, w_qkv, qkv_down, qkv_up, w_out, out_down, tables):
    rows = tokens.shape[0]
    heads_wide = w_out.shape[0]
    groups = w_qkv.shape[1] // (HD * (PER + 2))
    arrays = (tokens, gain.reshape(1, D), qkv_down, w_qkv, qkv_up) + tables + (w_out, out_down)
    return pl.pallas_call(
        forward_kernel,
        in_specs=[IN_SMEM] * 2 + [IN_HBM] * len(arrays),
        out_specs=[IN_VMEM] * 5,
        out_shape=[
            shape((rows, D), BF16),
            shape((rows, LANES), BF16),
            shape((rows, heads_wide), BF16),
            shape((rows, D), BF16),
            shape((rows, LANES), BF16),
        ],
        scratch_shapes=load_scratch(arrays)
        + [
            pltpu.VMEM((groups, rows // ROWS, PER * ROWS, HD), BF16),
            pltpu.VMEM((groups, rows, HD), BF16),
            pltpu.VMEM((groups, rows, HD), BF16),
        ],
        compiler_params=WHOLE_VMEM,
        cost_estimate=cost(6e9, 10e6),
        name="attention_forward",
    )(lengths, index, *arrays)


def experts_kernel(
    count, tokens_ref, base_ref, low_o_ref, out_up_ref, gain_ref, router_ref, routes_ref, cot_ref,
    weight_ref, residual_ref, moe_ref, grad_ref,
    normed_s, gates_s, part_s, moe_s, grad_s,
):
    step = pl.program_id(0)
    lane = lax.broadcasted_iota(jnp.int32, gates_s.shape, 1)
    width = weight_ref.shape[2] // 3

    @pl.when(step == 0)
    def _():
        residual = (
            tokens_ref[...].astype(F32)
            + base_ref[...].astype(F32)
            + dot(low_o_ref[...], out_up_ref[...])
        )
        residual_ref[...] = residual
        inv_root = lax.rsqrt(jnp.mean(residual * residual, axis=1, keepdims=True) + EPS)
        normed = (residual * inv_root * gain_ref[...]).astype(BF16)
        normed_s[...] = normed
        logits = dot(normed, router_ref[...])
        routed = lane == routes_ref[:, 0:1]
        for slot in range(1, TOP):
            routed = routed | (lane == routes_ref[:, slot : slot + 1])
        logits = jnp.where(routed, logits, -1e30)
        lifted = jnp.exp(logits - jnp.max(logits, axis=1, keepdims=True))
        gates_s[...] = lifted / jnp.sum(lifted, axis=1, keepdims=True)
        part_s[...] = jnp.zeros_like(part_s)
        moe_s[...] = jnp.zeros_like(moe_s)
        grad_s[...] = jnp.zeros_like(grad_s)

    normed = normed_s[...]
    cot = cot_ref[...]
    gates = gates_s[...]
    part = jnp.zeros(gates.shape, F32)
    downs = [
        jnp.concatenate(
            [
                weight_ref[expert, at * LANES : (at + 1) * LANES, 2 * width :]
                for at in range(D // LANES)
            ],
            axis=1,
        )
        for expert in range(count)
    ]
    hidden, grads = [], []
    for pair in range(count // 2):
        both_down = jnp.concatenate(downs[2 * pair : 2 * pair + 2], axis=0)
        both_raw = dot_nt(cot, both_down)
        for half in range(2):
            expert = 2 * pair + half
            joined = dot(normed, weight_ref[expert, :, : 2 * width])
            pre_gate = joined[:, :width]
            pre_up = joined[:, width:]
            raw = both_raw[:, half * width : (half + 1) * width]
            sigmoid = 0.5 * jnp.tanh(0.5 * pre_gate) + 0.5
            activated = pre_gate * sigmoid
            value = activated * pre_up
            here = lane == step * count + expert
            gate = jnp.sum(jnp.where(here, gates, 0.0), axis=1, keepdims=True)
            part += jnp.where(here, jnp.sum(value * raw, axis=1, keepdims=True), 0.0)
            hidden.append((gate * value).astype(BF16))
            inner = raw * gate
            grads.append((inner * pre_up * (sigmoid + activated * (1.0 - sigmoid))).astype(BF16))
            grads.append((inner * activated).astype(BF16))
    part_s[...] += part
    moe_s[...] += dot(jnp.concatenate(hidden, axis=1), jnp.concatenate(downs, axis=0))
    ups = jnp.concatenate([weight_ref[expert, :, : 2 * width] for expert in range(count)], axis=1)
    grad_s[...] += dot_nt(jnp.concatenate(grads, axis=1), ups)

    @pl.when(step == pl.num_programs(0) - 1)
    def _():
        gate_part = part_s[...]
        spread = jnp.sum(gates * gate_part, axis=1, keepdims=True)
        logit_grad = (gates * (gate_part - spread)).astype(BF16)
        moe_ref[...] = moe_s[...].astype(BF16)
        grad_ref[...] = (grad_s[...] + dot_nt(logit_grad, router_ref[...])).astype(BF16)


def experts_both(tokens, base, low_o, out_up, gain, router, routes, cot, weights, count=4):
    rows = tokens.shape[0]
    experts = weights.shape[0]
    arrays = (tokens, base, low_o, out_up, gain.reshape(1, D), router, routes, cot)
    whole = pl.BlockSpec((rows, D), lambda step: (0, 0))
    return pl.pallas_call(
        functools.partial(experts_kernel, count),
        grid=(experts // count,),
        in_specs=[pl.BlockSpec(array.shape, lambda step: (0, 0)) for array in arrays]
        + [pl.BlockSpec((count,) + weights.shape[1:], lambda step: (step, 0, 0))],
        out_specs=[whole] * 3,
        out_shape=[shape((rows, D), F32), shape((rows, D), BF16), shape((rows, D), BF16)],
        scratch_shapes=[
            pltpu.VMEM((rows, D), BF16),
            pltpu.VMEM((rows, experts), F32),
            pltpu.VMEM((rows, experts), F32),
            pltpu.VMEM((rows, D), F32),
            pltpu.VMEM((rows, D), F32),
        ],
        compiler_params=WHOLE_VMEM,
        cost_estimate=cost(25e9, 30e6),
        name="experts",
    )(*arrays, weights)


def norm_back(vectors, gain, upstream):
    inv_root = lax.rsqrt(jnp.mean(vectors * vectors, axis=1, keepdims=True) + EPS)
    weighted = upstream * gain
    slope = jnp.mean(vectors * weighted, axis=1, keepdims=True)
    return inv_root * weighted - vectors * (inv_root * inv_root * inv_root) * slope


BRANCH_LOADS = ("residual", "normed_grad", "gain", "cot", "out_up", "low_o", "head")


def branch_kernel(length_ref, index_ref, shares, *refs):
    count = len(BRANCH_LOADS)
    residual_grad_ref, head_grad_ref, part_ref = refs[count : count + 3]
    load_sem, w_out_s, sem = refs[2 * count + 3 :]
    loads = Loads(BRANCH_LOADS, refs[:count], refs[count + 3 : 2 * count + 3], load_sem)
    n_exp, n_tp, _, wide = shares.shape
    rows = residual_grad_ref.shape[0]
    out_rows = w_out_s.shape[1] // n_exp
    copies = []
    for z in range(n_tp):
        for e in range(n_exp):
            at = 0
            for left in range(0, D, wide):
                taken = min(wide, D + LANES - left)
                copies.append(
                    pltpu.make_async_copy(
                        shares.at[e, z, at : at + out_rows, :taken],
                        w_out_s.at[z, e * out_rows : (e + 1) * out_rows, left : left + taken],
                        sem.at[len(copies)],
                    )
                )
                at += out_rows
    for copy in copies:
        copy.start()
    mask = adapter_mask(length_ref, index_ref, rows, LANES)
    residual, normed_grad = loads["residual"][...], loads["normed_grad"][...].astype(F32)
    residual_grad_ref[...] = loads["cot"][...].astype(F32) + norm_back(
        residual, loads["gain"][...], normed_grad
    )
    branch_grad = residual_grad_ref[...].astype(BF16)
    low_o_grad = (dot_nt(branch_grad, loads["out_up"][...]) * mask).astype(BF16)
    low_o = loads["low_o"][...]
    for at in range(D // LANES):
        lanes = slice(at * LANES, (at + 1) * LANES)
        part_ref[lanes, :] = dot_tn(low_o, branch_grad[:, lanes]).astype(BF16)
    part_ref[D:, :] = dot_tn(loads["head"][...], low_o_grad).astype(BF16)
    for copy in copies:
        copy.wait()
    for z in range(n_tp):
        head_grad_ref[z] = (
            dot_nt(branch_grad, w_out_s[z, :, :D]) + dot_nt(low_o_grad, w_out_s[z, :, D:])
        ).astype(BF16)


def branch_back(lengths, index, residual, low_o, normed_grad, cot, gain, out_up, head, shares):
    rows, heads_wide = head.shape
    n_exp, n_tp, _, wide = shares.shape
    arrays = (residual, normed_grad, gain.reshape(1, D), cot, out_up, low_o, head)
    return pl.pallas_call(
        branch_kernel,
        in_specs=[IN_SMEM] * 2 + [IN_HBM] * (1 + len(arrays)),
        out_specs=[IN_VMEM] * 3,
        out_shape=[
            shape((rows, D), F32),
            shape((n_tp, rows, heads_wide), BF16),
            shape((D + heads_wide, LANES), BF16),
        ],
        scratch_shapes=load_scratch(arrays)
        + [
            pltpu.VMEM((n_tp, heads_wide, D + LANES), BF16),
            pltpu.SemaphoreType.DMA((n_tp * n_exp * -(-D // wide),)),
        ],
        compiler_params=WHOLE_VMEM,
        cost_estimate=cost(5e9, 20e6),
        name="branch_backward",
    )(lengths, index, shares, *arrays)


BACKWARD_LOADS = (
    "attn_in", "low_q", "cosine", "sine", "head_grad", "residual_grad", "tokens", "gain",
    "qkv_down",
)


def backward_kernel(place_ref, length_ref, index_ref, shares, *refs):
    count = len(BACKWARD_LOADS)
    input_grad_ref, part_ref = refs[count : count + 2]
    load_sem, w_qkv_s, q_s, k_s, v_s, g_s, grad_s, sum_s, sem = refs[2 * count + 2 :]
    loads = Loads(BACKWARD_LOADS, refs[:count], refs[count + 2 : 2 * count + 2], load_sem)
    n_exp, n_tp, _, wide = shares.shape
    rows = input_grad_ref.shape[0]
    blocks = rows // ROWS
    groups = k_s.shape[0] // n_tp
    flags = turned_pieces(groups)
    scale = 1.0 / math.sqrt(HD)
    qkv_rows, up_rows, _ = share_rows(n_exp, 0)
    copies = []
    for z in range(n_tp):
        for e in range(n_exp):
            for source, target in (
                (shares.at[e, z, :qkv_rows, :], pl.ds(e * qkv_rows, qkv_rows)),
                (
                    shares.at[e, z, qkv_rows : qkv_rows + up_rows, :],
                    pl.ds(D + e * up_rows, up_rows),
                ),
            ):
                copies.append(
                    pltpu.make_async_copy(source, w_qkv_s.at[z, target, :], sem.at[len(copies)])
                )
    for copy in copies:
        copy.start()
    first = first_keys(length_ref, rows)
    attn_in = loads["attn_in"][...]
    low_q = loads["low_q"][...]
    cosine, sine = loads["cosine"], loads["sine"]
    head_grad = loads["head_grad"]
    seen = [seen_block(first, block) for block in range(blocks)]
    for z in range(n_tp):
        for copy in copies[z * 2 * n_exp : (z + 1) * 2 * n_exp]:
            copy.wait()
        projected = dot(attn_in, w_qkv_s[z, :D, :]) + dot(low_q, w_qkv_s[z, D:, :])
        columns = turn(projected, cosine[...], sine[...], flags)
        store_heads(columns, z * groups, q_s, k_s, v_s)
        for head in range(groups * PER):
            group, kind = divmod(head, PER)
            part = head_grad[z, :, head * HD : (head + 1) * HD]
            for block in range(blocks):
                g_s[z * groups + group, block, kind * ROWS : (kind + 1) * ROWS, :] = part[
                    block * ROWS : (block + 1) * ROWS
                ]

    def one_place(z, carried):
        pieces = []
        for group in range(groups):
            at = z * groups + group
            key_grad = jnp.zeros((HD, rows), F32)
            value_grad = jnp.zeros((HD, rows), F32)
            query_grads = []
            for block in range(blocks):
                count = (block + 1) * ROWS
                query, grad = q_s[at, block], g_s[at, block]
                key, value = k_s[at, :count, :], v_s[at, :count, :]
                scores = jnp.where(seen[block], dot_nt(query, key), -1e30)
                lifted = jnp.exp(scores - jnp.max(scores, axis=1, keepdims=True))
                probs = lifted * (1.0 / jnp.sum(lifted, axis=1, keepdims=True))
                weight_grad = dot_nt(grad, value)
                spread = jnp.sum(probs * weight_grad, axis=1, keepdims=True)
                score_grad = (probs * (weight_grad - spread)).astype(BF16)
                query_grads.append(dot(score_grad, key) * scale)

                def widen(part):
                    if count == rows:
                        return part
                    return jnp.concatenate([part, jnp.zeros((HD, rows - count), F32)], axis=1)

                key_grad += widen(dot_tn(query, score_grad))
                value_grad += widen(dot_tn(grad, probs.astype(BF16)))
            for head in range(PER):
                here = slice(head * ROWS, (head + 1) * ROWS)
                pieces.append(jnp.concatenate([part[here] for part in query_grads], axis=0))
            pieces += [key_grad.T, value_grad.T]
        joined = jnp.concatenate(pieces, axis=1)
        columns = turn(joined, cosine[...], -sine[...], flags)
        for at, column in enumerate(columns):
            grad_s[z, :, at * LANES : (at + 1) * LANES] = column.astype(BF16)
        return carried

    lax.fori_loop(0, n_tp, one_place, 0)
    sum_s[...] = dot_nt(grad_s[0], w_qkv_s[0])
    for z in range(1, n_tp):
        sum_s[...] += dot_nt(grad_s[z], w_qkv_s[z])
    mask = adapter_mask(length_ref, index_ref, rows, LANES)
    low_q_grad = (sum_s[:, D:] * mask).astype(BF16)
    part_ref[:D, :] = dot_tn(attn_in, low_q_grad).astype(BF16)
    own = grad_s[place_ref[0]]
    for at in range(wide // LANES):
        lanes = slice(at * LANES, (at + 1) * LANES)
        part_ref[D + at * LANES : D + (at + 1) * LANES, :] = dot_tn(low_q, own[:, lanes]).astype(
            BF16
        )
    attn_grad = sum_s[:, :D] + dot_nt(low_q_grad, loads["qkv_down"][...])
    tokens, gain = loads["tokens"][...].astype(F32), loads["gain"][...]
    residual_grad = loads["residual_grad"][...]
    input_grad_ref[...] = (residual_grad + norm_back(tokens, gain, attn_grad)).astype(BF16)


def attention_back(
    place, lengths, index, attn_in, low_q, head_grad, residual_grad, tokens, gain, qkv_down, tables,
    shares,
):
    rows = tokens.shape[0]
    n_exp, n_tp, _, wide = shares.shape
    count = KV_HEADS
    blocks = rows // ROWS
    arrays = (attn_in, low_q) + tables
    arrays += (head_grad, residual_grad, tokens, gain.reshape(1, D), qkv_down)
    return pl.pallas_call(
        backward_kernel,
        in_specs=[IN_SMEM] * 3 + [IN_HBM] * (1 + len(arrays)),
        out_specs=[IN_VMEM] * 2,
        out_shape=[shape((rows, D), BF16), shape((D + wide, LANES), BF16)],
        scratch_shapes=load_scratch(arrays)
        + [
            pltpu.VMEM((n_tp, D + LANES, wide), BF16),
            pltpu.VMEM((count, blocks, PER * ROWS, HD), BF16),
            pltpu.VMEM((count, rows, HD), BF16),
            pltpu.VMEM((count, rows, HD), BF16),
            pltpu.VMEM((count, blocks, PER * ROWS, HD), BF16),
            pltpu.VMEM((n_tp, rows, wide), BF16),
            pltpu.VMEM((rows, D + LANES), F32),
            pltpu.SemaphoreType.DMA((n_tp * n_exp * 2,)),
        ],
        compiler_params=WHOLE_VMEM,
        cost_estimate=cost(35e9, 20e6),
        name="attention_backward",
    )(place, lengths, index, shares, *arrays)


def kernel_body(
    tokens, attn_gain, moe_gain, w_qkv, w_out, w_router, w_gate, w_up, w_down, qkv_down, qkv_up,
    out_down, out_up, lengths, adapter_index, loss_mask, routes, upstream,
):
    n_exp = lax.axis_size("exp")
    rows = tokens.shape[0]
    exp_place = lax.axis_index("exp").astype(jnp.int32).reshape(1)
    tp_place = lax.axis_index("tp").astype(jnp.int32).reshape(1)
    tables = turn_tables(rows)
    own_experts = pack_experts(w_gate, w_up, w_down)
    weights = lax.all_gather(own_experts, "exp", axis=0, tiled=True)
    inputs, _ = lax.optimization_barrier((tokens, own_experts))
    attn_in, low_q, head, base, low_o = forward(
        lengths, adapter_index, inputs, attn_gain, w_qkv, qkv_down, qkv_up, w_out, out_down, tables
    )
    own_share = pack_share(exp_place, w_qkv, qkv_up, w_out, out_down, n_exp)
    copies = jnp.broadcast_to(own_share[None], (lax.axis_size("tp"),) + own_share.shape)
    z_shares = lax.all_to_all(copies, "tp", 0, 0, tiled=True)
    base, low_o = lax.psum((base, low_o), "tp")
    split = sum(share_rows(n_exp, 0))
    out_share, _ = lax.optimization_barrier((z_shares[:, split:], weights))
    out_shares = lax.all_gather(out_share, "exp", axis=0)
    occupied = jnp.arange(rows, dtype=jnp.int32) < jnp.sum(lengths)
    kept = occupied & (loss_mask > 0)
    cot = jnp.where(kept[:, None], upstream, jnp.zeros((), BF16))
    residual, moe_part, normed_part = experts_both(
        tokens, base, low_o, out_up, moe_gain, w_router, routes, cot, weights
    )
    normed_part, _ = lax.optimization_barrier((normed_part, out_shares))
    normed_grad = lax.psum(normed_part, "tp")
    qkv_share, _ = lax.optimization_barrier((z_shares[:, :split], normed_part))
    qkv_shares = lax.all_gather(qkv_share, "exp", axis=0)
    moe_part, _ = lax.optimization_barrier((moe_part, normed_grad))
    moe_out = lax.psum(moe_part, "tp")
    normed_grad, _ = lax.optimization_barrier((normed_grad, qkv_shares))
    residual_grad, head_grad, out_part = branch_back(
        lengths, adapter_index, residual, low_o, normed_grad, cot, moe_gain, out_up, head,
        out_shares,
    )
    out_parts = lax.all_gather(out_part, "exp", axis=0)
    input_grad, qkv_part = attention_back(
        tp_place, lengths, adapter_index, attn_in, low_q, head_grad, residual_grad, tokens,
        attn_gain, qkv_down, tables, qkv_shares,
    )
    moe_out, out_parts, _ = lax.optimization_barrier((moe_out, out_parts, qkv_part))
    output = (residual + moe_out.astype(F32)).astype(BF16)
    out_sum = jnp.sum(out_parts.astype(F32), axis=0)
    share = qkv_part.shape[0] // n_exp
    parts = lax.all_to_all(qkv_part.reshape(n_exp, share, LANES), "exp", 0, 0, tiled=True)
    qkv_sum = jnp.sum(parts.astype(F32), axis=0).astype(BF16)
    spread = jnp.broadcast_to(qkv_sum[None], (n_exp, share, LANES))
    qkv_sum = lax.all_to_all(spread, "exp", 0, 0, tiled=True).astype(F32).reshape(-1, LANES)

    def side_by_side(stacked):
        pieces = stacked.reshape(-1, LANES, LANES)
        return pieces.transpose(1, 0, 2).reshape(LANES, -1)

    return (
        output,
        input_grad,
        qkv_sum[:D],
        side_by_side(qkv_sum[D:]),
        out_sum[D:],
        side_by_side(out_sum[:D]),
    )


def product(left_m, right_m):
    return jnp.dot(left_m, right_m, preferred_element_type=jnp.float32)


def contract(einsum_form, left_m, right_m):
    return jnp.einsum(einsum_form, left_m, right_m, preferred_element_type=jnp.float32)


def rms_norm(vectors, gain_vec):
    inv_root = lax.rsqrt(jnp.mean(vectors * vectors, axis=-1, keepdims=True) + EPS)
    return vectors * inv_root * gain_vec


def rms_norm_back(vectors, gain_vec, upstream_grad):
    inv_root = lax.rsqrt(jnp.mean(vectors * vectors, axis=-1, keepdims=True) + EPS)
    weighted = upstream_grad * gain_vec
    return inv_root * weighted - vectors * (inv_root * inv_root * inv_root) * jnp.mean(
        vectors * weighted, axis=-1, keepdims=True
    )


def layout(length_row, index_row):
    places = jnp.arange(TOK_DEV, dtype=jnp.int32)
    doc_ends = jnp.cumsum(length_row)
    doc_starts = doc_ends - length_row
    member = (places[:, None] >= doc_starts[None, :]) & (places[:, None] < doc_ends[None, :])
    occupied = jnp.any(member, axis=1)
    position = jnp.sum(jnp.where(member, places[:, None] - doc_starts[None, :], 0), axis=1)
    owner_doc = jnp.sum(jnp.where(member, jnp.arange(DOCS, dtype=jnp.int32)[None, :], 0), axis=1)
    doc_ident = jnp.where(occupied, owner_doc, DOCS + places)
    chosen = jnp.sum(jnp.where(member, index_row[None, :], 0), axis=1)
    adapter_pick = occupied[:, None] & (
        chosen[:, None] == jnp.arange(ADAPTERS, dtype=jnp.int32)[None, :]
    )
    rank_mask = jnp.repeat(jnp.where(adapter_pick, 1.0, 0.0).astype(jnp.float32), RANK, axis=1)
    return (occupied, position, doc_ident, rank_mask)


def angles(position):
    half_width = HD // 2
    frequency = jnp.exp(-math.log(ROPE_BASE) * jnp.arange(half_width, dtype=jnp.float32) * 2.0 / HD)
    turned = position.astype(jnp.float32)[:, None] * frequency[None, :]
    return (jnp.cos(turned), jnp.sin(turned))


def rotate(vectors, cosine, sine_table):
    half_width = vectors.shape[-1] // 2
    front_half = vectors[..., :half_width]
    back_half = vectors[..., half_width:]
    return jnp.concatenate(
        [
            front_half * cosine - back_half * sine_table,
            back_half * cosine + front_half * sine_table,
        ],
        axis=-1,
    )


def moe(normed, cot_low, gates, gate_up, down):
    width = down.shape[1]
    both = contract("td,edf->tef", normed, gate_up)
    pre_gate = both[:, :, :width]
    pre_up = both[:, :, width:]
    sigmoid_g = jax.nn.sigmoid(pre_gate)
    activated = pre_gate * sigmoid_g
    hidden = (activated * pre_up).astype(jnp.bfloat16).astype(jnp.float32)
    inner_raw = contract("td,efd->tef", cot_low, down)
    gate_part = jnp.sum(hidden * inner_raw, axis=-1)
    moe_part = contract("tef,efd->td", (gates[:, :, None] * hidden).astype(jnp.bfloat16), down)
    inner_grad = inner_raw * gates[:, :, None]
    grad_gate = inner_grad * pre_up * sigmoid_g * (1.0 + pre_gate * (1.0 - sigmoid_g))
    grad_up = inner_grad * activated
    grad_both = jnp.concatenate([grad_gate, grad_up], axis=2).astype(jnp.bfloat16)
    normed_part = contract("tef,edf->td", grad_both, gate_up)
    return (moe_part, gate_part, normed_part)


def body(
    tokens,
    attn_gain,
    moe_gain,
    w_qkv,
    w_out,
    w_router,
    w_gate,
    w_up,
    w_down,
    qkv_down,
    qkv_up,
    out_down,
    out_up,
    lengths,
    adapter_index,
    loss_mask,
    routes,
    upstream,
):
    n_exp = lax.axis_size("exp")
    groups = KV_HEADS // lax.axis_size("tp")
    per_group = HEADS // KV_HEADS
    experts = EXP_DEV * n_exp
    gate_up = lax.all_gather(jnp.concatenate([w_gate, w_up], axis=2), "exp", axis=0, tiled=True)
    down = lax.all_gather(w_down, "exp", axis=0, tiled=True)
    block_rows = min(512, TOK_DEV)
    blocks = TOK_DEV // block_rows
    score_scale = 1.0 / math.sqrt(HD)
    places = jnp.arange(TOK_DEV, dtype=jnp.int32)
    occupied, position, doc_ident, rank_mask = layout(lengths[0], adapter_index[0])
    mask_low = rank_mask.astype(jnp.bfloat16)
    cosine, sine_table = angles(position)
    inputs = tokens.astype(jnp.float32)
    attn_in = rms_norm(inputs, attn_gain).astype(jnp.bfloat16)
    low_q = (product(attn_in, qkv_down) * rank_mask).astype(jnp.bfloat16)
    projected = (product(attn_in, w_qkv) + product(low_q, qkv_up)).reshape(
        TOK_DEV, groups, per_group + 2, HD
    )
    query_rows = rotate(
        projected[:, :, :per_group], cosine[:, None, None], sine_table[:, None, None]
    ).astype(jnp.bfloat16)
    key_rows = rotate(projected[:, :, per_group], cosine[:, None], sine_table[:, None]).astype(
        jnp.bfloat16
    )
    val_rows = projected[:, :, per_group + 1].astype(jnp.bfloat16)

    def masked_scores(q_blk, q_place, q_ident):
        scores = contract("qgrd,kgd->grqk", q_blk, key_rows) * score_scale
        allowed = (q_ident[:, None] == doc_ident[None, :]) & (places[None, :] <= q_place[:, None])
        return jnp.where(allowed, scores, -1e30)

    def attend(pieces):
        q_blk, q_place, q_ident = pieces
        scores = masked_scores(q_blk, q_place, q_ident)
        row_max = jnp.max(scores, axis=-1, keepdims=True)
        lifted = jnp.exp(scores - row_max)
        row_total = jnp.sum(lifted, axis=-1, keepdims=True)
        weights = (lifted / row_total).astype(jnp.bfloat16)
        return (
            contract("grqk,kgd->qgrd", weights, val_rows),
            row_max[..., 0] + jnp.log(row_total[..., 0]),
        )

    query_blocks = query_rows.reshape(blocks, block_rows, groups, per_group, HD)
    place_blocks = places.reshape(blocks, block_rows)
    ident_blocks = doc_ident.reshape(blocks, block_rows)
    attended, log_totals = lax.map(attend, (query_blocks, place_blocks, ident_blocks))
    head_rows = attended.reshape(TOK_DEV, groups * per_group * HD).astype(jnp.bfloat16)
    attn_base, low_rank = (
        lax.psum(product(head_rows, w_out).astype(jnp.bfloat16), "tp").astype(jnp.float32),
        lax.psum((product(head_rows, out_down) * rank_mask).astype(jnp.bfloat16), "tp").astype(
            jnp.float32
        ),
    )
    low_o = low_rank.astype(jnp.bfloat16)
    residual = inputs + attn_base + product(low_o, out_up)
    normed = rms_norm(residual, moe_gain).astype(jnp.bfloat16)
    logits = product(normed, w_router)
    one_hot = routes[:, :, None] == jnp.arange(experts, dtype=jnp.int32)[None, None, :]
    routed = jnp.any(one_hot, axis=1)
    gates = jax.nn.softmax(jnp.where(routed, logits, -1e30), axis=-1)
    live_mask = jnp.where(occupied & (loss_mask > 0), 1.0, 0.0).astype(jnp.float32)
    cotangent = upstream.astype(jnp.float32) * live_mask[:, None]
    cot_low = cotangent.astype(jnp.bfloat16)
    moe_part, gate_part, normed_part = moe(normed, cot_low, gates, gate_up, down)
    logit_grad = (
        gates * (gate_part - jnp.sum(gates * gate_part, axis=-1, keepdims=True))
    ).astype(jnp.bfloat16)
    normed_part = (normed_part + product(logit_grad, w_router.T)).astype(jnp.bfloat16)
    normed_sum = lax.psum(normed_part, "tp")
    normed_sum, moe_part = lax.optimization_barrier((normed_sum, moe_part.astype(jnp.bfloat16)))
    normed_grad = normed_sum.astype(jnp.float32)
    moe_out = lax.psum(moe_part, "tp").astype(jnp.float32)
    output = (residual + moe_out).astype(jnp.bfloat16)
    residual_grad = cotangent + rms_norm_back(residual, moe_gain, normed_grad)
    branch_grad = residual_grad.astype(jnp.bfloat16)
    low_o_grad = product(branch_grad, out_up.T).astype(jnp.bfloat16) * mask_low
    out_up_part = contract("tr,td->rd", low_o, branch_grad)
    head_grad = (product(branch_grad, w_out.T) + product(low_o_grad, out_down.T)).astype(
        jnp.bfloat16
    )
    out_down_part = contract("tc,tr->cr", head_rows, low_o_grad)
    grad_blocks = head_grad.reshape(blocks, block_rows, groups, per_group, HD)

    def attend_back(carried, pieces):
        key_acc, val_acc = carried
        q_blk, q_place, q_ident, lse_blk, g_blk = pieces
        weights = jnp.exp(masked_scores(q_blk, q_place, q_ident) - lse_blk[..., None])
        weight_grad = contract("qgrd,kgd->grqk", g_blk, val_rows)
        score_grad = (
            weights * (weight_grad - jnp.sum(weights * weight_grad, axis=-1, keepdims=True))
        ).astype(jnp.bfloat16)
        query_grad = contract("grqk,kgd->qgrd", score_grad, key_rows) * score_scale
        key_acc = key_acc + contract("grqk,qgrd->kgd", score_grad, q_blk) * score_scale
        val_acc = val_acc + contract("grqk,qgrd->kgd", weights.astype(jnp.bfloat16), g_blk)
        return ((key_acc, val_acc), query_grad)

    zero_acc = jnp.zeros((TOK_DEV, groups, HD), jnp.float32)
    (key_grad, val_grad), query_grad = lax.scan(
        attend_back,
        (zero_acc, zero_acc),
        (query_blocks, place_blocks, ident_blocks, log_totals, grad_blocks),
    )
    query_grad = rotate(
        query_grad.reshape(TOK_DEV, groups, per_group, HD),
        cosine[:, None, None],
        -sine_table[:, None, None],
    )
    key_grad = rotate(key_grad, cosine[:, None], -sine_table[:, None])
    projected_grad = (
        jnp.concatenate([query_grad, key_grad[:, :, None], val_grad[:, :, None]], axis=2)
        .reshape(TOK_DEV, -1)
        .astype(jnp.bfloat16)
    )
    qkv_up_part = contract("tr,tc->rc", low_q, projected_grad)
    attn_grad, low_q_grad = (
        lax.psum(contract("tc,dc->td", projected_grad, w_qkv).astype(jnp.bfloat16), "tp").astype(
            jnp.float32
        ),
        lax.psum(contract("tc,rc->tr", projected_grad, qkv_up).astype(jnp.bfloat16), "tp").astype(
            jnp.float32
        ),
    )
    low_q_grad = low_q_grad.astype(jnp.bfloat16) * mask_low
    attn_grad = attn_grad + contract("tr,dr->td", low_q_grad, qkv_down)
    qkv_down_part = contract("td,tr->dr", attn_in, low_q_grad)
    input_grad = (residual_grad + rms_norm_back(inputs, attn_gain, attn_grad)).astype(jnp.bfloat16)
    summed = (
        lax.psum(qkv_down_part.astype(jnp.bfloat16), "exp").astype(jnp.float32),
        lax.psum(qkv_up_part.astype(jnp.bfloat16), "exp").astype(jnp.float32),
        lax.psum(out_down_part.astype(jnp.bfloat16), "exp").astype(jnp.float32),
        lax.psum(out_up_part.astype(jnp.bfloat16), "exp").astype(jnp.float32),
    )
    return (output, input_grad, summed[0], summed[1], summed[2], summed[3])


def kernels_fit(mesh):
    n_exp, n_tp = mesh.shape["exp"], mesh.shape["tp"]
    groups = KV_HEADS // n_tp
    return groups % 2 == 0 and FF // n_tp == LANES and LANES // n_exp % 16 == 0


def solution(mesh):
    placed = (
        P("exp", None),
        P(),
        P(),
        P(None, "tp"),
        P("tp", None),
        P(),
        P("exp", None, "tp"),
        P("exp", None, "tp"),
        P("exp", "tp", None),
        P(),
        P(None, "tp"),
        P("tp", None),
        P(),
        P("exp", None),
        P("exp", None),
        P("exp"),
        P("exp", None),
        P("exp", None),
    )
    return jax.shard_map(
        kernel_body if kernels_fit(mesh) else body,
        mesh=mesh,
        in_specs=placed,
        out_specs=(P("exp", None), P("exp", None), P(), P(None, "tp"), P("tp", None), P()),
        check_vma=False,
    )
```

```python
import functools
import math

import jax
import jax.numpy as jnp
import numpy as np
from jax import lax
from jax.experimental import pallas as pl
from jax.experimental.pallas import tpu as pltpu
from jax.sharding import PartitionSpec as P

D = 1536
HEADS = 24
KV_HEADS = 8
HD = 64
TOP = 8
RANK = 16
ADAPTERS = 8
EXP_DEV = 2
DOCS = 4
TOK_DEV = 512
LIVE = 448
FF = 512
EPS = 1e-06
ROPE_BASE = 10000.0

PER = HEADS // KV_HEADS
LANES = 128
ROWS = 128
BLOCKS = tuple((at, min(at + ROWS, TOK_DEV)) for at in range(0, TOK_DEV, ROWS))
LIVE_BLOCKS = tuple((at, min(at + ROWS, LIVE)) for at in range(0, LIVE, ROWS))
F32 = jnp.float32
BF16 = jnp.bfloat16
MIB = 2**20
NT = (((1,), (1,)), ((), ()))
TN = (((0,), (0,)), ((), ()))
WHOLE_VMEM = pltpu.CompilerParams(vmem_limit_bytes=63 * MIB)
IN_VMEM = pl.BlockSpec(memory_space=pltpu.VMEM)
IN_SMEM = pl.BlockSpec(memory_space=pltpu.SMEM)
IN_HBM = pl.BlockSpec(memory_space=pltpu.HBM)


def dot(left, right):
    return jnp.dot(left, right, preferred_element_type=F32)


def dot_nt(left, right):
    return lax.dot_general(left, right, NT, preferred_element_type=F32)


def dot_tn(left, right):
    return lax.dot_general(left, right, TN, preferred_element_type=F32)


def cost(flops, moved):
    return pl.CostEstimate(flops=int(flops), bytes_accessed=int(moved), transcendentals=0)


def shape(dims, dtype):
    return jax.ShapeDtypeStruct(dims, dtype)


def turn_tables(rows):
    half = HD // 2
    frequency = np.exp(-math.log(ROPE_BASE) * np.arange(half, dtype=np.float64) * 2.0 / HD)
    turned = np.arange(rows, dtype=np.float64)[:, None] * frequency[None, :]
    cosine, sine = np.cos(turned), np.sin(turned)
    return (
        jnp.asarray(np.concatenate([cosine] * 4, axis=1), F32),
        jnp.asarray(np.concatenate([-sine, sine, -sine, sine], axis=1), F32),
    )


def turned_pieces(groups):
    return [piece < PER + 1 for _ in range(groups) for piece in range(PER + 2)]


def turn(joined, cosine, sine, flags):
    lane = lax.broadcasted_iota(jnp.int32, cosine.shape, 1)
    front = (lane & 32) == 0
    left = lane < HD
    columns = []
    for at in range(joined.shape[1] // LANES):
        column = joined[:, at * LANES : (at + 1) * LANES]
        swapped = jnp.where(front, pltpu.roll(column, 96, 1), pltpu.roll(column, 32, 1))
        rotated = column * cosine + swapped * sine
        if not (flags[2 * at] and flags[2 * at + 1]):
            rotated = jnp.where(left if flags[2 * at] else jnp.logical_not(left), rotated, column)
        columns.append(rotated)
    return columns


def first_keys(length_ref, rows):
    row = lax.broadcasted_iota(jnp.int32, (rows, 1), 0)
    begin = jnp.zeros((rows, 1), jnp.int32)
    end = 0
    for doc in range(DOCS):
        if doc:
            begin = jnp.where(row >= end, end, begin)
        end = end + length_ref[0, doc]
    return jnp.where(row >= end, row, begin)


def adapter_mask(length_ref, index_ref, rows, width):
    row = lax.broadcasted_iota(jnp.int32, (rows, width), 0)
    adapter = lax.shift_right_logical(lax.broadcasted_iota(jnp.int32, (rows, width), 1), 4)
    mask = jnp.zeros((rows, width), F32)
    begin = 0
    for doc in range(DOCS):
        end = begin + length_ref[0, doc]
        inside = (row >= begin) & (row < end) & (adapter == index_ref[0, doc])
        mask = jnp.where(inside, 1.0, mask)
        begin = end
    return mask


def seen_block(first, begin, end):
    row = lax.broadcasted_iota(jnp.int32, (end - begin, end), 0) + begin
    key = lax.broadcasted_iota(jnp.int32, (end - begin, end), 1)
    seen = (key <= row) & (key >= first[begin:end])
    return jnp.concatenate([seen] * PER, axis=0)


def softmax_block(scores, seen):
    scores = jnp.where(seen, scores, -1e30)
    lifted = jnp.exp(scores - jnp.max(scores, axis=1, keepdims=True))
    return (lifted * (1.0 / jnp.sum(lifted, axis=1, keepdims=True))).astype(BF16)


def column_of(row_ref, rows):
    row = row_ref[...].astype(F32)
    at = lax.broadcasted_iota(jnp.int32, (rows, row.shape[1]), 0)
    lane = lax.broadcasted_iota(jnp.int32, (rows, row.shape[1]), 1)
    return jnp.sum(jnp.where(at == lane, row, 0.0), axis=1, keepdims=True)


def store_heads(columns, slot, blocks, q_s, k_s, v_s):
    scale = 1.0 / math.sqrt(HD)
    for at, column in enumerate(columns):
        halves = (column[:, :HD], pltpu.roll(column, HD, 1)[:, :HD])
        for piece, part in zip((2 * at, 2 * at + 1), halves):
            group, kind = divmod(piece, PER + 2)
            if kind == PER:
                k_s[slot + group] = part.astype(BF16)
            elif kind == PER + 1:
                v_s[slot + group] = part.astype(BF16)
            else:
                part = (part * scale).astype(BF16)
                for block, (begin, end) in enumerate(blocks):
                    size = end - begin
                    here = slice(kind * size, (kind + 1) * size)
                    q_s[slot + group, block, here, :] = part[begin:end]


def run_copies(pairs, sem):
    copies = [
        pltpu.make_async_copy(source, target, sem.at[number])
        for number, (source, target) in enumerate(pairs)
    ]
    for copy in copies:
        copy.start()
    for copy in copies:
        copy.wait()


def pack_experts_kernel(gate, up, down, packed, held, sem, out_sem):
    width = gate.shape[2]
    pairs = []
    for expert in range(gate.shape[0]):
        pairs.append((gate.at[expert], held.at[expert, :, :width]))
        pairs.append((up.at[expert], held.at[expert, :, width : 2 * width]))
        for at in range(D // LANES):
            lanes = slice(at * LANES, (at + 1) * LANES)
            pairs.append((down.at[expert, :, lanes], held.at[expert, lanes, 2 * width :]))
    run_copies(pairs, sem)
    run_copies([(held, packed)], out_sem)


def pack_experts(w_gate, w_up, w_down):
    count, _, width = w_gate.shape
    packed = shape((count, D, 3 * width), BF16)
    return pl.pallas_call(
        pack_experts_kernel,
        in_specs=[IN_HBM] * 3,
        out_specs=IN_HBM,
        out_shape=packed,
        scratch_shapes=[
            pltpu.VMEM(packed.shape, BF16),
            pltpu.SemaphoreType.DMA((count * (2 + D // LANES),)),
            pltpu.SemaphoreType.DMA((1,)),
        ],
        compiler_params=WHOLE_VMEM,
        cost_estimate=cost(0, 2 * 2 * count * D * 3 * width),
        name="pack_experts",
    )(w_gate, w_up, w_down)


def share_rows(n_exp, heads_wide):
    return (D // n_exp, LANES // n_exp, heads_wide // n_exp)


def pack_qkv_kernel(n_exp, place_ref, w_qkv, qkv_up, packed, held, sem, out_sem):
    qkv_rows, up_rows, _ = share_rows(n_exp, 0)
    own_qkv = pl.ds(pl.multiple_of(place_ref[0] * qkv_rows, 16), qkv_rows)
    own_up = pl.ds(pl.multiple_of(place_ref[0] * up_rows, 16), up_rows)
    pairs = [
        (w_qkv.at[own_qkv, :], held.at[:qkv_rows, :]),
        (qkv_up.at[own_up, :], held.at[qkv_rows:, :]),
    ]
    run_copies(pairs, sem)
    run_copies([(held, packed)], out_sem)


def pack_out_kernel(n_exp, place_ref, w_out, out_down, packed, held, sem, out_sem):
    out_rows = w_out.shape[0] // n_exp
    own = pl.ds(pl.multiple_of(place_ref[0] * out_rows, 16), out_rows)
    pairs = [
        (w_out.at[own, :], held.at[:, :D]),
        (out_down.at[own, :], held.at[:, D:]),
    ]
    run_copies(pairs, sem)
    run_copies([(held, packed)], out_sem)


def pack_share(kernel, name, place, first, second, rows, wide, n_exp):
    return pl.pallas_call(
        functools.partial(kernel, n_exp),
        in_specs=[IN_SMEM] + [IN_HBM] * 2,
        out_specs=IN_HBM,
        out_shape=shape((rows, wide), BF16),
        scratch_shapes=[
            pltpu.VMEM((rows, wide), BF16),
            pltpu.SemaphoreType.DMA((2,)),
            pltpu.SemaphoreType.DMA((1,)),
        ],
        compiler_params=WHOLE_VMEM,
        cost_estimate=cost(0, 8 * rows * wide),
        name=name,
    )(place, first, second)


class Loads:
    def __init__(self, names, sources, targets, sem):
        self.copies = {}
        for number, (name, source, target) in enumerate(zip(names, sources, targets)):
            if source.shape != target.shape:
                source = source.at[: target.shape[0]]
            self.copies[name] = pltpu.make_async_copy(source, target, sem.at[number])
        self.targets = dict(zip(names, targets))
        for copy in self.copies.values():
            copy.start()

    def __getitem__(self, name):
        copy = self.copies.pop(name, None)
        if copy is not None:
            copy.wait()
        return self.targets[name]


def load_scratch(arrays, rows=TOK_DEV):
    return [
        pltpu.VMEM((rows if array.shape[0] == TOK_DEV else array.shape[0],) + array.shape[1:], array.dtype)
        for array in arrays
    ] + [pltpu.SemaphoreType.DMA((len(arrays),))]


FORWARD_LOADS = (
    "tokens", "gains", "qkv_down", "w_qkv", "qkv_up", "cosine", "sine", "w_out", "out_down",
)


def forward_kernel(length_ref, index_ref, *refs):
    count = len(FORWARD_LOADS)
    attn_in_ref, low_q_ref, head_ref, base_ref, low_ref = refs[count : count + 5]
    load_sem, q_s, k_s, v_s = refs[2 * count + 5 :]
    loads = Loads(FORWARD_LOADS, refs[:count], refs[count + 5 : 2 * count + 5], load_sem)
    rows = attn_in_ref.shape[0]
    groups = k_s.shape[0]
    mask = adapter_mask(length_ref, index_ref, rows, LANES)
    first = first_keys(length_ref, rows)
    inputs = loads["tokens"][...].astype(F32)
    inv_root = lax.rsqrt(jnp.mean(inputs * inputs, axis=1, keepdims=True) + EPS)
    attn_in_ref[...] = (inputs * inv_root * loads["gains"][0:1, :]).astype(BF16)
    attn_in = attn_in_ref[...]
    low_q = (dot(attn_in, loads["qkv_down"][...]) * mask).astype(BF16)
    low_q_ref[...] = low_q
    projected = dot(attn_in, loads["w_qkv"][...]) + dot(low_q, loads["qkv_up"][...])
    cosine, sine = loads["cosine"][...], loads["sine"][...]
    columns = turn(projected, cosine, sine, turned_pieces(groups))
    store_heads(columns, 0, BLOCKS, q_s, k_s, v_s)
    for block, (begin, end) in enumerate(BLOCKS):
        seen = seen_block(first, begin, end)
        heads = []
        for group in range(groups):
            probs = softmax_block(dot_nt(q_s[group, block], k_s[group, :end, :]), seen)
            out = dot(probs, v_s[group, :end, :])
            heads += [out[head * ROWS : (head + 1) * ROWS] for head in range(PER)]
        head_ref[begin:end, :] = jnp.concatenate(heads, axis=1).astype(BF16)
    head_out = head_ref[...]
    base_ref[...] = dot(head_out, loads["w_out"][...]).astype(BF16)
    low_ref[...] = (dot(head_out, loads["out_down"][...]) * mask).astype(BF16)


def forward(lengths, index, tokens, gains, w_qkv, qkv_down, qkv_up, w_out, out_down, tables):
    rows = tokens.shape[0]
    heads_wide = w_out.shape[0]
    groups = w_qkv.shape[1] // (HD * (PER + 2))
    arrays = (tokens, gains, qkv_down, w_qkv, qkv_up) + tables + (w_out, out_down)
    return pl.pallas_call(
        forward_kernel,
        in_specs=[IN_SMEM] * 2 + [IN_HBM] * len(arrays),
        out_specs=[IN_VMEM] * 5,
        out_shape=[
            shape((rows, D), BF16),
            shape((rows, LANES), BF16),
            shape((rows, heads_wide), BF16),
            shape((rows, D), BF16),
            shape((rows, LANES), BF16),
        ],
        scratch_shapes=load_scratch(arrays)
        + [
            pltpu.VMEM((groups, rows // ROWS, PER * ROWS, HD), BF16),
            pltpu.VMEM((groups, rows, HD), BF16),
            pltpu.VMEM((groups, rows, HD), BF16),
        ],
        compiler_params=WHOLE_VMEM,
        cost_estimate=cost(6e9, 10e6),
        name="attention_forward",
    )(lengths, index, *arrays)


def experts_kernel(
    count, tokens_ref, base_ref, low_o_ref, out_up_ref, gains_ref, router_ref, routes_ref,
    upstream_ref, loss_ref, weight_ref, residual_ref, moe_ref, grad_ref,
    normed_s, cot_s, gates_s, part_s, moe_s, grad_s,
):
    step = pl.program_id(0)
    lane = lax.broadcasted_iota(jnp.int32, gates_s.shape, 1)
    width = weight_ref.shape[2] // 3

    @pl.when(step == 0)
    def _():
        residual = (
            tokens_ref[...].astype(F32)
            + base_ref[...].astype(F32)
            + dot(low_o_ref[...], out_up_ref[...])
        )
        residual_ref[...] = residual
        inv_root = lax.rsqrt(jnp.mean(residual * residual, axis=1, keepdims=True) + EPS)
        normed = (residual * inv_root * gains_ref[1:2, :]).astype(BF16)
        normed_s[...] = normed
        kept = column_of(loss_ref, LIVE) > 0.0
        cot_s[...] = jnp.where(kept, upstream_ref[:LIVE, :].astype(F32), 0.0).astype(BF16)
        logits = dot_nt(normed, router_ref[...])
        routes = routes_ref[...].astype(F32).T
        place = lane.astype(F32)
        routed = place == routes[:, 0:1]
        for slot in range(1, TOP):
            routed = routed | (place == routes[:, slot : slot + 1])
        logits = jnp.where(routed, logits, -1e30)
        lifted = jnp.exp(logits - jnp.max(logits, axis=1, keepdims=True))
        gates_s[...] = lifted / jnp.sum(lifted, axis=1, keepdims=True)
        part_s[...] = jnp.zeros_like(part_s)
        moe_s[...] = jnp.zeros_like(moe_s)
        grad_s[...] = jnp.zeros_like(grad_s)

    normed = normed_s[...]
    cot = cot_s[...]
    gates = gates_s[...]
    part = jnp.zeros(part_s.shape, F32)
    downs = [
        jnp.concatenate(
            [
                weight_ref[expert, at * LANES : (at + 1) * LANES, 2 * width :]
                for at in range(D // LANES)
            ],
            axis=1,
        )
        for expert in range(count)
    ]
    hidden, grads = [], []
    for pair in range(count // 2):
        both_down = jnp.concatenate(downs[2 * pair : 2 * pair + 2], axis=0)
        both_raw = dot_nt(cot, both_down)
        for half in range(2):
            expert = 2 * pair + half
            joined = dot(normed, weight_ref[expert, :, : 2 * width])
            pre_gate = joined[:, :width]
            pre_up = joined[:, width:]
            raw = both_raw[:, half * width : (half + 1) * width]
            sigmoid = 0.5 * jnp.tanh(0.5 * pre_gate) + 0.5
            activated = pre_gate * sigmoid
            value = activated * pre_up
            here = lane == step * count + expert
            gate = jnp.sum(jnp.where(here, gates, 0.0), axis=1, keepdims=True)
            hidden.append((gate * value).astype(BF16))
            gate_grad = jnp.sum(value[:LIVE] * raw, axis=1, keepdims=True)
            part += jnp.where(here[:LIVE], gate_grad, 0.0)
            inner = raw * gate[:LIVE]
            sigmoid, activated = sigmoid[:LIVE], activated[:LIVE]
            slope = sigmoid + activated * (1.0 - sigmoid)
            grads.append((inner * pre_up[:LIVE] * slope).astype(BF16))
            grads.append((inner * activated).astype(BF16))
    part_s[...] += part
    moe_s[...] += dot(jnp.concatenate(hidden, axis=1), jnp.concatenate(downs, axis=0))
    ups = jnp.concatenate([weight_ref[expert, :, : 2 * width] for expert in range(count)], axis=1)
    grad_s[...] += dot_nt(jnp.concatenate(grads, axis=1), ups)

    @pl.when(step == pl.num_programs(0) - 1)
    def _():
        live_gates, gate_part = gates[:LIVE], part_s[...]
        spread = jnp.sum(live_gates * gate_part, axis=1, keepdims=True)
        logit_grad = (live_gates * (gate_part - spread)).astype(BF16)
        moe_ref[...] = moe_s[...].astype(BF16)
        grad_ref[...] = (grad_s[...] + dot(logit_grad, router_ref[...])).astype(BF16)


def experts_both(
    tokens, base, low_o, out_up, gains, router, routes, upstream, loss_mask, weights, count=4
):
    rows = tokens.shape[0]
    experts = weights.shape[0]
    arrays = (tokens, base, low_o, out_up, gains, router.T, routes.T, upstream, loss_mask)
    whole = pl.BlockSpec((rows, D), lambda step: (0, 0))
    live = pl.BlockSpec((LIVE, D), lambda step: (0, 0))
    return pl.pallas_call(
        functools.partial(experts_kernel, count),
        grid=(experts // count,),
        in_specs=[pl.BlockSpec(array.shape, lambda step: (0, 0)) for array in arrays]
        + [pl.BlockSpec((count,) + weights.shape[1:], lambda step: (step, 0, 0))],
        out_specs=[whole, whole, live],
        out_shape=[shape((rows, D), F32), shape((rows, D), BF16), shape((LIVE, D), BF16)],
        scratch_shapes=[
            pltpu.VMEM((rows, D), BF16),
            pltpu.VMEM((LIVE, D), BF16),
            pltpu.VMEM((rows, experts), F32),
            pltpu.VMEM((LIVE, experts), F32),
            pltpu.VMEM((rows, D), F32),
            pltpu.VMEM((LIVE, D), F32),
        ],
        compiler_params=WHOLE_VMEM,
        cost_estimate=cost(25e9, 30e6),
        name="experts",
    )(*arrays, weights)


def norm_back(vectors, gain, upstream):
    inv_root = lax.rsqrt(jnp.mean(vectors * vectors, axis=1, keepdims=True) + EPS)
    weighted = upstream * gain
    slope = jnp.mean(vectors * weighted, axis=1, keepdims=True)
    return inv_root * weighted - vectors * (inv_root * inv_root * inv_root) * slope


BRANCH_LOADS = (
    "residual", "normed_grad", "gains", "loss", "upstream", "out_up", "low_o", "head",
)


def branch_kernel(place_ref, length_ref, index_ref, shares, *refs):
    count = len(BRANCH_LOADS)
    residual_grad_ref, head_grad_ref, part_ref = refs[count : count + 3]
    load_sem, w_out_s, sem = refs[2 * count + 3 :]
    loads = Loads(BRANCH_LOADS, refs[:count], refs[count + 3 : 2 * count + 3], load_sem)
    n_exp, n_tp, out_rows, _ = shares.shape
    copies = []
    for z in range(n_tp):
        for e in range(n_exp):
            target = w_out_s.at[z, e * out_rows : (e + 1) * out_rows, :]
            source = shares.at[e, from_place(place_ref, z, n_tp)]
            copies.append(pltpu.make_async_copy(source, target, sem.at[len(copies)]))
    for copy in copies:
        copy.start()
    mask = adapter_mask(length_ref, index_ref, LIVE, LANES)
    residual, normed_grad = loads["residual"][...], loads["normed_grad"][...].astype(F32)
    through = norm_back(residual, loads["gains"][1:2, :], normed_grad)
    kept = column_of(loads["loss"], LIVE) > 0.0
    residual_grad_ref[...] = through + jnp.where(kept, loads["upstream"][...].astype(F32), 0.0)
    branch_grad = residual_grad_ref[...].astype(BF16)
    low_o_grad = (dot_nt(branch_grad, loads["out_up"][...]) * mask).astype(BF16)
    low_o = loads["low_o"][...]
    for at in range(D // LANES):
        lanes = slice(at * LANES, (at + 1) * LANES)
        part_ref[lanes, :] = dot_tn(low_o, branch_grad[:, lanes]).astype(BF16)
    part_ref[D:, :] = dot_tn(loads["head"][...], low_o_grad).astype(BF16)
    for z in range(n_tp):
        for copy in copies[z * n_exp : (z + 1) * n_exp]:
            copy.wait()
        head_grad_ref[z] = (
            dot_nt(branch_grad, w_out_s[z, :, :D]) + dot_nt(low_o_grad, w_out_s[z, :, D:])
        ).astype(BF16)


def branch_back(
    place, lengths, index, residual, low_o, normed_grad, upstream, loss_mask, gains, out_up, head, shares
):
    heads_wide = head.shape[1]
    n_exp, n_tp, _, _ = shares.shape
    arrays = (residual, normed_grad, gains, loss_mask, upstream, out_up, low_o, head)
    return pl.pallas_call(
        branch_kernel,
        in_specs=[IN_SMEM] * 3 + [IN_HBM] * (1 + len(arrays)),
        out_specs=[IN_VMEM] * 3,
        out_shape=[
            shape((LIVE, D), F32),
            shape((n_tp, LIVE, heads_wide), BF16),
            shape((D + heads_wide, LANES), BF16),
        ],
        scratch_shapes=load_scratch(arrays, LIVE)
        + [
            pltpu.VMEM((n_tp, heads_wide, D + LANES), BF16),
            pltpu.SemaphoreType.DMA((n_tp * n_exp,)),
        ],
        compiler_params=WHOLE_VMEM,
        cost_estimate=cost(5e9, 20e6),
        name="branch_backward",
    )(place, lengths, index, shares, *arrays)


def share_copies(place_ref, shares, w_qkv_s, sem):
    n_exp, n_tp, _, _ = shares.shape
    qkv_rows, up_rows, _ = share_rows(n_exp, 0)
    copies = []
    for z in range(n_tp):
        here = []
        source_z = from_place(place_ref, z, n_tp)
        for e in range(n_exp):
            at = e * qkv_rows
            up_at = D + e * up_rows
            for source, target in (
                (shares.at[e, source_z, :qkv_rows, :], w_qkv_s.at[z, at : at + qkv_rows, :]),
                (shares.at[e, source_z, qkv_rows:, :], w_qkv_s.at[z, up_at : up_at + up_rows, :]),
            ):
                number = 2 * e + len(here) % 2
                here.append(pltpu.make_async_copy(source, target, sem.at[z, number]))
        copies.append(here)
    for here in copies:
        for copy in here:
            copy.start()
    return copies


PREPARE_LOADS = ("attn_in", "low_q", "cosine", "sine")


def prepare_kernel(place_ref, length_ref, shares, *refs):
    count = len(PREPARE_LOADS)
    results = 3 + len(LIVE_BLOCKS)
    q_ref, k_ref, v_ref = refs[count : count + 3]
    prob_refs = refs[count + 3 : count + results]
    load_sem, w_qkv_s, sem = refs[2 * count + results :]
    targets = refs[count + results : 2 * count + results]
    loads = Loads(PREPARE_LOADS, refs[:count], targets, load_sem)
    n_tp = shares.shape[1]
    groups = k_ref.shape[0] // n_tp
    copies = share_copies(place_ref, shares, w_qkv_s, sem)
    first = first_keys(length_ref, LIVE)
    attn_in = loads["attn_in"][...]
    low_q = loads["low_q"][...]
    cosine, sine = loads["cosine"][...], loads["sine"][...]
    seen = [seen_block(first, begin, end) for begin, end in LIVE_BLOCKS]
    for z in range(n_tp):
        for copy in copies[z]:
            copy.wait()
        projected = dot(attn_in, w_qkv_s[z, :D, :]) + dot(low_q, w_qkv_s[z, D:, :])
        columns = turn(projected, cosine, sine, turned_pieces(groups))
        store_heads(columns, z * groups, LIVE_BLOCKS, q_ref, k_ref, v_ref)

    def one_group(group, carried):
        for block, (begin, end) in enumerate(LIVE_BLOCKS):
            query = q_ref[group, block, : PER * (end - begin), :]
            scores = dot_nt(query, k_ref[group, :end, :])
            prob_refs[block][group] = softmax_block(scores, seen[block])
        return carried

    lax.fori_loop(0, k_ref.shape[0], one_group, 0)


def prepare(place, lengths, attn_in, low_q, tables, shares):
    n_exp, n_tp, _, wide = shares.shape
    arrays = (attn_in, low_q) + tables
    groups = KV_HEADS
    probs = [
        shape((groups, PER * (end - begin), end), BF16) for begin, end in LIVE_BLOCKS
    ]
    return pl.pallas_call(
        prepare_kernel,
        in_specs=[IN_SMEM] * 2 + [IN_HBM] * (1 + len(arrays)),
        out_specs=[IN_VMEM] * (3 + len(probs)),
        out_shape=[
            shape((groups, len(LIVE_BLOCKS), PER * ROWS, HD), BF16),
            shape((groups, LIVE, HD), BF16),
            shape((groups, LIVE, HD), BF16),
        ]
        + probs,
        scratch_shapes=load_scratch(arrays, LIVE)
        + [
            pltpu.VMEM((n_tp, D + LANES, wide), BF16),
            pltpu.SemaphoreType.DMA((n_tp, 2 * n_exp)),
        ],
        compiler_params=WHOLE_VMEM,
        cost_estimate=cost(12e9, 30e6),
        name="prepare_heads",
    )(place, lengths, shares, *arrays)


BACKWARD_LOADS = (
    "head_grad", "values", "keys", "queries", "cosine", "sine", "attn_in", "low_q",
    "residual_grad", "tokens", "gains", "qkv_down",
)


def backward_kernel(place_ref, length_ref, index_ref, shares, *refs):
    count = len(BACKWARD_LOADS)
    blocks = len(LIVE_BLOCKS)
    probs_hbm = refs[count : count + blocks]
    input_grad_ref, part_ref = refs[count + blocks : count + blocks + 2]
    scratch = refs[count + blocks + 2 :]
    loads = Loads(BACKWARD_LOADS, refs[:count], scratch[:count], scratch[count])
    w_qkv_s, g_s, grad_s, sum_s, sem, prob_sem = scratch[count + 1 : count + 7]
    probs_s = scratch[count + 7 :]
    n_exp, n_tp, _, wide = shares.shape
    groups = g_s.shape[0] // n_tp
    flags = turned_pieces(groups)
    scale = 1.0 / math.sqrt(HD)

    def prob_copy(z, block):
        here = pl.ds(z * groups, groups)
        return pltpu.make_async_copy(
            probs_hbm[block].at[here], probs_s[block].at[here], prob_sem.at[z, block]
        )

    for z in range(n_tp):
        for block in range(blocks):
            prob_copy(z, block).start()
    copies = share_copies(place_ref, shares, w_qkv_s, sem)
    input_grad_ref[LIVE:, :] = jnp.zeros((input_grad_ref.shape[0] - LIVE, D), BF16)
    head_grad = loads["head_grad"]
    for z in range(n_tp):
        for head in range(groups * PER):
            group, kind = divmod(head, PER)
            part = head_grad[z, :, head * HD : (head + 1) * HD]
            for block, (begin, end) in enumerate(LIVE_BLOCKS):
                size = end - begin
                here = slice(kind * size, (kind + 1) * size)
                g_s[z * groups + group, block, here, :] = part[begin:end]
    values, keys, queries = loads["values"], loads["keys"], loads["queries"]
    cosine, sine = loads["cosine"], loads["sine"]

    def one_place(z, carried):
        for block in range(blocks):
            prob_copy(z, block).wait()
        pieces = []
        for group in range(groups):
            at = z * groups + group
            key_grad = jnp.zeros((HD, LIVE), F32)
            value_grad = jnp.zeros((HD, LIVE), F32)
            query_grads = []
            for block, (begin, end) in enumerate(LIVE_BLOCKS):
                size = end - begin
                query = queries[at, block, : PER * size, :]
                grad = g_s[at, block, : PER * size, :]
                probs = probs_s[block][at]
                wide_probs = probs.astype(F32)
                weight_grad = dot_nt(grad, values[at, :end, :])
                spread = jnp.sum(wide_probs * weight_grad, axis=1, keepdims=True)
                score_grad = (wide_probs * (weight_grad - spread)).astype(BF16)
                query_grads.append(dot(score_grad, keys[at, :end, :]) * scale)

                def widen(part):
                    if end == LIVE:
                        return part
                    return jnp.concatenate([part, jnp.zeros((HD, LIVE - end), F32)], axis=1)

                key_grad += widen(dot_tn(query, score_grad))
                value_grad += widen(dot_tn(grad, probs))
            for head in range(PER):
                rows = [
                    part[head * (end - begin) : (head + 1) * (end - begin)]
                    for part, (begin, end) in zip(query_grads, LIVE_BLOCKS)
                ]
                pieces.append(jnp.concatenate(rows, axis=0))
            pieces += [key_grad.T, value_grad.T]
        joined = jnp.concatenate(pieces, axis=1)
        columns = turn(joined, cosine[...], -sine[...], flags)
        for at, column in enumerate(columns):
            grad_s[z, :, at * LANES : (at + 1) * LANES] = column.astype(BF16)
        return carried

    lax.fori_loop(0, n_tp, one_place, 0)
    for here in copies:
        for copy in here:
            copy.wait()
    sum_s[...] = dot_nt(grad_s[0], w_qkv_s[0])
    for z in range(1, n_tp):
        sum_s[...] += dot_nt(grad_s[z], w_qkv_s[z])
    mask = adapter_mask(length_ref, index_ref, LIVE, LANES)
    low_q_grad = (sum_s[:, D:] * mask).astype(BF16)
    part_ref[:D, :] = dot_tn(loads["attn_in"][...], low_q_grad).astype(BF16)
    low_q = loads["low_q"][...]
    own = grad_s[place_ref[0]]
    for at in range(wide // LANES):
        lanes = slice(at * LANES, (at + 1) * LANES)
        part_ref[D + at * LANES : D + (at + 1) * LANES, :] = dot_tn(low_q, own[:, lanes]).astype(
            BF16
        )
    attn_grad = sum_s[:, :D] + dot_nt(low_q_grad, loads["qkv_down"][...])
    tokens, gain = loads["tokens"][...].astype(F32), loads["gains"][0:1, :]
    residual_grad = loads["residual_grad"][...]
    input_grad_ref[:LIVE, :] = (residual_grad + norm_back(tokens, gain, attn_grad)).astype(BF16)


def attention_back(
    place, lengths, index, attn_in, low_q, heads, head_grad, residual_grad, tokens, gains,
    qkv_down, tables, shares,
):
    n_exp, n_tp, _, wide = shares.shape
    blocks = len(LIVE_BLOCKS)
    queries, keys, values = heads[:3]
    probs = heads[3:]
    arrays = (head_grad, values, keys, queries) + tables
    arrays += (attn_in, low_q, residual_grad, tokens, gains, qkv_down)
    return pl.pallas_call(
        backward_kernel,
        in_specs=[IN_SMEM] * 3 + [IN_HBM] * (1 + len(arrays) + blocks),
        out_specs=[IN_VMEM] * 2,
        out_shape=[shape(tokens.shape, BF16), shape((D + wide, LANES), BF16)],
        scratch_shapes=load_scratch(arrays, LIVE)
        + [
            pltpu.VMEM((n_tp, D + LANES, wide), BF16),
            pltpu.VMEM(queries.shape, BF16),
            pltpu.VMEM((n_tp, LIVE, wide), BF16),
            pltpu.VMEM((LIVE, D + LANES), F32),
            pltpu.SemaphoreType.DMA((n_tp, 2 * n_exp)),
            pltpu.SemaphoreType.DMA((n_tp, blocks)),
        ]
        + [pltpu.VMEM(part.shape, BF16) for part in probs],
        compiler_params=WHOLE_VMEM,
        cost_estimate=cost(25e9, 40e6),
        name="attention_backward",
    )(place, lengths, index, shares, *arrays, *probs)


def from_tp(share, count):
    around = [share]
    for shift in range(1, count):
        around.append(
            lax.ppermute(share, "tp", [(at, (at + shift) % count) for at in range(count)])
        )
    return around


def from_place(place_ref, z, count):
    return lax.rem(place_ref[0] - z + count, count)


def kernel_body(
    tokens, attn_gain, moe_gain, w_qkv, w_out, w_router, w_gate, w_up, w_down, qkv_down, qkv_up,
    out_down, out_up, lengths, adapter_index, loss_mask, routes, upstream,
):
    n_exp = lax.axis_size("exp")
    n_tp = lax.axis_size("tp")
    exp_place = lax.axis_index("exp").astype(jnp.int32).reshape(1)
    tp_place = lax.axis_index("tp").astype(jnp.int32).reshape(1)
    tables = turn_tables(tokens.shape[0])
    gains = jnp.stack([attn_gain, moe_gain])
    loss_row = loss_mask.reshape(1, -1)
    wide = w_qkv.shape[1]
    heads_wide = w_out.shape[0]

    own_experts = pack_experts(w_gate, w_up, w_down)
    weights = lax.all_gather(own_experts, "exp", axis=0, tiled=True)
    own_qkv = pack_share(
        pack_qkv_kernel, "pack_qkv", exp_place, w_qkv, qkv_up, (D + LANES) // n_exp, wide, n_exp
    )
    own_qkv, _ = lax.optimization_barrier((own_qkv, own_experts))
    z_qkv = from_tp(own_qkv, n_tp)
    inputs, _ = lax.optimization_barrier((tokens, own_qkv))
    attn_in, low_q, head, base, low_o = forward(
        lengths, adapter_index, inputs, gains, w_qkv, qkv_down, qkv_up, w_out, out_down, tables
    )
    base, low_o, z_qkv = lax.optimization_barrier((base, low_o, z_qkv))
    z_qkv = jnp.stack(z_qkv)
    base, low_o = lax.psum((base, low_o), "tp")
    own_out = pack_share(
        pack_out_kernel, "pack_out", exp_place, w_out, out_down, heads_wide // n_exp, D + LANES,
        n_exp,
    )
    own_out, _ = lax.optimization_barrier((own_out, base))
    z_out = from_tp(own_out, n_tp)
    z_qkv, _ = lax.optimization_barrier((z_qkv, weights))
    qkv_shares = lax.all_gather(z_qkv, "exp", axis=0)

    residual, moe_part, normed_part = experts_both(
        tokens, base, low_o, out_up, gains, w_router, routes, upstream, loss_row, weights
    )
    normed_part, z_out = lax.optimization_barrier((normed_part, z_out))
    z_out = jnp.stack(z_out)
    normed_grad = lax.psum(normed_part, "tp")
    z_out, _ = lax.optimization_barrier((z_out, qkv_shares))
    out_shares = lax.all_gather(z_out, "exp", axis=0)
    late_in, _ = lax.optimization_barrier((attn_in, normed_part))
    heads = prepare(tp_place, lengths, late_in, low_q, tables, qkv_shares)

    moe_part, _, _ = lax.optimization_barrier((moe_part, normed_grad, heads[0]))
    moe_out = lax.psum(moe_part, "tp")
    normed_grad, _, _ = lax.optimization_barrier((normed_grad, out_shares, heads[0]))
    residual_grad, head_grad, out_part = branch_back(
        tp_place, lengths, adapter_index, residual, low_o, normed_grad, upstream, loss_row, gains,
        out_up, head, out_shares,
    )
    out_parts = lax.all_gather(out_part, "exp", axis=0)
    input_grad, qkv_part = attention_back(
        tp_place, lengths, adapter_index, attn_in, low_q, heads, head_grad, residual_grad, tokens,
        gains, qkv_down, tables, qkv_shares,
    )
    moe_out, out_parts, _ = lax.optimization_barrier((moe_out, out_parts, qkv_part))
    output = (residual + moe_out.astype(F32)).astype(BF16)
    out_sum = jnp.sum(out_parts.astype(F32), axis=0)

    def side_by_side(stacked):
        pieces = stacked.reshape(-1, LANES, LANES)
        return pieces.transpose(1, 0, 2).reshape(LANES, -1)

    grad_out_down, grad_out_up = out_sum[D:], side_by_side(out_sum[:D])
    share = qkv_part.shape[0] // n_exp
    parts = lax.all_to_all(qkv_part.reshape(n_exp, share, LANES), "exp", 0, 0, tiled=True)
    qkv_sum = jnp.sum(parts.astype(F32), axis=0).astype(BF16)
    qkv_sum, output, grad_out_down, grad_out_up = lax.optimization_barrier(
        (qkv_sum, output, grad_out_down, grad_out_up)
    )
    spread = jnp.broadcast_to(qkv_sum[None], (n_exp, share, LANES))
    qkv_sum = lax.all_to_all(spread, "exp", 0, 0, tiled=True).astype(F32).reshape(-1, LANES)
    return (
        output,
        input_grad,
        qkv_sum[:D],
        side_by_side(qkv_sum[D:]),
        grad_out_down,
        grad_out_up,
    )


def product(left_m, right_m):
    return jnp.dot(left_m, right_m, preferred_element_type=jnp.float32)


def contract(einsum_form, left_m, right_m):
    return jnp.einsum(einsum_form, left_m, right_m, preferred_element_type=jnp.float32)


def rms_norm(vectors, gain_vec):
    inv_root = lax.rsqrt(jnp.mean(vectors * vectors, axis=-1, keepdims=True) + EPS)
    return vectors * inv_root * gain_vec


def rms_norm_back(vectors, gain_vec, upstream_grad):
    inv_root = lax.rsqrt(jnp.mean(vectors * vectors, axis=-1, keepdims=True) + EPS)
    weighted = upstream_grad * gain_vec
    return inv_root * weighted - vectors * (inv_root * inv_root * inv_root) * jnp.mean(
        vectors * weighted, axis=-1, keepdims=True
    )


def layout(length_row, index_row):
    places = jnp.arange(TOK_DEV, dtype=jnp.int32)
    doc_ends = jnp.cumsum(length_row)
    doc_starts = doc_ends - length_row
    member = (places[:, None] >= doc_starts[None, :]) & (places[:, None] < doc_ends[None, :])
    occupied = jnp.any(member, axis=1)
    position = jnp.sum(jnp.where(member, places[:, None] - doc_starts[None, :], 0), axis=1)
    owner_doc = jnp.sum(jnp.where(member, jnp.arange(DOCS, dtype=jnp.int32)[None, :], 0), axis=1)
    doc_ident = jnp.where(occupied, owner_doc, DOCS + places)
    chosen = jnp.sum(jnp.where(member, index_row[None, :], 0), axis=1)
    adapter_pick = occupied[:, None] & (
        chosen[:, None] == jnp.arange(ADAPTERS, dtype=jnp.int32)[None, :]
    )
    rank_mask = jnp.repeat(jnp.where(adapter_pick, 1.0, 0.0).astype(jnp.float32), RANK, axis=1)
    return (occupied, position, doc_ident, rank_mask)


def angles(position):
    half_width = HD // 2
    frequency = jnp.exp(-math.log(ROPE_BASE) * jnp.arange(half_width, dtype=jnp.float32) * 2.0 / HD)
    turned = position.astype(jnp.float32)[:, None] * frequency[None, :]
    return (jnp.cos(turned), jnp.sin(turned))


def rotate(vectors, cosine, sine_table):
    half_width = vectors.shape[-1] // 2
    front_half = vectors[..., :half_width]
    back_half = vectors[..., half_width:]
    return jnp.concatenate(
        [
            front_half * cosine - back_half * sine_table,
            back_half * cosine + front_half * sine_table,
        ],
        axis=-1,
    )


def moe(normed, cot_low, gates, gate_up, down):
    width = down.shape[1]
    both = contract("td,edf->tef", normed, gate_up)
    pre_gate = both[:, :, :width]
    pre_up = both[:, :, width:]
    sigmoid_g = jax.nn.sigmoid(pre_gate)
    activated = pre_gate * sigmoid_g
    hidden = (activated * pre_up).astype(jnp.bfloat16).astype(jnp.float32)
    inner_raw = contract("td,efd->tef", cot_low, down)
    gate_part = jnp.sum(hidden * inner_raw, axis=-1)
    moe_part = contract("tef,efd->td", (gates[:, :, None] * hidden).astype(jnp.bfloat16), down)
    inner_grad = inner_raw * gates[:, :, None]
    grad_gate = inner_grad * pre_up * sigmoid_g * (1.0 + pre_gate * (1.0 - sigmoid_g))
    grad_up = inner_grad * activated
    grad_both = jnp.concatenate([grad_gate, grad_up], axis=2).astype(jnp.bfloat16)
    normed_part = contract("tef,edf->td", grad_both, gate_up)
    return (moe_part, gate_part, normed_part)


def body(
    tokens,
    attn_gain,
    moe_gain,
    w_qkv,
    w_out,
    w_router,
    w_gate,
    w_up,
    w_down,
    qkv_down,
    qkv_up,
    out_down,
    out_up,
    lengths,
    adapter_index,
    loss_mask,
    routes,
    upstream,
):
    n_exp = lax.axis_size("exp")
    groups = KV_HEADS // lax.axis_size("tp")
    per_group = HEADS // KV_HEADS
    experts = EXP_DEV * n_exp
    gate_up = lax.all_gather(jnp.concatenate([w_gate, w_up], axis=2), "exp", axis=0, tiled=True)
    down = lax.all_gather(w_down, "exp", axis=0, tiled=True)
    block_rows = min(512, TOK_DEV)
    blocks = TOK_DEV // block_rows
    score_scale = 1.0 / math.sqrt(HD)
    places = jnp.arange(TOK_DEV, dtype=jnp.int32)
    occupied, position, doc_ident, rank_mask = layout(lengths[0], adapter_index[0])
    mask_low = rank_mask.astype(jnp.bfloat16)
    cosine, sine_table = angles(position)
    inputs = tokens.astype(jnp.float32)
    attn_in = rms_norm(inputs, attn_gain).astype(jnp.bfloat16)
    low_q = (product(attn_in, qkv_down) * rank_mask).astype(jnp.bfloat16)
    projected = (product(attn_in, w_qkv) + product(low_q, qkv_up)).reshape(
        TOK_DEV, groups, per_group + 2, HD
    )
    query_rows = rotate(
        projected[:, :, :per_group], cosine[:, None, None], sine_table[:, None, None]
    ).astype(jnp.bfloat16)
    key_rows = rotate(projected[:, :, per_group], cosine[:, None], sine_table[:, None]).astype(
        jnp.bfloat16
    )
    val_rows = projected[:, :, per_group + 1].astype(jnp.bfloat16)

    def masked_scores(q_blk, q_place, q_ident):
        scores = contract("qgrd,kgd->grqk", q_blk, key_rows) * score_scale
        allowed = (q_ident[:, None] == doc_ident[None, :]) & (places[None, :] <= q_place[:, None])
        return jnp.where(allowed, scores, -1e30)

    def attend(pieces):
        q_blk, q_place, q_ident = pieces
        scores = masked_scores(q_blk, q_place, q_ident)
        row_max = jnp.max(scores, axis=-1, keepdims=True)
        lifted = jnp.exp(scores - row_max)
        row_total = jnp.sum(lifted, axis=-1, keepdims=True)
        weights = (lifted / row_total).astype(jnp.bfloat16)
        return (
            contract("grqk,kgd->qgrd", weights, val_rows),
            row_max[..., 0] + jnp.log(row_total[..., 0]),
        )

    query_blocks = query_rows.reshape(blocks, block_rows, groups, per_group, HD)
    place_blocks = places.reshape(blocks, block_rows)
    ident_blocks = doc_ident.reshape(blocks, block_rows)
    attended, log_totals = lax.map(attend, (query_blocks, place_blocks, ident_blocks))
    head_rows = attended.reshape(TOK_DEV, groups * per_group * HD).astype(jnp.bfloat16)
    attn_base, low_rank = (
        lax.psum(product(head_rows, w_out).astype(jnp.bfloat16), "tp").astype(jnp.float32),
        lax.psum((product(head_rows, out_down) * rank_mask).astype(jnp.bfloat16), "tp").astype(
            jnp.float32
        ),
    )
    low_o = low_rank.astype(jnp.bfloat16)
    residual = inputs + attn_base + product(low_o, out_up)
    normed = rms_norm(residual, moe_gain).astype(jnp.bfloat16)
    logits = product(normed, w_router)
    one_hot = routes[:, :, None] == jnp.arange(experts, dtype=jnp.int32)[None, None, :]
    routed = jnp.any(one_hot, axis=1)
    gates = jax.nn.softmax(jnp.where(routed, logits, -1e30), axis=-1)
    live_mask = jnp.where(occupied & (loss_mask > 0), 1.0, 0.0).astype(jnp.float32)
    cotangent = upstream.astype(jnp.float32) * live_mask[:, None]
    cot_low = cotangent.astype(jnp.bfloat16)
    moe_part, gate_part, normed_part = moe(normed, cot_low, gates, gate_up, down)
    logit_grad = (
        gates * (gate_part - jnp.sum(gates * gate_part, axis=-1, keepdims=True))
    ).astype(jnp.bfloat16)
    normed_part = (normed_part + product(logit_grad, w_router.T)).astype(jnp.bfloat16)
    normed_sum = lax.psum(normed_part, "tp")
    normed_sum, moe_part = lax.optimization_barrier((normed_sum, moe_part.astype(jnp.bfloat16)))
    normed_grad = normed_sum.astype(jnp.float32)
    moe_out = lax.psum(moe_part, "tp").astype(jnp.float32)
    output = (residual + moe_out).astype(jnp.bfloat16)
    residual_grad = cotangent + rms_norm_back(residual, moe_gain, normed_grad)
    branch_grad = residual_grad.astype(jnp.bfloat16)
    low_o_grad = product(branch_grad, out_up.T).astype(jnp.bfloat16) * mask_low
    out_up_part = contract("tr,td->rd", low_o, branch_grad)
    head_grad = (product(branch_grad, w_out.T) + product(low_o_grad, out_down.T)).astype(
        jnp.bfloat16
    )
    out_down_part = contract("tc,tr->cr", head_rows, low_o_grad)
    grad_blocks = head_grad.reshape(blocks, block_rows, groups, per_group, HD)

    def attend_back(carried, pieces):
        key_acc, val_acc = carried
        q_blk, q_place, q_ident, lse_blk, g_blk = pieces
        weights = jnp.exp(masked_scores(q_blk, q_place, q_ident) - lse_blk[..., None])
        weight_grad = contract("qgrd,kgd->grqk", g_blk, val_rows)
        score_grad = (
            weights * (weight_grad - jnp.sum(weights * weight_grad, axis=-1, keepdims=True))
        ).astype(jnp.bfloat16)
        query_grad = contract("grqk,kgd->qgrd", score_grad, key_rows) * score_scale
        key_acc = key_acc + contract("grqk,qgrd->kgd", score_grad, q_blk) * score_scale
        val_acc = val_acc + contract("grqk,qgrd->kgd", weights.astype(jnp.bfloat16), g_blk)
        return ((key_acc, val_acc), query_grad)

    zero_acc = jnp.zeros((TOK_DEV, groups, HD), jnp.float32)
    (key_grad, val_grad), query_grad = lax.scan(
        attend_back,
        (zero_acc, zero_acc),
        (query_blocks, place_blocks, ident_blocks, log_totals, grad_blocks),
    )
    query_grad = rotate(
        query_grad.reshape(TOK_DEV, groups, per_group, HD),
        cosine[:, None, None],
        -sine_table[:, None, None],
    )
    key_grad = rotate(key_grad, cosine[:, None], -sine_table[:, None])
    projected_grad = (
        jnp.concatenate([query_grad, key_grad[:, :, None], val_grad[:, :, None]], axis=2)
        .reshape(TOK_DEV, -1)
        .astype(jnp.bfloat16)
    )
    qkv_up_part = contract("tr,tc->rc", low_q, projected_grad)
    attn_grad, low_q_grad = (
        lax.psum(contract("tc,dc->td", projected_grad, w_qkv).astype(jnp.bfloat16), "tp").astype(
            jnp.float32
        ),
        lax.psum(contract("tc,rc->tr", projected_grad, qkv_up).astype(jnp.bfloat16), "tp").astype(
            jnp.float32
        ),
    )
    low_q_grad = low_q_grad.astype(jnp.bfloat16) * mask_low
    attn_grad = attn_grad + contract("tr,dr->td", low_q_grad, qkv_down)
    qkv_down_part = contract("td,tr->dr", attn_in, low_q_grad)
    input_grad = (residual_grad + rms_norm_back(inputs, attn_gain, attn_grad)).astype(jnp.bfloat16)
    summed = (
        lax.psum(qkv_down_part.astype(jnp.bfloat16), "exp").astype(jnp.float32),
        lax.psum(qkv_up_part.astype(jnp.bfloat16), "exp").astype(jnp.float32),
        lax.psum(out_down_part.astype(jnp.bfloat16), "exp").astype(jnp.float32),
        lax.psum(out_up_part.astype(jnp.bfloat16), "exp").astype(jnp.float32),
    )
    return (output, input_grad, summed[0], summed[1], summed[2], summed[3])


def kernels_fit(mesh):
    n_exp, n_tp = mesh.shape["exp"], mesh.shape["tp"]
    groups = KV_HEADS // n_tp
    return groups % 2 == 0 and FF // n_tp == LANES and LANES // n_exp % 16 == 0


def solution(mesh):
    placed = (
        P("exp", None),
        P(),
        P(),
        P(None, "tp"),
        P("tp", None),
        P(),
        P("exp", None, "tp"),
        P("exp", None, "tp"),
        P("exp", "tp", None),
        P(),
        P(None, "tp"),
        P("tp", None),
        P(),
        P("exp", None),
        P("exp", None),
        P("exp"),
        P("exp", None),
        P("exp", None),
    )
    return jax.shard_map(
        kernel_body if kernels_fit(mesh) else body,
        mesh=mesh,
        in_specs=placed,
        out_specs=(P("exp", None), P("exp", None), P(), P(None, "tp"), P("tp", None), P()),
        check_vma=False,
    )
```

```python
import functools
import math

import jax
import jax.numpy as jnp
import numpy as np
from jax import lax
from jax.experimental import pallas as pl
from jax.experimental.pallas import tpu as pltpu
from jax.sharding import PartitionSpec as P

D = 1536
HEADS = 24
KV_HEADS = 8
HD = 64
TOP = 8
RANK = 16
ADAPTERS = 8
EXP_DEV = 2
DOCS = 4
TOK_DEV = 512
LIVE = 448
FF = 512
EPS = 1e-06
ROPE_BASE = 10000.0

PER = HEADS // KV_HEADS
LANES = 128
ROWS = 128
BLOCKS = tuple((at, min(at + ROWS, TOK_DEV)) for at in range(0, TOK_DEV, ROWS))
LIVE_BLOCKS = tuple((at, min(at + ROWS, LIVE)) for at in range(0, LIVE, ROWS))
F32 = jnp.float32
BF16 = jnp.bfloat16
MIB = 2**20
NT = (((1,), (1,)), ((), ()))
TN = (((0,), (0,)), ((), ()))
WHOLE_VMEM = pltpu.CompilerParams(vmem_limit_bytes=63 * MIB)
IN_VMEM = pl.BlockSpec(memory_space=pltpu.VMEM)
IN_SMEM = pl.BlockSpec(memory_space=pltpu.SMEM)
IN_HBM = pl.BlockSpec(memory_space=pltpu.HBM)


def dot(left, right):
    return jnp.dot(left, right, preferred_element_type=F32)


def dot_nt(left, right):
    return lax.dot_general(left, right, NT, preferred_element_type=F32)


def dot_tn(left, right):
    return lax.dot_general(left, right, TN, preferred_element_type=F32)


def cost(flops, moved):
    return pl.CostEstimate(flops=int(flops), bytes_accessed=int(moved), transcendentals=0)


def shape(dims, dtype):
    return jax.ShapeDtypeStruct(dims, dtype)


def turn_tables(rows):
    half = HD // 2
    frequency = np.exp(-math.log(ROPE_BASE) * np.arange(half, dtype=np.float64) * 2.0 / HD)
    turned = np.arange(rows, dtype=np.float64)[:, None] * frequency[None, :]
    cosine, sine = np.cos(turned), np.sin(turned)
    return (
        jnp.asarray(np.concatenate([cosine] * 4, axis=1), F32),
        jnp.asarray(np.concatenate([-sine, sine, -sine, sine], axis=1), F32),
    )


def turned_pieces(groups):
    return [piece < PER + 1 for _ in range(groups) for piece in range(PER + 2)]


def turn(joined, cosine, sine, flags):
    lane = lax.broadcasted_iota(jnp.int32, cosine.shape, 1)
    front = (lane & 32) == 0
    left = lane < HD
    columns = []
    for at in range(joined.shape[1] // LANES):
        column = joined[:, at * LANES : (at + 1) * LANES]
        swapped = jnp.where(front, pltpu.roll(column, 96, 1), pltpu.roll(column, 32, 1))
        rotated = column * cosine + swapped * sine
        if not (flags[2 * at] and flags[2 * at + 1]):
            rotated = jnp.where(left if flags[2 * at] else jnp.logical_not(left), rotated, column)
        columns.append(rotated)
    return columns


def first_keys(length_ref, rows):
    row = lax.broadcasted_iota(jnp.int32, (rows, 1), 0)
    begin = jnp.zeros((rows, 1), jnp.int32)
    end = 0
    for doc in range(DOCS):
        if doc:
            begin = jnp.where(row >= end, end, begin)
        end = end + length_ref[0, doc]
    return jnp.where(row >= end, row, begin)


def adapter_mask(length_ref, index_ref, rows, width):
    row = lax.broadcasted_iota(jnp.int32, (rows, width), 0)
    adapter = lax.shift_right_logical(lax.broadcasted_iota(jnp.int32, (rows, width), 1), 4)
    mask = jnp.zeros((rows, width), F32)
    begin = 0
    for doc in range(DOCS):
        end = begin + length_ref[0, doc]
        inside = (row >= begin) & (row < end) & (adapter == index_ref[0, doc])
        mask = jnp.where(inside, 1.0, mask)
        begin = end
    return mask


def folding():
    rank = lax.broadcasted_iota(jnp.int32, (RANK, LANES), 0)
    lane = lax.broadcasted_iota(jnp.int32, (RANK, LANES), 1)
    return jnp.where((lane & (RANK - 1)) == rank, 1.0, 0.0).astype(BF16)


def unfold(low_ref, length_ref, index_ref, rows):
    spread = dot_tn(low_ref[-RANK:, :rows], folding())
    return (spread * adapter_mask(length_ref, index_ref, rows, LANES)).astype(BF16)


def seen_block(first, begin, end):
    row = lax.broadcasted_iota(jnp.int32, (end - begin, end), 0) + begin
    key = lax.broadcasted_iota(jnp.int32, (end - begin, end), 1)
    seen = (key <= row) & (key >= first[begin:end])
    return jnp.concatenate([seen] * PER, axis=0)


def softmax_block(scores, seen):
    scores = jnp.where(seen, scores, -1e30)
    lifted = jnp.exp(scores - jnp.max(scores, axis=1, keepdims=True))
    return (lifted * (1.0 / jnp.sum(lifted, axis=1, keepdims=True))).astype(BF16)


def column_of(row_ref, rows):
    row = row_ref[...].astype(F32)
    at = lax.broadcasted_iota(jnp.int32, (rows, row.shape[1]), 0)
    lane = lax.broadcasted_iota(jnp.int32, (rows, row.shape[1]), 1)
    return jnp.sum(jnp.where(at == lane, row, 0.0), axis=1, keepdims=True)


def store_heads(columns, slot, blocks, q_s, k_s, v_s):
    scale = 1.0 / math.sqrt(HD)
    for at, column in enumerate(columns):
        halves = (column[:, :HD], pltpu.roll(column, HD, 1)[:, :HD])
        for piece, part in zip((2 * at, 2 * at + 1), halves):
            group, kind = divmod(piece, PER + 2)
            if kind == PER:
                k_s[slot + group] = part.astype(BF16)
            elif kind == PER + 1:
                v_s[slot + group] = part.astype(BF16)
            else:
                part = (part * scale).astype(BF16)
                for block, (begin, end) in enumerate(blocks):
                    size = end - begin
                    here = slice(kind * size, (kind + 1) * size)
                    q_s[slot + group, block, here, :] = part[begin:end]


def run_copies(pairs, sem):
    copies = [
        pltpu.make_async_copy(source, target, sem.at[number])
        for number, (source, target) in enumerate(pairs)
    ]
    for copy in copies:
        copy.start()
    for copy in copies:
        copy.wait()


def pack_experts_kernel(gate, up, down, packed, held, sem, out_sem):
    width = gate.shape[2]
    pairs = []
    for expert in range(gate.shape[0]):
        pairs.append((gate.at[expert], held.at[expert, :, :width]))
        pairs.append((up.at[expert], held.at[expert, :, width : 2 * width]))
        for at in range(D // LANES):
            lanes = slice(at * LANES, (at + 1) * LANES)
            pairs.append((down.at[expert, :, lanes], held.at[expert, lanes, 2 * width :]))
    run_copies(pairs, sem)
    run_copies([(held, packed)], out_sem)


def pack_experts(w_gate, w_up, w_down):
    count, _, width = w_gate.shape
    packed = shape((count, D, 3 * width), BF16)
    return pl.pallas_call(
        pack_experts_kernel,
        in_specs=[IN_HBM] * 3,
        out_specs=IN_HBM,
        out_shape=packed,
        scratch_shapes=[
            pltpu.VMEM(packed.shape, BF16),
            pltpu.SemaphoreType.DMA((count * (2 + D // LANES),)),
            pltpu.SemaphoreType.DMA((1,)),
        ],
        compiler_params=WHOLE_VMEM,
        cost_estimate=cost(0, 2 * 2 * count * D * 3 * width),
        name="pack_experts",
    )(w_gate, w_up, w_down)


def share_rows(n_exp, heads_wide):
    return (D // n_exp, LANES // n_exp, heads_wide // n_exp)


def pack_qkv_kernel(n_exp, place_ref, w_qkv, qkv_up, packed, held, sem, out_sem):
    qkv_rows, up_rows, _ = share_rows(n_exp, 0)
    own_qkv = pl.ds(pl.multiple_of(place_ref[0] * qkv_rows, 16), qkv_rows)
    own_up = pl.ds(pl.multiple_of(place_ref[0] * up_rows, 16), up_rows)
    pairs = [
        (w_qkv.at[own_qkv, :], held.at[:qkv_rows, :]),
        (qkv_up.at[own_up, :], held.at[qkv_rows:, :]),
    ]
    run_copies(pairs, sem)
    run_copies([(held, packed)], out_sem)


def pack_out_kernel(n_exp, place_ref, w_out, out_down, packed, held, sem, out_sem):
    out_rows = w_out.shape[0] // n_exp
    own = pl.ds(pl.multiple_of(place_ref[0] * out_rows, 16), out_rows)
    pairs = [
        (w_out.at[own, :], held.at[:, :D]),
        (out_down.at[own, :], held.at[:, D:]),
    ]
    run_copies(pairs, sem)
    run_copies([(held, packed)], out_sem)


def pack_share(kernel, name, place, first, second, rows, wide, n_exp):
    return pl.pallas_call(
        functools.partial(kernel, n_exp),
        in_specs=[IN_SMEM] + [IN_HBM] * 2,
        out_specs=IN_HBM,
        out_shape=shape((rows, wide), BF16),
        scratch_shapes=[
            pltpu.VMEM((rows, wide), BF16),
            pltpu.SemaphoreType.DMA((2,)),
            pltpu.SemaphoreType.DMA((1,)),
        ],
        compiler_params=WHOLE_VMEM,
        cost_estimate=cost(0, 8 * rows * wide),
        name=name,
    )(place, first, second)


class Loads:
    def __init__(self, names, sources, targets, sem):
        self.copies = {}
        for number, (name, source, target) in enumerate(zip(names, sources, targets)):
            if source.shape != target.shape:
                source = source.at[: target.shape[0]]
            self.copies[name] = pltpu.make_async_copy(source, target, sem.at[number])
        self.targets = dict(zip(names, targets))
        for copy in self.copies.values():
            copy.start()

    def __getitem__(self, name):
        copy = self.copies.pop(name, None)
        if copy is not None:
            copy.wait()
        return self.targets[name]


def load_scratch(arrays, rows=TOK_DEV):
    return [
        pltpu.VMEM((rows if array.shape[0] == TOK_DEV else array.shape[0],) + array.shape[1:], array.dtype)
        for array in arrays
    ] + [pltpu.SemaphoreType.DMA((len(arrays),))]


FORWARD_LOADS = (
    "tokens", "gains", "qkv_down", "w_qkv", "qkv_up", "cosine", "sine", "w_out", "out_down",
)


def forward_kernel(length_ref, index_ref, *refs):
    count = len(FORWARD_LOADS)
    attn_in_ref, low_q_ref, head_ref, base_ref = refs[count : count + 4]
    load_sem, q_s, k_s, v_s = refs[2 * count + 4 :]
    loads = Loads(FORWARD_LOADS, refs[:count], refs[count + 4 : 2 * count + 4], load_sem)
    rows = attn_in_ref.shape[0]
    groups = k_s.shape[0]
    mask = adapter_mask(length_ref, index_ref, rows, LANES)
    first = first_keys(length_ref, rows)
    inputs = loads["tokens"][...].astype(F32)
    inv_root = lax.rsqrt(jnp.mean(inputs * inputs, axis=1, keepdims=True) + EPS)
    attn_in_ref[...] = (inputs * inv_root * loads["gains"][0:1, :]).astype(BF16)
    attn_in = attn_in_ref[...]
    low_q = (dot(attn_in, loads["qkv_down"][...]) * mask).astype(BF16)
    low_q_ref[...] = low_q
    projected = dot(attn_in, loads["w_qkv"][...]) + dot(low_q, loads["qkv_up"][...])
    cosine, sine = loads["cosine"][...], loads["sine"][...]
    columns = turn(projected, cosine, sine, turned_pieces(groups))
    store_heads(columns, 0, BLOCKS, q_s, k_s, v_s)
    for block, (begin, end) in enumerate(BLOCKS):
        seen = seen_block(first, begin, end)
        heads = []
        for group in range(groups):
            probs = softmax_block(dot_nt(q_s[group, block], k_s[group, :end, :]), seen)
            out = dot(probs, v_s[group, :end, :])
            heads += [out[head * ROWS : (head + 1) * ROWS] for head in range(PER)]
        head_ref[begin:end, :] = jnp.concatenate(heads, axis=1).astype(BF16)
    head_out = head_ref[...]
    base_ref[:rows, :] = dot(head_out, loads["w_out"][...]).astype(BF16)
    low_o = (dot(head_out, loads["out_down"][...]) * mask).astype(BF16)
    base_ref[rows:, :rows] = dot_nt(folding(), low_o).astype(BF16)
    base_ref[rows:, rows:] = jnp.zeros((RANK, D - rows), BF16)


def forward(lengths, index, tokens, gains, w_qkv, qkv_down, qkv_up, w_out, out_down, tables):
    rows = tokens.shape[0]
    heads_wide = w_out.shape[0]
    groups = w_qkv.shape[1] // (HD * (PER + 2))
    arrays = (tokens, gains, qkv_down, w_qkv, qkv_up) + tables + (w_out, out_down)
    return pl.pallas_call(
        forward_kernel,
        in_specs=[IN_SMEM] * 2 + [IN_HBM] * len(arrays),
        out_specs=[IN_VMEM] * 4,
        out_shape=[
            shape((rows, D), BF16),
            shape((rows, LANES), BF16),
            shape((rows, heads_wide), BF16),
            shape((rows + RANK, D), BF16),
        ],
        scratch_shapes=load_scratch(arrays)
        + [
            pltpu.VMEM((groups, rows // ROWS, PER * ROWS, HD), BF16),
            pltpu.VMEM((groups, rows, HD), BF16),
            pltpu.VMEM((groups, rows, HD), BF16),
        ],
        compiler_params=WHOLE_VMEM,
        cost_estimate=cost(6e9, 10e6),
        name="attention_forward",
    )(lengths, index, *arrays)


def down_of(weight, width):
    columns = [
        weight[at * LANES : (at + 1) * LANES, 2 * width : 3 * width] for at in range(D // LANES)
    ]
    return jnp.concatenate(columns, axis=1)


def experts_kernel(
    length_ref, index_ref, tokens_ref, base_ref, out_up_ref, gains_ref, router_ref, routes_ref, upstream_ref,
    loss_ref, weight_ref, residual_ref, hidden_ref, grad_ref,
    normed_s, cot_s, gates_s, part_s, grad_s,
):
    step = pl.program_id(0)
    count, _, packed = weight_ref.shape
    width = packed // 3
    lane = lax.broadcasted_iota(jnp.int32, gates_s.shape, 1)

    @pl.when(step == 0)
    def _():
        residual = (
            tokens_ref[...].astype(F32)
            + base_ref[:TOK_DEV, :].astype(F32)
            + dot(unfold(base_ref, length_ref, index_ref, TOK_DEV), out_up_ref[...])
        )
        residual_ref[...] = residual
        inv_root = lax.rsqrt(jnp.mean(residual * residual, axis=1, keepdims=True) + EPS)
        normed = (residual * inv_root * gains_ref[1:2, :]).astype(BF16)
        normed_s[...] = normed
        kept = column_of(loss_ref, LIVE) > 0.0
        cot_s[...] = jnp.where(kept, upstream_ref[...].astype(F32), 0.0).astype(BF16)
        logits = dot_nt(normed, router_ref[...])
        routes = routes_ref[...].astype(F32).T
        place = lane.astype(F32)
        routed = place == routes[:, 0:1]
        for slot in range(1, TOP):
            routed = routed | (place == routes[:, slot : slot + 1])
        logits = jnp.where(routed, logits, -1e30)
        lifted = jnp.exp(logits - jnp.max(logits, axis=1, keepdims=True))
        gates_s[...] = lifted / jnp.sum(lifted, axis=1, keepdims=True)
        part_s[...] = jnp.zeros_like(part_s)
        grad_s[...] = jnp.zeros_like(grad_s)

    normed = normed_s[...]
    cot = cot_s[...]
    gates = gates_s[...]
    part = jnp.zeros(part_s.shape, F32)
    grads = []
    for pair in range(0, count, 2):
        pair_down = [down_of(weight_ref.at[pair + half], width) for half in range(2)]
        pair_raw = dot_nt(cot, jnp.concatenate(pair_down, axis=0))
        for half in range(2):
            expert = pair + half
            joined = dot(normed, weight_ref[expert, :, : 2 * width])
            pre_gate = joined[:, :width]
            pre_up = joined[:, width:]
            raw = pair_raw[:, half * width : (half + 1) * width]
            sigmoid = 0.5 * jnp.tanh(0.5 * pre_gate) + 0.5
            activated = pre_gate * sigmoid
            value = activated * pre_up
            here = lane == step * count + expert
            gate = jnp.sum(jnp.where(here, gates, 0.0), axis=1, keepdims=True)
            hidden_ref[:, expert * width : (expert + 1) * width] = (gate * value).astype(BF16)
            gate_grad = jnp.sum(value[:LIVE] * raw, axis=1, keepdims=True)
            part += jnp.where(here[:LIVE], gate_grad, 0.0)
            inner = raw * gate[:LIVE]
            sigmoid, activated = sigmoid[:LIVE], activated[:LIVE]
            slope = sigmoid + activated * (1.0 - sigmoid)
            grads.append((inner * pre_up[:LIVE] * slope).astype(BF16))
            grads.append((inner * activated).astype(BF16))
    part_s[...] += part
    ups = [weight_ref[expert, :, : 2 * width] for expert in range(count)]
    grad_s[...] += dot_nt(jnp.concatenate(grads, axis=1), jnp.concatenate(ups, axis=1))

    @pl.when(step == pl.num_programs(0) - 1)
    def _():
        live_gates, gate_part = gates[:LIVE], part_s[...]
        spread = jnp.sum(live_gates * gate_part, axis=1, keepdims=True)
        logit_grad = (live_gates * (gate_part - spread)).astype(BF16)
        grad_ref[...] = (grad_s[...] + dot(logit_grad, router_ref[...])).astype(BF16)


def experts_both(
    lengths, index, tokens, base, out_up, gains, router, routes, upstream, loss_mask, weights,
    count=4,
):
    rows = tokens.shape[0]
    experts, _, packed = weights.shape
    width = packed // 3
    arrays = (tokens, base, out_up, gains, router.T, routes.T, upstream, loss_mask)
    in_specs = [IN_SMEM] * 2
    in_specs += [pl.BlockSpec(array.shape, lambda step: (0, 0)) for array in arrays]
    in_specs[2 + 6] = pl.BlockSpec((LIVE, D), lambda step: (0, 0))
    in_specs.append(pl.BlockSpec((count, D, packed), lambda step: (step, 0, 0)))
    return pl.pallas_call(
        experts_kernel,
        grid=(experts // count,),
        in_specs=in_specs,
        out_specs=[
            pl.BlockSpec((rows, D), lambda step: (0, 0)),
            pl.BlockSpec((rows, count * width), lambda step: (0, step)),
            pl.BlockSpec((LIVE, D), lambda step: (0, 0)),
        ],
        out_shape=[
            shape((rows, D), F32),
            shape((rows, experts * width), BF16),
            shape((LIVE, D), BF16),
        ],
        scratch_shapes=[
            pltpu.VMEM((rows, D), BF16),
            pltpu.VMEM((LIVE, D), BF16),
            pltpu.VMEM((rows, experts), F32),
            pltpu.VMEM((LIVE, experts), F32),
            pltpu.VMEM((LIVE, D), F32),
        ],
        compiler_params=WHOLE_VMEM,
        cost_estimate=cost(20e9, 30e6),
        name="experts",
    )(lengths, index, *arrays, weights)


def combine_kernel(hidden_hbm, weights_hbm, moe_ref, hidden_s, downs_s, hidden_sem, sem):
    experts, _, width = downs_s.shape
    load = pltpu.make_async_copy(hidden_hbm, hidden_s, hidden_sem)
    load.start()
    copies = []
    for expert in range(experts):
        source, target = weights_hbm.at[expert, :, 2 * width :], downs_s.at[expert]
        copies.append(pltpu.make_async_copy(source, target, sem.at[expert]))
        copies[-1].start()
    load.wait()
    for copy in copies:
        copy.wait()
    for at in range(0, D, 2 * LANES):
        columns = []
        for expert in range(experts):
            pieces = [
                downs_s[expert, at + left : at + left + LANES, :] for left in (0, LANES)
            ]
            columns.append(jnp.concatenate(pieces, axis=1))
        moe_ref[:, at : at + 2 * LANES] = dot(
            hidden_s[...], jnp.concatenate(columns, axis=0)
        ).astype(BF16)


def combine(hidden, weights):
    rows = hidden.shape[0]
    experts, _, packed = weights.shape
    return pl.pallas_call(
        combine_kernel,
        in_specs=[IN_HBM] * 2,
        out_specs=IN_VMEM,
        out_shape=shape((rows, D), BF16),
        scratch_shapes=[
            pltpu.VMEM(hidden.shape, BF16),
            pltpu.VMEM((experts, D, packed // 3), BF16),
            pltpu.SemaphoreType.DMA(()),
            pltpu.SemaphoreType.DMA((experts,)),
        ],
        compiler_params=WHOLE_VMEM,
        cost_estimate=cost(4e9, 10e6),
        name="combine",
    )(hidden, weights)


def norm_back(vectors, gain, upstream):
    inv_root = lax.rsqrt(jnp.mean(vectors * vectors, axis=1, keepdims=True) + EPS)
    weighted = upstream * gain
    slope = jnp.mean(vectors * weighted, axis=1, keepdims=True)
    return inv_root * weighted - vectors * (inv_root * inv_root * inv_root) * slope


BRANCH_LOADS = (
    "residual", "normed_grad", "gains", "loss", "upstream", "out_up", "low_o", "head",
)


def branch_kernel(place_ref, length_ref, index_ref, shares, *refs):
    count = len(BRANCH_LOADS)
    branch_grad_ref, head_grad_ref, part_ref = refs[count : count + 3]
    load_sem, w_out_s, sem = refs[2 * count + 3 :]
    loads = Loads(BRANCH_LOADS, refs[:count], refs[count + 3 : 2 * count + 3], load_sem)
    n_exp, n_tp, out_rows, _ = shares.shape
    copies = []
    for z in range(n_tp):
        for e in range(n_exp):
            target = w_out_s.at[z, e * out_rows : (e + 1) * out_rows, :]
            source = shares.at[e, from_place(place_ref, z, n_tp)]
            copies.append(pltpu.make_async_copy(source, target, sem.at[len(copies)]))
    for copy in copies:
        copy.start()
    mask = adapter_mask(length_ref, index_ref, LIVE, LANES)
    residual, normed_grad = loads["residual"][...], loads["normed_grad"][...].astype(F32)
    through = norm_back(residual, loads["gains"][1:2, :], normed_grad)
    kept = column_of(loads["loss"], LIVE) > 0.0
    branch_grad_ref[...] = (
        through + jnp.where(kept, loads["upstream"][...].astype(F32), 0.0)
    ).astype(BF16)
    branch_grad = branch_grad_ref[...]
    low_o_grad = (dot_nt(branch_grad, loads["out_up"][...]) * mask).astype(BF16)
    low_o = unfold(loads["low_o"], length_ref, index_ref, LIVE)
    out_up_part = dot_tn(low_o, branch_grad).astype(BF16)
    for at in range(D // LANES):
        lanes = slice(at * LANES, (at + 1) * LANES)
        part_ref[lanes, :] = out_up_part[:, lanes]
    part_ref[D:, :] = dot_tn(loads["head"][...], low_o_grad).astype(BF16)
    for z in range(n_tp):
        for copy in copies[z * n_exp : (z + 1) * n_exp]:
            copy.wait()
        head_grad_ref[z] = (
            dot_nt(branch_grad, w_out_s[z, :, :D]) + dot_nt(low_o_grad, w_out_s[z, :, D:])
        ).astype(BF16)


def branch_back(
    place, lengths, index, residual, low_o, normed_grad, upstream, loss_mask, gains, out_up, head, shares
):
    heads_wide = head.shape[1]
    n_exp, n_tp, _, _ = shares.shape
    arrays = (residual, normed_grad, gains, loss_mask, upstream, out_up, low_o, head)
    return pl.pallas_call(
        branch_kernel,
        in_specs=[IN_SMEM] * 3 + [IN_HBM] * (1 + len(arrays)),
        out_specs=[IN_VMEM] * 3,
        out_shape=[
            shape((LIVE, D), BF16),
            shape((n_tp, LIVE, heads_wide), BF16),
            shape((D + heads_wide, LANES), BF16),
        ],
        scratch_shapes=load_scratch(arrays, LIVE)
        + [
            pltpu.VMEM((n_tp, heads_wide, D + LANES), BF16),
            pltpu.SemaphoreType.DMA((n_tp * n_exp,)),
        ],
        compiler_params=WHOLE_VMEM,
        cost_estimate=cost(1e9, 2e6),
        name="branch_backward",
    )(place, lengths, index, shares, *arrays)


def share_copies(place_ref, shares, w_qkv_s, sem):
    n_exp, n_tp, _, _ = shares.shape
    qkv_rows, up_rows, _ = share_rows(n_exp, 0)
    copies = []
    for z in range(n_tp):
        here = []
        source_z = from_place(place_ref, z, n_tp)
        for e in range(n_exp):
            at = e * qkv_rows
            up_at = D + e * up_rows
            for source, target in (
                (shares.at[e, source_z, :qkv_rows, :], w_qkv_s.at[z, at : at + qkv_rows, :]),
                (shares.at[e, source_z, qkv_rows:, :], w_qkv_s.at[z, up_at : up_at + up_rows, :]),
            ):
                number = 2 * e + len(here) % 2
                here.append(pltpu.make_async_copy(source, target, sem.at[z, number]))
        copies.append(here)
    for here in copies:
        for copy in here:
            copy.start()
    return copies


PREPARE_LOADS = ("attn_in", "low_q", "cosine", "sine")


def prepare_kernel(place_ref, length_ref, shares, *refs):
    count = len(PREPARE_LOADS)
    results = 1 + len(LIVE_BLOCKS)
    turned_ref = refs[count]
    prob_refs = refs[count + 1 : count + results]
    load_sem, w_qkv_s, q_s, k_s, v_s, sem = refs[2 * count + results :]
    targets = refs[count + results : 2 * count + results]
    loads = Loads(PREPARE_LOADS, refs[:count], targets, load_sem)
    n_tp = shares.shape[1]
    groups = k_s.shape[0]
    copies = share_copies(place_ref, shares, w_qkv_s, sem)
    first = first_keys(length_ref, LIVE)
    attn_in = loads["attn_in"][...]
    low_q = loads["low_q"][...]
    cosine, sine = loads["cosine"][...], loads["sine"][...]
    seen = [seen_block(first, begin, end) for begin, end in LIVE_BLOCKS]
    for here in copies:
        for copy in here:
            copy.wait()

    def one_place(z, carried):
        projected = dot(attn_in, w_qkv_s[z, :D, :]) + dot(low_q, w_qkv_s[z, D:, :])
        columns = turn(projected, cosine, sine, turned_pieces(groups))
        for at, column in enumerate(columns):
            turned_ref[z, :, at * LANES : (at + 1) * LANES] = column.astype(BF16)
        store_heads(columns, 0, LIVE_BLOCKS, q_s, k_s, v_s)
        for group in range(groups):
            for block, (begin, end) in enumerate(LIVE_BLOCKS):
                query = q_s[group, block, : PER * (end - begin), :]
                scores = dot_nt(query, k_s[group, :end, :])
                prob_refs[block][z * groups + group] = softmax_block(scores, seen[block])
        return carried

    lax.fori_loop(0, n_tp, one_place, 0)


def prepare(place, lengths, attn_in, low_q, tables, shares):
    n_exp, n_tp, _, wide = shares.shape
    arrays = (attn_in, low_q) + tables
    groups = KV_HEADS
    probs = [
        shape((groups, PER * (end - begin), end), BF16) for begin, end in LIVE_BLOCKS
    ]
    return pl.pallas_call(
        prepare_kernel,
        in_specs=[IN_SMEM] * 2 + [IN_HBM] * (1 + len(arrays)),
        out_specs=[IN_VMEM] * (1 + len(probs)),
        out_shape=[shape((n_tp, LIVE, wide), BF16)] + probs,
        scratch_shapes=load_scratch(arrays, LIVE)
        + [
            pltpu.VMEM((n_tp, D + LANES, wide), BF16),
            pltpu.VMEM((groups // n_tp, len(LIVE_BLOCKS), PER * ROWS, HD), BF16),
            pltpu.VMEM((groups // n_tp, LIVE, HD), BF16),
            pltpu.VMEM((groups // n_tp, LIVE, HD), BF16),
            pltpu.SemaphoreType.DMA((n_tp, 2 * n_exp)),
        ],
        compiler_params=WHOLE_VMEM,
        cost_estimate=cost(12e9, 30e6),
        name="prepare_heads",
    )(place, lengths, shares, *arrays)


HEADS_LOADS = (
    "head_grad", "turned", "cosine", "sine", "low_q", "attn_in",
)


def heads_back_kernel(place_ref, length_ref, index_ref, shares, *refs):
    count = len(HEADS_LOADS)
    blocks = len(LIVE_BLOCKS)
    probs_hbm = refs[count : count + blocks]
    grad_ref, low_grad_ref, part_ref = refs[count + blocks : count + blocks + 3]
    scratch = refs[count + blocks + 3 :]
    loads = Loads(HEADS_LOADS, refs[:count], scratch[:count], scratch[count])
    up_s, g_s, q_s, k_s, v_s, up_sem, prob_sem = scratch[count + 1 : count + 8]
    probs_s = scratch[count + 8 :]
    n_exp, n_tp, _, wide = shares.shape
    groups = g_s.shape[0]
    flags = turned_pieces(groups)
    scale = 1.0 / math.sqrt(HD)

    def prob_copy(z, block):
        here = pl.ds(z * groups, groups)
        return pltpu.make_async_copy(
            probs_hbm[block].at[here], probs_s[block].at[here], prob_sem.at[z, block]
        )

    for z in range(n_tp):
        for block in range(blocks):
            prob_copy(z, block).start()
    qkv_rows, up_rows, _ = share_rows(n_exp, 0)
    up_copies = []
    for z in range(n_tp):
        for e in range(n_exp):
            source = shares.at[e, from_place(place_ref, z, n_tp), qkv_rows:, :]
            target = up_s.at[z, e * up_rows : (e + 1) * up_rows, :]
            up_copies.append(pltpu.make_async_copy(source, target, up_sem.at[z, e]))
            up_copies[-1].start()
    head_grad, turned = loads["head_grad"], loads["turned"]
    cosine, sine = loads["cosine"], loads["sine"]

    def one_place(z, carried):
        columns = [
            turned[z, :, at * LANES : (at + 1) * LANES].astype(F32) for at in range(wide // LANES)
        ]
        store_heads(columns, 0, LIVE_BLOCKS, q_s, k_s, v_s)
        for head in range(groups * PER):
            group, kind = divmod(head, PER)
            part = head_grad[z, :, head * HD : (head + 1) * HD]
            for block, (begin, end) in enumerate(LIVE_BLOCKS):
                size = end - begin
                here = slice(kind * size, (kind + 1) * size)
                g_s[group, block, here, :] = part[begin:end]
        for block in range(blocks):
            prob_copy(z, block).wait()
        key_grads = [jnp.zeros((HD, LIVE), F32) for _ in range(groups)]
        value_grads = [jnp.zeros((HD, LIVE), F32) for _ in range(groups)]
        query_grads = [[] for _ in range(groups)]
        for block, (begin, end) in enumerate(LIVE_BLOCKS):
            size = end - begin

            def widen(part):
                if end == LIVE:
                    return part
                return jnp.concatenate([part, jnp.zeros((HD, LIVE - end), F32)], axis=1)

            some = range(groups)
            queries = [q_s[group, block, : PER * size, :] for group in some]
            head_grads = [g_s[group, block, : PER * size, :] for group in some]
            probs = [probs_s[block][z * groups + group] for group in some]
            weight_grads = [dot_nt(head_grads[group], v_s[group, :end, :]) for group in some]
            for group in some:
                value_grads[group] += widen(dot_tn(head_grads[group], probs[group]))
            wide_probs = [probs[group].astype(F32) for group in some]
            score_grads = []
            for group in some:
                product = wide_probs[group] * weight_grads[group]
                spread = jnp.sum(product, axis=1, keepdims=True)
                score_grads.append((product - wide_probs[group] * spread).astype(BF16))
            for group in some:
                score_grad = score_grads[group]
                query_grads[group].append(dot(score_grad, k_s[group, :end, :]) * scale)
                key_grads[group] += widen(dot_tn(queries[group], score_grad))
        pieces = []
        for group in range(groups):
            for head in range(PER):
                rows = [
                    part[head * (end - begin) : (head + 1) * (end - begin)]
                    for part, (begin, end) in zip(query_grads[group], LIVE_BLOCKS)
                ]
                pieces.append(jnp.concatenate(rows, axis=0))
            pieces += [key_grads[group].T, value_grads[group].T]
        joined = jnp.concatenate(pieces, axis=1)
        columns = turn(joined, cosine[...], -sine[...], flags)
        for at, column in enumerate(columns):
            grad_ref[z, :, at * LANES : (at + 1) * LANES] = column.astype(BF16)
        return carried

    lax.fori_loop(0, n_tp, one_place, 0)
    for copy in up_copies:
        copy.wait()
    low_grad = dot_nt(grad_ref[0], up_s[0])
    for z in range(1, n_tp):
        low_grad += dot_nt(grad_ref[z], up_s[z])
    mask = adapter_mask(length_ref, index_ref, LIVE, LANES)
    low_grad = (low_grad * mask).astype(BF16)
    low_grad_ref[...] = low_grad
    part_ref[:D, :] = dot_tn(loads["attn_in"][...], low_grad).astype(BF16)
    up_part = dot_tn(loads["low_q"][...], grad_ref[place_ref[0]]).astype(BF16)
    for at in range(wide // LANES):
        lanes = slice(at * LANES, (at + 1) * LANES)
        part_ref[D + at * LANES : D + (at + 1) * LANES, :] = up_part[:, lanes]


def heads_back(place, lengths, index, attn_in, low_q, heads, head_grad, tables, shares):
    n_exp, n_tp, _, wide = shares.shape
    blocks = len(LIVE_BLOCKS)
    turned, probs = heads[0], heads[1:]
    groups = KV_HEADS // n_tp
    arrays = (head_grad, turned) + tables + (low_q, attn_in)
    return pl.pallas_call(
        heads_back_kernel,
        in_specs=[IN_SMEM] * 3 + [IN_HBM] * (1 + len(arrays) + blocks),
        out_specs=[IN_VMEM] * 3,
        out_shape=[
            shape((n_tp, LIVE, wide), BF16),
            shape((LIVE, LANES), BF16),
            shape((D + wide, LANES), BF16),
        ],
        scratch_shapes=load_scratch(arrays, LIVE)
        + [
            pltpu.VMEM((n_tp, LANES, wide), BF16),
            pltpu.VMEM((groups, blocks, PER * ROWS, HD), BF16),
            pltpu.VMEM((groups, blocks, PER * ROWS, HD), BF16),
            pltpu.VMEM((groups, LIVE, HD), BF16),
            pltpu.VMEM((groups, LIVE, HD), BF16),
            pltpu.SemaphoreType.DMA((n_tp, n_exp)),
            pltpu.SemaphoreType.DMA((n_tp, blocks)),
        ]
        + [pltpu.VMEM(part.shape, BF16) for part in probs],
        compiler_params=WHOLE_VMEM,
        cost_estimate=cost(2e9, 3e6),
        name="heads_backward",
    )(place, lengths, index, shares, *arrays, *probs)


INPUT_LOADS = ("grads", "low_grad", "qkv_down", "tokens", "gains", "branch_grad")


def input_back_kernel(place_ref, shares, *refs):
    count = len(INPUT_LOADS)
    input_grad_ref = refs[count]
    load_sem, w_qkv_s, sum_s, sem = refs[2 * count + 1 :]
    n_exp, n_tp, _, _ = shares.shape
    qkv_rows, _, _ = share_rows(n_exp, 0)
    copies = []
    for z in range(n_tp):
        for e in range(n_exp):
            source = shares.at[e, from_place(place_ref, z, n_tp), :qkv_rows, :]
            target = w_qkv_s.at[z, e * qkv_rows : (e + 1) * qkv_rows, :]
            copies.append(pltpu.make_async_copy(source, target, sem.at[z, e]))
    loads = Loads(INPUT_LOADS, refs[:count], refs[count + 1 : 2 * count + 1], load_sem)
    for copy in copies:
        copy.start()
    input_grad_ref[LIVE:, :] = jnp.zeros((input_grad_ref.shape[0] - LIVE, D), BF16)
    grads = loads["grads"]
    sum_s[...] = dot_nt(loads["low_grad"][...], loads["qkv_down"][...])
    for z in range(n_tp):
        for copy in copies[z * n_exp : (z + 1) * n_exp]:
            copy.wait()
        sum_s[...] += dot_nt(grads[z], w_qkv_s[z])
    tokens, gain = loads["tokens"][...].astype(F32), loads["gains"][0:1, :]
    through = norm_back(tokens, gain, sum_s[...])
    input_grad_ref[:LIVE, :] = (loads["branch_grad"][...].astype(F32) + through).astype(BF16)


def input_back(place, grads, low_grad, qkv_down, tokens, gains, branch_grad, shares):
    n_exp, n_tp, _, wide = shares.shape
    arrays = (grads, low_grad, qkv_down, tokens, gains, branch_grad)
    return pl.pallas_call(
        input_back_kernel,
        in_specs=[IN_SMEM] + [IN_HBM] * (1 + len(arrays)),
        out_specs=IN_VMEM,
        out_shape=shape(tokens.shape, BF16),
        scratch_shapes=load_scratch(arrays, LIVE)
        + [
            pltpu.VMEM((n_tp, D, wide), BF16),
            pltpu.VMEM((LIVE, D), F32),
            pltpu.SemaphoreType.DMA((n_tp, n_exp)),
        ],
        compiler_params=WHOLE_VMEM,
        cost_estimate=cost(2e9, 2e6),
        name="input_backward",
    )(place, shares, *arrays)


FINISH_LOADS = ("out_parts", "residual", "moe_out", "qkv_sum")


def finish_kernel(*refs):
    count = len(FINISH_LOADS)
    output_ref, qkv_down_ref, qkv_up_ref, out_down_ref, out_up_ref = refs[count : count + 5]
    scratch = refs[count + 5 :]
    loads = Loads(FINISH_LOADS, refs[:count], scratch[:count], scratch[count])
    qkv_sum = loads["qkv_sum"]
    qkv_down_ref[...] = qkv_sum[:D, :].astype(F32)
    for at in range(0, qkv_up_ref.shape[1], LANES):
        qkv_up_ref[:, at : at + LANES] = qkv_sum[D + at : D + at + LANES, :].astype(F32)
    output_ref[...] = (loads["residual"][...] + loads["moe_out"][...].astype(F32)).astype(BF16)
    out_parts = loads["out_parts"]
    for at in range(0, out_parts.shape[1], LANES):
        total = out_parts[0, at : at + LANES, :].astype(F32)
        for part in range(1, out_parts.shape[0]):
            total += out_parts[part, at : at + LANES, :].astype(F32)
        if at < D:
            out_up_ref[:, at : at + LANES] = total
        else:
            out_down_ref[at - D : at - D + LANES, :] = total


def finish(residual, moe_out, out_parts, qkv_sum):
    arrays = (out_parts, residual, moe_out, qkv_sum)
    return pl.pallas_call(
        finish_kernel,
        in_specs=[IN_HBM] * len(arrays),
        out_specs=[IN_VMEM] * 5,
        out_shape=[
            shape(residual.shape, BF16),
            shape((D, LANES), F32),
            shape((LANES, qkv_sum.shape[0] - D), F32),
            shape((out_parts.shape[1] - D, LANES), F32),
            shape((LANES, D), F32),
        ],
        scratch_shapes=load_scratch(arrays),
        compiler_params=WHOLE_VMEM,
        cost_estimate=cost(0, 14e6),
        name="finish",
    )(*arrays)


def from_tp(share, count):
    around = [share]
    for shift in range(1, count):
        around.append(
            lax.ppermute(share, "tp", [(at, (at + shift) % count) for at in range(count)])
        )
    return around


def from_place(place_ref, z, count):
    return lax.rem(place_ref[0] - z + count, count)


def kernel_body(
    tokens, attn_gain, moe_gain, w_qkv, w_out, w_router, w_gate, w_up, w_down, qkv_down, qkv_up,
    out_down, out_up, lengths, adapter_index, loss_mask, routes, upstream,
):
    n_exp = lax.axis_size("exp")
    n_tp = lax.axis_size("tp")
    exp_place = lax.axis_index("exp").astype(jnp.int32).reshape(1)
    tp_place = lax.axis_index("tp").astype(jnp.int32).reshape(1)
    tables = turn_tables(tokens.shape[0])
    gains = jnp.stack([attn_gain, moe_gain])
    loss_row = loss_mask.reshape(1, -1)
    wide = w_qkv.shape[1]
    heads_wide = w_out.shape[0]

    own_experts = pack_experts(w_gate, w_up, w_down)
    weights = lax.all_gather(own_experts, "exp", axis=0, tiled=True)
    own_qkv = pack_share(
        pack_qkv_kernel, "pack_qkv", exp_place, w_qkv, qkv_up, (D + LANES) // n_exp, wide, n_exp
    )
    own_qkv, _ = lax.optimization_barrier((own_qkv, own_experts))
    z_qkv = from_tp(own_qkv, n_tp)
    inputs, _ = lax.optimization_barrier((tokens, own_qkv))
    attn_in, low_q, head, base = forward(
        lengths, adapter_index, inputs, gains, w_qkv, qkv_down, qkv_up, w_out, out_down, tables
    )
    base, z_qkv = lax.optimization_barrier((base, z_qkv))
    z_qkv = jnp.stack(z_qkv)
    base = lax.psum(base, "tp")
    own_out = pack_share(
        pack_out_kernel, "pack_out", exp_place, w_out, out_down, heads_wide // n_exp, D + LANES,
        n_exp,
    )
    own_out, _, _ = lax.optimization_barrier((own_out, base, head))
    z_out = from_tp(own_out, n_tp)
    z_qkv, _ = lax.optimization_barrier((z_qkv, weights))
    qkv_shares = lax.all_gather(z_qkv, "exp", axis=0)

    residual, hidden, normed_part = experts_both(
        lengths, adapter_index, tokens, base, out_up, gains, w_router, routes, upstream, loss_row,
        weights,
    )
    normed_part, z_out = lax.optimization_barrier((normed_part, z_out))
    z_out = jnp.stack(z_out)
    normed_grad = lax.psum(normed_part, "tp")
    z_out, _ = lax.optimization_barrier((z_out, qkv_shares))
    out_shares = lax.all_gather(z_out, "exp", axis=0)
    late_in, _ = lax.optimization_barrier((attn_in, normed_part))
    heads = prepare(tp_place, lengths, late_in, low_q, tables, qkv_shares)

    moe_part, normed_grad, _ = lax.optimization_barrier(
        (combine(hidden, weights), normed_grad, heads[0])
    )
    moe_out = lax.psum(moe_part, "tp")
    normed_grad, _ = lax.optimization_barrier((normed_grad, out_shares))
    branch_grad, head_grad, out_part = branch_back(
        tp_place, lengths, adapter_index, residual, base[-RANK:], normed_grad, upstream, loss_row,
        gains, out_up, head, out_shares,
    )
    out_parts = lax.all_gather(out_part, "exp", axis=0)
    grads, low_grad, qkv_part = heads_back(
        tp_place, lengths, adapter_index, attn_in, low_q, heads, head_grad, tables, qkv_shares
    )
    share = qkv_part.shape[0] // n_exp
    parts = lax.all_to_all(qkv_part.reshape(n_exp, share, LANES), "exp", 0, 0, tiled=True)
    input_grad = input_back(
        tp_place, grads, low_grad, qkv_down, tokens, gains, branch_grad, qkv_shares
    )
    parts, input_grad = lax.optimization_barrier((parts, input_grad))
    qkv_sum = jnp.sum(parts.astype(F32), axis=0).astype(BF16)
    spread = jnp.broadcast_to(qkv_sum[None], (n_exp, share, LANES))
    qkv_sum = lax.all_to_all(spread, "exp", 0, 0, tiled=True)
    out_parts, moe_out, _ = lax.optimization_barrier((out_parts, moe_out, spread))
    output, grad_qkv_down, grad_qkv_up, grad_out_down, grad_out_up = finish(
        residual, moe_out, out_parts, qkv_sum.reshape(-1, LANES)
    )
    return (output, input_grad, grad_qkv_down, grad_qkv_up, grad_out_down, grad_out_up)


def product(left_m, right_m):
    return jnp.dot(left_m, right_m, preferred_element_type=jnp.float32)


def contract(einsum_form, left_m, right_m):
    return jnp.einsum(einsum_form, left_m, right_m, preferred_element_type=jnp.float32)


def rms_norm(vectors, gain_vec):
    inv_root = lax.rsqrt(jnp.mean(vectors * vectors, axis=-1, keepdims=True) + EPS)
    return vectors * inv_root * gain_vec


def rms_norm_back(vectors, gain_vec, upstream_grad):
    inv_root = lax.rsqrt(jnp.mean(vectors * vectors, axis=-1, keepdims=True) + EPS)
    weighted = upstream_grad * gain_vec
    return inv_root * weighted - vectors * (inv_root * inv_root * inv_root) * jnp.mean(
        vectors * weighted, axis=-1, keepdims=True
    )


def layout(length_row, index_row):
    places = jnp.arange(TOK_DEV, dtype=jnp.int32)
    doc_ends = jnp.cumsum(length_row)
    doc_starts = doc_ends - length_row
    member = (places[:, None] >= doc_starts[None, :]) & (places[:, None] < doc_ends[None, :])
    occupied = jnp.any(member, axis=1)
    position = jnp.sum(jnp.where(member, places[:, None] - doc_starts[None, :], 0), axis=1)
    owner_doc = jnp.sum(jnp.where(member, jnp.arange(DOCS, dtype=jnp.int32)[None, :], 0), axis=1)
    doc_ident = jnp.where(occupied, owner_doc, DOCS + places)
    chosen = jnp.sum(jnp.where(member, index_row[None, :], 0), axis=1)
    adapter_pick = occupied[:, None] & (
        chosen[:, None] == jnp.arange(ADAPTERS, dtype=jnp.int32)[None, :]
    )
    rank_mask = jnp.repeat(jnp.where(adapter_pick, 1.0, 0.0).astype(jnp.float32), RANK, axis=1)
    return (occupied, position, doc_ident, rank_mask)


def angles(position):
    half_width = HD // 2
    frequency = jnp.exp(-math.log(ROPE_BASE) * jnp.arange(half_width, dtype=jnp.float32) * 2.0 / HD)
    turned = position.astype(jnp.float32)[:, None] * frequency[None, :]
    return (jnp.cos(turned), jnp.sin(turned))


def rotate(vectors, cosine, sine_table):
    half_width = vectors.shape[-1] // 2
    front_half = vectors[..., :half_width]
    back_half = vectors[..., half_width:]
    return jnp.concatenate(
        [
            front_half * cosine - back_half * sine_table,
            back_half * cosine + front_half * sine_table,
        ],
        axis=-1,
    )


def moe(normed, cot_low, gates, gate_up, down):
    width = down.shape[1]
    both = contract("td,edf->tef", normed, gate_up)
    pre_gate = both[:, :, :width]
    pre_up = both[:, :, width:]
    sigmoid_g = jax.nn.sigmoid(pre_gate)
    activated = pre_gate * sigmoid_g
    hidden = (activated * pre_up).astype(jnp.bfloat16).astype(jnp.float32)
    inner_raw = contract("td,efd->tef", cot_low, down)
    gate_part = jnp.sum(hidden * inner_raw, axis=-1)
    moe_part = contract("tef,efd->td", (gates[:, :, None] * hidden).astype(jnp.bfloat16), down)
    inner_grad = inner_raw * gates[:, :, None]
    grad_gate = inner_grad * pre_up * sigmoid_g * (1.0 + pre_gate * (1.0 - sigmoid_g))
    grad_up = inner_grad * activated
    grad_both = jnp.concatenate([grad_gate, grad_up], axis=2).astype(jnp.bfloat16)
    normed_part = contract("tef,edf->td", grad_both, gate_up)
    return (moe_part, gate_part, normed_part)


def body(
    tokens,
    attn_gain,
    moe_gain,
    w_qkv,
    w_out,
    w_router,
    w_gate,
    w_up,
    w_down,
    qkv_down,
    qkv_up,
    out_down,
    out_up,
    lengths,
    adapter_index,
    loss_mask,
    routes,
    upstream,
):
    n_exp = lax.axis_size("exp")
    groups = KV_HEADS // lax.axis_size("tp")
    per_group = HEADS // KV_HEADS
    experts = EXP_DEV * n_exp
    gate_up = lax.all_gather(jnp.concatenate([w_gate, w_up], axis=2), "exp", axis=0, tiled=True)
    down = lax.all_gather(w_down, "exp", axis=0, tiled=True)
    block_rows = min(512, TOK_DEV)
    blocks = TOK_DEV // block_rows
    score_scale = 1.0 / math.sqrt(HD)
    places = jnp.arange(TOK_DEV, dtype=jnp.int32)
    occupied, position, doc_ident, rank_mask = layout(lengths[0], adapter_index[0])
    mask_low = rank_mask.astype(jnp.bfloat16)
    cosine, sine_table = angles(position)
    inputs = tokens.astype(jnp.float32)
    attn_in = rms_norm(inputs, attn_gain).astype(jnp.bfloat16)
    low_q = (product(attn_in, qkv_down) * rank_mask).astype(jnp.bfloat16)
    projected = (product(attn_in, w_qkv) + product(low_q, qkv_up)).reshape(
        TOK_DEV, groups, per_group + 2, HD
    )
    query_rows = rotate(
        projected[:, :, :per_group], cosine[:, None, None], sine_table[:, None, None]
    ).astype(jnp.bfloat16)
    key_rows = rotate(projected[:, :, per_group], cosine[:, None], sine_table[:, None]).astype(
        jnp.bfloat16
    )
    val_rows = projected[:, :, per_group + 1].astype(jnp.bfloat16)

    def masked_scores(q_blk, q_place, q_ident):
        scores = contract("qgrd,kgd->grqk", q_blk, key_rows) * score_scale
        allowed = (q_ident[:, None] == doc_ident[None, :]) & (places[None, :] <= q_place[:, None])
        return jnp.where(allowed, scores, -1e30)

    def attend(pieces):
        q_blk, q_place, q_ident = pieces
        scores = masked_scores(q_blk, q_place, q_ident)
        row_max = jnp.max(scores, axis=-1, keepdims=True)
        lifted = jnp.exp(scores - row_max)
        row_total = jnp.sum(lifted, axis=-1, keepdims=True)
        weights = (lifted / row_total).astype(jnp.bfloat16)
        return (
            contract("grqk,kgd->qgrd", weights, val_rows),
            row_max[..., 0] + jnp.log(row_total[..., 0]),
        )

    query_blocks = query_rows.reshape(blocks, block_rows, groups, per_group, HD)
    place_blocks = places.reshape(blocks, block_rows)
    ident_blocks = doc_ident.reshape(blocks, block_rows)
    attended, log_totals = lax.map(attend, (query_blocks, place_blocks, ident_blocks))
    head_rows = attended.reshape(TOK_DEV, groups * per_group * HD).astype(jnp.bfloat16)
    attn_base, low_rank = (
        lax.psum(product(head_rows, w_out).astype(jnp.bfloat16), "tp").astype(jnp.float32),
        lax.psum((product(head_rows, out_down) * rank_mask).astype(jnp.bfloat16), "tp").astype(
            jnp.float32
        ),
    )
    low_o = low_rank.astype(jnp.bfloat16)
    residual = inputs + attn_base + product(low_o, out_up)
    normed = rms_norm(residual, moe_gain).astype(jnp.bfloat16)
    logits = product(normed, w_router)
    one_hot = routes[:, :, None] == jnp.arange(experts, dtype=jnp.int32)[None, None, :]
    routed = jnp.any(one_hot, axis=1)
    gates = jax.nn.softmax(jnp.where(routed, logits, -1e30), axis=-1)
    live_mask = jnp.where(occupied & (loss_mask > 0), 1.0, 0.0).astype(jnp.float32)
    cotangent = upstream.astype(jnp.float32) * live_mask[:, None]
    cot_low = cotangent.astype(jnp.bfloat16)
    moe_part, gate_part, normed_part = moe(normed, cot_low, gates, gate_up, down)
    logit_grad = (
        gates * (gate_part - jnp.sum(gates * gate_part, axis=-1, keepdims=True))
    ).astype(jnp.bfloat16)
    normed_part = (normed_part + product(logit_grad, w_router.T)).astype(jnp.bfloat16)
    normed_sum = lax.psum(normed_part, "tp")
    normed_sum, moe_part = lax.optimization_barrier((normed_sum, moe_part.astype(jnp.bfloat16)))
    normed_grad = normed_sum.astype(jnp.float32)
    moe_out = lax.psum(moe_part, "tp").astype(jnp.float32)
    output = (residual + moe_out).astype(jnp.bfloat16)
    residual_grad = cotangent + rms_norm_back(residual, moe_gain, normed_grad)
    branch_grad = residual_grad.astype(jnp.bfloat16)
    low_o_grad = product(branch_grad, out_up.T).astype(jnp.bfloat16) * mask_low
    out_up_part = contract("tr,td->rd", low_o, branch_grad)
    head_grad = (product(branch_grad, w_out.T) + product(low_o_grad, out_down.T)).astype(
        jnp.bfloat16
    )
    out_down_part = contract("tc,tr->cr", head_rows, low_o_grad)
    grad_blocks = head_grad.reshape(blocks, block_rows, groups, per_group, HD)

    def attend_back(carried, pieces):
        key_acc, val_acc = carried
        q_blk, q_place, q_ident, lse_blk, g_blk = pieces
        weights = jnp.exp(masked_scores(q_blk, q_place, q_ident) - lse_blk[..., None])
        weight_grad = contract("qgrd,kgd->grqk", g_blk, val_rows)
        score_grad = (
            weights * (weight_grad - jnp.sum(weights * weight_grad, axis=-1, keepdims=True))
        ).astype(jnp.bfloat16)
        query_grad = contract("grqk,kgd->qgrd", score_grad, key_rows) * score_scale
        key_acc = key_acc + contract("grqk,qgrd->kgd", score_grad, q_blk) * score_scale
        val_acc = val_acc + contract("grqk,qgrd->kgd", weights.astype(jnp.bfloat16), g_blk)
        return ((key_acc, val_acc), query_grad)

    zero_acc = jnp.zeros((TOK_DEV, groups, HD), jnp.float32)
    (key_grad, val_grad), query_grad = lax.scan(
        attend_back,
        (zero_acc, zero_acc),
        (query_blocks, place_blocks, ident_blocks, log_totals, grad_blocks),
    )
    query_grad = rotate(
        query_grad.reshape(TOK_DEV, groups, per_group, HD),
        cosine[:, None, None],
        -sine_table[:, None, None],
    )
    key_grad = rotate(key_grad, cosine[:, None], -sine_table[:, None])
    projected_grad = (
        jnp.concatenate([query_grad, key_grad[:, :, None], val_grad[:, :, None]], axis=2)
        .reshape(TOK_DEV, -1)
        .astype(jnp.bfloat16)
    )
    qkv_up_part = contract("tr,tc->rc", low_q, projected_grad)
    attn_grad, low_q_grad = (
        lax.psum(contract("tc,dc->td", projected_grad, w_qkv).astype(jnp.bfloat16), "tp").astype(
            jnp.float32
        ),
        lax.psum(contract("tc,rc->tr", projected_grad, qkv_up).astype(jnp.bfloat16), "tp").astype(
            jnp.float32
        ),
    )
    low_q_grad = low_q_grad.astype(jnp.bfloat16) * mask_low
    attn_grad = attn_grad + contract("tr,dr->td", low_q_grad, qkv_down)
    qkv_down_part = contract("td,tr->dr", attn_in, low_q_grad)
    input_grad = (residual_grad + rms_norm_back(inputs, attn_gain, attn_grad)).astype(jnp.bfloat16)
    summed = (
        lax.psum(qkv_down_part.astype(jnp.bfloat16), "exp").astype(jnp.float32),
        lax.psum(qkv_up_part.astype(jnp.bfloat16), "exp").astype(jnp.float32),
        lax.psum(out_down_part.astype(jnp.bfloat16), "exp").astype(jnp.float32),
        lax.psum(out_up_part.astype(jnp.bfloat16), "exp").astype(jnp.float32),
    )
    return (output, input_grad, summed[0], summed[1], summed[2], summed[3])


def kernels_fit(mesh):
    n_exp, n_tp = mesh.shape["exp"], mesh.shape["tp"]
    groups = KV_HEADS // n_tp
    return groups % 2 == 0 and FF // n_tp == LANES and LANES // n_exp % 16 == 0


def solution(mesh):
    placed = (
        P("exp", None),
        P(),
        P(),
        P(None, "tp"),
        P("tp", None),
        P(),
        P("exp", None, "tp"),
        P("exp", None, "tp"),
        P("exp", "tp", None),
        P(),
        P(None, "tp"),
        P("tp", None),
        P(),
        P("exp", None),
        P("exp", None),
        P("exp"),
        P("exp", None),
        P("exp", None),
    )
    return jax.shard_map(
        kernel_body if kernels_fit(mesh) else body,
        mesh=mesh,
        in_specs=placed,
        out_specs=(P("exp", None), P("exp", None), P(), P(None, "tp"), P("tp", None), P()),
        check_vma=False,
    )
```

```python
import functools
import math

import jax
import jax.numpy as jnp
import numpy as np
from jax import lax
from jax.experimental import pallas as pl
from jax.experimental.pallas import tpu as pltpu
from jax.sharding import PartitionSpec as P

D = 1536
HEADS = 24
KV_HEADS = 8
HD = 64
TOP = 8
RANK = 16
ADAPTERS = 8
EXP_DEV = 2
DOCS = 4
TOK_DEV = 512
LIVE = 448
FF = 512
EPS = 1e-06
ROPE_BASE = 10000.0

PER = HEADS // KV_HEADS
LANES = 128
ROWS = 128
BLOCKS = tuple((at, min(at + ROWS, TOK_DEV)) for at in range(0, TOK_DEV, ROWS))
LIVE_BLOCKS = tuple((at, min(at + ROWS, LIVE)) for at in range(0, LIVE, ROWS))
F32 = jnp.float32
BF16 = jnp.bfloat16
MIB = 2**20
NT = (((1,), (1,)), ((), ()))
TN = (((0,), (0,)), ((), ()))
WHOLE_VMEM = pltpu.CompilerParams(vmem_limit_bytes=63 * MIB)
IN_VMEM = pl.BlockSpec(memory_space=pltpu.VMEM)
IN_SMEM = pl.BlockSpec(memory_space=pltpu.SMEM)
IN_HBM = pl.BlockSpec(memory_space=pltpu.HBM)


def dot(left, right):
    return jnp.dot(left, right, preferred_element_type=F32)


def dot_nt(left, right):
    return lax.dot_general(left, right, NT, preferred_element_type=F32)


def dot_tn(left, right):
    return lax.dot_general(left, right, TN, preferred_element_type=F32)


def cost(flops, moved):
    return pl.CostEstimate(flops=int(flops), bytes_accessed=int(moved), transcendentals=0)


def shape(dims, dtype):
    return jax.ShapeDtypeStruct(dims, dtype)


def turn_tables(rows):
    half = HD // 2
    frequency = np.exp(-math.log(ROPE_BASE) * np.arange(half, dtype=np.float64) * 2.0 / HD)
    turned = np.arange(rows, dtype=np.float64)[:, None] * frequency[None, :]
    cosine, sine = np.cos(turned), np.sin(turned)
    return (
        jnp.asarray(np.concatenate([cosine] * 4, axis=1), F32),
        jnp.asarray(np.concatenate([-sine, sine, -sine, sine], axis=1), F32),
    )


def turned_pieces(groups):
    return [piece < PER + 1 for _ in range(groups) for piece in range(PER + 2)]


def turn(joined, cosine, sine, flags):
    lane = lax.broadcasted_iota(jnp.int32, cosine.shape, 1)
    front = (lane & 32) == 0
    left = lane < HD
    columns = []
    for at in range(joined.shape[1] // LANES):
        column = joined[:, at * LANES : (at + 1) * LANES]
        swapped = jnp.where(front, pltpu.roll(column, 96, 1), pltpu.roll(column, 32, 1))
        rotated = column * cosine + swapped * sine
        if not (flags[2 * at] and flags[2 * at + 1]):
            rotated = jnp.where(left if flags[2 * at] else jnp.logical_not(left), rotated, column)
        columns.append(rotated)
    return columns


def first_keys(length_ref, rows):
    row = lax.broadcasted_iota(jnp.int32, (rows, 1), 0)
    begin = jnp.zeros((rows, 1), jnp.int32)
    end = 0
    for doc in range(DOCS):
        if doc:
            begin = jnp.where(row >= end, end, begin)
        end = end + length_ref[0, doc]
    return jnp.where(row >= end, row, begin)


def adapter_mask(length_ref, index_ref, rows, width):
    row = lax.broadcasted_iota(jnp.int32, (rows, width), 0)
    adapter = lax.shift_right_logical(lax.broadcasted_iota(jnp.int32, (rows, width), 1), 4)
    mask = jnp.zeros((rows, width), F32)
    begin = 0
    for doc in range(DOCS):
        end = begin + length_ref[0, doc]
        inside = (row >= begin) & (row < end) & (adapter == index_ref[0, doc])
        mask = jnp.where(inside, 1.0, mask)
        begin = end
    return mask


def folding():
    rank = lax.broadcasted_iota(jnp.int32, (RANK, LANES), 0)
    lane = lax.broadcasted_iota(jnp.int32, (RANK, LANES), 1)
    return jnp.where((lane & (RANK - 1)) == rank, 1.0, 0.0).astype(BF16)


def unfold(low_ref, length_ref, index_ref, rows):
    spread = dot_tn(low_ref[-RANK:, :rows], folding())
    return (spread * adapter_mask(length_ref, index_ref, rows, LANES)).astype(BF16)


def seen_block(first, begin, end):
    row = lax.broadcasted_iota(jnp.int32, (end - begin, end), 0) + begin
    key = lax.broadcasted_iota(jnp.int32, (end - begin, end), 1)
    seen = (key <= row) & (key >= first[begin:end])
    return jnp.concatenate([seen] * PER, axis=0)


def softmax_block(scores, seen):
    scores = jnp.where(seen, scores, -1e30)
    lifted = jnp.exp(scores - jnp.max(scores, axis=1, keepdims=True))
    return (lifted * (1.0 / jnp.sum(lifted, axis=1, keepdims=True))).astype(BF16)


def column_of(row_ref, rows):
    row = row_ref[...].astype(F32)
    at = lax.broadcasted_iota(jnp.int32, (rows, row.shape[1]), 0)
    lane = lax.broadcasted_iota(jnp.int32, (rows, row.shape[1]), 1)
    return jnp.sum(jnp.where(at == lane, row, 0.0), axis=1, keepdims=True)


def store_heads(columns, slot, blocks, q_s, k_s, v_s):
    scale = 1.0 / math.sqrt(HD)
    for at, column in enumerate(columns):
        halves = (column[:, :HD], pltpu.roll(column, HD, 1)[:, :HD])
        for piece, part in zip((2 * at, 2 * at + 1), halves):
            group, kind = divmod(piece, PER + 2)
            if kind == PER:
                k_s[slot + group] = part.astype(BF16)
            elif kind == PER + 1:
                v_s[slot + group] = part.astype(BF16)
            else:
                part = (part * scale).astype(BF16)
                for block, (begin, end) in enumerate(blocks):
                    size = end - begin
                    here = slice(kind * size, (kind + 1) * size)
                    q_s[slot + group, block, here, :] = part[begin:end]


def run_copies(pairs, sem):
    copies = [
        pltpu.make_async_copy(source, target, sem.at[number])
        for number, (source, target) in enumerate(pairs)
    ]
    for copy in copies:
        copy.start()
    for copy in copies:
        copy.wait()


def pack_kernel(
    n_exp, place_ref, gate, up, down, w_qkv, qkv_up, packed, share, held, share_s, sem, out_sem
):
    width = gate.shape[2]
    pairs = []
    for expert in range(gate.shape[0]):
        pairs.append((gate.at[expert], held.at[expert, :, :width]))
        pairs.append((up.at[expert], held.at[expert, :, width : 2 * width]))
        for at in range(D // LANES):
            lanes = slice(at * LANES, (at + 1) * LANES)
            pairs.append((down.at[expert, :, lanes], held.at[expert, lanes, 2 * width :]))
    qkv_rows, up_rows, _ = share_rows(n_exp, 0)
    own_qkv = pl.ds(pl.multiple_of(place_ref[0] * qkv_rows, 16), qkv_rows)
    own_up = pl.ds(pl.multiple_of(place_ref[0] * up_rows, 16), up_rows)
    pairs.append((w_qkv.at[own_qkv, :], share_s.at[:qkv_rows, :]))
    pairs.append((qkv_up.at[own_up, :], share_s.at[qkv_rows:, :]))
    run_copies(pairs, sem)
    run_copies([(held, packed), (share_s, share)], out_sem)


def share_rows(n_exp, heads_wide):
    return (D // n_exp, LANES // n_exp, heads_wide // n_exp)


def pack(place, w_gate, w_up, w_down, w_qkv, qkv_up, n_exp):
    count, _, width = w_gate.shape
    packed = shape((count, D, 3 * width), BF16)
    share = shape(((D + LANES) // n_exp, w_qkv.shape[1]), BF16)
    return pl.pallas_call(
        functools.partial(pack_kernel, n_exp),
        in_specs=[IN_SMEM] + [IN_HBM] * 5,
        out_specs=[IN_HBM] * 2,
        out_shape=[packed, share],
        scratch_shapes=[
            pltpu.VMEM(packed.shape, BF16),
            pltpu.VMEM(share.shape, BF16),
            pltpu.SemaphoreType.DMA((count * (2 + D // LANES) + 2,)),
            pltpu.SemaphoreType.DMA((2,)),
        ],
        compiler_params=WHOLE_VMEM,
        cost_estimate=cost(0, 2 * 2 * count * D * 3 * width),
        name="pack_weights",
    )(place, w_gate, w_up, w_down, w_qkv, qkv_up)


class Loads:
    def __init__(self, names, sources, targets, sem):
        self.copies = {}
        for number, (name, source, target) in enumerate(zip(names, sources, targets)):
            if source.shape[0] == TOK_DEV + RANK:
                source = source.at[TOK_DEV:]
            elif source.shape != target.shape:
                source = source.at[: target.shape[0]]
            self.copies[name] = pltpu.make_async_copy(source, target, sem.at[number])
        self.targets = dict(zip(names, targets))
        for copy in self.copies.values():
            copy.start()

    def __getitem__(self, name):
        copy = self.copies.pop(name, None)
        if copy is not None:
            copy.wait()
        return self.targets[name]


def load_scratch(arrays, rows=TOK_DEV):
    kept = {TOK_DEV: rows, TOK_DEV + RANK: RANK}
    rooms = []
    for array in arrays:
        first = kept.get(array.shape[0], array.shape[0])
        rooms.append(pltpu.VMEM((first,) + array.shape[1:], array.dtype))
    return rooms + [pltpu.SemaphoreType.DMA((len(arrays),))]


FORWARD_LOADS = (
    "tokens", "gains", "qkv_down", "w_qkv", "qkv_up", "cosine", "sine", "w_out", "out_down",
)


def forward_kernel(place_ref, length_ref, index_ref, *refs):
    count = len(FORWARD_LOADS)
    attn_in_ref, low_q_ref, head_ref, base_ref, share_ref = refs[count : count + 5]
    load_sem, q_s, k_s, v_s = refs[2 * count + 5 :]
    loads = Loads(FORWARD_LOADS, refs[:count], refs[count + 5 : 2 * count + 5], load_sem)
    rows = attn_in_ref.shape[0]
    groups = k_s.shape[0]
    mask = adapter_mask(length_ref, index_ref, rows, LANES)
    first = first_keys(length_ref, rows)
    inputs = loads["tokens"][...].astype(F32)
    inv_root = lax.rsqrt(jnp.mean(inputs * inputs, axis=1, keepdims=True) + EPS)
    attn_in_ref[...] = (inputs * inv_root * loads["gains"][0:1, :]).astype(BF16)
    attn_in = attn_in_ref[...]
    low_q = (dot(attn_in, loads["qkv_down"][...]) * mask).astype(BF16)
    low_q_ref[...] = low_q
    projected = dot(attn_in, loads["w_qkv"][...]) + dot(low_q, loads["qkv_up"][...])
    cosine, sine = loads["cosine"][...], loads["sine"][...]
    columns = turn(projected, cosine, sine, turned_pieces(groups))
    store_heads(columns, 0, BLOCKS, q_s, k_s, v_s)
    for block, (begin, end) in enumerate(BLOCKS):
        seen = seen_block(first, begin, end)
        heads = []
        for group in range(groups):
            probs = softmax_block(dot_nt(q_s[group, block], k_s[group, :end, :]), seen)
            out = dot(probs, v_s[group, :end, :])
            heads += [out[head * ROWS : (head + 1) * ROWS] for head in range(PER)]
        head_ref[begin:end, :] = jnp.concatenate(heads, axis=1).astype(BF16)
    head_out = head_ref[...]
    base_ref[:rows, :] = dot(head_out, loads["w_out"][...]).astype(BF16)
    low_o = (dot(head_out, loads["out_down"][...]) * mask).astype(BF16)
    base_ref[rows:, :rows] = dot_nt(folding(), low_o).astype(BF16)
    base_ref[rows:, rows:] = jnp.zeros((RANK, D - rows), BF16)
    share_rows_count = share_ref.shape[0]
    own = pl.ds(pl.multiple_of(place_ref[0] * share_rows_count, 16), share_rows_count)
    share_ref[:, :D] = loads["w_out"][own, :]
    share_ref[:, D:] = loads["out_down"][own, :]


def forward(
    place, lengths, index, tokens, gains, w_qkv, qkv_down, qkv_up, w_out, out_down, tables, n_exp
):
    rows = tokens.shape[0]
    heads_wide = w_out.shape[0]
    groups = w_qkv.shape[1] // (HD * (PER + 2))
    arrays = (tokens, gains, qkv_down, w_qkv, qkv_up) + tables + (w_out, out_down)
    return pl.pallas_call(
        forward_kernel,
        in_specs=[IN_SMEM] * 3 + [IN_HBM] * len(arrays),
        out_specs=[IN_VMEM] * 5,
        out_shape=[
            shape((rows, D), BF16),
            shape((rows, LANES), BF16),
            shape((rows, heads_wide), BF16),
            shape((rows + RANK, D), BF16),
            shape((heads_wide // n_exp, D + LANES), BF16),
        ],
        scratch_shapes=load_scratch(arrays)
        + [
            pltpu.VMEM((groups, rows // ROWS, PER * ROWS, HD), BF16),
            pltpu.VMEM((groups, rows, HD), BF16),
            pltpu.VMEM((groups, rows, HD), BF16),
        ],
        compiler_params=WHOLE_VMEM,
        cost_estimate=cost(6e9, 10e6),
        name="attention_forward",
    )(place, lengths, index, *arrays)


def down_of(weight, width):
    columns = [
        weight[at * LANES : (at + 1) * LANES, 2 * width : 3 * width] for at in range(D // LANES)
    ]
    return jnp.concatenate(columns, axis=1)


def experts_kernel(
    length_ref, index_ref, tokens_ref, base_ref, out_up_ref, gains_ref, router_ref, routes_ref, upstream_ref,
    loss_ref, weight_ref, residual_ref, hidden_ref, grad_ref,
    normed_s, cot_s, gates_s, part_s, grad_s,
):
    step = pl.program_id(0)
    count, _, packed = weight_ref.shape
    width = packed // 3
    lane = lax.broadcasted_iota(jnp.int32, gates_s.shape, 1)

    @pl.when(step == 0)
    def _():
        residual = (
            tokens_ref[...].astype(F32)
            + base_ref[:TOK_DEV, :].astype(F32)
            + dot(unfold(base_ref, length_ref, index_ref, TOK_DEV), out_up_ref[...])
        )
        residual_ref[...] = residual
        inv_root = lax.rsqrt(jnp.mean(residual * residual, axis=1, keepdims=True) + EPS)
        normed = (residual * inv_root * gains_ref[1:2, :]).astype(BF16)
        normed_s[...] = normed
        kept = column_of(loss_ref, LIVE) > 0.0
        cot_s[...] = jnp.where(kept, upstream_ref[...].astype(F32), 0.0).astype(BF16)
        logits = dot_nt(normed, router_ref[...])
        routes = routes_ref[...].astype(F32).T
        place = lane.astype(F32)
        routed = place == routes[:, 0:1]
        for slot in range(1, TOP):
            routed = routed | (place == routes[:, slot : slot + 1])
        logits = jnp.where(routed, logits, -1e30)
        lifted = jnp.exp(logits - jnp.max(logits, axis=1, keepdims=True))
        gates_s[...] = lifted / jnp.sum(lifted, axis=1, keepdims=True)
        part_s[...] = jnp.zeros_like(part_s)
        grad_s[...] = jnp.zeros_like(grad_s)

    normed = normed_s[...]
    cot = cot_s[...]
    gates = gates_s[...]
    part = jnp.zeros(part_s.shape, F32)
    grads = []
    for pair in range(0, count, 2):
        pair_down = [down_of(weight_ref.at[pair + half], width) for half in range(2)]
        pair_raw = dot_nt(cot, jnp.concatenate(pair_down, axis=0))
        for half in range(2):
            expert = pair + half
            joined = dot(normed, weight_ref[expert, :, : 2 * width])
            pre_gate = joined[:, :width]
            pre_up = joined[:, width:]
            raw = pair_raw[:, half * width : (half + 1) * width]
            sigmoid = 0.5 * jnp.tanh(0.5 * pre_gate) + 0.5
            activated = pre_gate * sigmoid
            value = activated * pre_up
            here = lane == step * count + expert
            gate = jnp.sum(jnp.where(here, gates, 0.0), axis=1, keepdims=True)
            hidden_ref[:, expert * width : (expert + 1) * width] = (gate * value).astype(BF16)
            gate_grad = jnp.sum(value[:LIVE] * raw, axis=1, keepdims=True)
            part += jnp.where(here[:LIVE], gate_grad, 0.0)
            inner = raw * gate[:LIVE]
            sigmoid, activated = sigmoid[:LIVE], activated[:LIVE]
            slope = sigmoid + activated * (1.0 - sigmoid)
            grads.append((inner * pre_up[:LIVE] * slope).astype(BF16))
            grads.append((inner * activated).astype(BF16))
    part_s[...] += part
    ups = [weight_ref[expert, :, : 2 * width] for expert in range(count)]
    grad_s[...] += dot_nt(jnp.concatenate(grads, axis=1), jnp.concatenate(ups, axis=1))

    @pl.when(step == pl.num_programs(0) - 1)
    def _():
        live_gates, gate_part = gates[:LIVE], part_s[...]
        spread = jnp.sum(live_gates * gate_part, axis=1, keepdims=True)
        logit_grad = (live_gates * (gate_part - spread)).astype(BF16)
        grad_ref[...] = (grad_s[...] + dot(logit_grad, router_ref[...])).astype(BF16)


def experts_both(
    lengths, index, tokens, base, out_up, gains, router, routes, upstream, loss_mask, weights,
    count=4,
):
    rows = tokens.shape[0]
    experts, _, packed = weights.shape
    width = packed // 3
    arrays = (tokens, base, out_up, gains, router.T, routes.T, upstream, loss_mask)
    in_specs = [IN_SMEM] * 2
    in_specs += [pl.BlockSpec(array.shape, lambda step: (0, 0)) for array in arrays]
    in_specs[2 + 6] = pl.BlockSpec((LIVE, D), lambda step: (0, 0))
    in_specs.append(pl.BlockSpec((count, D, packed), lambda step: (step, 0, 0)))
    return pl.pallas_call(
        experts_kernel,
        grid=(experts // count,),
        in_specs=in_specs,
        out_specs=[
            pl.BlockSpec((rows, D), lambda step: (0, 0)),
            pl.BlockSpec((rows, count * width), lambda step: (0, step)),
            pl.BlockSpec((LIVE, D), lambda step: (0, 0)),
        ],
        out_shape=[
            shape((rows, D), F32),
            shape((rows, experts * width), BF16),
            shape((LIVE, D), BF16),
        ],
        scratch_shapes=[
            pltpu.VMEM((rows, D), BF16),
            pltpu.VMEM((LIVE, D), BF16),
            pltpu.VMEM((rows, experts), F32),
            pltpu.VMEM((LIVE, experts), F32),
            pltpu.VMEM((LIVE, D), F32),
        ],
        compiler_params=WHOLE_VMEM,
        cost_estimate=cost(0, 1000),
        name="experts",
    )(lengths, index, *arrays, weights)


def combine_kernel(hidden_hbm, weights_hbm, moe_ref, hidden_s, downs_s, hidden_sem, sem):
    experts, _, width = downs_s.shape
    load = pltpu.make_async_copy(hidden_hbm, hidden_s, hidden_sem)
    load.start()
    copies = []
    for expert in range(experts):
        source, target = weights_hbm.at[expert, :, 2 * width :], downs_s.at[expert]
        copies.append(pltpu.make_async_copy(source, target, sem.at[expert]))
        copies[-1].start()
    load.wait()
    for copy in copies:
        copy.wait()
    for at in range(0, D, 2 * LANES):
        columns = []
        for expert in range(experts):
            pieces = [
                downs_s[expert, at + left : at + left + LANES, :] for left in (0, LANES)
            ]
            columns.append(jnp.concatenate(pieces, axis=1))
        moe_ref[:, at : at + 2 * LANES] = dot(
            hidden_s[...], jnp.concatenate(columns, axis=0)
        ).astype(BF16)


def combine(hidden, weights):
    rows = hidden.shape[0]
    experts, _, packed = weights.shape
    return pl.pallas_call(
        combine_kernel,
        in_specs=[IN_HBM] * 2,
        out_specs=IN_VMEM,
        out_shape=shape((rows, D), BF16),
        scratch_shapes=[
            pltpu.VMEM(hidden.shape, BF16),
            pltpu.VMEM((experts, D, packed // 3), BF16),
            pltpu.SemaphoreType.DMA(()),
            pltpu.SemaphoreType.DMA((experts,)),
        ],
        compiler_params=WHOLE_VMEM,
        cost_estimate=cost(4e9, 10e6),
        name="combine",
    )(hidden, weights)


def norm_back(vectors, gain, upstream):
    inv_root = lax.rsqrt(jnp.mean(vectors * vectors, axis=1, keepdims=True) + EPS)
    weighted = upstream * gain
    slope = jnp.mean(vectors * weighted, axis=1, keepdims=True)
    return inv_root * weighted - vectors * (inv_root * inv_root * inv_root) * slope


BRANCH_LOADS = (
    "residual", "normed_grad", "gains", "loss", "upstream", "out_up", "low_o", "head",
)


def branch_kernel(length_ref, index_ref, *refs):
    count = len(BRANCH_LOADS)
    branch_grad_ref, low_grad_ref, part_ref = refs[count : count + 3]
    scratch = refs[count + 3 :]
    loads = Loads(BRANCH_LOADS, refs[:count], scratch[:count], scratch[count])
    mask = adapter_mask(length_ref, index_ref, LIVE, LANES)
    kept = column_of(loads["loss"], LIVE) > 0.0
    residual, normed_grad = loads["residual"][...], loads["normed_grad"][...].astype(F32)
    through = norm_back(residual, loads["gains"][1:2, :], normed_grad)
    branch_grad_ref[...] = (
        through + jnp.where(kept, loads["upstream"][...].astype(F32), 0.0)
    ).astype(BF16)
    branch_grad = branch_grad_ref[...]
    low_grad_ref[...] = (dot_nt(branch_grad, loads["out_up"][...]) * mask).astype(BF16)
    low_o = unfold(loads["low_o"], length_ref, index_ref, LIVE)
    out_up_part = dot_tn(low_o, branch_grad).astype(BF16)
    for at in range(D // LANES):
        lanes = slice(at * LANES, (at + 1) * LANES)
        part_ref[lanes, :] = out_up_part[:, lanes]
    part_ref[D:, :] = dot_tn(loads["head"][...], low_grad_ref[...]).astype(BF16)


def branch_back(
    lengths, index, residual, base, normed_grad, upstream, loss_mask, gains, out_up, head
):
    arrays = (residual, normed_grad, gains, loss_mask, upstream, out_up, base, head)
    return pl.pallas_call(
        branch_kernel,
        in_specs=[IN_SMEM] * 2 + [IN_HBM] * len(arrays),
        out_specs=[IN_VMEM] * 3,
        out_shape=[
            shape((LIVE, D), BF16),
            shape((LIVE, LANES), BF16),
            shape((D + head.shape[1], LANES), BF16),
        ],
        scratch_shapes=load_scratch(arrays, LIVE),
        compiler_params=WHOLE_VMEM,
        cost_estimate=cost(1e9, 2e6),
        name="branch_backward",
    )(lengths, index, *arrays)


def share_copies(place_ref, shares, w_qkv_s, sem):
    n_exp, n_tp, _, _ = shares.shape
    qkv_rows, up_rows, _ = share_rows(n_exp, 0)
    copies = []
    for z in range(n_tp):
        here = []
        source_z = from_place(place_ref, z, n_tp)
        for e in range(n_exp):
            at = e * qkv_rows
            up_at = D + e * up_rows
            for source, target in (
                (shares.at[e, source_z, :qkv_rows, :], w_qkv_s.at[z, at : at + qkv_rows, :]),
                (shares.at[e, source_z, qkv_rows:, :], w_qkv_s.at[z, up_at : up_at + up_rows, :]),
            ):
                number = 2 * e + len(here) % 2
                here.append(pltpu.make_async_copy(source, target, sem.at[z, number]))
        copies.append(here)
    for here in copies:
        for copy in here:
            copy.start()
    return copies


PREPARE_LOADS = ("attn_in", "low_q", "cosine", "sine")


def prepare_kernel(place_ref, length_ref, shares, *refs):
    count = len(PREPARE_LOADS)
    results = 1 + len(LIVE_BLOCKS)
    turned_ref = refs[count]
    prob_refs = refs[count + 1 : count + results]
    load_sem, w_qkv_s, q_s, k_s, v_s, sem = refs[2 * count + results :]
    targets = refs[count + results : 2 * count + results]
    loads = Loads(PREPARE_LOADS, refs[:count], targets, load_sem)
    n_tp = shares.shape[1]
    groups = k_s.shape[0]
    copies = share_copies(place_ref, shares, w_qkv_s, sem)
    first = first_keys(length_ref, LIVE)
    attn_in = loads["attn_in"][...]
    low_q = loads["low_q"][...]
    cosine, sine = loads["cosine"][...], loads["sine"][...]
    seen = [seen_block(first, begin, end) for begin, end in LIVE_BLOCKS]
    for here in copies:
        for copy in here:
            copy.wait()

    def one_place(z, carried):
        projected = dot(attn_in, w_qkv_s[z, :D, :]) + dot(low_q, w_qkv_s[z, D:, :])
        columns = turn(projected, cosine, sine, turned_pieces(groups))
        for at, column in enumerate(columns):
            turned_ref[z, :, at * LANES : (at + 1) * LANES] = column.astype(BF16)
        store_heads(columns, 0, LIVE_BLOCKS, q_s, k_s, v_s)
        for group in range(groups):
            for block, (begin, end) in enumerate(LIVE_BLOCKS):
                query = q_s[group, block, : PER * (end - begin), :]
                scores = dot_nt(query, k_s[group, :end, :])
                prob_refs[block][z * groups + group] = softmax_block(scores, seen[block])
        return carried

    lax.fori_loop(0, n_tp, one_place, 0)


def prepare(place, lengths, attn_in, low_q, tables, shares):
    n_exp, n_tp, _, wide = shares.shape
    arrays = (attn_in, low_q) + tables
    groups = KV_HEADS
    probs = [
        shape((groups, PER * (end - begin), end), BF16) for begin, end in LIVE_BLOCKS
    ]
    return pl.pallas_call(
        prepare_kernel,
        in_specs=[IN_SMEM] * 2 + [IN_HBM] * (1 + len(arrays)),
        out_specs=[IN_VMEM] * (1 + len(probs)),
        out_shape=[shape((n_tp, LIVE, wide), BF16)] + probs,
        scratch_shapes=load_scratch(arrays, LIVE)
        + [
            pltpu.VMEM((n_tp, D + LANES, wide), BF16),
            pltpu.VMEM((groups // n_tp, len(LIVE_BLOCKS), PER * ROWS, HD), BF16),
            pltpu.VMEM((groups // n_tp, LIVE, HD), BF16),
            pltpu.VMEM((groups // n_tp, LIVE, HD), BF16),
            pltpu.SemaphoreType.DMA((n_tp, 2 * n_exp)),
        ],
        compiler_params=WHOLE_VMEM,
        cost_estimate=cost(12e9, 30e6),
        name="prepare_heads",
    )(place, lengths, shares, *arrays)


HEADS_LOADS = (
    "branch_grad", "low_o_grad", "turned", "cosine", "sine", "low_q", "attn_in",
)


def heads_back_kernel(place_ref, length_ref, index_ref, shares, out_shares, *refs):
    count = len(HEADS_LOADS)
    blocks = len(LIVE_BLOCKS)
    probs_hbm = refs[count : count + blocks]
    grad_ref, low_grad_ref, part_ref = refs[count + blocks : count + blocks + 3]
    scratch = refs[count + blocks + 3 :]
    loads = Loads(HEADS_LOADS, refs[:count], scratch[:count], scratch[count])
    up_s, w_out_s, g_s, q_s, k_s, v_s, up_sem, out_sem, prob_sem = scratch[count + 1 : count + 10]
    probs_s = scratch[count + 10 :]
    n_exp, n_tp, _, wide = shares.shape
    groups = g_s.shape[0]
    flags = turned_pieces(groups)
    scale = 1.0 / math.sqrt(HD)

    def prob_copy(z, block):
        here = pl.ds(z * groups, groups)
        return pltpu.make_async_copy(
            probs_hbm[block].at[here], probs_s[block].at[here], prob_sem.at[z, block]
        )

    out_rows = out_shares.shape[2]

    def out_copy(z, e):
        return pltpu.make_async_copy(
            out_shares.at[e, from_place(place_ref, z, n_tp)],
            w_out_s.at[z, e * out_rows : (e + 1) * out_rows, :],
            out_sem.at[z, e],
        )

    for z in range(n_tp):
        for e in range(n_exp):
            out_copy(z, e).start()
        for block in range(blocks):
            prob_copy(z, block).start()
    qkv_rows, up_rows, _ = share_rows(n_exp, 0)
    up_copies = []
    for z in range(n_tp):
        for e in range(n_exp):
            source = shares.at[e, from_place(place_ref, z, n_tp), qkv_rows:, :]
            target = up_s.at[z, e * up_rows : (e + 1) * up_rows, :]
            up_copies.append(pltpu.make_async_copy(source, target, up_sem.at[z, e]))
            up_copies[-1].start()
    branch_grad, low_o_grad = loads["branch_grad"], loads["low_o_grad"]
    turned = loads["turned"]
    cosine, sine = loads["cosine"], loads["sine"]

    def one_place(z, carried):
        columns = [
            turned[z, :, at * LANES : (at + 1) * LANES].astype(F32) for at in range(wide // LANES)
        ]
        store_heads(columns, 0, LIVE_BLOCKS, q_s, k_s, v_s)
        for e in range(n_exp):
            out_copy(z, e).wait()
        head_grad = (
            dot_nt(branch_grad[...], w_out_s[z, :, :D]) + dot_nt(low_o_grad[...], w_out_s[z, :, D:])
        ).astype(BF16)
        for head in range(groups * PER):
            group, kind = divmod(head, PER)
            part = head_grad[:, head * HD : (head + 1) * HD]
            for block, (begin, end) in enumerate(LIVE_BLOCKS):
                size = end - begin
                here = slice(kind * size, (kind + 1) * size)
                g_s[group, block, here, :] = part[begin:end]
        for block in range(blocks):
            prob_copy(z, block).wait()
        key_grads = [jnp.zeros((HD, LIVE), F32) for _ in range(groups)]
        value_grads = [jnp.zeros((HD, LIVE), F32) for _ in range(groups)]
        query_grads = [[] for _ in range(groups)]
        for block, (begin, end) in enumerate(LIVE_BLOCKS):
            size = end - begin

            def widen(part):
                if end == LIVE:
                    return part
                return jnp.concatenate([part, jnp.zeros((HD, LIVE - end), F32)], axis=1)

            some = range(groups)
            queries = [q_s[group, block, : PER * size, :] for group in some]
            head_grads = [g_s[group, block, : PER * size, :] for group in some]
            probs = [probs_s[block][z * groups + group] for group in some]
            weight_grads = [dot_nt(head_grads[group], v_s[group, :end, :]) for group in some]
            for group in some:
                value_grads[group] += widen(dot_tn(head_grads[group], probs[group]))
            wide_probs = [probs[group].astype(F32) for group in some]
            score_grads = []
            for group in some:
                product = wide_probs[group] * weight_grads[group]
                spread = jnp.sum(product, axis=1, keepdims=True)
                score_grads.append((product - wide_probs[group] * spread).astype(BF16))
            for group in some:
                score_grad = score_grads[group]
                query_grads[group].append(dot(score_grad, k_s[group, :end, :]) * scale)
                key_grads[group] += widen(dot_tn(queries[group], score_grad))
        pieces = []
        for group in range(groups):
            for head in range(PER):
                rows = [
                    part[head * (end - begin) : (head + 1) * (end - begin)]
                    for part, (begin, end) in zip(query_grads[group], LIVE_BLOCKS)
                ]
                pieces.append(jnp.concatenate(rows, axis=0))
            pieces += [key_grads[group].T, value_grads[group].T]
        joined = jnp.concatenate(pieces, axis=1)
        columns = turn(joined, cosine[...], -sine[...], flags)
        for at, column in enumerate(columns):
            grad_ref[z, :, at * LANES : (at + 1) * LANES] = column.astype(BF16)
        return carried

    lax.fori_loop(0, n_tp, one_place, 0)
    for copy in up_copies:
        copy.wait()
    low_grad = dot_nt(grad_ref[0], up_s[0])
    for z in range(1, n_tp):
        low_grad += dot_nt(grad_ref[z], up_s[z])
    mask = adapter_mask(length_ref, index_ref, LIVE, LANES)
    low_grad = (low_grad * mask).astype(BF16)
    low_grad_ref[...] = low_grad
    part_ref[:D, :] = dot_tn(loads["attn_in"][...], low_grad).astype(BF16)
    up_part = dot_tn(loads["low_q"][...], grad_ref[place_ref[0]]).astype(BF16)
    for at in range(wide // LANES):
        lanes = slice(at * LANES, (at + 1) * LANES)
        part_ref[D + at * LANES : D + (at + 1) * LANES, :] = up_part[:, lanes]


def heads_back(
    place, lengths, index, attn_in, low_q, heads, branch_grad, low_o_grad, tables, shares, out_shares
):
    n_exp, n_tp, _, wide = shares.shape
    blocks = len(LIVE_BLOCKS)
    turned, probs = heads[0], heads[1:]
    groups = KV_HEADS // n_tp
    heads_wide = groups * PER * HD
    arrays = (branch_grad, low_o_grad, turned) + tables + (low_q, attn_in)
    return pl.pallas_call(
        heads_back_kernel,
        in_specs=[IN_SMEM] * 3 + [IN_HBM] * (2 + len(arrays) + blocks),
        out_specs=[IN_VMEM] * 3,
        out_shape=[
            shape((n_tp, LIVE, wide), BF16),
            shape((LIVE, LANES), BF16),
            shape((D + wide, LANES), BF16),
        ],
        scratch_shapes=load_scratch(arrays, LIVE)
        + [
            pltpu.VMEM((n_tp, LANES, wide), BF16),
            pltpu.VMEM((n_tp, heads_wide, D + LANES), BF16),
            pltpu.VMEM((groups, blocks, PER * ROWS, HD), BF16),
            pltpu.VMEM((groups, blocks, PER * ROWS, HD), BF16),
            pltpu.VMEM((groups, LIVE, HD), BF16),
            pltpu.VMEM((groups, LIVE, HD), BF16),
            pltpu.SemaphoreType.DMA((n_tp, n_exp)),
            pltpu.SemaphoreType.DMA((n_tp, n_exp)),
            pltpu.SemaphoreType.DMA((n_tp, blocks)),
        ]
        + [pltpu.VMEM(part.shape, BF16) for part in probs],
        compiler_params=WHOLE_VMEM,
        cost_estimate=cost(2e9, 3e6),
        name="heads_backward",
    )(place, lengths, index, shares, out_shares, *arrays, *probs)


INPUT_LOADS = ("grads", "low_grad", "qkv_down", "tokens", "gains", "branch_grad")


def input_back_kernel(place_ref, shares, *refs):
    count = len(INPUT_LOADS)
    input_grad_ref = refs[count]
    load_sem, w_qkv_s, sum_s, sem = refs[2 * count + 1 :]
    n_exp, n_tp, _, _ = shares.shape
    qkv_rows, _, _ = share_rows(n_exp, 0)
    copies = []
    for z in range(n_tp):
        for e in range(n_exp):
            source = shares.at[e, from_place(place_ref, z, n_tp), :qkv_rows, :]
            target = w_qkv_s.at[z, e * qkv_rows : (e + 1) * qkv_rows, :]
            copies.append(pltpu.make_async_copy(source, target, sem.at[z, e]))
    loads = Loads(INPUT_LOADS, refs[:count], refs[count + 1 : 2 * count + 1], load_sem)
    for copy in copies:
        copy.start()
    input_grad_ref[LIVE:, :] = jnp.zeros((input_grad_ref.shape[0] - LIVE, D), BF16)
    grads = loads["grads"]
    sum_s[...] = dot_nt(loads["low_grad"][...], loads["qkv_down"][...])
    for z in range(n_tp):
        for copy in copies[z * n_exp : (z + 1) * n_exp]:
            copy.wait()
        sum_s[...] += dot_nt(grads[z], w_qkv_s[z])
    tokens, gain = loads["tokens"][...].astype(F32), loads["gains"][0:1, :]
    through = norm_back(tokens, gain, sum_s[...])
    input_grad_ref[:LIVE, :] = (loads["branch_grad"][...].astype(F32) + through).astype(BF16)


def input_back(place, grads, low_grad, qkv_down, tokens, gains, branch_grad, shares):
    n_exp, n_tp, _, wide = shares.shape
    arrays = (grads, low_grad, qkv_down, tokens, gains, branch_grad)
    return pl.pallas_call(
        input_back_kernel,
        in_specs=[IN_SMEM] + [IN_HBM] * (1 + len(arrays)),
        out_specs=IN_VMEM,
        out_shape=shape(tokens.shape, BF16),
        scratch_shapes=load_scratch(arrays, LIVE)
        + [
            pltpu.VMEM((n_tp, D, wide), BF16),
            pltpu.VMEM((LIVE, D), F32),
            pltpu.SemaphoreType.DMA((n_tp, n_exp)),
        ],
        compiler_params=WHOLE_VMEM,
        cost_estimate=cost(2e9, 2e6),
        name="input_backward",
    )(place, shares, *arrays)


FINISH_LOADS = ("out_parts", "residual", "moe_out", "qkv_sum")


def finish_kernel(*refs):
    count = len(FINISH_LOADS)
    output_ref, qkv_down_ref, qkv_up_ref, out_down_ref, out_up_ref = refs[count : count + 5]
    scratch = refs[count + 5 :]
    loads = Loads(FINISH_LOADS, refs[:count], scratch[:count], scratch[count])
    qkv_sum = loads["qkv_sum"]
    qkv_down_ref[...] = qkv_sum[:D, :].astype(F32)
    for at in range(0, qkv_up_ref.shape[1], LANES):
        qkv_up_ref[:, at : at + LANES] = qkv_sum[D + at : D + at + LANES, :].astype(F32)
    output_ref[...] = (loads["residual"][...] + loads["moe_out"][...].astype(F32)).astype(BF16)
    out_parts = loads["out_parts"]
    for at in range(0, out_parts.shape[1], LANES):
        total = out_parts[0, at : at + LANES, :].astype(F32)
        for part in range(1, out_parts.shape[0]):
            total += out_parts[part, at : at + LANES, :].astype(F32)
        if at < D:
            out_up_ref[:, at : at + LANES] = total
        else:
            out_down_ref[at - D : at - D + LANES, :] = total


def finish(residual, moe_out, out_parts, qkv_sum):
    arrays = (out_parts, residual, moe_out, qkv_sum)
    return pl.pallas_call(
        finish_kernel,
        in_specs=[IN_HBM] * len(arrays),
        out_specs=[IN_VMEM] * 5,
        out_shape=[
            shape(residual.shape, BF16),
            shape((D, LANES), F32),
            shape((LANES, qkv_sum.shape[0] - D), F32),
            shape((out_parts.shape[1] - D, LANES), F32),
            shape((LANES, D), F32),
        ],
        scratch_shapes=load_scratch(arrays),
        compiler_params=WHOLE_VMEM,
        cost_estimate=cost(0, 14e6),
        name="finish",
    )(*arrays)


def from_tp(share, count):
    around = [share]
    for shift in range(1, count):
        around.append(
            lax.ppermute(share, "tp", [(at, (at + shift) % count) for at in range(count)])
        )
    return around


def from_place(place_ref, z, count):
    return lax.rem(place_ref[0] - z + count, count)


def kernel_body(
    tokens, attn_gain, moe_gain, w_qkv, w_out, w_router, w_gate, w_up, w_down, qkv_down, qkv_up,
    out_down, out_up, lengths, adapter_index, loss_mask, routes, upstream,
):
    n_exp = lax.axis_size("exp")
    n_tp = lax.axis_size("tp")
    exp_place = lax.axis_index("exp").astype(jnp.int32).reshape(1)
    tp_place = lax.axis_index("tp").astype(jnp.int32).reshape(1)
    tables = turn_tables(tokens.shape[0])
    gains = jnp.stack([attn_gain, moe_gain])
    loss_row = loss_mask.reshape(1, -1)

    own_experts, own_qkv = pack(exp_place, w_gate, w_up, w_down, w_qkv, qkv_up, n_exp)
    weights = lax.all_gather(own_experts, "exp", axis=0, tiled=True)
    z_qkv = from_tp(own_qkv, n_tp)
    inputs, _ = lax.optimization_barrier((tokens, own_qkv))
    attn_in, low_q, head, base, own_out = forward(
        exp_place, lengths, adapter_index, inputs, gains, w_qkv, qkv_down, qkv_up, w_out, out_down,
        tables, n_exp,
    )
    base, z_qkv = lax.optimization_barrier((base, z_qkv))
    z_qkv = jnp.stack(z_qkv)
    base = lax.psum(base, "tp")
    own_out, _ = lax.optimization_barrier((own_out, base))
    z_out = from_tp(own_out, n_tp)
    z_qkv, _ = lax.optimization_barrier((z_qkv, weights))
    qkv_shares = lax.all_gather(z_qkv, "exp", axis=0)

    residual, hidden, normed_part = experts_both(
        lengths, adapter_index, tokens, base, out_up, gains, w_router, routes, upstream, loss_row,
        weights,
    )
    normed_part, z_out = lax.optimization_barrier((normed_part, z_out))
    z_out = jnp.stack(z_out)
    normed_grad = lax.psum(normed_part, "tp")
    z_out, _ = lax.optimization_barrier((z_out, qkv_shares))
    out_shares = lax.all_gather(z_out, "exp", axis=0)
    late_in, _ = lax.optimization_barrier((attn_in, normed_part))
    heads = prepare(tp_place, lengths, late_in, low_q, tables, qkv_shares)

    moe_part, normed_grad, _ = lax.optimization_barrier(
        (combine(hidden, weights), normed_grad, heads[0])
    )
    moe_out = lax.psum(moe_part, "tp")
    branch_grad, low_o_grad, out_part = branch_back(
        lengths, adapter_index, residual, base, normed_grad, upstream, loss_row, gains, out_up, head
    )
    out_parts = lax.all_gather(out_part, "exp", axis=0)
    grads, low_grad, qkv_part = heads_back(
        tp_place, lengths, adapter_index, attn_in, low_q, heads, branch_grad, low_o_grad, tables,
        qkv_shares, out_shares,
    )
    share = qkv_part.shape[0] // n_exp
    parts = lax.all_to_all(qkv_part.reshape(n_exp, share, LANES), "exp", 0, 0, tiled=True)
    input_grad = input_back(
        tp_place, grads, low_grad, qkv_down, tokens, gains, branch_grad, qkv_shares
    )
    parts, input_grad = lax.optimization_barrier((parts, input_grad))
    qkv_sum = jnp.sum(parts.astype(F32), axis=0).astype(BF16)
    qkv_sum = lax.all_gather(qkv_sum, "exp", axis=0, tiled=True)
    out_parts, moe_out, _ = lax.optimization_barrier((out_parts, moe_out, qkv_sum))
    output, grad_qkv_down, grad_qkv_up, grad_out_down, grad_out_up = finish(
        residual, moe_out, out_parts, qkv_sum
    )
    return (output, input_grad, grad_qkv_down, grad_qkv_up, grad_out_down, grad_out_up)


def product(left_m, right_m):
    return jnp.dot(left_m, right_m, preferred_element_type=jnp.float32)


def contract(einsum_form, left_m, right_m):
    return jnp.einsum(einsum_form, left_m, right_m, preferred_element_type=jnp.float32)


def rms_norm(vectors, gain_vec):
    inv_root = lax.rsqrt(jnp.mean(vectors * vectors, axis=-1, keepdims=True) + EPS)
    return vectors * inv_root * gain_vec


def rms_norm_back(vectors, gain_vec, upstream_grad):
    inv_root = lax.rsqrt(jnp.mean(vectors * vectors, axis=-1, keepdims=True) + EPS)
    weighted = upstream_grad * gain_vec
    return inv_root * weighted - vectors * (inv_root * inv_root * inv_root) * jnp.mean(
        vectors * weighted, axis=-1, keepdims=True
    )


def layout(length_row, index_row):
    places = jnp.arange(TOK_DEV, dtype=jnp.int32)
    doc_ends = jnp.cumsum(length_row)
    doc_starts = doc_ends - length_row
    member = (places[:, None] >= doc_starts[None, :]) & (places[:, None] < doc_ends[None, :])
    occupied = jnp.any(member, axis=1)
    position = jnp.sum(jnp.where(member, places[:, None] - doc_starts[None, :], 0), axis=1)
    owner_doc = jnp.sum(jnp.where(member, jnp.arange(DOCS, dtype=jnp.int32)[None, :], 0), axis=1)
    doc_ident = jnp.where(occupied, owner_doc, DOCS + places)
    chosen = jnp.sum(jnp.where(member, index_row[None, :], 0), axis=1)
    adapter_pick = occupied[:, None] & (
        chosen[:, None] == jnp.arange(ADAPTERS, dtype=jnp.int32)[None, :]
    )
    rank_mask = jnp.repeat(jnp.where(adapter_pick, 1.0, 0.0).astype(jnp.float32), RANK, axis=1)
    return (occupied, position, doc_ident, rank_mask)


def angles(position):
    half_width = HD // 2
    frequency = jnp.exp(-math.log(ROPE_BASE) * jnp.arange(half_width, dtype=jnp.float32) * 2.0 / HD)
    turned = position.astype(jnp.float32)[:, None] * frequency[None, :]
    return (jnp.cos(turned), jnp.sin(turned))


def rotate(vectors, cosine, sine_table):
    half_width = vectors.shape[-1] // 2
    front_half = vectors[..., :half_width]
    back_half = vectors[..., half_width:]
    return jnp.concatenate(
        [
            front_half * cosine - back_half * sine_table,
            back_half * cosine + front_half * sine_table,
        ],
        axis=-1,
    )


def moe(normed, cot_low, gates, gate_up, down):
    width = down.shape[1]
    both = contract("td,edf->tef", normed, gate_up)
    pre_gate = both[:, :, :width]
    pre_up = both[:, :, width:]
    sigmoid_g = jax.nn.sigmoid(pre_gate)
    activated = pre_gate * sigmoid_g
    hidden = (activated * pre_up).astype(jnp.bfloat16).astype(jnp.float32)
    inner_raw = contract("td,efd->tef", cot_low, down)
    gate_part = jnp.sum(hidden * inner_raw, axis=-1)
    moe_part = contract("tef,efd->td", (gates[:, :, None] * hidden).astype(jnp.bfloat16), down)
    inner_grad = inner_raw * gates[:, :, None]
    grad_gate = inner_grad * pre_up * sigmoid_g * (1.0 + pre_gate * (1.0 - sigmoid_g))
    grad_up = inner_grad * activated
    grad_both = jnp.concatenate([grad_gate, grad_up], axis=2).astype(jnp.bfloat16)
    normed_part = contract("tef,edf->td", grad_both, gate_up)
    return (moe_part, gate_part, normed_part)


def body(
    tokens,
    attn_gain,
    moe_gain,
    w_qkv,
    w_out,
    w_router,
    w_gate,
    w_up,
    w_down,
    qkv_down,
    qkv_up,
    out_down,
    out_up,
    lengths,
    adapter_index,
    loss_mask,
    routes,
    upstream,
):
    n_exp = lax.axis_size("exp")
    groups = KV_HEADS // lax.axis_size("tp")
    per_group = HEADS // KV_HEADS
    experts = EXP_DEV * n_exp
    gate_up = lax.all_gather(jnp.concatenate([w_gate, w_up], axis=2), "exp", axis=0, tiled=True)
    down = lax.all_gather(w_down, "exp", axis=0, tiled=True)
    block_rows = min(512, TOK_DEV)
    blocks = TOK_DEV // block_rows
    score_scale = 1.0 / math.sqrt(HD)
    places = jnp.arange(TOK_DEV, dtype=jnp.int32)
    occupied, position, doc_ident, rank_mask = layout(lengths[0], adapter_index[0])
    mask_low = rank_mask.astype(jnp.bfloat16)
    cosine, sine_table = angles(position)
    inputs = tokens.astype(jnp.float32)
    attn_in = rms_norm(inputs, attn_gain).astype(jnp.bfloat16)
    low_q = (product(attn_in, qkv_down) * rank_mask).astype(jnp.bfloat16)
    projected = (product(attn_in, w_qkv) + product(low_q, qkv_up)).reshape(
        TOK_DEV, groups, per_group + 2, HD
    )
    query_rows = rotate(
        projected[:, :, :per_group], cosine[:, None, None], sine_table[:, None, None]
    ).astype(jnp.bfloat16)
    key_rows = rotate(projected[:, :, per_group], cosine[:, None], sine_table[:, None]).astype(
        jnp.bfloat16
    )
    val_rows = projected[:, :, per_group + 1].astype(jnp.bfloat16)

    def masked_scores(q_blk, q_place, q_ident):
        scores = contract("qgrd,kgd->grqk", q_blk, key_rows) * score_scale
        allowed = (q_ident[:, None] == doc_ident[None, :]) & (places[None, :] <= q_place[:, None])
        return jnp.where(allowed, scores, -1e30)

    def attend(pieces):
        q_blk, q_place, q_ident = pieces
        scores = masked_scores(q_blk, q_place, q_ident)
        row_max = jnp.max(scores, axis=-1, keepdims=True)
        lifted = jnp.exp(scores - row_max)
        row_total = jnp.sum(lifted, axis=-1, keepdims=True)
        weights = (lifted / row_total).astype(jnp.bfloat16)
        return (
            contract("grqk,kgd->qgrd", weights, val_rows),
            row_max[..., 0] + jnp.log(row_total[..., 0]),
        )

    query_blocks = query_rows.reshape(blocks, block_rows, groups, per_group, HD)
    place_blocks = places.reshape(blocks, block_rows)
    ident_blocks = doc_ident.reshape(blocks, block_rows)
    attended, log_totals = lax.map(attend, (query_blocks, place_blocks, ident_blocks))
    head_rows = attended.reshape(TOK_DEV, groups * per_group * HD).astype(jnp.bfloat16)
    attn_base, low_rank = (
        lax.psum(product(head_rows, w_out).astype(jnp.bfloat16), "tp").astype(jnp.float32),
        lax.psum((product(head_rows, out_down) * rank_mask).astype(jnp.bfloat16), "tp").astype(
            jnp.float32
        ),
    )
    low_o = low_rank.astype(jnp.bfloat16)
    residual = inputs + attn_base + product(low_o, out_up)
    normed = rms_norm(residual, moe_gain).astype(jnp.bfloat16)
    logits = product(normed, w_router)
    one_hot = routes[:, :, None] == jnp.arange(experts, dtype=jnp.int32)[None, None, :]
    routed = jnp.any(one_hot, axis=1)
    gates = jax.nn.softmax(jnp.where(routed, logits, -1e30), axis=-1)
    live_mask = jnp.where(occupied & (loss_mask > 0), 1.0, 0.0).astype(jnp.float32)
    cotangent = upstream.astype(jnp.float32) * live_mask[:, None]
    cot_low = cotangent.astype(jnp.bfloat16)
    moe_part, gate_part, normed_part = moe(normed, cot_low, gates, gate_up, down)
    logit_grad = (
        gates * (gate_part - jnp.sum(gates * gate_part, axis=-1, keepdims=True))
    ).astype(jnp.bfloat16)
    normed_part = (normed_part + product(logit_grad, w_router.T)).astype(jnp.bfloat16)
    normed_sum = lax.psum(normed_part, "tp")
    normed_sum, moe_part = lax.optimization_barrier((normed_sum, moe_part.astype(jnp.bfloat16)))
    normed_grad = normed_sum.astype(jnp.float32)
    moe_out = lax.psum(moe_part, "tp").astype(jnp.float32)
    output = (residual + moe_out).astype(jnp.bfloat16)
    residual_grad = cotangent + rms_norm_back(residual, moe_gain, normed_grad)
    branch_grad = residual_grad.astype(jnp.bfloat16)
    low_o_grad = product(branch_grad, out_up.T).astype(jnp.bfloat16) * mask_low
    out_up_part = contract("tr,td->rd", low_o, branch_grad)
    head_grad = (product(branch_grad, w_out.T) + product(low_o_grad, out_down.T)).astype(
        jnp.bfloat16
    )
    out_down_part = contract("tc,tr->cr", head_rows, low_o_grad)
    grad_blocks = head_grad.reshape(blocks, block_rows, groups, per_group, HD)

    def attend_back(carried, pieces):
        key_acc, val_acc = carried
        q_blk, q_place, q_ident, lse_blk, g_blk = pieces
        weights = jnp.exp(masked_scores(q_blk, q_place, q_ident) - lse_blk[..., None])
        weight_grad = contract("qgrd,kgd->grqk", g_blk, val_rows)
        score_grad = (
            weights * (weight_grad - jnp.sum(weights * weight_grad, axis=-1, keepdims=True))
        ).astype(jnp.bfloat16)
        query_grad = contract("grqk,kgd->qgrd", score_grad, key_rows) * score_scale
        key_acc = key_acc + contract("grqk,qgrd->kgd", score_grad, q_blk) * score_scale
        val_acc = val_acc + contract("grqk,qgrd->kgd", weights.astype(jnp.bfloat16), g_blk)
        return ((key_acc, val_acc), query_grad)

    zero_acc = jnp.zeros((TOK_DEV, groups, HD), jnp.float32)
    (key_grad, val_grad), query_grad = lax.scan(
        attend_back,
        (zero_acc, zero_acc),
        (query_blocks, place_blocks, ident_blocks, log_totals, grad_blocks),
    )
    query_grad = rotate(
        query_grad.reshape(TOK_DEV, groups, per_group, HD),
        cosine[:, None, None],
        -sine_table[:, None, None],
    )
    key_grad = rotate(key_grad, cosine[:, None], -sine_table[:, None])
    projected_grad = (
        jnp.concatenate([query_grad, key_grad[:, :, None], val_grad[:, :, None]], axis=2)
        .reshape(TOK_DEV, -1)
        .astype(jnp.bfloat16)
    )
    qkv_up_part = contract("tr,tc->rc", low_q, projected_grad)
    attn_grad, low_q_grad = (
        lax.psum(contract("tc,dc->td", projected_grad, w_qkv).astype(jnp.bfloat16), "tp").astype(
            jnp.float32
        ),
        lax.psum(contract("tc,rc->tr", projected_grad, qkv_up).astype(jnp.bfloat16), "tp").astype(
            jnp.float32
        ),
    )
    low_q_grad = low_q_grad.astype(jnp.bfloat16) * mask_low
    attn_grad = attn_grad + contract("tr,dr->td", low_q_grad, qkv_down)
    qkv_down_part = contract("td,tr->dr", attn_in, low_q_grad)
    input_grad = (residual_grad + rms_norm_back(inputs, attn_gain, attn_grad)).astype(jnp.bfloat16)
    summed = (
        lax.psum(qkv_down_part.astype(jnp.bfloat16), "exp").astype(jnp.float32),
        lax.psum(qkv_up_part.astype(jnp.bfloat16), "exp").astype(jnp.float32),
        lax.psum(out_down_part.astype(jnp.bfloat16), "exp").astype(jnp.float32),
        lax.psum(out_up_part.astype(jnp.bfloat16), "exp").astype(jnp.float32),
    )
    return (output, input_grad, summed[0], summed[1], summed[2], summed[3])


def kernels_fit(mesh):
    n_exp, n_tp = mesh.shape["exp"], mesh.shape["tp"]
    groups = KV_HEADS // n_tp
    return groups % 2 == 0 and FF // n_tp == LANES and LANES // n_exp % 16 == 0


def solution(mesh):
    placed = (
        P("exp", None),
        P(),
        P(),
        P(None, "tp"),
        P("tp", None),
        P(),
        P("exp", None, "tp"),
        P("exp", None, "tp"),
        P("exp", "tp", None),
        P(),
        P(None, "tp"),
        P("tp", None),
        P(),
        P("exp", None),
        P("exp", None),
        P("exp"),
        P("exp", None),
        P("exp", None),
    )
    return jax.shard_map(
        kernel_body if kernels_fit(mesh) else body,
        mesh=mesh,
        in_specs=placed,
        out_specs=(P("exp", None), P("exp", None), P(), P(None, "tp"), P("tp", None), P()),
        check_vma=False,
    )
```

```python
import functools
import math

import jax
import jax.numpy as jnp
import numpy as np
from jax import lax
from jax.experimental import pallas as pl
from jax.experimental.pallas import tpu as pltpu
from jax.sharding import PartitionSpec as P

D = 1536
HEADS = 24
KV_HEADS = 8
HD = 64
TOP = 8
RANK = 16
ADAPTERS = 8
EXP_DEV = 2
DOCS = 4
TOK_DEV = 512
LIVE = 448
FF = 512
EPS = 1e-06
ROPE_BASE = 10000.0

PER = HEADS // KV_HEADS
LANES = 128
ROWS = 128
BLOCKS = tuple((at, min(at + ROWS, TOK_DEV)) for at in range(0, TOK_DEV, ROWS))
LIVE_BLOCKS = tuple((at, min(at + ROWS, LIVE)) for at in range(0, LIVE, ROWS))
F32 = jnp.float32
BF16 = jnp.bfloat16
MIB = 2**20
NT = (((1,), (1,)), ((), ()))
TN = (((0,), (0,)), ((), ()))
WHOLE_VMEM = pltpu.CompilerParams(vmem_limit_bytes=63 * MIB)
IN_VMEM = pl.BlockSpec(memory_space=pltpu.VMEM)
IN_SMEM = pl.BlockSpec(memory_space=pltpu.SMEM)
IN_HBM = pl.BlockSpec(memory_space=pltpu.HBM)


def dot(left, right):
    return jnp.dot(left, right, preferred_element_type=F32)


def dot_nt(left, right):
    return lax.dot_general(left, right, NT, preferred_element_type=F32)


def dot_tn(left, right):
    return lax.dot_general(left, right, TN, preferred_element_type=F32)


def cost(flops, moved):
    return pl.CostEstimate(flops=int(flops), bytes_accessed=int(moved), transcendentals=0)


def shape(dims, dtype):
    return jax.ShapeDtypeStruct(dims, dtype)


def turn_tables(rows):
    half = HD // 2
    frequency = np.exp(-math.log(ROPE_BASE) * np.arange(half, dtype=np.float64) * 2.0 / HD)
    turned = np.arange(rows, dtype=np.float64)[:, None] * frequency[None, :]
    cosine, sine = np.cos(turned), np.sin(turned)
    return (
        jnp.asarray(np.concatenate([cosine] * 4, axis=1), F32),
        jnp.asarray(np.concatenate([-sine, sine, -sine, sine], axis=1), F32),
    )


def turned_pieces(groups):
    return [piece < PER + 1 for _ in range(groups) for piece in range(PER + 2)]


def turn(joined, cosine, sine, flags):
    lane = lax.broadcasted_iota(jnp.int32, cosine.shape, 1)
    front = (lane & 32) == 0
    left = lane < HD
    columns = []
    for at in range(joined.shape[1] // LANES):
        column = joined[:, at * LANES : (at + 1) * LANES]
        swapped = jnp.where(front, pltpu.roll(column, 96, 1), pltpu.roll(column, 32, 1))
        rotated = column * cosine + swapped * sine
        if not (flags[2 * at] and flags[2 * at + 1]):
            rotated = jnp.where(left if flags[2 * at] else jnp.logical_not(left), rotated, column)
        columns.append(rotated)
    return columns


def first_keys(length_ref, rows):
    row = lax.broadcasted_iota(jnp.int32, (rows, 1), 0)
    begin = jnp.zeros((rows, 1), jnp.int32)
    end = 0
    for doc in range(DOCS):
        if doc:
            begin = jnp.where(row >= end, end, begin)
        end = end + length_ref[0, doc]
    return jnp.where(row >= end, row, begin)


def adapter_mask(length_ref, index_ref, rows, width):
    row = lax.broadcasted_iota(jnp.int32, (rows, width), 0)
    adapter = lax.shift_right_logical(lax.broadcasted_iota(jnp.int32, (rows, width), 1), 4)
    mask = jnp.zeros((rows, width), F32)
    begin = 0
    for doc in range(DOCS):
        end = begin + length_ref[0, doc]
        inside = (row >= begin) & (row < end) & (adapter == index_ref[0, doc])
        mask = jnp.where(inside, 1.0, mask)
        begin = end
    return mask


def folding():
    rank = lax.broadcasted_iota(jnp.int32, (RANK, LANES), 0)
    lane = lax.broadcasted_iota(jnp.int32, (RANK, LANES), 1)
    return jnp.where((lane & (RANK - 1)) == rank, 1.0, 0.0).astype(BF16)


def unfold(low_ref, length_ref, index_ref, rows):
    spread = dot_tn(low_ref[-RANK:, :rows], folding())
    return (spread * adapter_mask(length_ref, index_ref, rows, LANES)).astype(BF16)


def seen_block(first, begin, end):
    row = lax.broadcasted_iota(jnp.int32, (end - begin, end), 0) + begin
    key = lax.broadcasted_iota(jnp.int32, (end - begin, end), 1)
    seen = (key <= row) & (key >= first[begin:end])
    return jnp.concatenate([seen] * PER, axis=0)


def softmax_block(scores, seen):
    scores = jnp.where(seen, scores, -1e30)
    lifted = jnp.exp(scores - jnp.max(scores, axis=1, keepdims=True))
    return (lifted * (1.0 / jnp.sum(lifted, axis=1, keepdims=True))).astype(BF16)


def store_heads(columns, slot, blocks, q_s, k_s, v_s):
    scale = 1.0 / math.sqrt(HD)
    for at, column in enumerate(columns):
        halves = (column[:, :HD], pltpu.roll(column, HD, 1)[:, :HD])
        for piece, part in zip((2 * at, 2 * at + 1), halves):
            group, kind = divmod(piece, PER + 2)
            if kind == PER:
                k_s[slot + group] = part.astype(BF16)
            elif kind == PER + 1:
                v_s[slot + group] = part.astype(BF16)
            else:
                part = (part * scale).astype(BF16)
                for block, (begin, end) in enumerate(blocks):
                    size = end - begin
                    here = slice(kind * size, (kind + 1) * size)
                    q_s[slot + group, block, here, :] = part[begin:end]


def run_copies(pairs, sem):
    copies = [
        pltpu.make_async_copy(source, target, sem.at[number])
        for number, (source, target) in enumerate(pairs)
    ]
    for copy in copies:
        copy.start()
    for copy in copies:
        copy.wait()


def pack_kernel(
    n_exp, place_ref, gate, up, down, w_qkv, qkv_up, packed, share, held, share_s, sem, out_sem
):
    width = gate.shape[2]
    pairs = []
    for expert in range(gate.shape[0]):
        pairs.append((gate.at[expert], held.at[expert, :, :width]))
        pairs.append((up.at[expert], held.at[expert, :, width : 2 * width]))
        for at in range(D // LANES):
            lanes = slice(at * LANES, (at + 1) * LANES)
            pairs.append((down.at[expert, :, lanes], held.at[expert, lanes, 2 * width :]))
    qkv_rows, up_rows, _ = share_rows(n_exp, 0)
    own_qkv = pl.ds(pl.multiple_of(place_ref[0] * qkv_rows, 16), qkv_rows)
    own_up = pl.ds(pl.multiple_of(place_ref[0] * up_rows, 16), up_rows)
    pairs.append((w_qkv.at[own_qkv, :], share_s.at[:qkv_rows, :]))
    pairs.append((qkv_up.at[own_up, :], share_s.at[qkv_rows:, :]))
    run_copies(pairs, sem)
    run_copies([(held, packed), (share_s, share)], out_sem)


def share_rows(n_exp, heads_wide):
    return (D // n_exp, LANES // n_exp, heads_wide // n_exp)


def pack(place, w_gate, w_up, w_down, w_qkv, qkv_up, n_exp):
    count, _, width = w_gate.shape
    packed = shape((count, D, 3 * width), BF16)
    share = shape(((D + LANES) // n_exp, w_qkv.shape[1]), BF16)
    return pl.pallas_call(
        functools.partial(pack_kernel, n_exp),
        in_specs=[IN_SMEM] + [IN_HBM] * 5,
        out_specs=[IN_HBM] * 2,
        out_shape=[packed, share],
        scratch_shapes=[
            pltpu.VMEM(packed.shape, BF16),
            pltpu.VMEM(share.shape, BF16),
            pltpu.SemaphoreType.DMA((count * (2 + D // LANES) + 2,)),
            pltpu.SemaphoreType.DMA((2,)),
        ],
        compiler_params=WHOLE_VMEM,
        cost_estimate=cost(0, 2 * 2 * count * D * 3 * width),
        name="pack_weights",
    )(place, w_gate, w_up, w_down, w_qkv, qkv_up)


class Loads:
    def __init__(self, names, sources, targets, sem):
        self.copies = {}
        for number, (name, source, target) in enumerate(zip(names, sources, targets)):
            if source.shape[0] == TOK_DEV + RANK:
                source = source.at[TOK_DEV:]
            elif source.shape != target.shape:
                source = source.at[: target.shape[0]]
            self.copies[name] = pltpu.make_async_copy(source, target, sem.at[number])
        self.targets = dict(zip(names, targets))
        for copy in self.copies.values():
            copy.start()

    def __getitem__(self, name):
        copy = self.copies.pop(name, None)
        if copy is not None:
            copy.wait()
        return self.targets[name]


def load_scratch(arrays, rows=TOK_DEV):
    kept = {TOK_DEV: rows, TOK_DEV + RANK: RANK}
    rooms = []
    for array in arrays:
        first = kept.get(array.shape[0], array.shape[0])
        rooms.append(pltpu.VMEM((first,) + array.shape[1:], array.dtype))
    return rooms + [pltpu.SemaphoreType.DMA((len(arrays),))]


FORWARD_LOADS = (
    "tokens", "gains", "qkv_down", "w_qkv", "qkv_up", "cosine", "sine", "w_out", "out_down",
)


def forward_kernel(place_ref, length_ref, index_ref, *refs):
    count = len(FORWARD_LOADS)
    attn_in_ref, low_q_ref, head_ref, base_ref, share_ref = refs[count : count + 5]
    load_sem, q_s, k_s, v_s = refs[2 * count + 5 :]
    loads = Loads(FORWARD_LOADS, refs[:count], refs[count + 5 : 2 * count + 5], load_sem)
    rows = attn_in_ref.shape[0]
    groups = k_s.shape[0]
    mask = adapter_mask(length_ref, index_ref, rows, LANES)
    first = first_keys(length_ref, rows)
    inputs = loads["tokens"][...].astype(F32)
    inv_root = lax.rsqrt(jnp.mean(inputs * inputs, axis=1, keepdims=True) + EPS)
    attn_in_ref[...] = (inputs * inv_root * loads["gains"][0:1, :]).astype(BF16)
    attn_in = attn_in_ref[...]
    low_q = (dot(attn_in, loads["qkv_down"][...]) * mask).astype(BF16)
    low_q_ref[...] = low_q
    projected = dot(attn_in, loads["w_qkv"][...]) + dot(low_q, loads["qkv_up"][...])
    cosine, sine = loads["cosine"][...], loads["sine"][...]
    columns = turn(projected, cosine, sine, turned_pieces(groups))
    store_heads(columns, 0, BLOCKS, q_s, k_s, v_s)
    for block, (begin, end) in enumerate(BLOCKS):
        seen = seen_block(first, begin, end)
        scores = [dot_nt(q_s[group, block], k_s[group, :end, :]) for group in range(groups)]
        probs = [softmax_block(part, seen) for part in scores]
        heads = []
        for group in range(groups):
            out = dot(probs[group], v_s[group, :end, :])
            heads += [out[head * ROWS : (head + 1) * ROWS] for head in range(PER)]
        head_ref[begin:end, :] = jnp.concatenate(heads, axis=1).astype(BF16)
    head_out = head_ref[...]
    base_ref[:rows, :] = dot(head_out, loads["w_out"][...]).astype(BF16)
    low_o = (dot(head_out, loads["out_down"][...]) * mask).astype(BF16)
    base_ref[rows:, :rows] = dot_nt(folding(), low_o).astype(BF16)
    base_ref[rows:, rows:] = jnp.zeros((RANK, D - rows), BF16)
    share_rows_count = share_ref.shape[0]
    own = pl.ds(pl.multiple_of(place_ref[0] * share_rows_count, 16), share_rows_count)
    share_ref[:, :D] = loads["w_out"][own, :]
    share_ref[:, D:] = loads["out_down"][own, :]


def forward(
    place, lengths, index, tokens, gains, w_qkv, qkv_down, qkv_up, w_out, out_down, tables, n_exp
):
    rows = tokens.shape[0]
    heads_wide = w_out.shape[0]
    groups = w_qkv.shape[1] // (HD * (PER + 2))
    arrays = (tokens, gains, qkv_down, w_qkv, qkv_up) + tables + (w_out, out_down)
    return pl.pallas_call(
        forward_kernel,
        in_specs=[IN_SMEM] * 3 + [IN_HBM] * len(arrays),
        out_specs=[IN_VMEM] * 5,
        out_shape=[
            shape((rows, D), BF16),
            shape((rows, LANES), BF16),
            shape((rows, heads_wide), BF16),
            shape((rows + RANK, D), BF16),
            shape((heads_wide // n_exp, D + LANES), BF16),
        ],
        scratch_shapes=load_scratch(arrays)
        + [
            pltpu.VMEM((groups, rows // ROWS, PER * ROWS, HD), BF16),
            pltpu.VMEM((groups, rows, HD), BF16),
            pltpu.VMEM((groups, rows, HD), BF16),
        ],
        compiler_params=WHOLE_VMEM,
        cost_estimate=cost(6e9, 10e6),
        name="attention_forward",
    )(place, lengths, index, *arrays)


def down_of(weight, width):
    columns = [
        weight[at * LANES : (at + 1) * LANES, 2 * width : 3 * width] for at in range(D // LANES)
    ]
    return jnp.concatenate(columns, axis=1)


def experts_kernel(
    length_ref, index_ref, tokens_ref, base_ref, out_up_ref, gains_ref, router_ref, bias_ref,
    cot_ref, weight_ref, residual_ref, hidden_ref, grad_ref,
    normed_s, gates_s, part_s, grad_s,
):
    step = pl.program_id(0)
    count, _, packed = weight_ref.shape
    width = packed // 3
    lane = lax.broadcasted_iota(jnp.int32, gates_s.shape, 1)

    @pl.when(step == 0)
    def _():
        residual = (
            tokens_ref[...].astype(F32)
            + base_ref[:TOK_DEV, :].astype(F32)
            + dot(unfold(base_ref, length_ref, index_ref, TOK_DEV), out_up_ref[...])
        )
        residual_ref[...] = residual.astype(BF16)
        inv_root = lax.rsqrt(jnp.mean(residual * residual, axis=1, keepdims=True) + EPS)
        normed = (residual * inv_root * gains_ref[1:2, :]).astype(BF16)
        normed_s[...] = normed
        logits = dot_nt(normed, router_ref[...]) + bias_ref[...]
        lifted = jnp.exp(logits - jnp.max(logits, axis=1, keepdims=True))
        gates_s[...] = lifted / jnp.sum(lifted, axis=1, keepdims=True)
        part_s[...] = jnp.zeros_like(part_s)
        grad_s[...] = jnp.zeros_like(grad_s)

    normed = normed_s[...]
    cot = cot_ref[...]
    gates = gates_s[...]
    part = jnp.zeros(part_s.shape, F32)
    grads = []
    for pair in range(0, count, 2):
        pair_down = [down_of(weight_ref.at[pair + half], width) for half in range(2)]
        pair_raw = dot_nt(cot, jnp.concatenate(pair_down, axis=0))
        for half in range(2):
            expert = pair + half
            joined = dot(normed, weight_ref[expert, :, : 2 * width])
            pre_gate = joined[:, :width]
            pre_up = joined[:, width:]
            raw = pair_raw[:, half * width : (half + 1) * width]
            sigmoid = 0.5 * jnp.tanh(0.5 * pre_gate) + 0.5
            activated = pre_gate * sigmoid
            value = activated * pre_up
            here = lane == step * count + expert
            gate = jnp.sum(jnp.where(here, gates, 0.0), axis=1, keepdims=True)
            hidden_ref[:, expert * width : (expert + 1) * width] = (gate * value).astype(BF16)
            gate_grad = jnp.sum(value[:LIVE] * raw, axis=1, keepdims=True)
            part += jnp.where(here[:LIVE], gate_grad, 0.0)
            inner = raw * gate[:LIVE]
            sigmoid, activated = sigmoid[:LIVE], activated[:LIVE]
            slope = sigmoid + activated * (1.0 - sigmoid)
            grads.append((inner * pre_up[:LIVE] * slope).astype(BF16))
            grads.append((inner * activated).astype(BF16))
    part_s[...] += part
    ups = [weight_ref[expert, :, : 2 * width] for expert in range(count)]
    grad_s[...] += dot_nt(jnp.concatenate(grads, axis=1), jnp.concatenate(ups, axis=1))

    @pl.when(step == pl.num_programs(0) - 1)
    def _():
        live_gates, gate_part = gates[:LIVE], part_s[...]
        spread = jnp.sum(live_gates * gate_part, axis=1, keepdims=True)
        logit_grad = (live_gates * (gate_part - spread)).astype(BF16)
        grad_ref[...] = (grad_s[...] + dot(logit_grad, router_ref[...])).astype(BF16)


def experts_both(
    lengths, index, tokens, base, out_up, gains, router, bias, cot, weights, count=4,
):
    rows = tokens.shape[0]
    experts, _, packed = weights.shape
    width = packed // 3
    arrays = (tokens, base, out_up, gains, router.T, bias, cot)
    in_specs = [IN_SMEM] * 2
    in_specs += [pl.BlockSpec(array.shape, lambda step: (0, 0)) for array in arrays]
    in_specs.append(pl.BlockSpec((count, D, packed), lambda step: (step, 0, 0)))
    return pl.pallas_call(
        experts_kernel,
        grid=(experts // count,),
        in_specs=in_specs,
        out_specs=[
            pl.BlockSpec((rows, D), lambda step: (0, 0)),
            pl.BlockSpec((rows, count * width), lambda step: (0, step)),
            pl.BlockSpec((LIVE, D), lambda step: (0, 0)),
        ],
        out_shape=[
            shape((rows, D), BF16),
            shape((rows, experts * width), BF16),
            shape((LIVE, D), BF16),
        ],
        scratch_shapes=[
            pltpu.VMEM((rows, D), BF16),
            pltpu.VMEM((rows, experts), F32),
            pltpu.VMEM((LIVE, experts), F32),
            pltpu.VMEM((LIVE, D), F32),
        ],
        compiler_params=WHOLE_VMEM,
        cost_estimate=cost(0, 1000),
        name="experts",
    )(lengths, index, *arrays, weights)


def combine_kernel(
    place_ref, hidden_hbm, residual_hbm, weights_hbm, moe_ref, hidden_s, residual_s, downs_s,
    hidden_sem, residual_sem, sem,
):
    experts, _, width = downs_s.shape
    load = pltpu.make_async_copy(hidden_hbm, hidden_s, hidden_sem)
    load.start()
    residual_load = pltpu.make_async_copy(residual_hbm, residual_s, residual_sem)
    residual_load.start()
    own = jnp.where(place_ref[0] == 0, 1.0, 0.0).astype(F32)
    copies = []
    for expert in range(experts):
        source, target = weights_hbm.at[expert, :, 2 * width :], downs_s.at[expert]
        copies.append(pltpu.make_async_copy(source, target, sem.at[expert]))
        copies[-1].start()
    load.wait()
    residual_load.wait()
    for copy in copies:
        copy.wait()
    for at in range(0, D, 2 * LANES):
        columns = []
        for expert in range(experts):
            pieces = [
                downs_s[expert, at + left : at + left + LANES, :] for left in (0, LANES)
            ]
            columns.append(jnp.concatenate(pieces, axis=1))
        moe = dot(hidden_s[...], jnp.concatenate(columns, axis=0))
        here = slice(at, at + 2 * LANES)
        moe_ref[:, here] = (moe + own * residual_s[:, here].astype(F32)).astype(BF16)


def combine(place, hidden, residual, weights):
    rows = hidden.shape[0]
    experts, _, packed = weights.shape
    return pl.pallas_call(
        combine_kernel,
        in_specs=[IN_SMEM] + [IN_HBM] * 3,
        out_specs=IN_VMEM,
        out_shape=shape((rows, D), BF16),
        scratch_shapes=[
            pltpu.VMEM(hidden.shape, BF16),
            pltpu.VMEM(residual.shape, BF16),
            pltpu.VMEM((experts, D, packed // 3), BF16),
            pltpu.SemaphoreType.DMA(()),
            pltpu.SemaphoreType.DMA(()),
            pltpu.SemaphoreType.DMA((experts,)),
        ],
        compiler_params=WHOLE_VMEM,
        cost_estimate=cost(4e9, 10e6),
        name="combine",
    )(place, hidden, residual, weights)


def norm_back(vectors, gain, upstream):
    inv_root = lax.rsqrt(jnp.mean(vectors * vectors, axis=1, keepdims=True) + EPS)
    weighted = upstream * gain
    slope = jnp.mean(vectors * weighted, axis=1, keepdims=True)
    return inv_root * weighted - vectors * (inv_root * inv_root * inv_root) * slope


BRANCH_LOADS = (
    "residual", "normed_grad", "gains", "cot", "out_up", "low_o", "head",
)


def branch_kernel(length_ref, index_ref, *refs):
    count = len(BRANCH_LOADS)
    branch_grad_ref, low_grad_ref, part_ref = refs[count : count + 3]
    scratch = refs[count + 3 :]
    loads = Loads(BRANCH_LOADS, refs[:count], scratch[:count], scratch[count])
    mask = adapter_mask(length_ref, index_ref, LIVE, LANES)
    residual = loads["residual"][...].astype(F32)
    through = norm_back(residual, loads["gains"][1:2, :], loads["normed_grad"][...].astype(F32))
    branch_grad_ref[...] = (through + loads["cot"][...].astype(F32)).astype(BF16)
    branch_grad = branch_grad_ref[...]
    low_grad_ref[...] = (dot_nt(branch_grad, loads["out_up"][...]) * mask).astype(BF16)
    low_o = unfold(loads["low_o"], length_ref, index_ref, LIVE)
    out_up_part = dot_tn(low_o, branch_grad).astype(BF16)
    for at in range(D // LANES):
        lanes = slice(at * LANES, (at + 1) * LANES)
        part_ref[lanes, :] = out_up_part[:, lanes]
    part_ref[D:, :] = dot_tn(loads["head"][...], low_grad_ref[...]).astype(BF16)


def branch_back(
    lengths, index, residual, base, normed_grad, cot, gains, out_up, head
):
    arrays = (residual, normed_grad, gains, cot, out_up, base, head)
    return pl.pallas_call(
        branch_kernel,
        in_specs=[IN_SMEM] * 2 + [IN_HBM] * len(arrays),
        out_specs=[IN_VMEM] * 3,
        out_shape=[
            shape((LIVE, D), BF16),
            shape((LIVE, LANES), BF16),
            shape((D + head.shape[1], LANES), BF16),
        ],
        scratch_shapes=load_scratch(arrays, LIVE),
        compiler_params=WHOLE_VMEM,
        cost_estimate=cost(1e9, 2e6),
        name="branch_backward",
    )(lengths, index, *arrays)


def share_copies(place_ref, shares, w_qkv_s, sem):
    n_exp, n_tp, _, _ = shares.shape
    qkv_rows, up_rows, _ = share_rows(n_exp, 0)
    copies = []
    for z in range(n_tp):
        here = []
        source_z = from_place(place_ref, z, n_tp)
        for e in range(n_exp):
            at = e * qkv_rows
            up_at = D + e * up_rows
            for source, target in (
                (shares.at[e, source_z, :qkv_rows, :], w_qkv_s.at[z, at : at + qkv_rows, :]),
                (shares.at[e, source_z, qkv_rows:, :], w_qkv_s.at[z, up_at : up_at + up_rows, :]),
            ):
                number = 2 * e + len(here) % 2
                here.append(pltpu.make_async_copy(source, target, sem.at[z, number]))
        copies.append(here)
    for here in copies:
        for copy in here:
            copy.start()
    return copies


PREPARE_LOADS = ("attn_in", "low_q", "cosine", "sine")


def prepare_kernel(place_ref, length_ref, shares, *refs):
    count = len(PREPARE_LOADS)
    results = 1 + len(LIVE_BLOCKS)
    turned_ref = refs[count]
    prob_refs = refs[count + 1 : count + results]
    load_sem, w_qkv_s, q_s, k_s, v_s, sem = refs[2 * count + results :]
    targets = refs[count + results : 2 * count + results]
    loads = Loads(PREPARE_LOADS, refs[:count], targets, load_sem)
    n_tp = shares.shape[1]
    groups = k_s.shape[0]
    copies = share_copies(place_ref, shares, w_qkv_s, sem)
    first = first_keys(length_ref, LIVE)
    attn_in = loads["attn_in"][...]
    low_q = loads["low_q"][...]
    cosine, sine = loads["cosine"][...], loads["sine"][...]
    seen = [seen_block(first, begin, end) for begin, end in LIVE_BLOCKS]
    for here in copies:
        for copy in here:
            copy.wait()

    def one_place(z, carried):
        projected = dot(attn_in, w_qkv_s[z, :D, :]) + dot(low_q, w_qkv_s[z, D:, :])
        columns = turn(projected, cosine, sine, turned_pieces(groups))
        for at, column in enumerate(columns):
            turned_ref[z, :, at * LANES : (at + 1) * LANES] = column.astype(BF16)
        store_heads(columns, 0, LIVE_BLOCKS, q_s, k_s, v_s)
        for group in range(groups):
            for block, (begin, end) in enumerate(LIVE_BLOCKS):
                query = q_s[group, block, : PER * (end - begin), :]
                scores = dot_nt(query, k_s[group, :end, :])
                prob_refs[block][z * groups + group] = softmax_block(scores, seen[block])
        return carried

    lax.fori_loop(0, n_tp, one_place, 0)


def prepare(place, lengths, attn_in, low_q, tables, shares):
    n_exp, n_tp, _, wide = shares.shape
    arrays = (attn_in, low_q) + tables
    groups = KV_HEADS
    probs = [
        shape((groups, PER * (end - begin), end), BF16) for begin, end in LIVE_BLOCKS
    ]
    return pl.pallas_call(
        prepare_kernel,
        in_specs=[IN_SMEM] * 2 + [IN_HBM] * (1 + len(arrays)),
        out_specs=[IN_VMEM] * (1 + len(probs)),
        out_shape=[shape((n_tp, LIVE, wide), BF16)] + probs,
        scratch_shapes=load_scratch(arrays, LIVE)
        + [
            pltpu.VMEM((n_tp, D + LANES, wide), BF16),
            pltpu.VMEM((groups // n_tp, len(LIVE_BLOCKS), PER * ROWS, HD), BF16),
            pltpu.VMEM((groups // n_tp, LIVE, HD), BF16),
            pltpu.VMEM((groups // n_tp, LIVE, HD), BF16),
            pltpu.SemaphoreType.DMA((n_tp, 2 * n_exp)),
        ],
        compiler_params=WHOLE_VMEM,
        cost_estimate=cost(12e9, 30e6),
        name="prepare_heads",
    )(place, lengths, shares, *arrays)


HEADS_LOADS = (
    "branch_grad", "low_o_grad", "turned", "cosine", "sine", "low_q", "attn_in",
)


def heads_back_kernel(place_ref, length_ref, index_ref, shares, out_shares, *refs):
    count = len(HEADS_LOADS)
    blocks = len(LIVE_BLOCKS)
    probs_hbm = refs[count : count + blocks]
    grad_ref, low_grad_ref, part_ref = refs[count + blocks : count + blocks + 3]
    scratch = refs[count + blocks + 3 :]
    loads = Loads(HEADS_LOADS, refs[:count], scratch[:count], scratch[count])
    up_s, w_out_s, g_s, q_s, k_s, v_s, up_sem, out_sem, prob_sem = scratch[count + 1 : count + 10]
    probs_s = scratch[count + 10 :]
    n_exp, n_tp, _, wide = shares.shape
    groups = g_s.shape[0]
    flags = turned_pieces(groups)
    scale = 1.0 / math.sqrt(HD)

    def prob_copy(z, block):
        here = pl.ds(z * groups, groups)
        return pltpu.make_async_copy(
            probs_hbm[block].at[here], probs_s[block].at[here], prob_sem.at[z, block]
        )

    out_rows = out_shares.shape[2]

    def out_copy(z, e):
        return pltpu.make_async_copy(
            out_shares.at[e, from_place(place_ref, z, n_tp)],
            w_out_s.at[z, e * out_rows : (e + 1) * out_rows, :],
            out_sem.at[z, e],
        )

    for z in range(n_tp):
        for e in range(n_exp):
            out_copy(z, e).start()
        for block in range(blocks):
            prob_copy(z, block).start()
    qkv_rows, up_rows, _ = share_rows(n_exp, 0)
    up_copies = []
    for z in range(n_tp):
        for e in range(n_exp):
            source = shares.at[e, from_place(place_ref, z, n_tp), qkv_rows:, :]
            target = up_s.at[z, e * up_rows : (e + 1) * up_rows, :]
            up_copies.append(pltpu.make_async_copy(source, target, up_sem.at[z, e]))
            up_copies[-1].start()
    branch_grad, low_o_grad = loads["branch_grad"], loads["low_o_grad"]
    turned = loads["turned"]
    cosine, sine = loads["cosine"], loads["sine"]

    def one_place(z, carried):
        columns = [
            turned[z, :, at * LANES : (at + 1) * LANES].astype(F32) for at in range(wide // LANES)
        ]
        store_heads(columns, 0, LIVE_BLOCKS, q_s, k_s, v_s)
        for e in range(n_exp):
            out_copy(z, e).wait()
        head_grad = (
            dot_nt(branch_grad[...], w_out_s[z, :, :D]) + dot_nt(low_o_grad[...], w_out_s[z, :, D:])
        ).astype(BF16)
        for head in range(groups * PER):
            group, kind = divmod(head, PER)
            part = head_grad[:, head * HD : (head + 1) * HD]
            for block, (begin, end) in enumerate(LIVE_BLOCKS):
                size = end - begin
                here = slice(kind * size, (kind + 1) * size)
                g_s[group, block, here, :] = part[begin:end]
        for block in range(blocks):
            prob_copy(z, block).wait()
        key_grads = [jnp.zeros((HD, LIVE), F32) for _ in range(groups)]
        value_grads = [jnp.zeros((HD, LIVE), F32) for _ in range(groups)]
        query_grads = [[] for _ in range(groups)]
        for block, (begin, end) in enumerate(LIVE_BLOCKS):
            size = end - begin

            def widen(part):
                if end == LIVE:
                    return part
                return jnp.concatenate([part, jnp.zeros((HD, LIVE - end), F32)], axis=1)

            some = range(groups)
            queries = [q_s[group, block, : PER * size, :] for group in some]
            head_grads = [g_s[group, block, : PER * size, :] for group in some]
            probs = [probs_s[block][z * groups + group] for group in some]
            weight_grads = [dot_nt(head_grads[group], v_s[group, :end, :]) for group in some]
            for group in some:
                value_grads[group] += widen(dot_tn(head_grads[group], probs[group]))
            wide_probs = [probs[group].astype(F32) for group in some]
            score_grads = []
            for group in some:
                product = wide_probs[group] * weight_grads[group]
                spread = jnp.sum(product, axis=1, keepdims=True)
                score_grads.append((product - wide_probs[group] * spread).astype(BF16))
            for group in some:
                score_grad = score_grads[group]
                query_grads[group].append(dot(score_grad, k_s[group, :end, :]) * scale)
                key_grads[group] += widen(dot_tn(queries[group], score_grad))
        pieces = []
        for group in range(groups):
            for head in range(PER):
                rows = [
                    part[head * (end - begin) : (head + 1) * (end - begin)]
                    for part, (begin, end) in zip(query_grads[group], LIVE_BLOCKS)
                ]
                pieces.append(jnp.concatenate(rows, axis=0))
            pieces += [key_grads[group].T, value_grads[group].T]
        joined = jnp.concatenate(pieces, axis=1)
        columns = turn(joined, cosine[...], -sine[...], flags)
        for at, column in enumerate(columns):
            grad_ref[z, :, at * LANES : (at + 1) * LANES] = column.astype(BF16)
        return carried

    lax.fori_loop(0, n_tp, one_place, 0)
    for copy in up_copies:
        copy.wait()
    low_grad = dot_nt(grad_ref[0], up_s[0])
    for z in range(1, n_tp):
        low_grad += dot_nt(grad_ref[z], up_s[z])
    mask = adapter_mask(length_ref, index_ref, LIVE, LANES)
    low_grad = (low_grad * mask).astype(BF16)
    low_grad_ref[...] = low_grad
    part_ref[:D, :] = dot_tn(loads["attn_in"][...], low_grad).astype(BF16)
    up_part = dot_tn(loads["low_q"][...], grad_ref[place_ref[0]]).astype(BF16)
    for at in range(wide // LANES):
        lanes = slice(at * LANES, (at + 1) * LANES)
        part_ref[D + at * LANES : D + (at + 1) * LANES, :] = up_part[:, lanes]


def heads_back(
    place, lengths, index, attn_in, low_q, heads, branch_grad, low_o_grad, tables, shares, out_shares
):
    n_exp, n_tp, _, wide = shares.shape
    blocks = len(LIVE_BLOCKS)
    turned, probs = heads[0], heads[1:]
    groups = KV_HEADS // n_tp
    heads_wide = groups * PER * HD
    arrays = (branch_grad, low_o_grad, turned) + tables + (low_q, attn_in)
    return pl.pallas_call(
        heads_back_kernel,
        in_specs=[IN_SMEM] * 3 + [IN_HBM] * (2 + len(arrays) + blocks),
        out_specs=[IN_VMEM] * 3,
        out_shape=[
            shape((n_tp, LIVE, wide), BF16),
            shape((LIVE, LANES), BF16),
            shape((D + wide, LANES), BF16),
        ],
        scratch_shapes=load_scratch(arrays, LIVE)
        + [
            pltpu.VMEM((n_tp, LANES, wide), BF16),
            pltpu.VMEM((n_tp, heads_wide, D + LANES), BF16),
            pltpu.VMEM((groups, blocks, PER * ROWS, HD), BF16),
            pltpu.VMEM((groups, blocks, PER * ROWS, HD), BF16),
            pltpu.VMEM((groups, LIVE, HD), BF16),
            pltpu.VMEM((groups, LIVE, HD), BF16),
            pltpu.SemaphoreType.DMA((n_tp, n_exp)),
            pltpu.SemaphoreType.DMA((n_tp, n_exp)),
            pltpu.SemaphoreType.DMA((n_tp, blocks)),
        ]
        + [pltpu.VMEM(part.shape, BF16) for part in probs],
        compiler_params=WHOLE_VMEM,
        cost_estimate=cost(2e9, 3e6),
        name="heads_backward",
    )(place, lengths, index, shares, out_shares, *arrays, *probs)


INPUT_LOADS = ("grads", "low_grad", "qkv_down", "tokens", "gains", "branch_grad")


def input_back_kernel(place_ref, shares, *refs):
    count = len(INPUT_LOADS)
    input_grad_ref = refs[count]
    load_sem, w_qkv_s, sum_s, sem = refs[2 * count + 1 :]
    n_exp, n_tp, _, _ = shares.shape
    qkv_rows, _, _ = share_rows(n_exp, 0)
    copies = []
    for z in range(n_tp):
        for e in range(n_exp):
            source = shares.at[e, from_place(place_ref, z, n_tp), :qkv_rows, :]
            target = w_qkv_s.at[z, e * qkv_rows : (e + 1) * qkv_rows, :]
            copies.append(pltpu.make_async_copy(source, target, sem.at[z, e]))
    loads = Loads(INPUT_LOADS, refs[:count], refs[count + 1 : 2 * count + 1], load_sem)
    for copy in copies:
        copy.start()
    input_grad_ref[LIVE:, :] = jnp.zeros((input_grad_ref.shape[0] - LIVE, D), BF16)
    grads = loads["grads"]
    sum_s[...] = dot_nt(loads["low_grad"][...], loads["qkv_down"][...])
    for z in range(n_tp):
        for copy in copies[z * n_exp : (z + 1) * n_exp]:
            copy.wait()
        sum_s[...] += dot_nt(grads[z], w_qkv_s[z])
    tokens, gain = loads["tokens"][...].astype(F32), loads["gains"][0:1, :]
    through = norm_back(tokens, gain, sum_s[...])
    input_grad_ref[:LIVE, :] = (loads["branch_grad"][...].astype(F32) + through).astype(BF16)


def input_back(place, grads, low_grad, qkv_down, tokens, gains, branch_grad, shares):
    n_exp, n_tp, _, wide = shares.shape
    arrays = (grads, low_grad, qkv_down, tokens, gains, branch_grad)
    return pl.pallas_call(
        input_back_kernel,
        in_specs=[IN_SMEM] + [IN_HBM] * (1 + len(arrays)),
        out_specs=IN_VMEM,
        out_shape=shape(tokens.shape, BF16),
        scratch_shapes=load_scratch(arrays, LIVE)
        + [
            pltpu.VMEM((n_tp, D, wide), BF16),
            pltpu.VMEM((LIVE, D), F32),
            pltpu.SemaphoreType.DMA((n_tp, n_exp)),
        ],
        compiler_params=WHOLE_VMEM,
        cost_estimate=cost(2e9, 2e6),
        name="input_backward",
    )(place, shares, *arrays)


FINISH_LOADS = ("output", "qkv_sum", "out_parts")


def finish_kernel(*refs):
    count = len(FINISH_LOADS)
    output_hbm, qkv_down_ref, qkv_up_ref, out_down_ref, out_up_ref = refs[count : count + 5]
    scratch = refs[count + 5 :]
    loads = Loads(FINISH_LOADS, refs[:count], scratch[:count], scratch[count])
    handed_on = pltpu.make_async_copy(loads["output"], output_hbm, scratch[count + 1])
    handed_on.start()
    qkv_sum = loads["qkv_sum"]
    qkv_down_ref[...] = qkv_sum[:D, :].astype(F32)
    for at in range(0, qkv_up_ref.shape[1], LANES):
        qkv_up_ref[:, at : at + LANES] = qkv_sum[D + at : D + at + LANES, :].astype(F32)
    out_parts = loads["out_parts"]
    for at in range(0, out_parts.shape[1], LANES):
        total = out_parts[0, at : at + LANES, :].astype(F32)
        for part in range(1, out_parts.shape[0]):
            total += out_parts[part, at : at + LANES, :].astype(F32)
        if at < D:
            out_up_ref[:, at : at + LANES] = total
        else:
            out_down_ref[at - D : at - D + LANES, :] = total
    handed_on.wait()


def finish(output, out_parts, qkv_sum):
    arrays = (output, qkv_sum, out_parts)
    return pl.pallas_call(
        finish_kernel,
        in_specs=[IN_HBM] * len(arrays),
        out_specs=[IN_HBM] + [IN_VMEM] * 4,
        out_shape=[
            shape(output.shape, BF16),
            shape((D, LANES), F32),
            shape((LANES, qkv_sum.shape[0] - D), F32),
            shape((out_parts.shape[1] - D, LANES), F32),
            shape((LANES, D), F32),
        ],
        scratch_shapes=load_scratch(arrays) + [pltpu.SemaphoreType.DMA(())],
        compiler_params=WHOLE_VMEM,
        cost_estimate=cost(0, 6e6),
        name="finish",
    )(*arrays)


def from_tp(share, count):
    around = [share]
    for shift in range(1, count):
        around.append(
            lax.ppermute(share, "tp", [(at, (at + shift) % count) for at in range(count)])
        )
    return around


def from_place(place_ref, z, count):
    return lax.rem(place_ref[0] - z + count, count)


def kernel_body(
    tokens, attn_gain, moe_gain, w_qkv, w_out, w_router, w_gate, w_up, w_down, qkv_down, qkv_up,
    out_down, out_up, lengths, adapter_index, loss_mask, routes, upstream,
):
    n_exp = lax.axis_size("exp")
    n_tp = lax.axis_size("tp")
    exp_place = lax.axis_index("exp").astype(jnp.int32).reshape(1)
    tp_place = lax.axis_index("tp").astype(jnp.int32).reshape(1)
    tables = turn_tables(tokens.shape[0])
    gains = jnp.stack([attn_gain, moe_gain])

    own_experts, own_qkv = pack(exp_place, w_gate, w_up, w_down, w_qkv, qkv_up, n_exp)
    weights = lax.all_gather(own_experts, "exp", axis=0, tiled=True)
    z_qkv = from_tp(own_qkv, n_tp)
    inputs, _ = lax.optimization_barrier((tokens, own_qkv))
    attn_in, low_q, head, base, own_out = forward(
        exp_place, lengths, adapter_index, inputs, gains, w_qkv, qkv_down, qkv_up, w_out, out_down,
        tables, n_exp,
    )
    live_loss = lax.slice_in_dim(loss_mask, 0, LIVE)
    cot = jnp.where(live_loss[:, None] > 0, upstream[:LIVE], jnp.zeros((), BF16))
    expert = jnp.arange(w_router.shape[1], dtype=jnp.int32)
    routed = jnp.any(routes[:, :, None] == expert[None, None, :], axis=1)
    bias = jnp.where(routed, 0.0, -1e30).astype(F32)
    base, z_qkv, cot, bias = lax.optimization_barrier((base, z_qkv, cot, bias))
    z_qkv = jnp.stack(z_qkv)
    base = lax.psum(base, "tp")
    own_out, _ = lax.optimization_barrier((own_out, base))
    z_out = from_tp(own_out, n_tp)
    z_qkv, _ = lax.optimization_barrier((z_qkv, weights))
    qkv_shares = lax.all_gather(z_qkv, "exp", axis=0)

    residual, hidden, normed_part = experts_both(
        lengths, adapter_index, tokens, base, out_up, gains, w_router, bias, cot, weights
    )
    normed_part, z_out = lax.optimization_barrier((normed_part, z_out))
    z_out = jnp.stack(z_out)
    normed_grad = lax.psum(normed_part, "tp")
    z_out, _ = lax.optimization_barrier((z_out, qkv_shares))
    out_shares = lax.all_gather(z_out, "exp", axis=0)
    late_in, _ = lax.optimization_barrier((attn_in, normed_part))
    heads = prepare(tp_place, lengths, late_in, low_q, tables, qkv_shares)

    moe_part, normed_grad, _ = lax.optimization_barrier(
        (combine(tp_place, hidden, residual, weights), normed_grad, heads[0])
    )
    output = lax.psum(moe_part, "tp")
    branch_grad, low_o_grad, out_part = branch_back(
        lengths, adapter_index, residual, base, normed_grad, cot, gains, out_up, head
    )
    out_parts = lax.all_gather(out_part, "exp", axis=0)
    grads, low_grad, qkv_part = heads_back(
        tp_place, lengths, adapter_index, attn_in, low_q, heads, branch_grad, low_o_grad, tables,
        qkv_shares, out_shares,
    )
    share = qkv_part.shape[0] // n_exp
    parts = lax.all_to_all(qkv_part.reshape(n_exp, share, LANES), "exp", 0, 0, tiled=True)
    input_grad = input_back(
        tp_place, grads, low_grad, qkv_down, tokens, gains, branch_grad, qkv_shares
    )
    parts, input_grad = lax.optimization_barrier((parts, input_grad))
    qkv_sum = jnp.sum(parts.astype(F32), axis=0).astype(BF16)
    qkv_sum = lax.all_gather(qkv_sum, "exp", axis=0, tiled=True)
    out_parts, output, _ = lax.optimization_barrier((out_parts, output, qkv_sum))
    output, *adapters = finish(output, out_parts, qkv_sum)
    return (output, input_grad) + tuple(adapters)


def product(left_m, right_m):
    return jnp.dot(left_m, right_m, preferred_element_type=jnp.float32)


def contract(einsum_form, left_m, right_m):
    return jnp.einsum(einsum_form, left_m, right_m, preferred_element_type=jnp.float32)


def rms_norm(vectors, gain_vec):
    inv_root = lax.rsqrt(jnp.mean(vectors * vectors, axis=-1, keepdims=True) + EPS)
    return vectors * inv_root * gain_vec


def rms_norm_back(vectors, gain_vec, upstream_grad):
    inv_root = lax.rsqrt(jnp.mean(vectors * vectors, axis=-1, keepdims=True) + EPS)
    weighted = upstream_grad * gain_vec
    return inv_root * weighted - vectors * (inv_root * inv_root * inv_root) * jnp.mean(
        vectors * weighted, axis=-1, keepdims=True
    )


def layout(length_row, index_row):
    places = jnp.arange(TOK_DEV, dtype=jnp.int32)
    doc_ends = jnp.cumsum(length_row)
    doc_starts = doc_ends - length_row
    member = (places[:, None] >= doc_starts[None, :]) & (places[:, None] < doc_ends[None, :])
    occupied = jnp.any(member, axis=1)
    position = jnp.sum(jnp.where(member, places[:, None] - doc_starts[None, :], 0), axis=1)
    owner_doc = jnp.sum(jnp.where(member, jnp.arange(DOCS, dtype=jnp.int32)[None, :], 0), axis=1)
    doc_ident = jnp.where(occupied, owner_doc, DOCS + places)
    chosen = jnp.sum(jnp.where(member, index_row[None, :], 0), axis=1)
    adapter_pick = occupied[:, None] & (
        chosen[:, None] == jnp.arange(ADAPTERS, dtype=jnp.int32)[None, :]
    )
    rank_mask = jnp.repeat(jnp.where(adapter_pick, 1.0, 0.0).astype(jnp.float32), RANK, axis=1)
    return (occupied, position, doc_ident, rank_mask)


def angles(position):
    half_width = HD // 2
    frequency = jnp.exp(-math.log(ROPE_BASE) * jnp.arange(half_width, dtype=jnp.float32) * 2.0 / HD)
    turned = position.astype(jnp.float32)[:, None] * frequency[None, :]
    return (jnp.cos(turned), jnp.sin(turned))


def rotate(vectors, cosine, sine_table):
    half_width = vectors.shape[-1] // 2
    front_half = vectors[..., :half_width]
    back_half = vectors[..., half_width:]
    return jnp.concatenate(
        [
            front_half * cosine - back_half * sine_table,
            back_half * cosine + front_half * sine_table,
        ],
        axis=-1,
    )


def moe(normed, cot_low, gates, gate_up, down):
    width = down.shape[1]
    both = contract("td,edf->tef", normed, gate_up)
    pre_gate = both[:, :, :width]
    pre_up = both[:, :, width:]
    sigmoid_g = jax.nn.sigmoid(pre_gate)
    activated = pre_gate * sigmoid_g
    hidden = (activated * pre_up).astype(jnp.bfloat16).astype(jnp.float32)
    inner_raw = contract("td,efd->tef", cot_low, down)
    gate_part = jnp.sum(hidden * inner_raw, axis=-1)
    moe_part = contract("tef,efd->td", (gates[:, :, None] * hidden).astype(jnp.bfloat16), down)
    inner_grad = inner_raw * gates[:, :, None]
    grad_gate = inner_grad * pre_up * sigmoid_g * (1.0 + pre_gate * (1.0 - sigmoid_g))
    grad_up = inner_grad * activated
    grad_both = jnp.concatenate([grad_gate, grad_up], axis=2).astype(jnp.bfloat16)
    normed_part = contract("tef,edf->td", grad_both, gate_up)
    return (moe_part, gate_part, normed_part)


def body(
    tokens,
    attn_gain,
    moe_gain,
    w_qkv,
    w_out,
    w_router,
    w_gate,
    w_up,
    w_down,
    qkv_down,
    qkv_up,
    out_down,
    out_up,
    lengths,
    adapter_index,
    loss_mask,
    routes,
    upstream,
):
    n_exp = lax.axis_size("exp")
    groups = KV_HEADS // lax.axis_size("tp")
    per_group = HEADS // KV_HEADS
    experts = EXP_DEV * n_exp
    gate_up = lax.all_gather(jnp.concatenate([w_gate, w_up], axis=2), "exp", axis=0, tiled=True)
    down = lax.all_gather(w_down, "exp", axis=0, tiled=True)
    block_rows = min(512, TOK_DEV)
    blocks = TOK_DEV // block_rows
    score_scale = 1.0 / math.sqrt(HD)
    places = jnp.arange(TOK_DEV, dtype=jnp.int32)
    occupied, position, doc_ident, rank_mask = layout(lengths[0], adapter_index[0])
    mask_low = rank_mask.astype(jnp.bfloat16)
    cosine, sine_table = angles(position)
    inputs = tokens.astype(jnp.float32)
    attn_in = rms_norm(inputs, attn_gain).astype(jnp.bfloat16)
    low_q = (product(attn_in, qkv_down) * rank_mask).astype(jnp.bfloat16)
    projected = (product(attn_in, w_qkv) + product(low_q, qkv_up)).reshape(
        TOK_DEV, groups, per_group + 2, HD
    )
    query_rows = rotate(
        projected[:, :, :per_group], cosine[:, None, None], sine_table[:, None, None]
    ).astype(jnp.bfloat16)
    key_rows = rotate(projected[:, :, per_group], cosine[:, None], sine_table[:, None]).astype(
        jnp.bfloat16
    )
    val_rows = projected[:, :, per_group + 1].astype(jnp.bfloat16)

    def masked_scores(q_blk, q_place, q_ident):
        scores = contract("qgrd,kgd->grqk", q_blk, key_rows) * score_scale
        allowed = (q_ident[:, None] == doc_ident[None, :]) & (places[None, :] <= q_place[:, None])
        return jnp.where(allowed, scores, -1e30)

    def attend(pieces):
        q_blk, q_place, q_ident = pieces
        scores = masked_scores(q_blk, q_place, q_ident)
        row_max = jnp.max(scores, axis=-1, keepdims=True)
        lifted = jnp.exp(scores - row_max)
        row_total = jnp.sum(lifted, axis=-1, keepdims=True)
        weights = (lifted / row_total).astype(jnp.bfloat16)
        return (
            contract("grqk,kgd->qgrd", weights, val_rows),
            row_max[..., 0] + jnp.log(row_total[..., 0]),
        )

    query_blocks = query_rows.reshape(blocks, block_rows, groups, per_group, HD)
    place_blocks = places.reshape(blocks, block_rows)
    ident_blocks = doc_ident.reshape(blocks, block_rows)
    attended, log_totals = lax.map(attend, (query_blocks, place_blocks, ident_blocks))
    head_rows = attended.reshape(TOK_DEV, groups * per_group * HD).astype(jnp.bfloat16)
    attn_base, low_rank = (
        lax.psum(product(head_rows, w_out).astype(jnp.bfloat16), "tp").astype(jnp.float32),
        lax.psum((product(head_rows, out_down) * rank_mask).astype(jnp.bfloat16), "tp").astype(
            jnp.float32
        ),
    )
    low_o = low_rank.astype(jnp.bfloat16)
    residual = inputs + attn_base + product(low_o, out_up)
    normed = rms_norm(residual, moe_gain).astype(jnp.bfloat16)
    logits = product(normed, w_router)
    one_hot = routes[:, :, None] == jnp.arange(experts, dtype=jnp.int32)[None, None, :]
    routed = jnp.any(one_hot, axis=1)
    gates = jax.nn.softmax(jnp.where(routed, logits, -1e30), axis=-1)
    live_mask = jnp.where(occupied & (loss_mask > 0), 1.0, 0.0).astype(jnp.float32)
    cotangent = upstream.astype(jnp.float32) * live_mask[:, None]
    cot_low = cotangent.astype(jnp.bfloat16)
    moe_part, gate_part, normed_part = moe(normed, cot_low, gates, gate_up, down)
    logit_grad = (
        gates * (gate_part - jnp.sum(gates * gate_part, axis=-1, keepdims=True))
    ).astype(jnp.bfloat16)
    normed_part = (normed_part + product(logit_grad, w_router.T)).astype(jnp.bfloat16)
    normed_sum = lax.psum(normed_part, "tp")
    normed_sum, moe_part = lax.optimization_barrier((normed_sum, moe_part.astype(jnp.bfloat16)))
    normed_grad = normed_sum.astype(jnp.float32)
    moe_out = lax.psum(moe_part, "tp").astype(jnp.float32)
    output = (residual + moe_out).astype(jnp.bfloat16)
    residual_grad = cotangent + rms_norm_back(residual, moe_gain, normed_grad)
    branch_grad = residual_grad.astype(jnp.bfloat16)
    low_o_grad = product(branch_grad, out_up.T).astype(jnp.bfloat16) * mask_low
    out_up_part = contract("tr,td->rd", low_o, branch_grad)
    head_grad = (product(branch_grad, w_out.T) + product(low_o_grad, out_down.T)).astype(
        jnp.bfloat16
    )
    out_down_part = contract("tc,tr->cr", head_rows, low_o_grad)
    grad_blocks = head_grad.reshape(blocks, block_rows, groups, per_group, HD)

    def attend_back(carried, pieces):
        key_acc, val_acc = carried
        q_blk, q_place, q_ident, lse_blk, g_blk = pieces
        weights = jnp.exp(masked_scores(q_blk, q_place, q_ident) - lse_blk[..., None])
        weight_grad = contract("qgrd,kgd->grqk", g_blk, val_rows)
        score_grad = (
            weights * (weight_grad - jnp.sum(weights * weight_grad, axis=-1, keepdims=True))
        ).astype(jnp.bfloat16)
        query_grad = contract("grqk,kgd->qgrd", score_grad, key_rows) * score_scale
        key_acc = key_acc + contract("grqk,qgrd->kgd", score_grad, q_blk) * score_scale
        val_acc = val_acc + contract("grqk,qgrd->kgd", weights.astype(jnp.bfloat16), g_blk)
        return ((key_acc, val_acc), query_grad)

    zero_acc = jnp.zeros((TOK_DEV, groups, HD), jnp.float32)
    (key_grad, val_grad), query_grad = lax.scan(
        attend_back,
        (zero_acc, zero_acc),
        (query_blocks, place_blocks, ident_blocks, log_totals, grad_blocks),
    )
    query_grad = rotate(
        query_grad.reshape(TOK_DEV, groups, per_group, HD),
        cosine[:, None, None],
        -sine_table[:, None, None],
    )
    key_grad = rotate(key_grad, cosine[:, None], -sine_table[:, None])
    projected_grad = (
        jnp.concatenate([query_grad, key_grad[:, :, None], val_grad[:, :, None]], axis=2)
        .reshape(TOK_DEV, -1)
        .astype(jnp.bfloat16)
    )
    qkv_up_part = contract("tr,tc->rc", low_q, projected_grad)
    attn_grad, low_q_grad = (
        lax.psum(contract("tc,dc->td", projected_grad, w_qkv).astype(jnp.bfloat16), "tp").astype(
            jnp.float32
        ),
        lax.psum(contract("tc,rc->tr", projected_grad, qkv_up).astype(jnp.bfloat16), "tp").astype(
            jnp.float32
        ),
    )
    low_q_grad = low_q_grad.astype(jnp.bfloat16) * mask_low
    attn_grad = attn_grad + contract("tr,dr->td", low_q_grad, qkv_down)
    qkv_down_part = contract("td,tr->dr", attn_in, low_q_grad)
    input_grad = (residual_grad + rms_norm_back(inputs, attn_gain, attn_grad)).astype(jnp.bfloat16)
    summed = (
        lax.psum(qkv_down_part.astype(jnp.bfloat16), "exp").astype(jnp.float32),
        lax.psum(qkv_up_part.astype(jnp.bfloat16), "exp").astype(jnp.float32),
        lax.psum(out_down_part.astype(jnp.bfloat16), "exp").astype(jnp.float32),
        lax.psum(out_up_part.astype(jnp.bfloat16), "exp").astype(jnp.float32),
    )
    return (output, input_grad, summed[0], summed[1], summed[2], summed[3])


def kernels_fit(mesh):
    n_exp, n_tp = mesh.shape["exp"], mesh.shape["tp"]
    groups = KV_HEADS // n_tp
    return groups % 2 == 0 and FF // n_tp == LANES and LANES // n_exp % 16 == 0


def solution(mesh):
    placed = (
        P("exp", None),
        P(),
        P(),
        P(None, "tp"),
        P("tp", None),
        P(),
        P("exp", None, "tp"),
        P("exp", None, "tp"),
        P("exp", "tp", None),
        P(),
        P(None, "tp"),
        P("tp", None),
        P(),
        P("exp", None),
        P("exp", None),
        P("exp"),
        P("exp", None),
        P("exp", None),
    )
    return jax.shard_map(
        kernel_body if kernels_fit(mesh) else body,
        mesh=mesh,
        in_specs=placed,
        out_specs=(P("exp", None), P("exp", None), P(), P(None, "tp"), P("tp", None), P()),
        check_vma=False,
    )
```

```python
import functools
import math

import jax
import jax.numpy as jnp
import numpy as np
from jax import lax
from jax.experimental import pallas as pl
from jax.experimental.pallas import tpu as pltpu
from jax.sharding import PartitionSpec as P

D = 1536
HEADS = 24
KV_HEADS = 8
HD = 64
TOP = 8
RANK = 16
ADAPTERS = 8
EXP_DEV = 2
DOCS = 4
TOK_DEV = 512
LIVE = 448
FF = 512
EPS = 1e-06
ROPE_BASE = 10000.0

PER = HEADS // KV_HEADS
LANES = 128
ROWS = 128
BLOCKS = tuple((at, min(at + ROWS, TOK_DEV)) for at in range(0, TOK_DEV, ROWS))
LIVE_BLOCKS = tuple((at, min(at + ROWS, LIVE)) for at in range(0, LIVE, ROWS))
F32 = jnp.float32
BF16 = jnp.bfloat16
MIB = 2**20
NT = (((1,), (1,)), ((), ()))
TN = (((0,), (0,)), ((), ()))
WHOLE_VMEM = pltpu.CompilerParams(vmem_limit_bytes=63 * MIB)
IN_VMEM = pl.BlockSpec(memory_space=pltpu.VMEM)
IN_SMEM = pl.BlockSpec(memory_space=pltpu.SMEM)
IN_HBM = pl.BlockSpec(memory_space=pltpu.HBM)


def dot(left, right):
    return jnp.dot(left, right, preferred_element_type=F32)


def dot_nt(left, right):
    return lax.dot_general(left, right, NT, preferred_element_type=F32)


def dot_tn(left, right):
    return lax.dot_general(left, right, TN, preferred_element_type=F32)


def cost(flops, moved):
    return pl.CostEstimate(flops=int(flops), bytes_accessed=int(moved), transcendentals=0)


def shape(dims, dtype):
    return jax.ShapeDtypeStruct(dims, dtype)


def turn_tables(rows):
    half = HD // 2
    frequency = np.exp(-math.log(ROPE_BASE) * np.arange(half, dtype=np.float64) * 2.0 / HD)
    turned = np.arange(rows, dtype=np.float64)[:, None] * frequency[None, :]
    cosine, sine = np.cos(turned), np.sin(turned)
    return (
        jnp.asarray(np.concatenate([cosine] * 4, axis=1), F32),
        jnp.asarray(np.concatenate([-sine, sine, -sine, sine], axis=1), F32),
    )


def turned_pieces(groups):
    return [piece < PER + 1 for _ in range(groups) for piece in range(PER + 2)]


def turn(joined, cosine, sine, flags):
    lane = lax.broadcasted_iota(jnp.int32, cosine.shape, 1)
    front = (lane & 32) == 0
    left = lane < HD
    columns = []
    for at in range(joined.shape[1] // LANES):
        column = joined[:, at * LANES : (at + 1) * LANES]
        swapped = jnp.where(front, pltpu.roll(column, 96, 1), pltpu.roll(column, 32, 1))
        rotated = column * cosine + swapped * sine
        if not (flags[2 * at] and flags[2 * at + 1]):
            rotated = jnp.where(left if flags[2 * at] else jnp.logical_not(left), rotated, column)
        columns.append(rotated)
    return columns


def first_keys(length_ref, rows):
    row = lax.broadcasted_iota(jnp.int32, (rows, 1), 0)
    begin = jnp.zeros((rows, 1), jnp.int32)
    end = 0
    for doc in range(DOCS):
        if doc:
            begin = jnp.where(row >= end, end, begin)
        end = end + length_ref[0, doc]
    return jnp.where(row >= end, row, begin)


def adapter_mask(length_ref, index_ref, rows, width):
    row = lax.broadcasted_iota(jnp.int32, (rows, width), 0)
    adapter = lax.shift_right_logical(lax.broadcasted_iota(jnp.int32, (rows, width), 1), 4)
    mask = jnp.zeros((rows, width), F32)
    begin = 0
    for doc in range(DOCS):
        end = begin + length_ref[0, doc]
        inside = (row >= begin) & (row < end) & (adapter == index_ref[0, doc])
        mask = jnp.where(inside, 1.0, mask)
        begin = end
    return mask


def folding():
    rank = lax.broadcasted_iota(jnp.int32, (RANK, LANES), 0)
    lane = lax.broadcasted_iota(jnp.int32, (RANK, LANES), 1)
    return jnp.where((lane & (RANK - 1)) == rank, 1.0, 0.0).astype(BF16)


def unfold(low_ref, length_ref, index_ref, rows):
    spread = dot_tn(low_ref[-RANK:, :rows], folding())
    return (spread * adapter_mask(length_ref, index_ref, rows, LANES)).astype(BF16)


def seen_block(first, begin, end):
    row = lax.broadcasted_iota(jnp.int32, (end - begin, end), 0) + begin
    key = lax.broadcasted_iota(jnp.int32, (end - begin, end), 1)
    seen = (key <= row) & (key >= first[begin:end])
    return jnp.concatenate([seen] * PER, axis=0)


def softmax_block(scores, seen):
    scores = jnp.where(seen, scores, -1e30)
    lifted = jnp.exp(scores - jnp.max(scores, axis=1, keepdims=True))
    return (lifted * (1.0 / jnp.sum(lifted, axis=1, keepdims=True))).astype(BF16)


def store_heads(columns, slot, blocks, q_s, k_s, v_s):
    scale = 1.0 / math.sqrt(HD)
    for at, column in enumerate(columns):
        halves = (column[:, :HD], pltpu.roll(column, HD, 1)[:, :HD])
        for piece, part in zip((2 * at, 2 * at + 1), halves):
            group, kind = divmod(piece, PER + 2)
            if kind == PER:
                k_s[slot + group] = part.astype(BF16)
            elif kind == PER + 1:
                v_s[slot + group] = part.astype(BF16)
            else:
                part = (part * scale).astype(BF16)
                for block, (begin, end) in enumerate(blocks):
                    size = end - begin
                    here = slice(kind * size, (kind + 1) * size)
                    q_s[slot + group, block, here, :] = part[begin:end]


def run_copies(pairs, sem):
    copies = [
        pltpu.make_async_copy(source, target, sem.at[number])
        for number, (source, target) in enumerate(pairs)
    ]
    for copy in copies:
        copy.start()
    for copy in copies:
        copy.wait()


def pack_kernel(
    n_exp, place_ref, gate, up, down, w_qkv, qkv_up, packed, share, held, share_s, sem, out_sem
):
    width = gate.shape[2]
    pairs = []
    for expert in range(gate.shape[0]):
        pairs.append((gate.at[expert], held.at[expert, :, :width]))
        pairs.append((up.at[expert], held.at[expert, :, width : 2 * width]))
        for at in range(D // LANES):
            lanes = slice(at * LANES, (at + 1) * LANES)
            pairs.append((down.at[expert, :, lanes], held.at[expert, lanes, 2 * width :]))
    qkv_rows, up_rows, _ = share_rows(n_exp, 0)
    own_qkv = pl.ds(pl.multiple_of(place_ref[0] * qkv_rows, 16), qkv_rows)
    own_up = pl.ds(pl.multiple_of(place_ref[0] * up_rows, 16), up_rows)
    pairs.append((w_qkv.at[own_qkv, :], share_s.at[:qkv_rows, :]))
    pairs.append((qkv_up.at[own_up, :], share_s.at[qkv_rows:, :]))
    run_copies(pairs, sem)
    run_copies([(held, packed), (share_s, share)], out_sem)


def share_rows(n_exp, heads_wide):
    return (D // n_exp, LANES // n_exp, heads_wide // n_exp)


def pack(place, w_gate, w_up, w_down, w_qkv, qkv_up, n_exp):
    count, _, width = w_gate.shape
    packed = shape((count, D, 3 * width), BF16)
    share = shape(((D + LANES) // n_exp, w_qkv.shape[1]), BF16)
    return pl.pallas_call(
        functools.partial(pack_kernel, n_exp),
        in_specs=[IN_SMEM] + [IN_HBM] * 5,
        out_specs=[IN_HBM] * 2,
        out_shape=[packed, share],
        scratch_shapes=[
            pltpu.VMEM(packed.shape, BF16),
            pltpu.VMEM(share.shape, BF16),
            pltpu.SemaphoreType.DMA((count * (2 + D // LANES) + 2,)),
            pltpu.SemaphoreType.DMA((2,)),
        ],
        compiler_params=WHOLE_VMEM,
        cost_estimate=cost(0, 2 * 2 * count * D * 3 * width),
        name="pack_weights",
    )(place, w_gate, w_up, w_down, w_qkv, qkv_up)


class Loads:
    def __init__(self, names, sources, targets, sem):
        self.copies = {}
        for number, (name, source, target) in enumerate(zip(names, sources, targets)):
            if source.shape[0] == TOK_DEV + RANK:
                source = source.at[TOK_DEV:]
            elif source.shape != target.shape:
                source = source.at[: target.shape[0]]
            self.copies[name] = pltpu.make_async_copy(source, target, sem.at[number])
        self.targets = dict(zip(names, targets))
        for copy in self.copies.values():
            copy.start()

    def __getitem__(self, name):
        copy = self.copies.pop(name, None)
        if copy is not None:
            copy.wait()
        return self.targets[name]


def load_scratch(arrays, rows=TOK_DEV):
    kept = {TOK_DEV: rows, TOK_DEV + RANK: RANK}
    rooms = []
    for array in arrays:
        first = kept.get(array.shape[0], array.shape[0])
        rooms.append(pltpu.VMEM((first,) + array.shape[1:], array.dtype))
    return rooms + [pltpu.SemaphoreType.DMA((len(arrays),))]


FORWARD_LOADS = (
    "tokens", "gains", "qkv_down", "w_qkv", "qkv_up", "cosine", "sine", "w_out", "out_down",
)


def forward_kernel(place_ref, length_ref, index_ref, *refs):
    count = len(FORWARD_LOADS)
    attn_in_ref, low_q_ref, head_ref, base_ref, share_ref = refs[count : count + 5]
    load_sem, q_s, k_s, v_s = refs[2 * count + 5 :]
    loads = Loads(FORWARD_LOADS, refs[:count], refs[count + 5 : 2 * count + 5], load_sem)
    rows = attn_in_ref.shape[0]
    groups = k_s.shape[0]
    mask = adapter_mask(length_ref, index_ref, rows, LANES)
    first = first_keys(length_ref, rows)
    inputs = loads["tokens"][...].astype(F32)
    inv_root = lax.rsqrt(jnp.mean(inputs * inputs, axis=1, keepdims=True) + EPS)
    attn_in_ref[...] = (inputs * inv_root * loads["gains"][0:1, :]).astype(BF16)
    attn_in = attn_in_ref[...]
    low_q = (dot(attn_in, loads["qkv_down"][...]) * mask).astype(BF16)
    low_q_ref[...] = low_q
    projected = dot(attn_in, loads["w_qkv"][...]) + dot(low_q, loads["qkv_up"][...])
    cosine, sine = loads["cosine"][...], loads["sine"][...]
    columns = turn(projected, cosine, sine, turned_pieces(groups))
    store_heads(columns, 0, BLOCKS, q_s, k_s, v_s)
    for block, (begin, end) in enumerate(BLOCKS):
        seen = seen_block(first, begin, end)
        scores = [dot_nt(q_s[group, block], k_s[group, :end, :]) for group in range(groups)]
        probs = [softmax_block(part, seen) for part in scores]
        heads = []
        for group in range(groups):
            out = dot(probs[group], v_s[group, :end, :])
            heads += [out[head * ROWS : (head + 1) * ROWS] for head in range(PER)]
        head_ref[begin:end, :] = jnp.concatenate(heads, axis=1).astype(BF16)
    head_out = head_ref[...]
    base_ref[:rows, :] = dot(head_out, loads["w_out"][...]).astype(BF16)
    low_o = (dot(head_out, loads["out_down"][...]) * mask).astype(BF16)
    base_ref[rows:, :rows] = dot_nt(folding(), low_o).astype(BF16)
    base_ref[rows:, rows:] = jnp.zeros((RANK, D - rows), BF16)
    share_rows_count = share_ref.shape[0]
    own = pl.ds(pl.multiple_of(place_ref[0] * share_rows_count, 16), share_rows_count)
    share_ref[:, :D] = loads["w_out"][own, :]
    share_ref[:, D:] = loads["out_down"][own, :]


def forward(
    place, lengths, index, tokens, gains, w_qkv, qkv_down, qkv_up, w_out, out_down, tables, n_exp
):
    rows = tokens.shape[0]
    heads_wide = w_out.shape[0]
    groups = w_qkv.shape[1] // (HD * (PER + 2))
    arrays = (tokens, gains, qkv_down, w_qkv, qkv_up) + tables + (w_out, out_down)
    return pl.pallas_call(
        forward_kernel,
        in_specs=[IN_SMEM] * 3 + [IN_HBM] * len(arrays),
        out_specs=[IN_VMEM] * 5,
        out_shape=[
            shape((rows, D), BF16),
            shape((rows, LANES), BF16),
            shape((rows, heads_wide), BF16),
            shape((rows + RANK, D), BF16),
            shape((heads_wide // n_exp, D + LANES), BF16),
        ],
        scratch_shapes=load_scratch(arrays)
        + [
            pltpu.VMEM((groups, rows // ROWS, PER * ROWS, HD), BF16),
            pltpu.VMEM((groups, rows, HD), BF16),
            pltpu.VMEM((groups, rows, HD), BF16),
        ],
        compiler_params=WHOLE_VMEM,
        cost_estimate=cost(6e9, 10e6),
        name="attention_forward",
    )(place, lengths, index, *arrays)


def down_of(weight, width):
    columns = [
        weight[at * LANES : (at + 1) * LANES, 2 * width : 3 * width] for at in range(D // LANES)
    ]
    return jnp.concatenate(columns, axis=1)


def experts_kernel(
    length_ref, index_ref, tokens_ref, base_ref, out_up_ref, gains_ref, router_ref, bias_ref,
    cot_ref, weight_ref, residual_ref, hidden_ref, grad_ref,
    normed_s, gates_s, part_s, grad_s,
):
    step = pl.program_id(0)
    count, _, packed = weight_ref.shape
    width = packed // 3
    lane = lax.broadcasted_iota(jnp.int32, gates_s.shape, 1)

    @pl.when(step == 0)
    def _():
        residual = (
            tokens_ref[...].astype(F32)
            + base_ref[:TOK_DEV, :].astype(F32)
            + dot(unfold(base_ref, length_ref, index_ref, TOK_DEV), out_up_ref[...])
        )
        residual_ref[...] = residual.astype(BF16)
        inv_root = lax.rsqrt(jnp.mean(residual * residual, axis=1, keepdims=True) + EPS)
        normed = (residual * inv_root * gains_ref[1:2, :]).astype(BF16)
        normed_s[...] = normed
        logits = dot_nt(normed, router_ref[...]) + bias_ref[...]
        lifted = jnp.exp(logits - jnp.max(logits, axis=1, keepdims=True))
        gates_s[...] = lifted / jnp.sum(lifted, axis=1, keepdims=True)
        part_s[...] = jnp.zeros_like(part_s)
        grad_s[...] = jnp.zeros_like(grad_s)

    normed = normed_s[...]
    cot = cot_ref[...]
    gates = gates_s[...]
    part = jnp.zeros(part_s.shape, F32)
    grads = []
    for pair in range(0, count, 2):
        pair_down = [down_of(weight_ref.at[pair + half], width) for half in range(2)]
        pair_raw = dot_nt(cot, jnp.concatenate(pair_down, axis=0))
        for half in range(2):
            expert = pair + half
            joined = dot(normed, weight_ref[expert, :, : 2 * width])
            pre_gate = joined[:, :width]
            pre_up = joined[:, width:]
            raw = pair_raw[:, half * width : (half + 1) * width]
            sigmoid = 0.5 * jnp.tanh(0.5 * pre_gate) + 0.5
            activated = pre_gate * sigmoid
            value = activated * pre_up
            here = lane == step * count + expert
            gate = jnp.sum(jnp.where(here, gates, 0.0), axis=1, keepdims=True)
            hidden_ref[:, expert * width : (expert + 1) * width] = (gate * value).astype(BF16)
            gate_grad = jnp.sum(value[:LIVE] * raw, axis=1, keepdims=True)
            part += jnp.where(here[:LIVE], gate_grad, 0.0)
            inner = raw * gate[:LIVE]
            sigmoid, activated = sigmoid[:LIVE], activated[:LIVE]
            slope = sigmoid + activated * (1.0 - sigmoid)
            grads.append((inner * pre_up[:LIVE] * slope).astype(BF16))
            grads.append((inner * activated).astype(BF16))
    part_s[...] += part
    ups = [weight_ref[expert, :, : 2 * width] for expert in range(count)]
    grad_s[...] += dot_nt(jnp.concatenate(grads, axis=1), jnp.concatenate(ups, axis=1))

    @pl.when(step == pl.num_programs(0) - 1)
    def _():
        live_gates, gate_part = gates[:LIVE], part_s[...]
        spread = jnp.sum(live_gates * gate_part, axis=1, keepdims=True)
        logit_grad = (live_gates * (gate_part - spread)).astype(BF16)
        grad_ref[...] = (grad_s[...] + dot(logit_grad, router_ref[...])).astype(BF16)


def experts_both(
    lengths, index, tokens, base, out_up, gains, router, bias, cot, weights, count=4,
):
    rows = tokens.shape[0]
    experts, _, packed = weights.shape
    width = packed // 3
    arrays = (tokens, base, out_up, gains, router.T, bias, cot)
    in_specs = [IN_SMEM] * 2
    in_specs += [pl.BlockSpec(array.shape, lambda step: (0, 0)) for array in arrays]
    in_specs.append(pl.BlockSpec((count, D, packed), lambda step: (step, 0, 0)))
    return pl.pallas_call(
        experts_kernel,
        grid=(experts // count,),
        in_specs=in_specs,
        out_specs=[
            pl.BlockSpec((rows, D), lambda step: (0, 0)),
            pl.BlockSpec((rows, count * width), lambda step: (0, step)),
            pl.BlockSpec((LIVE, D), lambda step: (0, 0)),
        ],
        out_shape=[
            shape((rows, D), BF16),
            shape((rows, experts * width), BF16),
            shape((LIVE, D), BF16),
        ],
        scratch_shapes=[
            pltpu.VMEM((rows, D), BF16),
            pltpu.VMEM((rows, experts), F32),
            pltpu.VMEM((LIVE, experts), F32),
            pltpu.VMEM((LIVE, D), F32),
        ],
        compiler_params=WHOLE_VMEM,
        cost_estimate=cost(0, 1000),
        name="experts",
    )(lengths, index, *arrays, weights)


def combine_kernel(
    place_ref, hidden_hbm, residual_hbm, weights_hbm, moe_ref, hidden_s, residual_s, downs_s,
    hidden_sem, residual_sem, sem,
):
    experts, _, width = downs_s.shape
    load = pltpu.make_async_copy(hidden_hbm, hidden_s, hidden_sem)
    load.start()
    residual_load = pltpu.make_async_copy(residual_hbm, residual_s, residual_sem)
    residual_load.start()
    own = jnp.where(place_ref[0] == 0, 1.0, 0.0).astype(F32)
    copies = []
    for expert in range(experts):
        source, target = weights_hbm.at[expert, :, 2 * width :], downs_s.at[expert]
        copies.append(pltpu.make_async_copy(source, target, sem.at[expert]))
        copies[-1].start()
    load.wait()
    residual_load.wait()
    for copy in copies:
        copy.wait()
    for at in range(0, D, 2 * LANES):
        columns = []
        for expert in range(experts):
            pieces = [
                downs_s[expert, at + left : at + left + LANES, :] for left in (0, LANES)
            ]
            columns.append(jnp.concatenate(pieces, axis=1))
        moe = dot(hidden_s[...], jnp.concatenate(columns, axis=0))
        here = slice(at, at + 2 * LANES)
        moe_ref[:, here] = (moe + own * residual_s[:, here].astype(F32)).astype(BF16)


def combine(place, hidden, residual, weights):
    rows = hidden.shape[0]
    experts, _, packed = weights.shape
    return pl.pallas_call(
        combine_kernel,
        in_specs=[IN_SMEM] + [IN_HBM] * 3,
        out_specs=IN_VMEM,
        out_shape=shape((rows, D), BF16),
        scratch_shapes=[
            pltpu.VMEM(hidden.shape, BF16),
            pltpu.VMEM(residual.shape, BF16),
            pltpu.VMEM((experts, D, packed // 3), BF16),
            pltpu.SemaphoreType.DMA(()),
            pltpu.SemaphoreType.DMA(()),
            pltpu.SemaphoreType.DMA((experts,)),
        ],
        compiler_params=WHOLE_VMEM,
        cost_estimate=cost(4e9, 10e6),
        name="combine",
    )(place, hidden, residual, weights)


def norm_back(vectors, gain, upstream):
    inv_root = lax.rsqrt(jnp.mean(vectors * vectors, axis=1, keepdims=True) + EPS)
    weighted = upstream * gain
    slope = jnp.mean(vectors * weighted, axis=1, keepdims=True)
    return inv_root * weighted - vectors * (inv_root * inv_root * inv_root) * slope


BRANCH_LOADS = (
    "residual", "normed_grad", "gains", "cot", "out_up", "low_o", "head",
)


def branch_kernel(length_ref, index_ref, *refs):
    count = len(BRANCH_LOADS)
    branch_grad_ref, low_grad_ref, part_ref = refs[count : count + 3]
    scratch = refs[count + 3 :]
    loads = Loads(BRANCH_LOADS, refs[:count], scratch[:count], scratch[count])
    mask = adapter_mask(length_ref, index_ref, LIVE, LANES)
    residual = loads["residual"][...].astype(F32)
    through = norm_back(residual, loads["gains"][1:2, :], loads["normed_grad"][...].astype(F32))
    branch_grad_ref[...] = (through + loads["cot"][...].astype(F32)).astype(BF16)
    branch_grad = branch_grad_ref[...]
    low_grad_ref[...] = (dot_nt(branch_grad, loads["out_up"][...]) * mask).astype(BF16)
    low_o = unfold(loads["low_o"], length_ref, index_ref, LIVE)
    out_up_part = dot_tn(low_o, branch_grad).astype(BF16)
    for at in range(D // LANES):
        lanes = slice(at * LANES, (at + 1) * LANES)
        part_ref[lanes, :] = out_up_part[:, lanes]
    part_ref[D:, :] = dot_tn(loads["head"][...], low_grad_ref[...]).astype(BF16)


def branch_back(
    lengths, index, residual, base, normed_grad, cot, gains, out_up, head
):
    arrays = (residual, normed_grad, gains, cot, out_up, base, head)
    return pl.pallas_call(
        branch_kernel,
        in_specs=[IN_SMEM] * 2 + [IN_HBM] * len(arrays),
        out_specs=[IN_VMEM] * 3,
        out_shape=[
            shape((LIVE, D), BF16),
            shape((LIVE, LANES), BF16),
            shape((D + head.shape[1], LANES), BF16),
        ],
        scratch_shapes=load_scratch(arrays, LIVE),
        compiler_params=WHOLE_VMEM,
        cost_estimate=cost(1e9, 2e6),
        name="branch_backward",
    )(lengths, index, *arrays)


def share_copies(place_ref, shares, w_qkv_s, sem):
    n_exp, n_tp, _, _ = shares.shape
    qkv_rows, up_rows, _ = share_rows(n_exp, 0)
    copies = []
    for z in range(n_tp):
        here = []
        source_z = from_place(place_ref, z, n_tp)
        for e in range(n_exp):
            at = e * qkv_rows
            up_at = D + e * up_rows
            for source, target in (
                (shares.at[e, source_z, :qkv_rows, :], w_qkv_s.at[z, at : at + qkv_rows, :]),
                (shares.at[e, source_z, qkv_rows:, :], w_qkv_s.at[z, up_at : up_at + up_rows, :]),
            ):
                number = 2 * e + len(here) % 2
                here.append(pltpu.make_async_copy(source, target, sem.at[z, number]))
        copies.append(here)
    for here in copies:
        for copy in here:
            copy.start()
    return copies


PREPARE_LOADS = ("attn_in", "low_q", "cosine", "sine")


def prepare_kernel(place_ref, length_ref, shares, *refs):
    count = len(PREPARE_LOADS)
    results = 1 + len(LIVE_BLOCKS)
    turned_ref = refs[count]
    prob_refs = refs[count + 1 : count + results]
    load_sem, w_qkv_s, q_s, k_s, v_s, sem = refs[2 * count + results :]
    targets = refs[count + results : 2 * count + results]
    loads = Loads(PREPARE_LOADS, refs[:count], targets, load_sem)
    n_tp = shares.shape[1]
    groups = k_s.shape[0]
    copies = share_copies(place_ref, shares, w_qkv_s, sem)
    first = first_keys(length_ref, LIVE)
    attn_in = loads["attn_in"][...]
    low_q = loads["low_q"][...]
    cosine, sine = loads["cosine"][...], loads["sine"][...]
    seen = [seen_block(first, begin, end) for begin, end in LIVE_BLOCKS]
    for here in copies:
        for copy in here:
            copy.wait()

    def one_place(z, carried):
        projected = dot(attn_in, w_qkv_s[z, :D, :]) + dot(low_q, w_qkv_s[z, D:, :])
        columns = turn(projected, cosine, sine, turned_pieces(groups))
        for at, column in enumerate(columns):
            turned_ref[z, :, at * LANES : (at + 1) * LANES] = column.astype(BF16)
        store_heads(columns, 0, LIVE_BLOCKS, q_s, k_s, v_s)
        for group in range(groups):
            for block, (begin, end) in enumerate(LIVE_BLOCKS):
                query = q_s[group, block, : PER * (end - begin), :]
                scores = dot_nt(query, k_s[group, :end, :])
                prob_refs[block][z * groups + group] = softmax_block(scores, seen[block])
        return carried

    lax.fori_loop(0, n_tp, one_place, 0)


def prepare(place, lengths, attn_in, low_q, tables, shares):
    n_exp, n_tp, _, wide = shares.shape
    arrays = (attn_in, low_q) + tables
    groups = KV_HEADS
    probs = [
        shape((groups, PER * (end - begin), end), BF16) for begin, end in LIVE_BLOCKS
    ]
    return pl.pallas_call(
        prepare_kernel,
        in_specs=[IN_SMEM] * 2 + [IN_HBM] * (1 + len(arrays)),
        out_specs=[IN_VMEM] * (1 + len(probs)),
        out_shape=[shape((n_tp, LIVE, wide), BF16)] + probs,
        scratch_shapes=load_scratch(arrays, LIVE)
        + [
            pltpu.VMEM((n_tp, D + LANES, wide), BF16),
            pltpu.VMEM((groups // n_tp, len(LIVE_BLOCKS), PER * ROWS, HD), BF16),
            pltpu.VMEM((groups // n_tp, LIVE, HD), BF16),
            pltpu.VMEM((groups // n_tp, LIVE, HD), BF16),
            pltpu.SemaphoreType.DMA((n_tp, 2 * n_exp)),
        ],
        compiler_params=WHOLE_VMEM,
        cost_estimate=cost(12e9, 30e6),
        name="prepare_heads",
    )(place, lengths, shares, *arrays)


HEADS_LOADS = (
    "branch_grad", "low_o_grad", "turned", "cosine", "sine", "low_q", "attn_in",
)


def heads_back_kernel(place_ref, length_ref, index_ref, shares, out_shares, *refs):
    count = len(HEADS_LOADS)
    blocks = len(LIVE_BLOCKS)
    probs_hbm = refs[count : count + blocks]
    grad_ref, low_grad_ref, part_ref = refs[count + blocks : count + blocks + 3]
    scratch = refs[count + blocks + 3 :]
    loads = Loads(HEADS_LOADS, refs[:count], scratch[:count], scratch[count])
    up_s, w_out_s, g_s, q_s, k_s, v_s, up_sem, out_sem, prob_sem = scratch[count + 1 : count + 10]
    probs_s = scratch[count + 10 :]
    n_exp, n_tp, _, wide = shares.shape
    groups = g_s.shape[0]
    flags = turned_pieces(groups)
    scale = 1.0 / math.sqrt(HD)

    def prob_copy(z, block):
        here = pl.ds(z * groups, groups)
        return pltpu.make_async_copy(
            probs_hbm[block].at[here], probs_s[block].at[here], prob_sem.at[z, block]
        )

    out_rows = out_shares.shape[2]

    def out_copy(z, e):
        return pltpu.make_async_copy(
            out_shares.at[e, jnp.bitwise_xor(place_ref[0], z)],
            w_out_s.at[z, e * out_rows : (e + 1) * out_rows, :],
            out_sem.at[z, e],
        )

    for z in range(n_tp):
        for e in range(n_exp):
            out_copy(z, e).start()
        for block in range(blocks):
            prob_copy(z, block).start()
    qkv_rows, up_rows, _ = share_rows(n_exp, 0)
    up_copies = []
    for z in range(n_tp):
        for e in range(n_exp):
            source = shares.at[e, from_place(place_ref, z, n_tp), qkv_rows:, :]
            target = up_s.at[z, e * up_rows : (e + 1) * up_rows, :]
            up_copies.append(pltpu.make_async_copy(source, target, up_sem.at[z, e]))
            up_copies[-1].start()
    branch_grad, low_o_grad = loads["branch_grad"], loads["low_o_grad"]
    turned = loads["turned"]
    cosine, sine = loads["cosine"], loads["sine"]

    def one_place(z, carried):
        columns = [
            turned[z, :, at * LANES : (at + 1) * LANES].astype(F32) for at in range(wide // LANES)
        ]
        store_heads(columns, 0, LIVE_BLOCKS, q_s, k_s, v_s)
        for e in range(n_exp):
            out_copy(z, e).wait()
        head_grad = (
            dot_nt(branch_grad[...], w_out_s[z, :, :D]) + dot_nt(low_o_grad[...], w_out_s[z, :, D:])
        ).astype(BF16)
        for head in range(groups * PER):
            group, kind = divmod(head, PER)
            part = head_grad[:, head * HD : (head + 1) * HD]
            for block, (begin, end) in enumerate(LIVE_BLOCKS):
                size = end - begin
                here = slice(kind * size, (kind + 1) * size)
                g_s[group, block, here, :] = part[begin:end]
        for block in range(blocks):
            prob_copy(z, block).wait()
        key_grads = [jnp.zeros((HD, LIVE), F32) for _ in range(groups)]
        value_grads = [jnp.zeros((HD, LIVE), F32) for _ in range(groups)]
        query_grads = [[] for _ in range(groups)]
        for block, (begin, end) in enumerate(LIVE_BLOCKS):
            size = end - begin

            def widen(part):
                if end == LIVE:
                    return part
                return jnp.concatenate([part, jnp.zeros((HD, LIVE - end), F32)], axis=1)

            some = range(groups)
            queries = [q_s[group, block, : PER * size, :] for group in some]
            head_grads = [g_s[group, block, : PER * size, :] for group in some]
            probs = [probs_s[block][z * groups + group] for group in some]
            weight_grads = [dot_nt(head_grads[group], v_s[group, :end, :]) for group in some]
            for group in some:
                value_grads[group] += widen(dot_tn(head_grads[group], probs[group]))
            wide_probs = [probs[group].astype(F32) for group in some]
            score_grads = []
            for group in some:
                product = wide_probs[group] * weight_grads[group]
                spread = jnp.sum(product, axis=1, keepdims=True)
                score_grads.append((product - wide_probs[group] * spread).astype(BF16))
            for group in some:
                score_grad = score_grads[group]
                query_grads[group].append(dot(score_grad, k_s[group, :end, :]) * scale)
                key_grads[group] += widen(dot_tn(queries[group], score_grad))
        pieces = []
        for group in range(groups):
            for head in range(PER):
                rows = [
                    part[head * (end - begin) : (head + 1) * (end - begin)]
                    for part, (begin, end) in zip(query_grads[group], LIVE_BLOCKS)
                ]
                pieces.append(jnp.concatenate(rows, axis=0))
            pieces += [key_grads[group].T, value_grads[group].T]
        joined = jnp.concatenate(pieces, axis=1)
        columns = turn(joined, cosine[...], -sine[...], flags)
        for at, column in enumerate(columns):
            grad_ref[z, :, at * LANES : (at + 1) * LANES] = column.astype(BF16)
        return carried

    lax.fori_loop(0, n_tp, one_place, 0)
    for copy in up_copies:
        copy.wait()
    low_grad = dot_nt(grad_ref[0], up_s[0])
    for z in range(1, n_tp):
        low_grad += dot_nt(grad_ref[z], up_s[z])
    mask = adapter_mask(length_ref, index_ref, LIVE, LANES)
    low_grad = (low_grad * mask).astype(BF16)
    low_grad_ref[...] = low_grad
    part_ref[:D, :] = dot_tn(loads["attn_in"][...], low_grad).astype(BF16)
    up_part = dot_tn(loads["low_q"][...], grad_ref[place_ref[0]]).astype(BF16)
    for at in range(wide // LANES):
        lanes = slice(at * LANES, (at + 1) * LANES)
        part_ref[D + at * LANES : D + (at + 1) * LANES, :] = up_part[:, lanes]


def heads_back(
    place, lengths, index, attn_in, low_q, heads, branch_grad, low_o_grad, tables, shares, out_shares
):
    n_exp, n_tp, _, wide = shares.shape
    blocks = len(LIVE_BLOCKS)
    turned, probs = heads[0], heads[1:]
    groups = KV_HEADS // n_tp
    heads_wide = groups * PER * HD
    arrays = (branch_grad, low_o_grad, turned) + tables + (low_q, attn_in)
    return pl.pallas_call(
        heads_back_kernel,
        in_specs=[IN_SMEM] * 3 + [IN_HBM] * (2 + len(arrays) + blocks),
        out_specs=[IN_VMEM] * 3,
        out_shape=[
            shape((n_tp, LIVE, wide), BF16),
            shape((LIVE, LANES), BF16),
            shape((D + wide, LANES), BF16),
        ],
        scratch_shapes=load_scratch(arrays, LIVE)
        + [
            pltpu.VMEM((n_tp, LANES, wide), BF16),
            pltpu.VMEM((n_tp, heads_wide, D + LANES), BF16),
            pltpu.VMEM((groups, blocks, PER * ROWS, HD), BF16),
            pltpu.VMEM((groups, blocks, PER * ROWS, HD), BF16),
            pltpu.VMEM((groups, LIVE, HD), BF16),
            pltpu.VMEM((groups, LIVE, HD), BF16),
            pltpu.SemaphoreType.DMA((n_tp, n_exp)),
            pltpu.SemaphoreType.DMA((n_tp, n_exp)),
            pltpu.SemaphoreType.DMA((n_tp, blocks)),
        ]
        + [pltpu.VMEM(part.shape, BF16) for part in probs],
        compiler_params=WHOLE_VMEM,
        cost_estimate=cost(2e9, 3e6),
        name="heads_backward",
    )(place, lengths, index, shares, out_shares, *arrays, *probs)


INPUT_LOADS = ("grads", "low_grad", "qkv_down", "tokens", "gains", "branch_grad")


def input_back_kernel(place_ref, shares, *refs):
    count = len(INPUT_LOADS)
    input_grad_ref = refs[count]
    load_sem, w_qkv_s, sum_s, sem = refs[2 * count + 1 :]
    n_exp, n_tp, _, _ = shares.shape
    qkv_rows, _, _ = share_rows(n_exp, 0)
    copies = []
    for z in range(n_tp):
        for e in range(n_exp):
            source = shares.at[e, from_place(place_ref, z, n_tp), :qkv_rows, :]
            target = w_qkv_s.at[z, e * qkv_rows : (e + 1) * qkv_rows, :]
            copies.append(pltpu.make_async_copy(source, target, sem.at[z, e]))
    loads = Loads(INPUT_LOADS, refs[:count], refs[count + 1 : 2 * count + 1], load_sem)
    for copy in copies:
        copy.start()
    input_grad_ref[LIVE:, :] = jnp.zeros((input_grad_ref.shape[0] - LIVE, D), BF16)
    grads = loads["grads"]
    sum_s[...] = dot_nt(loads["low_grad"][...], loads["qkv_down"][...])
    for z in range(n_tp):
        for copy in copies[z * n_exp : (z + 1) * n_exp]:
            copy.wait()
        sum_s[...] += dot_nt(grads[z], w_qkv_s[z])
    tokens, gain = loads["tokens"][...].astype(F32), loads["gains"][0:1, :]
    through = norm_back(tokens, gain, sum_s[...])
    input_grad_ref[:LIVE, :] = (loads["branch_grad"][...].astype(F32) + through).astype(BF16)


def input_back(place, grads, low_grad, qkv_down, tokens, gains, branch_grad, shares):
    n_exp, n_tp, _, wide = shares.shape
    arrays = (grads, low_grad, qkv_down, tokens, gains, branch_grad)
    return pl.pallas_call(
        input_back_kernel,
        in_specs=[IN_SMEM] + [IN_HBM] * (1 + len(arrays)),
        out_specs=IN_VMEM,
        out_shape=shape(tokens.shape, BF16),
        scratch_shapes=load_scratch(arrays, LIVE)
        + [
            pltpu.VMEM((n_tp, D, wide), BF16),
            pltpu.VMEM((LIVE, D), F32),
            pltpu.SemaphoreType.DMA((n_tp, n_exp)),
        ],
        compiler_params=WHOLE_VMEM,
        cost_estimate=cost(2e9, 2e6),
        name="input_backward",
    )(place, shares, *arrays)


FINISH_LOADS = ("output", "qkv_sum", "out_parts")


def finish_kernel(*refs):
    count = len(FINISH_LOADS)
    output_hbm, qkv_down_ref, qkv_up_ref, out_down_ref, out_up_ref = refs[count : count + 5]
    scratch = refs[count + 5 :]
    loads = Loads(FINISH_LOADS, refs[:count], scratch[:count], scratch[count])
    handed_on = pltpu.make_async_copy(loads["output"], output_hbm, scratch[count + 1])
    handed_on.start()
    qkv_sum = loads["qkv_sum"]
    qkv_down_ref[...] = qkv_sum[:D, :].astype(F32)
    for at in range(0, qkv_up_ref.shape[1], LANES):
        qkv_up_ref[:, at : at + LANES] = qkv_sum[D + at : D + at + LANES, :].astype(F32)
    out_parts = loads["out_parts"]
    for at in range(0, out_parts.shape[1], LANES):
        total = out_parts[0, at : at + LANES, :].astype(F32)
        for part in range(1, out_parts.shape[0]):
            total += out_parts[part, at : at + LANES, :].astype(F32)
        if at < D:
            out_up_ref[:, at : at + LANES] = total
        else:
            out_down_ref[at - D : at - D + LANES, :] = total
    handed_on.wait()


def finish(output, out_parts, qkv_sum):
    arrays = (output, qkv_sum, out_parts)
    return pl.pallas_call(
        finish_kernel,
        in_specs=[IN_HBM] * len(arrays),
        out_specs=[IN_HBM] + [IN_VMEM] * 4,
        out_shape=[
            shape(output.shape, BF16),
            shape((D, LANES), F32),
            shape((LANES, qkv_sum.shape[0] - D), F32),
            shape((out_parts.shape[1] - D, LANES), F32),
            shape((LANES, D), F32),
        ],
        scratch_shapes=load_scratch(arrays) + [pltpu.SemaphoreType.DMA(())],
        compiler_params=WHOLE_VMEM,
        cost_estimate=cost(0, 6e6),
        name="finish",
    )(*arrays)


def from_tp(share, count):
    around = [share]
    for shift in range(1, count):
        around.append(
            lax.ppermute(share, "tp", [(at, (at + shift) % count) for at in range(count)])
        )
    return around


def from_place(place_ref, z, count):
    return lax.rem(place_ref[0] - z + count, count)


def kernel_body(
    tokens, attn_gain, moe_gain, w_qkv, w_out, w_router, w_gate, w_up, w_down, qkv_down, qkv_up,
    out_down, out_up, lengths, adapter_index, loss_mask, routes, upstream,
):
    n_exp = lax.axis_size("exp")
    n_tp = lax.axis_size("tp")
    exp_place = lax.axis_index("exp").astype(jnp.int32).reshape(1)
    tp_place = lax.axis_index("tp").astype(jnp.int32).reshape(1)
    tables = turn_tables(tokens.shape[0])
    gains = jnp.stack([attn_gain, moe_gain])

    own_experts, own_qkv = pack(exp_place, w_gate, w_up, w_down, w_qkv, qkv_up, n_exp)
    weights = lax.all_gather(own_experts, "exp", axis=0, tiled=True)
    z_qkv = from_tp(own_qkv, n_tp)
    inputs, _ = lax.optimization_barrier((tokens, own_qkv))
    attn_in, low_q, head, base, own_out = forward(
        exp_place, lengths, adapter_index, inputs, gains, w_qkv, qkv_down, qkv_up, w_out, out_down,
        tables, n_exp,
    )
    live_loss = lax.slice_in_dim(loss_mask, 0, LIVE)
    cot = jnp.where(live_loss[:, None] > 0, upstream[:LIVE], jnp.zeros((), BF16))
    expert = jnp.arange(w_router.shape[1], dtype=jnp.int32)
    routed = jnp.any(routes[:, :, None] == expert[None, None, :], axis=1)
    bias = jnp.where(routed, 0.0, -1e30).astype(F32)
    base, z_qkv, cot, bias = lax.optimization_barrier((base, z_qkv, cot, bias))
    z_qkv = jnp.stack(z_qkv)
    base = lax.psum(base, "tp")
    near_out = lax.ppermute(own_out, "tp", [(at, at ^ 1) for at in range(n_tp)])
    z_qkv, _, near_out = lax.optimization_barrier((z_qkv, weights, near_out))
    pair_out, _ = lax.optimization_barrier((jnp.stack([own_out, near_out]), base))
    far_out = lax.ppermute(pair_out, "tp", [(at, at ^ 2) for at in range(n_tp)])
    qkv_shares = lax.all_gather(z_qkv, "exp", axis=0)

    residual, hidden, normed_part = experts_both(
        lengths, adapter_index, tokens, base, out_up, gains, w_router, bias, cot, weights
    )
    normed_part, far_out = lax.optimization_barrier((normed_part, far_out))
    z_out = jnp.concatenate([pair_out, far_out])
    normed_grad = lax.psum(normed_part, "tp")
    z_out, _ = lax.optimization_barrier((z_out, qkv_shares))
    out_shares = lax.all_gather(z_out, "exp", axis=0)
    late_in, _ = lax.optimization_barrier((attn_in, normed_part))
    heads = prepare(tp_place, lengths, late_in, low_q, tables, qkv_shares)

    moe_part, normed_grad, _ = lax.optimization_barrier(
        (combine(tp_place, hidden, residual, weights), normed_grad, heads[0])
    )
    output = lax.psum(moe_part, "tp")
    branch_grad, low_o_grad, out_part = branch_back(
        lengths, adapter_index, residual, base, normed_grad, cot, gains, out_up, head
    )
    out_parts = lax.all_gather(out_part, "exp", axis=0)
    grads, low_grad, qkv_part = heads_back(
        tp_place, lengths, adapter_index, attn_in, low_q, heads, branch_grad, low_o_grad, tables,
        qkv_shares, out_shares,
    )
    share = qkv_part.shape[0] // n_exp
    parts = lax.all_to_all(qkv_part.reshape(n_exp, share, LANES), "exp", 0, 0, tiled=True)
    input_grad = input_back(
        tp_place, grads, low_grad, qkv_down, tokens, gains, branch_grad, qkv_shares
    )
    parts, input_grad = lax.optimization_barrier((parts, input_grad))
    qkv_sum = jnp.sum(parts.astype(F32), axis=0).astype(BF16)
    qkv_sum = lax.all_gather(qkv_sum, "exp", axis=0, tiled=True)
    out_parts, output, _ = lax.optimization_barrier((out_parts, output, qkv_sum))
    output, *adapters = finish(output, out_parts, qkv_sum)
    return (output, input_grad) + tuple(adapters)


def product(left_m, right_m):
    return jnp.dot(left_m, right_m, preferred_element_type=jnp.float32)


def contract(einsum_form, left_m, right_m):
    return jnp.einsum(einsum_form, left_m, right_m, preferred_element_type=jnp.float32)


def rms_norm(vectors, gain_vec):
    inv_root = lax.rsqrt(jnp.mean(vectors * vectors, axis=-1, keepdims=True) + EPS)
    return vectors * inv_root * gain_vec


def rms_norm_back(vectors, gain_vec, upstream_grad):
    inv_root = lax.rsqrt(jnp.mean(vectors * vectors, axis=-1, keepdims=True) + EPS)
    weighted = upstream_grad * gain_vec
    return inv_root * weighted - vectors * (inv_root * inv_root * inv_root) * jnp.mean(
        vectors * weighted, axis=-1, keepdims=True
    )


def layout(length_row, index_row):
    places = jnp.arange(TOK_DEV, dtype=jnp.int32)
    doc_ends = jnp.cumsum(length_row)
    doc_starts = doc_ends - length_row
    member = (places[:, None] >= doc_starts[None, :]) & (places[:, None] < doc_ends[None, :])
    occupied = jnp.any(member, axis=1)
    position = jnp.sum(jnp.where(member, places[:, None] - doc_starts[None, :], 0), axis=1)
    owner_doc = jnp.sum(jnp.where(member, jnp.arange(DOCS, dtype=jnp.int32)[None, :], 0), axis=1)
    doc_ident = jnp.where(occupied, owner_doc, DOCS + places)
    chosen = jnp.sum(jnp.where(member, index_row[None, :], 0), axis=1)
    adapter_pick = occupied[:, None] & (
        chosen[:, None] == jnp.arange(ADAPTERS, dtype=jnp.int32)[None, :]
    )
    rank_mask = jnp.repeat(jnp.where(adapter_pick, 1.0, 0.0).astype(jnp.float32), RANK, axis=1)
    return (occupied, position, doc_ident, rank_mask)


def angles(position):
    half_width = HD // 2
    frequency = jnp.exp(-math.log(ROPE_BASE) * jnp.arange(half_width, dtype=jnp.float32) * 2.0 / HD)
    turned = position.astype(jnp.float32)[:, None] * frequency[None, :]
    return (jnp.cos(turned), jnp.sin(turned))


def rotate(vectors, cosine, sine_table):
    half_width = vectors.shape[-1] // 2
    front_half = vectors[..., :half_width]
    back_half = vectors[..., half_width:]
    return jnp.concatenate(
        [
            front_half * cosine - back_half * sine_table,
            back_half * cosine + front_half * sine_table,
        ],
        axis=-1,
    )


def moe(normed, cot_low, gates, gate_up, down):
    width = down.shape[1]
    both = contract("td,edf->tef", normed, gate_up)
    pre_gate = both[:, :, :width]
    pre_up = both[:, :, width:]
    sigmoid_g = jax.nn.sigmoid(pre_gate)
    activated = pre_gate * sigmoid_g
    hidden = (activated * pre_up).astype(jnp.bfloat16).astype(jnp.float32)
    inner_raw = contract("td,efd->tef", cot_low, down)
    gate_part = jnp.sum(hidden * inner_raw, axis=-1)
    moe_part = contract("tef,efd->td", (gates[:, :, None] * hidden).astype(jnp.bfloat16), down)
    inner_grad = inner_raw * gates[:, :, None]
    grad_gate = inner_grad * pre_up * sigmoid_g * (1.0 + pre_gate * (1.0 - sigmoid_g))
    grad_up = inner_grad * activated
    grad_both = jnp.concatenate([grad_gate, grad_up], axis=2).astype(jnp.bfloat16)
    normed_part = contract("tef,edf->td", grad_both, gate_up)
    return (moe_part, gate_part, normed_part)


def body(
    tokens,
    attn_gain,
    moe_gain,
    w_qkv,
    w_out,
    w_router,
    w_gate,
    w_up,
    w_down,
    qkv_down,
    qkv_up,
    out_down,
    out_up,
    lengths,
    adapter_index,
    loss_mask,
    routes,
    upstream,
):
    n_exp = lax.axis_size("exp")
    groups = KV_HEADS // lax.axis_size("tp")
    per_group = HEADS // KV_HEADS
    experts = EXP_DEV * n_exp
    gate_up = lax.all_gather(jnp.concatenate([w_gate, w_up], axis=2), "exp", axis=0, tiled=True)
    down = lax.all_gather(w_down, "exp", axis=0, tiled=True)
    block_rows = min(512, TOK_DEV)
    blocks = TOK_DEV // block_rows
    score_scale = 1.0 / math.sqrt(HD)
    places = jnp.arange(TOK_DEV, dtype=jnp.int32)
    occupied, position, doc_ident, rank_mask = layout(lengths[0], adapter_index[0])
    mask_low = rank_mask.astype(jnp.bfloat16)
    cosine, sine_table = angles(position)
    inputs = tokens.astype(jnp.float32)
    attn_in = rms_norm(inputs, attn_gain).astype(jnp.bfloat16)
    low_q = (product(attn_in, qkv_down) * rank_mask).astype(jnp.bfloat16)
    projected = (product(attn_in, w_qkv) + product(low_q, qkv_up)).reshape(
        TOK_DEV, groups, per_group + 2, HD
    )
    query_rows = rotate(
        projected[:, :, :per_group], cosine[:, None, None], sine_table[:, None, None]
    ).astype(jnp.bfloat16)
    key_rows = rotate(projected[:, :, per_group], cosine[:, None], sine_table[:, None]).astype(
        jnp.bfloat16
    )
    val_rows = projected[:, :, per_group + 1].astype(jnp.bfloat16)

    def masked_scores(q_blk, q_place, q_ident):
        scores = contract("qgrd,kgd->grqk", q_blk, key_rows) * score_scale
        allowed = (q_ident[:, None] == doc_ident[None, :]) & (places[None, :] <= q_place[:, None])
        return jnp.where(allowed, scores, -1e30)

    def attend(pieces):
        q_blk, q_place, q_ident = pieces
        scores = masked_scores(q_blk, q_place, q_ident)
        row_max = jnp.max(scores, axis=-1, keepdims=True)
        lifted = jnp.exp(scores - row_max)
        row_total = jnp.sum(lifted, axis=-1, keepdims=True)
        weights = (lifted / row_total).astype(jnp.bfloat16)
        return (
            contract("grqk,kgd->qgrd", weights, val_rows),
            row_max[..., 0] + jnp.log(row_total[..., 0]),
        )

    query_blocks = query_rows.reshape(blocks, block_rows, groups, per_group, HD)
    place_blocks = places.reshape(blocks, block_rows)
    ident_blocks = doc_ident.reshape(blocks, block_rows)
    attended, log_totals = lax.map(attend, (query_blocks, place_blocks, ident_blocks))
    head_rows = attended.reshape(TOK_DEV, groups * per_group * HD).astype(jnp.bfloat16)
    attn_base, low_rank = (
        lax.psum(product(head_rows, w_out).astype(jnp.bfloat16), "tp").astype(jnp.float32),
        lax.psum((product(head_rows, out_down) * rank_mask).astype(jnp.bfloat16), "tp").astype(
            jnp.float32
        ),
    )
    low_o = low_rank.astype(jnp.bfloat16)
    residual = inputs + attn_base + product(low_o, out_up)
    normed = rms_norm(residual, moe_gain).astype(jnp.bfloat16)
    logits = product(normed, w_router)
    one_hot = routes[:, :, None] == jnp.arange(experts, dtype=jnp.int32)[None, None, :]
    routed = jnp.any(one_hot, axis=1)
    gates = jax.nn.softmax(jnp.where(routed, logits, -1e30), axis=-1)
    live_mask = jnp.where(occupied & (loss_mask > 0), 1.0, 0.0).astype(jnp.float32)
    cotangent = upstream.astype(jnp.float32) * live_mask[:, None]
    cot_low = cotangent.astype(jnp.bfloat16)
    moe_part, gate_part, normed_part = moe(normed, cot_low, gates, gate_up, down)
    logit_grad = (
        gates * (gate_part - jnp.sum(gates * gate_part, axis=-1, keepdims=True))
    ).astype(jnp.bfloat16)
    normed_part = (normed_part + product(logit_grad, w_router.T)).astype(jnp.bfloat16)
    normed_sum = lax.psum(normed_part, "tp")
    normed_sum, moe_part = lax.optimization_barrier((normed_sum, moe_part.astype(jnp.bfloat16)))
    normed_grad = normed_sum.astype(jnp.float32)
    moe_out = lax.psum(moe_part, "tp").astype(jnp.float32)
    output = (residual + moe_out).astype(jnp.bfloat16)
    residual_grad = cotangent + rms_norm_back(residual, moe_gain, normed_grad)
    branch_grad = residual_grad.astype(jnp.bfloat16)
    low_o_grad = product(branch_grad, out_up.T).astype(jnp.bfloat16) * mask_low
    out_up_part = contract("tr,td->rd", low_o, branch_grad)
    head_grad = (product(branch_grad, w_out.T) + product(low_o_grad, out_down.T)).astype(
        jnp.bfloat16
    )
    out_down_part = contract("tc,tr->cr", head_rows, low_o_grad)
    grad_blocks = head_grad.reshape(blocks, block_rows, groups, per_group, HD)

    def attend_back(carried, pieces):
        key_acc, val_acc = carried
        q_blk, q_place, q_ident, lse_blk, g_blk = pieces
        weights = jnp.exp(masked_scores(q_blk, q_place, q_ident) - lse_blk[..., None])
        weight_grad = contract("qgrd,kgd->grqk", g_blk, val_rows)
        score_grad = (
            weights * (weight_grad - jnp.sum(weights * weight_grad, axis=-1, keepdims=True))
        ).astype(jnp.bfloat16)
        query_grad = contract("grqk,kgd->qgrd", score_grad, key_rows) * score_scale
        key_acc = key_acc + contract("grqk,qgrd->kgd", score_grad, q_blk) * score_scale
        val_acc = val_acc + contract("grqk,qgrd->kgd", weights.astype(jnp.bfloat16), g_blk)
        return ((key_acc, val_acc), query_grad)

    zero_acc = jnp.zeros((TOK_DEV, groups, HD), jnp.float32)
    (key_grad, val_grad), query_grad = lax.scan(
        attend_back,
        (zero_acc, zero_acc),
        (query_blocks, place_blocks, ident_blocks, log_totals, grad_blocks),
    )
    query_grad = rotate(
        query_grad.reshape(TOK_DEV, groups, per_group, HD),
        cosine[:, None, None],
        -sine_table[:, None, None],
    )
    key_grad = rotate(key_grad, cosine[:, None], -sine_table[:, None])
    projected_grad = (
        jnp.concatenate([query_grad, key_grad[:, :, None], val_grad[:, :, None]], axis=2)
        .reshape(TOK_DEV, -1)
        .astype(jnp.bfloat16)
    )
    qkv_up_part = contract("tr,tc->rc", low_q, projected_grad)
    attn_grad, low_q_grad = (
        lax.psum(contract("tc,dc->td", projected_grad, w_qkv).astype(jnp.bfloat16), "tp").astype(
            jnp.float32
        ),
        lax.psum(contract("tc,rc->tr", projected_grad, qkv_up).astype(jnp.bfloat16), "tp").astype(
            jnp.float32
        ),
    )
    low_q_grad = low_q_grad.astype(jnp.bfloat16) * mask_low
    attn_grad = attn_grad + contract("tr,dr->td", low_q_grad, qkv_down)
    qkv_down_part = contract("td,tr->dr", attn_in, low_q_grad)
    input_grad = (residual_grad + rms_norm_back(inputs, attn_gain, attn_grad)).astype(jnp.bfloat16)
    summed = (
        lax.psum(qkv_down_part.astype(jnp.bfloat16), "exp").astype(jnp.float32),
        lax.psum(qkv_up_part.astype(jnp.bfloat16), "exp").astype(jnp.float32),
        lax.psum(out_down_part.astype(jnp.bfloat16), "exp").astype(jnp.float32),
        lax.psum(out_up_part.astype(jnp.bfloat16), "exp").astype(jnp.float32),
    )
    return (output, input_grad, summed[0], summed[1], summed[2], summed[3])


def kernels_fit(mesh):
    n_exp, n_tp = mesh.shape["exp"], mesh.shape["tp"]
    groups = KV_HEADS // n_tp
    return groups % 2 == 0 and FF // n_tp == LANES and LANES // n_exp % 16 == 0


def solution(mesh):
    placed = (
        P("exp", None),
        P(),
        P(),
        P(None, "tp"),
        P("tp", None),
        P(),
        P("exp", None, "tp"),
        P("exp", None, "tp"),
        P("exp", "tp", None),
        P(),
        P(None, "tp"),
        P("tp", None),
        P(),
        P("exp", None),
        P("exp", None),
        P("exp"),
        P("exp", None),
        P("exp", None),
    )
    return jax.shard_map(
        kernel_body if kernels_fit(mesh) else body,
        mesh=mesh,
        in_specs=placed,
        out_specs=(P("exp", None), P("exp", None), P(), P(None, "tp"), P("tp", None), P()),
        check_vma=False,
    )
```

```python
import functools
import math

import jax
import jax.numpy as jnp
import numpy as np
from jax import lax
from jax.experimental import pallas as pl
from jax.experimental.pallas import tpu as pltpu
from jax.sharding import PartitionSpec as P

D = 1536
HEADS = 24
KV_HEADS = 8
HD = 64
TOP = 8
RANK = 16
ADAPTERS = 8
EXP_DEV = 2
DOCS = 4
TOK_DEV = 512
LIVE = 448
FF = 512
EPS = 1e-06
ROPE_BASE = 10000.0

PER = HEADS // KV_HEADS
LANES = 128
ROWS = 128
BLOCKS = tuple((at, min(at + ROWS, TOK_DEV)) for at in range(0, TOK_DEV, ROWS))
LIVE_BLOCKS = tuple((at, min(at + ROWS, LIVE)) for at in range(0, LIVE, ROWS))
F32 = jnp.float32
BF16 = jnp.bfloat16
MIB = 2**20
NT = (((1,), (1,)), ((), ()))
TN = (((0,), (0,)), ((), ()))
WHOLE_VMEM = pltpu.CompilerParams(vmem_limit_bytes=63 * MIB)
IN_VMEM = pl.BlockSpec(memory_space=pltpu.VMEM)
IN_SMEM = pl.BlockSpec(memory_space=pltpu.SMEM)
IN_HBM = pl.BlockSpec(memory_space=pltpu.HBM)


def dot(left, right):
    return jnp.dot(left, right, preferred_element_type=F32)


def dot_nt(left, right):
    return lax.dot_general(left, right, NT, preferred_element_type=F32)


def dot_tn(left, right):
    return lax.dot_general(left, right, TN, preferred_element_type=F32)


def cost(flops, moved):
    return pl.CostEstimate(flops=int(flops), bytes_accessed=int(moved), transcendentals=0)


def shape(dims, dtype):
    return jax.ShapeDtypeStruct(dims, dtype)


def turn_tables(rows):
    half = HD // 2
    frequency = np.exp(-math.log(ROPE_BASE) * np.arange(half, dtype=np.float64) * 2.0 / HD)
    turned = np.arange(rows, dtype=np.float64)[:, None] * frequency[None, :]
    cosine, sine = np.cos(turned), np.sin(turned)
    return (
        jnp.asarray(np.concatenate([cosine] * 4, axis=1), F32),
        jnp.asarray(np.concatenate([-sine, sine, -sine, sine], axis=1), F32),
    )


def turned_pieces(groups):
    return [piece < PER + 1 for _ in range(groups) for piece in range(PER + 2)]


def turn(joined, cosine, sine, flags):
    lane = lax.broadcasted_iota(jnp.int32, cosine.shape, 1)
    front = (lane & 32) == 0
    left = lane < HD
    columns = []
    for at in range(joined.shape[1] // LANES):
        column = joined[:, at * LANES : (at + 1) * LANES]
        swapped = jnp.where(front, pltpu.roll(column, 96, 1), pltpu.roll(column, 32, 1))
        rotated = column * cosine + swapped * sine
        if not (flags[2 * at] and flags[2 * at + 1]):
            rotated = jnp.where(left if flags[2 * at] else jnp.logical_not(left), rotated, column)
        columns.append(rotated)
    return columns


def first_keys(length_ref, rows):
    row = lax.broadcasted_iota(jnp.int32, (rows, 1), 0)
    begin = jnp.zeros((rows, 1), jnp.int32)
    end = 0
    for doc in range(DOCS):
        if doc:
            begin = jnp.where(row >= end, end, begin)
        end = end + length_ref[0, doc]
    return jnp.where(row >= end, row, begin)


def adapter_mask(length_ref, index_ref, rows, width):
    row = lax.broadcasted_iota(jnp.int32, (rows, width), 0)
    adapter = lax.shift_right_logical(lax.broadcasted_iota(jnp.int32, (rows, width), 1), 4)
    mask = jnp.zeros((rows, width), F32)
    begin = 0
    for doc in range(DOCS):
        end = begin + length_ref[0, doc]
        inside = (row >= begin) & (row < end) & (adapter == index_ref[0, doc])
        mask = jnp.where(inside, 1.0, mask)
        begin = end
    return mask


def folding():
    rank = lax.broadcasted_iota(jnp.int32, (RANK, LANES), 0)
    lane = lax.broadcasted_iota(jnp.int32, (RANK, LANES), 1)
    return jnp.where((lane & (RANK - 1)) == rank, 1.0, 0.0).astype(BF16)


def unfold(low_ref, length_ref, index_ref, rows):
    spread = dot_tn(low_ref[-RANK:, :rows], folding())
    return (spread * adapter_mask(length_ref, index_ref, rows, LANES)).astype(BF16)


def seen_block(first, begin, end):
    row = lax.broadcasted_iota(jnp.int32, (end - begin, end), 0) + begin
    key = lax.broadcasted_iota(jnp.int32, (end - begin, end), 1)
    seen = (key <= row) & (key >= first[begin:end])
    return jnp.concatenate([seen] * PER, axis=0)


def softmax_block(scores, seen):
    scores = jnp.where(seen, scores, -1e30)
    lifted = jnp.exp(scores - jnp.max(scores, axis=1, keepdims=True))
    return (lifted * (1.0 / jnp.sum(lifted, axis=1, keepdims=True))).astype(BF16)


def store_heads(columns, slot, blocks, q_s, k_s, v_s):
    scale = 1.0 / math.sqrt(HD)
    for at, column in enumerate(columns):
        halves = (column[:, :HD], pltpu.roll(column, HD, 1)[:, :HD])
        for piece, part in zip((2 * at, 2 * at + 1), halves):
            group, kind = divmod(piece, PER + 2)
            if kind == PER:
                k_s[slot + group] = part.astype(BF16)
            elif kind == PER + 1:
                v_s[slot + group] = part.astype(BF16)
            else:
                part = (part * scale).astype(BF16)
                for block, (begin, end) in enumerate(blocks):
                    size = end - begin
                    here = slice(kind * size, (kind + 1) * size)
                    q_s[slot + group, block, here, :] = part[begin:end]


def run_copies(pairs, sem):
    copies = [
        pltpu.make_async_copy(source, target, sem.at[number])
        for number, (source, target) in enumerate(pairs)
    ]
    for copy in copies:
        copy.start()
    for copy in copies:
        copy.wait()


def pack_kernel(
    n_exp, place_ref, gate, up, down, w_qkv, qkv_up, packed, share, held, share_s, sem, out_sem
):
    width = gate.shape[2]
    pairs = []
    for expert in range(gate.shape[0]):
        pairs.append((gate.at[expert], held.at[expert, :, :width]))
        pairs.append((up.at[expert], held.at[expert, :, width : 2 * width]))
        for at in range(D // LANES):
            lanes = slice(at * LANES, (at + 1) * LANES)
            pairs.append((down.at[expert, :, lanes], held.at[expert, lanes, 2 * width :]))
    qkv_rows, up_rows, _ = share_rows(n_exp, 0)
    own_qkv = pl.ds(pl.multiple_of(place_ref[0] * qkv_rows, 16), qkv_rows)
    own_up = pl.ds(pl.multiple_of(place_ref[0] * up_rows, 16), up_rows)
    pairs.append((w_qkv.at[own_qkv, :], share_s.at[:qkv_rows, :]))
    pairs.append((qkv_up.at[own_up, :], share_s.at[qkv_rows:, :]))
    run_copies(pairs, sem)
    run_copies([(held, packed), (share_s, share)], out_sem)


def share_rows(n_exp, heads_wide):
    return (D // n_exp, LANES // n_exp, heads_wide // n_exp)


def pack(place, w_gate, w_up, w_down, w_qkv, qkv_up, n_exp):
    count, _, width = w_gate.shape
    packed = shape((count, D, 3 * width), BF16)
    share = shape(((D + LANES) // n_exp, w_qkv.shape[1]), BF16)
    return pl.pallas_call(
        functools.partial(pack_kernel, n_exp),
        in_specs=[IN_SMEM] + [IN_HBM] * 5,
        out_specs=[IN_HBM] * 2,
        out_shape=[packed, share],
        scratch_shapes=[
            pltpu.VMEM(packed.shape, BF16),
            pltpu.VMEM(share.shape, BF16),
            pltpu.SemaphoreType.DMA((count * (2 + D // LANES) + 2,)),
            pltpu.SemaphoreType.DMA((2,)),
        ],
        compiler_params=WHOLE_VMEM,
        cost_estimate=cost(0, 2 * 2 * count * D * 3 * width),
        name="pack_weights",
    )(place, w_gate, w_up, w_down, w_qkv, qkv_up)


class Loads:
    def __init__(self, names, sources, targets, sem):
        self.copies = {}
        for number, (name, source, target) in enumerate(zip(names, sources, targets)):
            if source.shape[0] == TOK_DEV + RANK:
                source = source.at[TOK_DEV:]
            elif source.shape != target.shape:
                source = source.at[: target.shape[0]]
            self.copies[name] = pltpu.make_async_copy(source, target, sem.at[number])
        self.targets = dict(zip(names, targets))
        for copy in self.copies.values():
            copy.start()

    def __getitem__(self, name):
        copy = self.copies.pop(name, None)
        if copy is not None:
            copy.wait()
        return self.targets[name]


def load_scratch(arrays, rows=TOK_DEV):
    kept = {TOK_DEV: rows, TOK_DEV + RANK: RANK}
    rooms = []
    for array in arrays:
        first = kept.get(array.shape[0], array.shape[0])
        rooms.append(pltpu.VMEM((first,) + array.shape[1:], array.dtype))
    return rooms + [pltpu.SemaphoreType.DMA((len(arrays),))]


FORWARD_LOADS = (
    "tokens", "gains", "qkv_down", "w_qkv", "qkv_up", "cosine", "sine", "w_out", "out_down",
)


def forward_kernel(place_ref, length_ref, index_ref, *refs):
    count = len(FORWARD_LOADS)
    attn_in_ref, low_q_ref, head_ref, base_ref, share_ref = refs[count : count + 5]
    load_sem, q_s, k_s, v_s = refs[2 * count + 5 :]
    loads = Loads(FORWARD_LOADS, refs[:count], refs[count + 5 : 2 * count + 5], load_sem)
    rows = attn_in_ref.shape[0]
    groups = k_s.shape[0]
    mask = adapter_mask(length_ref, index_ref, rows, LANES)
    first = first_keys(length_ref, rows)
    inputs = loads["tokens"][...].astype(F32)
    inv_root = lax.rsqrt(jnp.mean(inputs * inputs, axis=1, keepdims=True) + EPS)
    attn_in_ref[...] = (inputs * inv_root * loads["gains"][0:1, :]).astype(BF16)
    attn_in = attn_in_ref[...]
    low_q = (dot(attn_in, loads["qkv_down"][...]) * mask).astype(BF16)
    low_q_ref[...] = low_q
    projected = dot(attn_in, loads["w_qkv"][...]) + dot(low_q, loads["qkv_up"][...])
    cosine, sine = loads["cosine"][...], loads["sine"][...]
    columns = turn(projected, cosine, sine, turned_pieces(groups))
    store_heads(columns, 0, BLOCKS, q_s, k_s, v_s)
    for block, (begin, end) in enumerate(BLOCKS):
        seen = seen_block(first, begin, end)
        scores = [dot_nt(q_s[group, block], k_s[group, :end, :]) for group in range(groups)]
        probs = [softmax_block(part, seen) for part in scores]
        heads = []
        for group in range(groups):
            out = dot(probs[group], v_s[group, :end, :])
            heads += [out[head * ROWS : (head + 1) * ROWS] for head in range(PER)]
        head_ref[begin:end, :] = jnp.concatenate(heads, axis=1).astype(BF16)
    head_out = head_ref[...]
    base_ref[:rows, :] = dot(head_out, loads["w_out"][...]).astype(BF16)
    low_o = (dot(head_out, loads["out_down"][...]) * mask).astype(BF16)
    base_ref[rows:, :rows] = dot_nt(folding(), low_o).astype(BF16)
    base_ref[rows:, rows:] = jnp.zeros((RANK, D - rows), BF16)
    share_rows_count = share_ref.shape[0]
    own = pl.ds(pl.multiple_of(place_ref[0] * share_rows_count, 16), share_rows_count)
    share_ref[:, :D] = loads["w_out"][own, :]
    share_ref[:, D:] = loads["out_down"][own, :]


def forward(
    place, lengths, index, tokens, gains, w_qkv, qkv_down, qkv_up, w_out, out_down, tables, n_exp
):
    rows = tokens.shape[0]
    heads_wide = w_out.shape[0]
    groups = w_qkv.shape[1] // (HD * (PER + 2))
    arrays = (tokens, gains, qkv_down, w_qkv, qkv_up) + tables + (w_out, out_down)
    return pl.pallas_call(
        forward_kernel,
        in_specs=[IN_SMEM] * 3 + [IN_HBM] * len(arrays),
        out_specs=[IN_VMEM] * 5,
        out_shape=[
            shape((rows, D), BF16),
            shape((rows, LANES), BF16),
            shape((rows, heads_wide), BF16),
            shape((rows + RANK, D), BF16),
            shape((heads_wide // n_exp, D + LANES), BF16),
        ],
        scratch_shapes=load_scratch(arrays)
        + [
            pltpu.VMEM((groups, rows // ROWS, PER * ROWS, HD), BF16),
            pltpu.VMEM((groups, rows, HD), BF16),
            pltpu.VMEM((groups, rows, HD), BF16),
        ],
        compiler_params=WHOLE_VMEM,
        cost_estimate=cost(6e9, 10e6),
        name="attention_forward",
    )(place, lengths, index, *arrays)


def down_of(weight, width):
    columns = [
        weight[at * LANES : (at + 1) * LANES, 2 * width : 3 * width] for at in range(D // LANES)
    ]
    return jnp.concatenate(columns, axis=1)


def experts_kernel(
    length_ref, index_ref, tokens_ref, base_ref, out_up_ref, gains_ref, router_ref, bias_ref,
    cot_ref, weight_ref, residual_ref, hidden_ref, grad_ref,
    normed_s, gates_s, part_s, grad_s,
):
    step = pl.program_id(0)
    count, _, packed = weight_ref.shape
    width = packed // 3
    lane = lax.broadcasted_iota(jnp.int32, gates_s.shape, 1)

    @pl.when(step == 0)
    def _():
        residual = (
            tokens_ref[...].astype(F32)
            + base_ref[:TOK_DEV, :].astype(F32)
            + dot(unfold(base_ref, length_ref, index_ref, TOK_DEV), out_up_ref[...])
        )
        residual_ref[...] = residual.astype(BF16)
        inv_root = lax.rsqrt(jnp.mean(residual * residual, axis=1, keepdims=True) + EPS)
        normed = (residual * inv_root * gains_ref[1:2, :]).astype(BF16)
        normed_s[...] = normed
        logits = dot_nt(normed, router_ref[...]) + bias_ref[...]
        lifted = jnp.exp(logits - jnp.max(logits, axis=1, keepdims=True))
        gates_s[...] = lifted / jnp.sum(lifted, axis=1, keepdims=True)
        part_s[...] = jnp.zeros_like(part_s)
        grad_s[...] = jnp.zeros_like(grad_s)

    normed = normed_s[...]
    cot = cot_ref[...]
    gates = gates_s[...]
    part = jnp.zeros(part_s.shape, F32)
    grads = []
    for pair in range(0, count, 2):
        pair_down = [down_of(weight_ref.at[pair + half], width) for half in range(2)]
        pair_raw = dot_nt(cot, jnp.concatenate(pair_down, axis=0))
        for half in range(2):
            expert = pair + half
            joined = dot(normed, weight_ref[expert, :, : 2 * width])
            pre_gate = joined[:, :width]
            pre_up = joined[:, width:]
            raw = pair_raw[:, half * width : (half + 1) * width]
            sigmoid = 0.5 * jnp.tanh(0.5 * pre_gate) + 0.5
            activated = pre_gate * sigmoid
            value = activated * pre_up
            here = lane == step * count + expert
            gate = jnp.sum(jnp.where(here, gates, 0.0), axis=1, keepdims=True)
            hidden_ref[:, expert * width : (expert + 1) * width] = (gate * value).astype(BF16)
            gate_grad = jnp.sum(value[:LIVE] * raw, axis=1, keepdims=True)
            part += jnp.where(here[:LIVE], gate_grad, 0.0)
            inner = raw * gate[:LIVE]
            sigmoid, activated = sigmoid[:LIVE], activated[:LIVE]
            slope = sigmoid + activated * (1.0 - sigmoid)
            grads.append((inner * pre_up[:LIVE] * slope).astype(BF16))
            grads.append((inner * activated).astype(BF16))
    part_s[...] += part
    ups = [weight_ref[expert, :, : 2 * width] for expert in range(count)]
    grad_s[...] += dot_nt(jnp.concatenate(grads, axis=1), jnp.concatenate(ups, axis=1))

    @pl.when(step == pl.num_programs(0) - 1)
    def _():
        live_gates, gate_part = gates[:LIVE], part_s[...]
        spread = jnp.sum(live_gates * gate_part, axis=1, keepdims=True)
        logit_grad = (live_gates * (gate_part - spread)).astype(BF16)
        grad_ref[...] = (grad_s[...] + dot(logit_grad, router_ref[...])).astype(BF16)


def experts_both(
    lengths, index, tokens, base, out_up, gains, router, bias, cot, weights, count=4,
):
    rows = tokens.shape[0]
    experts, _, packed = weights.shape
    width = packed // 3
    arrays = (tokens, base, out_up, gains, router.T, bias, cot)
    in_specs = [IN_SMEM] * 2
    in_specs += [pl.BlockSpec(array.shape, lambda step: (0, 0)) for array in arrays]
    in_specs.append(pl.BlockSpec((count, D, packed), lambda step: (step, 0, 0)))
    return pl.pallas_call(
        experts_kernel,
        grid=(experts // count,),
        in_specs=in_specs,
        out_specs=[
            pl.BlockSpec((rows, D), lambda step: (0, 0)),
            pl.BlockSpec((rows, count * width), lambda step: (0, step)),
            pl.BlockSpec((LIVE, D), lambda step: (0, 0)),
        ],
        out_shape=[
            shape((rows, D), BF16),
            shape((rows, experts * width), BF16),
            shape((LIVE, D), BF16),
        ],
        scratch_shapes=[
            pltpu.VMEM((rows, D), BF16),
            pltpu.VMEM((rows, experts), F32),
            pltpu.VMEM((LIVE, experts), F32),
            pltpu.VMEM((LIVE, D), F32),
        ],
        compiler_params=WHOLE_VMEM,
        cost_estimate=cost(0, 1000),
        name="experts",
    )(lengths, index, *arrays, weights)


def combine_kernel(
    place_ref, hidden_hbm, residual_hbm, weights_hbm, moe_ref, hidden_s, residual_s, downs_s,
    hidden_sem, residual_sem, sem,
):
    experts, _, width = downs_s.shape
    load = pltpu.make_async_copy(hidden_hbm, hidden_s, hidden_sem)
    load.start()
    residual_load = pltpu.make_async_copy(residual_hbm, residual_s, residual_sem)
    residual_load.start()
    own = jnp.where(place_ref[0] == 0, 1.0, 0.0).astype(F32)
    copies = []
    for expert in range(experts):
        source, target = weights_hbm.at[expert, :, 2 * width :], downs_s.at[expert]
        copies.append(pltpu.make_async_copy(source, target, sem.at[expert]))
        copies[-1].start()
    load.wait()
    residual_load.wait()
    for copy in copies:
        copy.wait()
    for at in range(0, D, 2 * LANES):
        columns = []
        for expert in range(experts):
            pieces = [
                downs_s[expert, at + left : at + left + LANES, :] for left in (0, LANES)
            ]
            columns.append(jnp.concatenate(pieces, axis=1))
        moe = dot(hidden_s[...], jnp.concatenate(columns, axis=0))
        here = slice(at, at + 2 * LANES)
        moe_ref[:, here] = (moe + own * residual_s[:, here].astype(F32)).astype(BF16)


def combine(place, hidden, residual, weights):
    rows = hidden.shape[0]
    experts, _, packed = weights.shape
    return pl.pallas_call(
        combine_kernel,
        in_specs=[IN_SMEM] + [IN_HBM] * 3,
        out_specs=IN_VMEM,
        out_shape=shape((rows, D), BF16),
        scratch_shapes=[
            pltpu.VMEM(hidden.shape, BF16),
            pltpu.VMEM(residual.shape, BF16),
            pltpu.VMEM((experts, D, packed // 3), BF16),
            pltpu.SemaphoreType.DMA(()),
            pltpu.SemaphoreType.DMA(()),
            pltpu.SemaphoreType.DMA((experts,)),
        ],
        compiler_params=WHOLE_VMEM,
        cost_estimate=cost(4e9, 10e6),
        name="combine",
    )(place, hidden, residual, weights)


def norm_back(vectors, gain, upstream):
    inv_root = lax.rsqrt(jnp.mean(vectors * vectors, axis=1, keepdims=True) + EPS)
    weighted = upstream * gain
    slope = jnp.mean(vectors * weighted, axis=1, keepdims=True)
    return inv_root * weighted - vectors * (inv_root * inv_root * inv_root) * slope


BRANCH_LOADS = (
    "residual", "normed_grad", "gains", "cot", "out_up", "low_o", "head",
)


def branch_kernel(length_ref, index_ref, *refs):
    count = len(BRANCH_LOADS)
    branch_grad_ref, low_grad_ref, part_ref = refs[count : count + 3]
    scratch = refs[count + 3 :]
    loads = Loads(BRANCH_LOADS, refs[:count], scratch[:count], scratch[count])
    mask = adapter_mask(length_ref, index_ref, LIVE, LANES)
    residual = loads["residual"][...].astype(F32)
    through = norm_back(residual, loads["gains"][1:2, :], loads["normed_grad"][...].astype(F32))
    branch_grad_ref[...] = (through + loads["cot"][...].astype(F32)).astype(BF16)
    branch_grad = branch_grad_ref[...]
    low_grad_ref[...] = (dot_nt(branch_grad, loads["out_up"][...]) * mask).astype(BF16)
    low_o = unfold(loads["low_o"], length_ref, index_ref, LIVE)
    out_up_part = dot_tn(low_o, branch_grad).astype(BF16)
    for at in range(D // LANES):
        lanes = slice(at * LANES, (at + 1) * LANES)
        part_ref[lanes, :] = out_up_part[:, lanes]
    part_ref[D:, :] = dot_tn(loads["head"][...], low_grad_ref[...]).astype(BF16)


def branch_back(
    lengths, index, residual, base, normed_grad, cot, gains, out_up, head
):
    arrays = (residual, normed_grad, gains, cot, out_up, base, head)
    return pl.pallas_call(
        branch_kernel,
        in_specs=[IN_SMEM] * 2 + [IN_HBM] * len(arrays),
        out_specs=[IN_VMEM] * 3,
        out_shape=[
            shape((LIVE, D), BF16),
            shape((LIVE, LANES), BF16),
            shape((D + head.shape[1], LANES), BF16),
        ],
        scratch_shapes=load_scratch(arrays, LIVE),
        compiler_params=WHOLE_VMEM,
        cost_estimate=cost(1e9, 2e6),
        name="branch_backward",
    )(lengths, index, *arrays)


def share_copies(place_ref, shares, w_qkv_s, sem):
    n_exp, n_tp, _, _ = shares.shape
    qkv_rows, up_rows, _ = share_rows(n_exp, 0)
    copies = []
    for z in range(n_tp):
        here = []
        source_z = from_place(place_ref, z, n_tp)
        for e in range(n_exp):
            at = e * qkv_rows
            up_at = D + e * up_rows
            for source, target in (
                (shares.at[e, source_z, :qkv_rows, :], w_qkv_s.at[z, at : at + qkv_rows, :]),
                (shares.at[e, source_z, qkv_rows:, :], w_qkv_s.at[z, up_at : up_at + up_rows, :]),
            ):
                number = 2 * e + len(here) % 2
                here.append(pltpu.make_async_copy(source, target, sem.at[z, number]))
        copies.append(here)
    for here in copies:
        for copy in here:
            copy.start()
    return copies


PREPARE_LOADS = ("attn_in", "low_q", "cosine", "sine")


def prepare_kernel(place_ref, length_ref, shares, *refs):
    count = len(PREPARE_LOADS)
    results = 1 + len(LIVE_BLOCKS)
    turned_ref = refs[count]
    prob_refs = refs[count + 1 : count + results]
    load_sem, w_qkv_s, q_s, k_s, v_s, sem = refs[2 * count + results :]
    targets = refs[count + results : 2 * count + results]
    loads = Loads(PREPARE_LOADS, refs[:count], targets, load_sem)
    n_tp = shares.shape[1]
    groups = k_s.shape[0]
    copies = share_copies(place_ref, shares, w_qkv_s, sem)
    first = first_keys(length_ref, LIVE)
    attn_in = loads["attn_in"][...]
    low_q = loads["low_q"][...]
    cosine, sine = loads["cosine"][...], loads["sine"][...]
    seen = [seen_block(first, begin, end) for begin, end in LIVE_BLOCKS]
    for here in copies:
        for copy in here:
            copy.wait()

    def one_place(z, carried):
        projected = dot(attn_in, w_qkv_s[z, :D, :]) + dot(low_q, w_qkv_s[z, D:, :])
        columns = turn(projected, cosine, sine, turned_pieces(groups))
        for at, column in enumerate(columns):
            turned_ref[z, :, at * LANES : (at + 1) * LANES] = column.astype(BF16)
        store_heads(columns, 0, LIVE_BLOCKS, q_s, k_s, v_s)
        for group in range(groups):
            for block, (begin, end) in enumerate(LIVE_BLOCKS):
                query = q_s[group, block, : PER * (end - begin), :]
                scores = dot_nt(query, k_s[group, :end, :])
                prob_refs[block][z * groups + group] = softmax_block(scores, seen[block])
        return carried

    lax.fori_loop(0, n_tp, one_place, 0)


def prepare(place, lengths, attn_in, low_q, tables, shares):
    n_exp, n_tp, _, wide = shares.shape
    arrays = (attn_in, low_q) + tables
    groups = KV_HEADS
    probs = [
        shape((groups, PER * (end - begin), end), BF16) for begin, end in LIVE_BLOCKS
    ]
    return pl.pallas_call(
        prepare_kernel,
        in_specs=[IN_SMEM] * 2 + [IN_HBM] * (1 + len(arrays)),
        out_specs=[IN_VMEM] * (1 + len(probs)),
        out_shape=[shape((n_tp, LIVE, wide), BF16)] + probs,
        scratch_shapes=load_scratch(arrays, LIVE)
        + [
            pltpu.VMEM((n_tp, D + LANES, wide), BF16),
            pltpu.VMEM((groups // n_tp, len(LIVE_BLOCKS), PER * ROWS, HD), BF16),
            pltpu.VMEM((groups // n_tp, LIVE, HD), BF16),
            pltpu.VMEM((groups // n_tp, LIVE, HD), BF16),
            pltpu.SemaphoreType.DMA((n_tp, 2 * n_exp)),
        ],
        compiler_params=WHOLE_VMEM,
        cost_estimate=cost(12e9, 30e6),
        name="prepare_heads",
    )(place, lengths, shares, *arrays)


HEADS_LOADS = (
    "branch_grad", "low_o_grad", "turned", "cosine", "sine", "low_q", "attn_in",
)


def heads_back_kernel(place_ref, length_ref, index_ref, shares, out_shares, *refs):
    count = len(HEADS_LOADS)
    blocks = len(LIVE_BLOCKS)
    probs_hbm = refs[count : count + blocks]
    grad_ref, low_grad_ref, part_ref = refs[count + blocks : count + blocks + 3]
    scratch = refs[count + blocks + 3 :]
    loads = Loads(HEADS_LOADS, refs[:count], scratch[:count], scratch[count])
    up_s, w_out_s, g_s, q_s, k_s, v_s, up_sem, out_sem, prob_sem = scratch[count + 1 : count + 10]
    probs_s = scratch[count + 10 :]
    n_exp, n_tp, _, wide = shares.shape
    groups = g_s.shape[0]
    flags = turned_pieces(groups)
    scale = 1.0 / math.sqrt(HD)

    def prob_copy(z, block):
        here = pl.ds(z * groups, groups)
        return pltpu.make_async_copy(
            probs_hbm[block].at[here], probs_s[block].at[here], prob_sem.at[z, block]
        )

    out_rows = out_shares.shape[2]

    def out_copy(z, e):
        return pltpu.make_async_copy(
            out_shares.at[e, jnp.bitwise_xor(place_ref[0], z)],
            w_out_s.at[z, e * out_rows : (e + 1) * out_rows, :],
            out_sem.at[z, e],
        )

    for z in range(n_tp):
        for e in range(n_exp):
            out_copy(z, e).start()
        for block in range(blocks):
            prob_copy(z, block).start()
    qkv_rows, up_rows, _ = share_rows(n_exp, 0)
    up_copies = []
    for z in range(n_tp):
        for e in range(n_exp):
            source = shares.at[e, from_place(place_ref, z, n_tp), qkv_rows:, :]
            target = up_s.at[z, e * up_rows : (e + 1) * up_rows, :]
            up_copies.append(pltpu.make_async_copy(source, target, up_sem.at[z, e]))
            up_copies[-1].start()
    branch_grad, low_o_grad = loads["branch_grad"], loads["low_o_grad"]
    turned = loads["turned"]
    cosine, sine = loads["cosine"], loads["sine"]

    def one_place(z, carried):
        columns = [
            turned[z, :, at * LANES : (at + 1) * LANES].astype(F32) for at in range(wide // LANES)
        ]
        store_heads(columns, 0, LIVE_BLOCKS, q_s, k_s, v_s)
        for e in range(n_exp):
            out_copy(z, e).wait()
        head_grad = (
            dot_nt(branch_grad[...], w_out_s[z, :, :D]) + dot_nt(low_o_grad[...], w_out_s[z, :, D:])
        ).astype(BF16)
        for head in range(groups * PER):
            group, kind = divmod(head, PER)
            part = head_grad[:, head * HD : (head + 1) * HD]
            for block, (begin, end) in enumerate(LIVE_BLOCKS):
                size = end - begin
                here = slice(kind * size, (kind + 1) * size)
                g_s[group, block, here, :] = part[begin:end]
        for block in range(blocks):
            prob_copy(z, block).wait()
        key_grads = [jnp.zeros((HD, LIVE), F32) for _ in range(groups)]
        value_grads = [jnp.zeros((HD, LIVE), F32) for _ in range(groups)]
        query_grads = [[] for _ in range(groups)]
        for block, (begin, end) in enumerate(LIVE_BLOCKS):
            size = end - begin

            def widen(part):
                if end == LIVE:
                    return part
                return jnp.concatenate([part, jnp.zeros((HD, LIVE - end), F32)], axis=1)

            some = range(groups)
            queries = [q_s[group, block, : PER * size, :] for group in some]
            head_grads = [g_s[group, block, : PER * size, :] for group in some]
            probs = [probs_s[block][z * groups + group] for group in some]
            weight_grads = [dot_nt(head_grads[group], v_s[group, :end, :]) for group in some]
            for group in some:
                value_grads[group] += widen(dot_tn(head_grads[group], probs[group]))
            wide_probs = [probs[group].astype(F32) for group in some]
            score_grads = []
            for group in some:
                product = wide_probs[group] * weight_grads[group]
                spread = jnp.sum(product, axis=1, keepdims=True)
                score_grads.append((product - wide_probs[group] * spread).astype(BF16))
            for group in some:
                score_grad = score_grads[group]
                query_grads[group].append(dot(score_grad, k_s[group, :end, :]) * scale)
                key_grads[group] += widen(dot_tn(queries[group], score_grad))
        pieces = []
        for group in range(groups):
            for head in range(PER):
                rows = [
                    part[head * (end - begin) : (head + 1) * (end - begin)]
                    for part, (begin, end) in zip(query_grads[group], LIVE_BLOCKS)
                ]
                pieces.append(jnp.concatenate(rows, axis=0))
            pieces += [key_grads[group].T, value_grads[group].T]
        joined = jnp.concatenate(pieces, axis=1)
        columns = turn(joined, cosine[...], -sine[...], flags)
        for at, column in enumerate(columns):
            grad_ref[z, :, at * LANES : (at + 1) * LANES] = column.astype(BF16)
        return carried

    lax.fori_loop(0, n_tp, one_place, 0)
    for copy in up_copies:
        copy.wait()
    low_grad = dot_nt(grad_ref[0], up_s[0])
    for z in range(1, n_tp):
        low_grad += dot_nt(grad_ref[z], up_s[z])
    mask = adapter_mask(length_ref, index_ref, LIVE, LANES)
    low_grad = (low_grad * mask).astype(BF16)
    low_grad_ref[...] = low_grad
    part_ref[:D, :] = dot_tn(loads["attn_in"][...], low_grad).astype(BF16)
    up_part = dot_tn(loads["low_q"][...], grad_ref[place_ref[0]]).astype(BF16)
    for at in range(wide // LANES):
        lanes = slice(at * LANES, (at + 1) * LANES)
        part_ref[D + at * LANES : D + (at + 1) * LANES, :] = up_part[:, lanes]


def heads_back(
    place, lengths, index, attn_in, low_q, heads, branch_grad, low_o_grad, tables, shares, out_shares
):
    n_exp, n_tp, _, wide = shares.shape
    blocks = len(LIVE_BLOCKS)
    turned, probs = heads[0], heads[1:]
    groups = KV_HEADS // n_tp
    heads_wide = groups * PER * HD
    arrays = (branch_grad, low_o_grad, turned) + tables + (low_q, attn_in)
    return pl.pallas_call(
        heads_back_kernel,
        in_specs=[IN_SMEM] * 3 + [IN_HBM] * (2 + len(arrays) + blocks),
        out_specs=[IN_VMEM] * 3,
        out_shape=[
            shape((n_tp, LIVE, wide), BF16),
            shape((LIVE, LANES), BF16),
            shape((D + wide, LANES), BF16),
        ],
        scratch_shapes=load_scratch(arrays, LIVE)
        + [
            pltpu.VMEM((n_tp, LANES, wide), BF16),
            pltpu.VMEM((n_tp, heads_wide, D + LANES), BF16),
            pltpu.VMEM((groups, blocks, PER * ROWS, HD), BF16),
            pltpu.VMEM((groups, blocks, PER * ROWS, HD), BF16),
            pltpu.VMEM((groups, LIVE, HD), BF16),
            pltpu.VMEM((groups, LIVE, HD), BF16),
            pltpu.SemaphoreType.DMA((n_tp, n_exp)),
            pltpu.SemaphoreType.DMA((n_tp, n_exp)),
            pltpu.SemaphoreType.DMA((n_tp, blocks)),
        ]
        + [pltpu.VMEM(part.shape, BF16) for part in probs],
        compiler_params=WHOLE_VMEM,
        cost_estimate=cost(2e9, 3e6),
        name="heads_backward",
    )(place, lengths, index, shares, out_shares, *arrays, *probs)


INPUT_LOADS = ("grads", "low_grad", "qkv_down", "tokens", "gains", "branch_grad")


def input_back_kernel(place_ref, shares, *refs):
    count = len(INPUT_LOADS)
    input_grad_ref = refs[count]
    load_sem, w_qkv_s, sum_s, sem = refs[2 * count + 1 :]
    n_exp, n_tp, _, _ = shares.shape
    qkv_rows, _, _ = share_rows(n_exp, 0)
    copies = []
    for z in range(n_tp):
        for e in range(n_exp):
            source = shares.at[e, from_place(place_ref, z, n_tp), :qkv_rows, :]
            target = w_qkv_s.at[z, e * qkv_rows : (e + 1) * qkv_rows, :]
            copies.append(pltpu.make_async_copy(source, target, sem.at[z, e]))
    loads = Loads(INPUT_LOADS, refs[:count], refs[count + 1 : 2 * count + 1], load_sem)
    for copy in copies:
        copy.start()
    input_grad_ref[LIVE:, :] = jnp.zeros((input_grad_ref.shape[0] - LIVE, D), BF16)
    grads = loads["grads"]
    sum_s[...] = dot_nt(loads["low_grad"][...], loads["qkv_down"][...])
    for z in range(n_tp):
        for copy in copies[z * n_exp : (z + 1) * n_exp]:
            copy.wait()
        sum_s[...] += dot_nt(grads[z], w_qkv_s[z])
    tokens, gain = loads["tokens"][...].astype(F32), loads["gains"][0:1, :]
    through = norm_back(tokens, gain, sum_s[...])
    input_grad_ref[:LIVE, :] = (loads["branch_grad"][...].astype(F32) + through).astype(BF16)


def input_back(place, grads, low_grad, qkv_down, tokens, gains, branch_grad, shares):
    n_exp, n_tp, _, wide = shares.shape
    arrays = (grads, low_grad, qkv_down, tokens, gains, branch_grad)
    return pl.pallas_call(
        input_back_kernel,
        in_specs=[IN_SMEM] + [IN_HBM] * (1 + len(arrays)),
        out_specs=IN_VMEM,
        out_shape=shape(tokens.shape, BF16),
        scratch_shapes=load_scratch(arrays, LIVE)
        + [
            pltpu.VMEM((n_tp, D, wide), BF16),
            pltpu.VMEM((LIVE, D), F32),
            pltpu.SemaphoreType.DMA((n_tp, n_exp)),
        ],
        compiler_params=WHOLE_VMEM,
        cost_estimate=cost(2e9, 2e6),
        name="input_backward",
    )(place, shares, *arrays)


FINISH_LOADS = ("output", "qkv_sum", "out_parts")


def finish_kernel(*refs):
    count = len(FINISH_LOADS)
    output_hbm, qkv_down_ref, qkv_up_ref, out_down_ref, out_up_ref = refs[count : count + 5]
    scratch = refs[count + 5 :]
    loads = Loads(FINISH_LOADS, refs[:count], scratch[:count], scratch[count])
    handed_on = pltpu.make_async_copy(loads["output"], output_hbm, scratch[count + 1])
    handed_on.start()
    qkv_sum = loads["qkv_sum"]
    qkv_down_ref[...] = qkv_sum[:D, :].astype(F32)
    for at in range(0, qkv_up_ref.shape[1], LANES):
        qkv_up_ref[:, at : at + LANES] = qkv_sum[D + at : D + at + LANES, :].astype(F32)
    out_parts = loads["out_parts"]
    for at in range(0, out_parts.shape[1], LANES):
        total = out_parts[0, at : at + LANES, :].astype(F32)
        for part in range(1, out_parts.shape[0]):
            total += out_parts[part, at : at + LANES, :].astype(F32)
        if at < D:
            out_up_ref[:, at : at + LANES] = total
        else:
            out_down_ref[at - D : at - D + LANES, :] = total
    handed_on.wait()


def finish(output, out_parts, qkv_sum):
    arrays = (output, qkv_sum, out_parts)
    return pl.pallas_call(
        finish_kernel,
        in_specs=[IN_HBM] * len(arrays),
        out_specs=[IN_HBM] + [IN_VMEM] * 4,
        out_shape=[
            shape(output.shape, BF16),
            shape((D, LANES), F32),
            shape((LANES, qkv_sum.shape[0] - D), F32),
            shape((out_parts.shape[1] - D, LANES), F32),
            shape((LANES, D), F32),
        ],
        scratch_shapes=load_scratch(arrays) + [pltpu.SemaphoreType.DMA(())],
        compiler_params=WHOLE_VMEM,
        cost_estimate=cost(0, 6e6),
        name="finish",
    )(*arrays)


def from_tp(share, count):
    around = [share]
    for shift in range(1, count):
        around.append(
            lax.ppermute(share, "tp", [(at, (at + shift) % count) for at in range(count)])
        )
    return around


def from_place(place_ref, z, count):
    return lax.rem(place_ref[0] - z + count, count)


def kernel_body(
    tokens, attn_gain, moe_gain, w_qkv, w_out, w_router, w_gate, w_up, w_down, qkv_down, qkv_up,
    out_down, out_up, lengths, adapter_index, loss_mask, routes, upstream,
):
    n_exp = lax.axis_size("exp")
    n_tp = lax.axis_size("tp")
    exp_place = lax.axis_index("exp").astype(jnp.int32).reshape(1)
    tp_place = lax.axis_index("tp").astype(jnp.int32).reshape(1)
    tables = turn_tables(tokens.shape[0])
    gains = jnp.stack([attn_gain, moe_gain])

    own_experts, own_qkv = pack(exp_place, w_gate, w_up, w_down, w_qkv, qkv_up, n_exp)
    weights = lax.all_gather(own_experts, "exp", axis=0, tiled=True)
    z_qkv = from_tp(own_qkv, n_tp)
    inputs, _ = lax.optimization_barrier((tokens, own_qkv))
    attn_in, low_q, head, base, own_out = forward(
        exp_place, lengths, adapter_index, inputs, gains, w_qkv, qkv_down, qkv_up, w_out, out_down,
        tables, n_exp,
    )
    live_loss = lax.slice_in_dim(loss_mask, 0, LIVE)
    cot = jnp.where(live_loss[:, None] > 0, upstream[:LIVE], jnp.zeros((), BF16))
    expert = jnp.arange(w_router.shape[1], dtype=jnp.int32)
    routed = jnp.any(routes[:, :, None] == expert[None, None, :], axis=1)
    bias = jnp.where(routed, 0.0, -1e30).astype(F32)
    base, z_qkv = lax.optimization_barrier((base, z_qkv))
    z_qkv = jnp.stack(z_qkv)
    base = lax.psum(base, "tp")
    near_out = lax.ppermute(own_out, "tp", [(at, at ^ 1) for at in range(n_tp)])
    z_qkv, _, near_out, cot, bias = lax.optimization_barrier(
        (z_qkv, weights, near_out, cot, bias)
    )
    pair_out, _ = lax.optimization_barrier((jnp.stack([own_out, near_out]), base))
    far_out = lax.ppermute(pair_out, "tp", [(at, at ^ 2) for at in range(n_tp)])
    qkv_shares = lax.all_gather(z_qkv, "exp", axis=0)

    residual, hidden, normed_part = experts_both(
        lengths, adapter_index, tokens, base, out_up, gains, w_router, bias, cot, weights
    )
    normed_part, far_out = lax.optimization_barrier((normed_part, far_out))
    z_out = jnp.concatenate([pair_out, far_out])
    normed_grad = lax.psum(normed_part, "tp")
    z_out, _ = lax.optimization_barrier((z_out, qkv_shares))
    out_shares = lax.all_gather(z_out, "exp", axis=0)
    late_in, _ = lax.optimization_barrier((attn_in, normed_part))
    heads = prepare(tp_place, lengths, late_in, low_q, tables, qkv_shares)

    moe_part, normed_grad, _ = lax.optimization_barrier(
        (combine(tp_place, hidden, residual, weights), normed_grad, heads[0])
    )
    output = lax.psum(moe_part, "tp")
    branch_grad, low_o_grad, out_part = branch_back(
        lengths, adapter_index, residual, base, normed_grad, cot, gains, out_up, head
    )
    out_parts = lax.all_gather(out_part, "exp", axis=0)
    grads, low_grad, qkv_part = heads_back(
        tp_place, lengths, adapter_index, attn_in, low_q, heads, branch_grad, low_o_grad, tables,
        qkv_shares, out_shares,
    )
    share = qkv_part.shape[0] // n_exp
    parts = lax.all_to_all(qkv_part.reshape(n_exp, share, LANES), "exp", 0, 0, tiled=True)
    input_grad = input_back(
        tp_place, grads, low_grad, qkv_down, tokens, gains, branch_grad, qkv_shares
    )
    parts, input_grad = lax.optimization_barrier((parts, input_grad))
    qkv_sum = jnp.sum(parts.astype(F32), axis=0).astype(BF16)
    qkv_sum = lax.all_gather(qkv_sum, "exp", axis=0, tiled=True)
    out_parts, output, _ = lax.optimization_barrier((out_parts, output, qkv_sum))
    output, *adapters = finish(output, out_parts, qkv_sum)
    return (output, input_grad) + tuple(adapters)


def product(left_m, right_m):
    return jnp.dot(left_m, right_m, preferred_element_type=jnp.float32)


def contract(einsum_form, left_m, right_m):
    return jnp.einsum(einsum_form, left_m, right_m, preferred_element_type=jnp.float32)


def rms_norm(vectors, gain_vec):
    inv_root = lax.rsqrt(jnp.mean(vectors * vectors, axis=-1, keepdims=True) + EPS)
    return vectors * inv_root * gain_vec


def rms_norm_back(vectors, gain_vec, upstream_grad):
    inv_root = lax.rsqrt(jnp.mean(vectors * vectors, axis=-1, keepdims=True) + EPS)
    weighted = upstream_grad * gain_vec
    return inv_root * weighted - vectors * (inv_root * inv_root * inv_root) * jnp.mean(
        vectors * weighted, axis=-1, keepdims=True
    )


def layout(length_row, index_row):
    places = jnp.arange(TOK_DEV, dtype=jnp.int32)
    doc_ends = jnp.cumsum(length_row)
    doc_starts = doc_ends - length_row
    member = (places[:, None] >= doc_starts[None, :]) & (places[:, None] < doc_ends[None, :])
    occupied = jnp.any(member, axis=1)
    position = jnp.sum(jnp.where(member, places[:, None] - doc_starts[None, :], 0), axis=1)
    owner_doc = jnp.sum(jnp.where(member, jnp.arange(DOCS, dtype=jnp.int32)[None, :], 0), axis=1)
    doc_ident = jnp.where(occupied, owner_doc, DOCS + places)
    chosen = jnp.sum(jnp.where(member, index_row[None, :], 0), axis=1)
    adapter_pick = occupied[:, None] & (
        chosen[:, None] == jnp.arange(ADAPTERS, dtype=jnp.int32)[None, :]
    )
    rank_mask = jnp.repeat(jnp.where(adapter_pick, 1.0, 0.0).astype(jnp.float32), RANK, axis=1)
    return (occupied, position, doc_ident, rank_mask)


def angles(position):
    half_width = HD // 2
    frequency = jnp.exp(-math.log(ROPE_BASE) * jnp.arange(half_width, dtype=jnp.float32) * 2.0 / HD)
    turned = position.astype(jnp.float32)[:, None] * frequency[None, :]
    return (jnp.cos(turned), jnp.sin(turned))


def rotate(vectors, cosine, sine_table):
    half_width = vectors.shape[-1] // 2
    front_half = vectors[..., :half_width]
    back_half = vectors[..., half_width:]
    return jnp.concatenate(
        [
            front_half * cosine - back_half * sine_table,
            back_half * cosine + front_half * sine_table,
        ],
        axis=-1,
    )


def moe(normed, cot_low, gates, gate_up, down):
    width = down.shape[1]
    both = contract("td,edf->tef", normed, gate_up)
    pre_gate = both[:, :, :width]
    pre_up = both[:, :, width:]
    sigmoid_g = jax.nn.sigmoid(pre_gate)
    activated = pre_gate * sigmoid_g
    hidden = (activated * pre_up).astype(jnp.bfloat16).astype(jnp.float32)
    inner_raw = contract("td,efd->tef", cot_low, down)
    gate_part = jnp.sum(hidden * inner_raw, axis=-1)
    moe_part = contract("tef,efd->td", (gates[:, :, None] * hidden).astype(jnp.bfloat16), down)
    inner_grad = inner_raw * gates[:, :, None]
    grad_gate = inner_grad * pre_up * sigmoid_g * (1.0 + pre_gate * (1.0 - sigmoid_g))
    grad_up = inner_grad * activated
    grad_both = jnp.concatenate([grad_gate, grad_up], axis=2).astype(jnp.bfloat16)
    normed_part = contract("tef,edf->td", grad_both, gate_up)
    return (moe_part, gate_part, normed_part)


def body(
    tokens,
    attn_gain,
    moe_gain,
    w_qkv,
    w_out,
    w_router,
    w_gate,
    w_up,
    w_down,
    qkv_down,
    qkv_up,
    out_down,
    out_up,
    lengths,
    adapter_index,
    loss_mask,
    routes,
    upstream,
):
    n_exp = lax.axis_size("exp")
    groups = KV_HEADS // lax.axis_size("tp")
    per_group = HEADS // KV_HEADS
    experts = EXP_DEV * n_exp
    gate_up = lax.all_gather(jnp.concatenate([w_gate, w_up], axis=2), "exp", axis=0, tiled=True)
    down = lax.all_gather(w_down, "exp", axis=0, tiled=True)
    block_rows = min(512, TOK_DEV)
    blocks = TOK_DEV // block_rows
    score_scale = 1.0 / math.sqrt(HD)
    places = jnp.arange(TOK_DEV, dtype=jnp.int32)
    occupied, position, doc_ident, rank_mask = layout(lengths[0], adapter_index[0])
    mask_low = rank_mask.astype(jnp.bfloat16)
    cosine, sine_table = angles(position)
    inputs = tokens.astype(jnp.float32)
    attn_in = rms_norm(inputs, attn_gain).astype(jnp.bfloat16)
    low_q = (product(attn_in, qkv_down) * rank_mask).astype(jnp.bfloat16)
    projected = (product(attn_in, w_qkv) + product(low_q, qkv_up)).reshape(
        TOK_DEV, groups, per_group + 2, HD
    )
    query_rows = rotate(
        projected[:, :, :per_group], cosine[:, None, None], sine_table[:, None, None]
    ).astype(jnp.bfloat16)
    key_rows = rotate(projected[:, :, per_group], cosine[:, None], sine_table[:, None]).astype(
        jnp.bfloat16
    )
    val_rows = projected[:, :, per_group + 1].astype(jnp.bfloat16)

    def masked_scores(q_blk, q_place, q_ident):
        scores = contract("qgrd,kgd->grqk", q_blk, key_rows) * score_scale
        allowed = (q_ident[:, None] == doc_ident[None, :]) & (places[None, :] <= q_place[:, None])
        return jnp.where(allowed, scores, -1e30)

    def attend(pieces):
        q_blk, q_place, q_ident = pieces
        scores = masked_scores(q_blk, q_place, q_ident)
        row_max = jnp.max(scores, axis=-1, keepdims=True)
        lifted = jnp.exp(scores - row_max)
        row_total = jnp.sum(lifted, axis=-1, keepdims=True)
        weights = (lifted / row_total).astype(jnp.bfloat16)
        return (
            contract("grqk,kgd->qgrd", weights, val_rows),
            row_max[..., 0] + jnp.log(row_total[..., 0]),
        )

    query_blocks = query_rows.reshape(blocks, block_rows, groups, per_group, HD)
    place_blocks = places.reshape(blocks, block_rows)
    ident_blocks = doc_ident.reshape(blocks, block_rows)
    attended, log_totals = lax.map(attend, (query_blocks, place_blocks, ident_blocks))
    head_rows = attended.reshape(TOK_DEV, groups * per_group * HD).astype(jnp.bfloat16)
    attn_base, low_rank = (
        lax.psum(product(head_rows, w_out).astype(jnp.bfloat16), "tp").astype(jnp.float32),
        lax.psum((product(head_rows, out_down) * rank_mask).astype(jnp.bfloat16), "tp").astype(
            jnp.float32
        ),
    )
    low_o = low_rank.astype(jnp.bfloat16)
    residual = inputs + attn_base + product(low_o, out_up)
    normed = rms_norm(residual, moe_gain).astype(jnp.bfloat16)
    logits = product(normed, w_router)
    one_hot = routes[:, :, None] == jnp.arange(experts, dtype=jnp.int32)[None, None, :]
    routed = jnp.any(one_hot, axis=1)
    gates = jax.nn.softmax(jnp.where(routed, logits, -1e30), axis=-1)
    live_mask = jnp.where(occupied & (loss_mask > 0), 1.0, 0.0).astype(jnp.float32)
    cotangent = upstream.astype(jnp.float32) * live_mask[:, None]
    cot_low = cotangent.astype(jnp.bfloat16)
    moe_part, gate_part, normed_part = moe(normed, cot_low, gates, gate_up, down)
    logit_grad = (
        gates * (gate_part - jnp.sum(gates * gate_part, axis=-1, keepdims=True))
    ).astype(jnp.bfloat16)
    normed_part = (normed_part + product(logit_grad, w_router.T)).astype(jnp.bfloat16)
    normed_sum = lax.psum(normed_part, "tp")
    normed_sum, moe_part = lax.optimization_barrier((normed_sum, moe_part.astype(jnp.bfloat16)))
    normed_grad = normed_sum.astype(jnp.float32)
    moe_out = lax.psum(moe_part, "tp").astype(jnp.float32)
    output = (residual + moe_out).astype(jnp.bfloat16)
    residual_grad = cotangent + rms_norm_back(residual, moe_gain, normed_grad)
    branch_grad = residual_grad.astype(jnp.bfloat16)
    low_o_grad = product(branch_grad, out_up.T).astype(jnp.bfloat16) * mask_low
    out_up_part = contract("tr,td->rd", low_o, branch_grad)
    head_grad = (product(branch_grad, w_out.T) + product(low_o_grad, out_down.T)).astype(
        jnp.bfloat16
    )
    out_down_part = contract("tc,tr->cr", head_rows, low_o_grad)
    grad_blocks = head_grad.reshape(blocks, block_rows, groups, per_group, HD)

    def attend_back(carried, pieces):
        key_acc, val_acc = carried
        q_blk, q_place, q_ident, lse_blk, g_blk = pieces
        weights = jnp.exp(masked_scores(q_blk, q_place, q_ident) - lse_blk[..., None])
        weight_grad = contract("qgrd,kgd->grqk", g_blk, val_rows)
        score_grad = (
            weights * (weight_grad - jnp.sum(weights * weight_grad, axis=-1, keepdims=True))
        ).astype(jnp.bfloat16)
        query_grad = contract("grqk,kgd->qgrd", score_grad, key_rows) * score_scale
        key_acc = key_acc + contract("grqk,qgrd->kgd", score_grad, q_blk) * score_scale
        val_acc = val_acc + contract("grqk,qgrd->kgd", weights.astype(jnp.bfloat16), g_blk)
        return ((key_acc, val_acc), query_grad)

    zero_acc = jnp.zeros((TOK_DEV, groups, HD), jnp.float32)
    (key_grad, val_grad), query_grad = lax.scan(
        attend_back,
        (zero_acc, zero_acc),
        (query_blocks, place_blocks, ident_blocks, log_totals, grad_blocks),
    )
    query_grad = rotate(
        query_grad.reshape(TOK_DEV, groups, per_group, HD),
        cosine[:, None, None],
        -sine_table[:, None, None],
    )
    key_grad = rotate(key_grad, cosine[:, None], -sine_table[:, None])
    projected_grad = (
        jnp.concatenate([query_grad, key_grad[:, :, None], val_grad[:, :, None]], axis=2)
        .reshape(TOK_DEV, -1)
        .astype(jnp.bfloat16)
    )
    qkv_up_part = contract("tr,tc->rc", low_q, projected_grad)
    attn_grad, low_q_grad = (
        lax.psum(contract("tc,dc->td", projected_grad, w_qkv).astype(jnp.bfloat16), "tp").astype(
            jnp.float32
        ),
        lax.psum(contract("tc,rc->tr", projected_grad, qkv_up).astype(jnp.bfloat16), "tp").astype(
            jnp.float32
        ),
    )
    low_q_grad = low_q_grad.astype(jnp.bfloat16) * mask_low
    attn_grad = attn_grad + contract("tr,dr->td", low_q_grad, qkv_down)
    qkv_down_part = contract("td,tr->dr", attn_in, low_q_grad)
    input_grad = (residual_grad + rms_norm_back(inputs, attn_gain, attn_grad)).astype(jnp.bfloat16)
    summed = (
        lax.psum(qkv_down_part.astype(jnp.bfloat16), "exp").astype(jnp.float32),
        lax.psum(qkv_up_part.astype(jnp.bfloat16), "exp").astype(jnp.float32),
        lax.psum(out_down_part.astype(jnp.bfloat16), "exp").astype(jnp.float32),
        lax.psum(out_up_part.astype(jnp.bfloat16), "exp").astype(jnp.float32),
    )
    return (output, input_grad, summed[0], summed[1], summed[2], summed[3])


def kernels_fit(mesh):
    n_exp, n_tp = mesh.shape["exp"], mesh.shape["tp"]
    groups = KV_HEADS // n_tp
    return groups % 2 == 0 and FF // n_tp == LANES and LANES // n_exp % 16 == 0


def solution(mesh):
    placed = (
        P("exp", None),
        P(),
        P(),
        P(None, "tp"),
        P("tp", None),
        P(),
        P("exp", None, "tp"),
        P("exp", None, "tp"),
        P("exp", "tp", None),
        P(),
        P(None, "tp"),
        P("tp", None),
        P(),
        P("exp", None),
        P("exp", None),
        P("exp"),
        P("exp", None),
        P("exp", None),
    )
    return jax.shard_map(
        kernel_body if kernels_fit(mesh) else body,
        mesh=mesh,
        in_specs=placed,
        out_specs=(P("exp", None), P("exp", None), P(), P(None, "tp"), P("tp", None), P()),
        check_vma=False,
    )
```
